32 devices in a mesh: grp: 2 (over y), sec: 16 (over z, x, core).
Axes of the slice: x: 2, y: 2, z: 4, core: 2. Of those that a mesh axis runs over, the one named last changes fastest.
Arguments:
- green: bfloat16 [16, 4, 1024, 1024], P('sec', 'grp'), parts along dimension 1, may hold values from -0.1875 to 0.1875
- injected: bfloat16 [16, 4, 1024, 128], P('sec', 'grp'), parts along dimension 1, may hold values from -0.8984375 to 0.8984375
- coupling: bfloat16 [16, 1024, 256], P('sec'), may hold values from -0.4375 to 0.4375
- pattern: int32 [16, 8, 2], P('sec'), may hold values 0 or 1
- owner: int32 [256, 1], P('sec'), may hold values from 0 to 15; in each aligned block of 16 rows (0 to 15, 16 to 31, ...) at most 2 rows name the same one
- pair_blocks: int32 [256, 2], P('sec'), may hold values from 0 to 31
Outputs:
- waves: bfloat16 [16, 4, 1024, 128], P('sec', 'grp'), parts along dimension 1
The draws below stay inside these ranges and needn't reach their ends.
There are 2 independent parts, one for each index of `grp`. The reference program is written for one: setup_inputs(seed, part) draws one part's arguments, and reference() takes and returns one part's arrays. A program takes and returns all parts, laid end to end along the dimension named above; an argument that names none is the same for every part. Nothing has to cross between parts.
Inputs may be any that keep to these rules, and one draw needn't show every extreme that they name: Among the 16 rows of one slab no owner appears more than 2 times.
All inputs are finite; a program needn't handle non-finite values. No bound on the sum of `pattern` on one device may be relied on, other than what follows from the above.
Results may differ from the reference program's by a relative error of at most 0.0057.
Values may be sent and summed in bfloat16 or wider, within the bound.
No kernel may reach another device: no remote copies, remote signals or barrier semaphores. Data moves between devices by JAX's collectives and lax.ppermute only.
A program may use at most 256 MiB of HBM per device.

```python
import math
import jax
import jax.numpy as jnp
import numpy as np
from jax import lax

ORB = 1024
FACE = 256
COLS = 128
BLK = 32
CAP = 2
ENERG = 2
SLABS = 16
PAIRS = 16


def place_ends(drawn, stream_key, smallest, high):
    shape = drawn.shape
    index_at = [jax.random.randint(jax.random.fold_in(stream_key, axis), (), 0, shape[axis]) for axis in range(len(shape))]
    drawn = drawn.at[tuple(index_at)].set(smallest)
    longest = shape.index(max(shape))
    index_at[longest] = (index_at[longest] + 1) % shape[longest]
    return drawn.at[tuple(index_at)].set(high)


def steps_of(stream_key, extent, shards, least, top_value):
    level, own = 1.0, jax.random.fold_in(stream_key, 6)
    for axis_at, blocks in shards:
        draws = jnp.exp(jax.random.uniform(jax.random.fold_in(own, axis_at), (blocks,), jnp.float32, least / len(shards), top_value / len(shards)))
        level = level * jnp.repeat(draws, extent[axis_at] // blocks).reshape([-1 if axis == axis_at else 1 for axis in range(len(extent))])
    return level


def deal_out(own_key, own, number, rows, amount, top, most, skew):
    sequence = jax.random.permutation(own_key, amount)
    crowded, ordinary = load_shares(amount, rows * top, most, skew, True), load_shares(amount, rows * top, most, skew, False)
    places = jnp.arange(amount)

    def named(sizes, turn):
        used = int((sizes > 0).sum())
        fixed = max(1, used // 4)
        moved = fixed + (places - fixed + turn * (used - fixed)) % max(1, amount - fixed)
        return jnp.zeros((amount,), jnp.int32).at[sequence[jnp.where(places < fixed, places, moved)]].set(jnp.asarray(sizes, jnp.int32))

    sizes = jnp.where(number % 4 == 0, named(crowded, number // 4), named(ordinary, number - number // 4 - 1))
    mixed = jax.random.permutation(jax.random.fold_in(own, 3), amount)
    source_of, sink = mixed[0:amount // 2 * 2:2], mixed[1:amount // 2 * 2:2]
    room = jnp.minimum(sizes[source_of] - 1, most - sizes[sink]) // 2
    room = jnp.where((source_of == sequence[0]) | (sink == sequence[0]) | (sizes[sink] == 0), 0, jnp.maximum(room, 0))
    moved = jax.random.randint(jax.random.fold_in(own, 4), (amount // 2,), 0, 1 << 20) % (room + 1)
    sizes = sizes.at[source_of].add(-moved).at[sink].add(moved)
    members = jnp.searchsorted(jnp.cumsum(sizes), jnp.arange(rows * top), side="right").astype(jnp.int32)
    table = members.reshape(top, rows).T
    table = table[jax.random.permutation(jax.random.fold_in(own, 1), rows)]
    turn = jax.random.randint(jax.random.fold_in(own, 2), (rows, 1), 0, top)
    return jnp.take_along_axis(table, (jnp.arange(top)[None, :] + turn) % top, axis=1)


def load_shares(count, total, reach, skew, full):
    loads = [(1 << 20) // math.isqrt(grade ** skew) + 1 for grade in range(1, count + 1)]
    largest = reach if full else min(reach, max(-(-total // count), total * loads[0] // sum(loads)))
    least = 1 if total - largest >= count - 1 else 0
    holding, rest = [largest] + [least] * (count - 1), total - largest - least * (count - 1)
    while rest > 0:
        movable = [i for i in range(1, count) if holding[i] < largest] or [i for i in range(1, count) if holding[i] < reach]
        pool, budget = sum([loads[i] for i in movable]), rest
        for i in movable:
            addition = min(reach - holding[i], max(1, budget * loads[i] // pool), rest)
            holding[i] = holding[i] + addition
            rest = rest - addition
    return np.array(holding)


def centred(rng, extent, spread, bound, split=(), held_as=jnp.bfloat16):
    entries = spread * jax.random.normal(rng, extent, jnp.float32)
    if split:
        entries = entries * steps_of(rng, extent, split, -0.22, 0.18)
    return jnp.clip(entries, -bound, bound).astype(held_as)


def setup_inputs(seed: int = 0, part: int = 0) -> dict:
    splits = jax.random.split(jax.random.key(seed), 7)
    own_keys = jax.random.split(jax.random.fold_in(splits[6], part), 7)
    green = centred(own_keys[0], (SLABS, ENERG, ORB, ORB), ORB ** -0.5, 0.1875, ((0, 16),))
    injected = centred(own_keys[1], (SLABS, ENERG, ORB, COLS), 0.15, 0.8984375, ((0, 16),))
    coupling = centred(splits[2], (SLABS, ORB, FACE), (FACE * 49 // 64) ** -0.5, 0.4375, ((0, 16),))
    pattern = place_ends((jax.random.randint(splits[3], (SLABS, 8, 2), 0, 4) < 3).astype(jnp.int32), jax.random.fold_in(splits[3], 1), 0, 1)
    owner_keys = jax.random.split(jax.random.fold_in(splits[4], 1), (SLABS * PAIRS) // PAIRS)
    owner_turns = jax.random.permutation(jax.random.fold_in(splits[4], 3), (SLABS * PAIRS) // PAIRS)
    owner = jax.vmap(lambda own, number: deal_out(jax.random.fold_in(splits[4], 2), own, number, PAIRS, SLABS, 1, CAP, 2))(owner_keys, owner_turns).reshape((SLABS * PAIRS, 1))
    pair_blocks = place_ends(jax.random.randint(splits[5], (SLABS * PAIRS, 2), 0, ORB // BLK), jax.random.fold_in(splits[5], 1), 0, (ORB // BLK) - 1).astype(jnp.int32)
    return dict(green=green, injected=injected, coupling=coupling, pattern=pattern, owner=owner, pair_blocks=pair_blocks)


HIGH = lax.Precision.HIGHEST


def expand_pattern(pattern_slab):
    tile_rows = jnp.repeat(pattern_slab, ORB // 8, axis=0)
    return jnp.repeat(tile_rows, FACE // 2, axis=1)


def reference(green, injected, coupling, pattern, owner, pair_blocks):
    nblock = ORB // BLK
    pair_grid = pair_blocks.reshape(SLABS, PAIRS, 2)

    def slab_parts(items):
        green_slab, inject_slab, blocks_slab = items
        tiled = green_slab.reshape(ENERG, nblock, BLK, ORB)
        rows = jnp.take(tiled, blocks_slab[:, 0], axis=1).astype(jnp.float32)
        parts = jnp.einsum('epbo,eok->pebk', rows, inject_slab.astype(jnp.float32), precision=HIGH)
        return parts.astype(jnp.bfloat16)

    parts = lax.map(slab_parts, (green, injected, pair_grid))
    parts = parts.reshape(SLABS * PAIRS, ENERG, BLK, COLS).astype(jnp.float32)
    placed = jnp.zeros((SLABS, nblock, ENERG, BLK, COLS), jnp.float32)
    placed = placed.at[owner[:, 0], pair_blocks[:, 1]].add(parts)
    placed = jnp.transpose(placed, (0, 2, 1, 3, 4)).reshape(SLABS, ENERG, ORB, COLS)
    source = (injected.astype(jnp.float32) + placed).astype(jnp.bfloat16)

    def sweep(carry, items):
        green_slab, source_slab, couple_slab, pattern_slab = items
        couple = jnp.where(expand_pattern(pattern_slab) == 1, couple_slab, jnp.zeros_like(couple_slab))
        green_wide = green_slab.astype(jnp.float32)
        prop_full = jnp.einsum('eij,jf->eif', green_wide, couple.astype(jnp.float32), precision=HIGH)
        image = jnp.einsum('eij,ejk->eik', green_wide, source_slab.astype(jnp.float32), precision=HIGH)
        wave = jnp.einsum('eif,efk->eik', prop_full, carry, precision=HIGH) + image
        return wave[:, ORB - FACE:, :], wave.astype(jnp.bfloat16)

    start = jnp.zeros((ENERG, FACE, COLS), jnp.float32)
    final_face, waves = lax.scan(sweep, start, (green, source, coupling, pattern))
    return waves
```

```python
import jax
import jax.numpy as jnp
from jax import lax
from jax.sharding import PartitionSpec as P

BLK = 32
CAP = 2
GROUP = 4
HEAD = 16

HIGH = lax.Precision.HIGHEST


def pack(cols):
    half = cols.shape[-2] // 2
    return jnp.concatenate([cols[..., :half, :], cols[..., half:, :]], axis=-1)


def unpack(packed):
    half = packed.shape[-1] // 2
    return jnp.concatenate([packed[..., :half], packed[..., half:]], axis=-2)


def outgoing_pairs(green, inject, owner, blocks, sections):
    energies, orbitals, _ = green.shape
    columns = inject.shape[2]
    count = owner.shape[0]
    order = jnp.arange(count, dtype=jnp.int32)
    same = owner[:, None] == owner[None, :]
    rank = jnp.sum((same & (order[None, :] < order[:, None])).astype(jnp.int32), axis=1)
    slot = owner * CAP + rank
    full = jnp.einsum("eij,ejk->eik", green, inject, preferred_element_type=jnp.float32)
    full = full.astype(jnp.bfloat16).reshape(energies, orbitals // BLK, BLK, columns)
    parts = jnp.take(full, blocks[:, 0], axis=1)
    parts = jnp.swapaxes(parts, 0, 1)
    packets = jnp.zeros((sections * CAP, energies, BLK, columns), jnp.bfloat16).at[slot].set(parts)
    heads = jnp.full((sections * CAP,), -1, jnp.int32).at[slot].set(blocks[:, 1])
    heads = heads.reshape(sections, 1, CAP).astype(jnp.bfloat16)
    heads = jnp.pad(heads, ((0, 0), (0, HEAD - 1), (0, columns - CAP)))
    packets = packets.reshape(sections, CAP * energies * BLK, columns)
    return jnp.concatenate([packets, heads], axis=1)


def placed_source(inject, received):
    energies, orbitals, columns = inject.shape
    sections = received.shape[0]
    rows = CAP * energies * BLK
    targets = received[:, rows, :CAP].astype(jnp.int32).reshape(-1)
    data = received[:, :rows].reshape(sections * CAP, energies, BLK, columns)
    levels = jnp.arange(orbitals // BLK, dtype=jnp.int32)
    table = (targets[:, None] == levels[None, :]).astype(jnp.bfloat16)
    placed = jnp.einsum("sn,sebk->enbk", table, data, preferred_element_type=jnp.float32)
    placed = placed.reshape(energies, orbitals, columns)
    return (inject.astype(jnp.float32) + placed).astype(jnp.bfloat16)


def mm(a, b):
    return jnp.dot(a, b, precision=HIGH, preferred_element_type=jnp.float32)


def plane_shift(sections, k):
    return [(s, s // GROUP * GROUP + (s % GROUP + k) % GROUP) for s in range(sections)]


def up_shift(sections, k):
    return [(s, s + GROUP * k) for s in range(sections - GROUP * k)]


def in_plane(items, here, sections):
    got = [lax.dynamic_index_in_dim(items, here, 0, False)]
    for k in range(1, GROUP):
        out = lax.dynamic_index_in_dim(items, (here + k) % GROUP, 0, False)
        got.append(lax.ppermute(out, "sec", plane_shift(sections, k)))
    got = jnp.stack(got)
    return jnp.take(got, (here - jnp.arange(GROUP)) % GROUP, axis=0)


def from_below(total_map, total_source, sections):
    planes = sections // GROUP
    if planes <= 4:
        below = [lax.ppermute(total_source, "sec", up_shift(sections, k)) for k in range(1, planes)]
        maps = [lax.ppermute(total_map, "sec", up_shift(sections, k)) for k in range(1, planes - 1)]
        state = unpack(below[-1]).astype(jnp.float32)
        for k in range(planes - 3, -1, -1):
            state = unpack(below[k]).astype(jnp.float32) + mm(maps[k], state)
        return state
    shift = lax.ppermute(unpack(total_source).astype(jnp.float32), "sec", up_shift(sections, 1))
    joined = lax.ppermute(total_map, "sec", up_shift(sections, 1))
    stride = 1
    while stride < planes:
        other = lax.ppermute(shift, "sec", up_shift(sections, stride))
        other_map = lax.ppermute(joined, "sec", up_shift(sections, stride))
        shift = shift + mm(joined, other)
        joined = mm(joined, other_map)
        stride *= 2
    return shift


def per_device(green, injected, coupling, pattern, owner, pair_blocks):
    sections = lax.axis_size("sec")
    here = lax.axis_index("sec") % GROUP
    green = green[0]
    inject = injected[0]
    energies, orbitals, _ = green.shape
    columns = inject.shape[2]
    face = coupling.shape[2]
    split = GROUP // energies

    outgoing = outgoing_pairs(green, inject, owner[:, 0], pair_blocks, sections)
    received = lax.all_to_all(outgoing, "sec", split_axis=0, concat_axis=0, tiled=True)

    tile_rows = jnp.repeat(pattern[0], orbitals // 8, axis=0)
    present = jnp.repeat(tile_rows, face // 2, axis=1)
    couple = jnp.where(present == 1, coupling[0], jnp.zeros_like(coupling[0]))
    prop = jnp.einsum("eij,jf->eif", green, couple, preferred_element_type=jnp.float32)
    face_map = prop[:, orbitals - face :, :]
    maps = in_plane(jnp.repeat(face_map, split, axis=0), here, sections)
    upto = [maps[0]]
    for j in range(1, GROUP):
        upto.append(mm(maps[j], upto[-1]))
    after = [maps[GROUP - 1]]
    for j in range(GROUP - 2, 0, -1):
        after.append(mm(after[-1], maps[j]))

    source = placed_source(inject, received)
    face_source = jnp.einsum("eij,ejk->eik", green[:, orbitals - face :], source, preferred_element_type=jnp.float32)
    quarters = face_source.astype(jnp.bfloat16).reshape(energies, face, split, columns // split)
    quarters = pack(jnp.swapaxes(quarters, 1, 2).reshape(GROUP, face, columns // split))
    shifts = unpack(in_plane(quarters, here, sections)).astype(jnp.float32)
    total = shifts[GROUP - 1]
    for j in range(GROUP - 1):
        total = total + mm(after[GROUP - 2 - j], shifts[j])
    base = from_below(upto[GROUP - 1], pack(total).astype(jnp.bfloat16), sections)
    local = [jnp.zeros_like(total), shifts[0]]
    for j in range(1, GROUP - 1):
        local.append(shifts[j] + mm(maps[j], local[-1]))
    entering = jnp.stack([base] + [local[j] + mm(upto[j - 1], base) for j in range(1, GROUP)])
    arrived = unpack(in_plane(pack(entering).astype(jnp.bfloat16), here, sections))
    incoming = arrived.reshape(energies, split, face, columns // split)
    incoming = jnp.swapaxes(incoming, 1, 2).reshape(energies, face, columns)

    image = jnp.einsum("eij,ejk->eik", green, source, preferred_element_type=jnp.float32)
    wave = jnp.einsum("eif,efk->eik", prop.astype(jnp.bfloat16), incoming, preferred_element_type=jnp.float32) + image
    return wave.astype(jnp.bfloat16)[None]


def solution(mesh):
    in_specs = (
        P("sec", "grp", None, None),
        P("sec", "grp", None, None),
        P("sec", None, None),
        P("sec", None, None),
        P("sec", None),
        P("sec", None),
    )
    out_specs = P("sec", "grp", None, None)
    return jax.shard_map(
        per_device, mesh=mesh, in_specs=in_specs, out_specs=out_specs, check_vma=False
    )
```

```python
import functools

import jax
import jax.numpy as jnp
from jax import lax
from jax.experimental import pallas as pl
from jax.experimental.pallas import tpu as pltpu
from jax.sharding import PartitionSpec as P

BLK = 32
CAP = 2
GROUP = 4
HEAD = 16

HIGH = lax.Precision.HIGHEST
F32 = jnp.float32
BF16 = jnp.bfloat16
VMEM_BYTES = 40 * 1024 * 1024

IN_VMEM = pl.BlockSpec(memory_space=pltpu.VMEM)
IN_SMEM = pl.BlockSpec(memory_space=pltpu.SMEM)
IN_PLACE = pl.BlockSpec(memory_space=pl.ANY)


def shape(*dims, dtype=BF16):
    return jax.ShapeDtypeStruct(dims, dtype)


def call(body, name, ins, outs, scratch, flops, moved):
    return pl.pallas_call(
        body,
        name=name,
        in_specs=ins,
        out_shape=outs,
        out_specs=jax.tree.map(lambda _: IN_VMEM, outs),
        scratch_shapes=scratch,
        compiler_params=pltpu.CompilerParams(vmem_limit_bytes=VMEM_BYTES),
        cost_estimate=pl.CostEstimate(flops=flops, bytes_accessed=moved, transcendentals=0),
    )


def place():
    return lax.axis_index("sec") % GROUP


def dot(a, b):
    return jnp.dot(a, b, preferred_element_type=F32)


def dot_wide(a, b):
    return jnp.dot(a, b, precision=HIGH, preferred_element_type=F32)


def two_parts(x):
    high = x.astype(BF16)
    return high, (x - high.astype(F32)).astype(BF16)


def left_lanes(x):
    return lax.broadcasted_iota(jnp.int32, x.shape, 1) < x.shape[1] // 2


def swap_lanes(x):
    return pltpu.roll(x, x.shape[1] // 2, 1)


def pack(tall):
    half = tall.shape[0] // 2
    top, low = tall[:half], tall[half:]
    return jnp.where(left_lanes(top), top, swap_lanes(low))


def unpack(packed):
    return jnp.concatenate([packed, swap_lanes(packed)], axis=0)


def copies(green, held, sem, rows, steps):
    energies = green.shape[0]
    size = rows.size // steps
    out = []
    for e in range(energies):
        for c in range(steps):
            src = green.at[e, pl.ds(rows.start + c * size, size)]
            out.append((e, c * size, pltpu.make_async_copy(src, held.at[e, pl.ds(c * size, size)], sem.at[e, c])))
    return size, out


def pairs_kernel(owner, blocks, green, inject, out, held, full, slot_of, counts, sem):
    energies, orbitals, _ = green.shape
    sections = out.shape[0]
    count = owner.shape[0]
    size, moves = copies(green, held, sem, pl.ds(0, orbitals), sem.shape[1])
    for _, _, move in moves:
        move.start()
    out[...] = jnp.zeros_like(out)

    def clear(d, _):
        counts[d] = 0
        return 0

    lax.fori_loop(0, sections, clear, 0)
    rows = CAP * energies * BLK
    lane = lax.broadcasted_iota(jnp.int32, (HEAD, out.shape[2]), 1)
    none = jnp.where(lane < CAP, -1.0, 0.0).astype(BF16)

    def blank(d, _):
        out[d, rows : rows + HEAD, :] = none
        return 0

    lax.fori_loop(0, sections, blank, 0)

    def rank(q, _):
        d = owner[q]
        r = counts[d]
        counts[d] = r + 1
        slot_of[q] = r
        head = out[d, rows : rows + HEAD, :].astype(F32)
        head = jnp.where(lane == r, blocks[q, 1].astype(F32), head)
        out[d, rows : rows + HEAD, :] = head.astype(BF16)
        return 0

    lax.fori_loop(0, count, rank, 0)
    for e, first, move in moves:
        move.wait()
        full[e, first : first + size, :] = dot(held[e, first : first + size, :], inject[e]).astype(BF16)

    def fill(q, _):
        d, r = owner[q], slot_of[q]
        first = pl.multiple_of(blocks[q, 0] * BLK, BLK)
        for e in range(energies):
            to = pl.multiple_of((r * energies + e) * BLK, BLK)
            out[d, pl.ds(to, BLK), :] = full[e, pl.ds(first, BLK), :]
        return 0

    lax.fori_loop(0, count, fill, 0)


def outgoing_pairs(owner, blocks, green, inject, sections):
    energies, orbitals, _ = green.shape
    columns = inject.shape[2]
    steps = 4
    return call(
        pairs_kernel,
        "pairs",
        [IN_SMEM, IN_SMEM, IN_PLACE, IN_VMEM],
        shape(sections, CAP * energies * BLK + HEAD, columns),
        [
            pltpu.VMEM(green.shape, BF16),
            pltpu.VMEM(inject.shape, BF16),
            pltpu.SMEM(owner.shape, jnp.int32),
            pltpu.SMEM((sections,), jnp.int32),
            pltpu.SemaphoreType.DMA((energies, steps)),
        ],
        2 * energies * orbitals * orbitals * columns,
        2 * green.size,
    )(owner, blocks, green, inject)


def maps_kernel(pattern, green, coupling, face_map, couple, held, sem):
    energies, orbitals, _ = green.shape
    face = coupling.shape[1]
    size, moves = copies(green, held, sem, pl.ds(orbitals - face, face), sem.shape[1])
    for _, _, move in moves:
        move.start()
    high, wide = orbitals // pattern.shape[0], face // pattern.shape[1]
    for i in range(pattern.shape[0]):
        for j in range(pattern.shape[1]):
            at = (slice(i * high, (i + 1) * high), slice(j * wide, (j + 1) * wide))
            tile = coupling[at]
            couple[at] = jnp.where(pattern[i, j] == 1, tile, jnp.zeros_like(tile))
    for e, first, move in moves:
        move.wait()
        face_map[e, first : first + size, :] = dot(held[e, first : first + size, :], couple[...])


def face_maps(pattern, green, coupling):
    energies, orbitals, _ = green.shape
    face = coupling.shape[1]
    return call(
        maps_kernel,
        "face_maps",
        [IN_SMEM, IN_PLACE, IN_VMEM],
        [shape(energies, face, face, dtype=F32), shape(orbitals, face)],
        [pltpu.VMEM((energies, face, orbitals), BF16), pltpu.SemaphoreType.DMA((energies, 1))],
        2 * energies * face * orbitals * face,
        2 * energies * face * orbitals,
    )(pattern, green, coupling)


def product_kernel(green, right, out, held, sem):
    orbitals = green.shape[1]
    size, moves = copies(green, held, sem, pl.ds(0, orbitals), sem.shape[1])
    for _, _, move in moves:
        move.start()
    for e, first, move in moves:
        move.wait()
        factor = right[e] if len(right.shape) == 3 else right[...]
        out[e, first : first + size, :] = dot(held[e, first : first + size, :], factor).astype(out.dtype)


def product(green, right, dtype, name):
    energies, orbitals, _ = green.shape
    wide = right.shape[-1]
    return call(
        product_kernel,
        name,
        [IN_PLACE, IN_VMEM],
        shape(energies, orbitals, wide, dtype=dtype),
        [pltpu.VMEM(green.shape, BF16), pltpu.SemaphoreType.DMA((energies, 4))],
        2 * energies * orbitals * orbitals * wide,
        2 * green.size,
    )(green, right)


def chain_kernel(own, got1, got2, got3, total_out, after_out, within_out, upto_out, maps):
    here = place()
    split = GROUP // own.shape[0]
    maps[here] = own[here // split]
    for k, got in enumerate((got1, got2, got3), 1):
        maps[(here + GROUP - k) % GROUP] = got[...]
    first, second, third, fourth = (maps[j] for j in range(GROUP))
    face = first.shape[0]
    upto2 = dot_wide(second, first)
    upto3 = dot_wide(third, upto2)
    after1 = dot_wide(fourth, third)
    after0 = dot_wide(after1, second)
    total_out[...] = dot_wide(fourth, upto3).astype(total_out.dtype)
    for out, items in (
        (after_out, (after0, after1, fourth)),
        (within_out, (second, third, dot_wide(third, second))),
        (upto_out, (first, upto2, upto3)),
    ):
        for j, item in enumerate(items):
            high, low = two_parts(item)
            out[0, j * face : (j + 1) * face, :] = high
            out[1, j * face : (j + 1) * face, :] = low


def chain(own, got, total_dtype):
    face = own.shape[1]
    stack = shape(2, (GROUP - 1) * face, face)
    return call(
        chain_kernel,
        "chain_maps",
        [IN_VMEM] * GROUP,
        [shape(face, face, dtype=total_dtype), stack, stack, stack],
        [pltpu.VMEM((GROUP, face, face), F32)],
        2 * 6 * 6 * face**3,
        4 * 10 * face * face,
    )(own, *got)


def source_kernel(received, inject, green, source, own, send1, send2, send3, held, total, heads, targets, quarters, sem, head_sem):
    energies, orbitals, columns = inject.shape
    sections = received.shape[0]
    face = held.shape[1]
    size, moves = copies(green, held, sem, pl.ds(orbitals - face, face), sem.shape[1])
    for _, _, move in moves:
        move.start()
    rows = CAP * energies * BLK

    def read(s, _):
        block = received[s, rows : rows + HEAD, :].astype(F32)
        heads[pl.ds(s, 1), :] = block[:1].astype(jnp.int32)
        return 0

    lax.fori_loop(0, sections, read, 0, unroll=min(sections, 8))
    fetch = pltpu.make_async_copy(heads, targets, head_sem)
    fetch.start()
    total[...] = inject[...].astype(F32)
    fetch.wait()

    def add(s, _):
        for r in range(CAP):
            first = pl.multiple_of(jnp.maximum(targets[s, r], 0) * BLK, BLK)
            for e in range(energies):
                item = received[s, (r * energies + e) * BLK : (r * energies + e + 1) * BLK, :]
                total[e, pl.ds(first, BLK), :] += item.astype(F32)
        return 0

    lax.fori_loop(0, sections, add, 0, unroll=2)
    split = GROUP // energies
    for e in range(energies):
        source[e] = total[e].astype(BF16)
    for e, first, move in moves:
        move.wait()
        tall = dot(held[e], source[e])
        quarters[e * split] = pack(tall)
        half = face // 2
        quarters[e * split + 1] = jnp.where(left_lanes(tall[:half]), swap_lanes(tall[:half]), tall[half:])
    here = place()
    for k, out in enumerate((own, send1, send2, send3)):
        out[...] = quarters[(here + k) % GROUP].astype(BF16)


def placed_source(received, inject, green, face):
    energies, orbitals, columns = inject.shape
    sections = received.shape[0]
    quarter = shape(face // 2, columns)
    return call(
        source_kernel,
        "source_and_face",
        [IN_VMEM, IN_VMEM, IN_PLACE],
        [shape(*inject.shape), quarter, quarter, quarter, quarter],
        [
            pltpu.VMEM((energies, face, orbitals), BF16),
            pltpu.VMEM(inject.shape, F32),
            pltpu.VMEM((sections, columns), jnp.int32),
            pltpu.SMEM((sections, columns), jnp.int32),
            pltpu.VMEM((GROUP, face // 2, columns), F32),
            pltpu.SemaphoreType.DMA((energies, 1)),
            pltpu.SemaphoreType.DMA,
        ],
        2 * energies * face * orbitals * columns,
        2 * energies * face * orbitals + 2 * received.size,
    )(received, inject, green)


def gathered(refs, held):
    here = place()
    for k, ref in enumerate(refs):
        held[(here + GROUP - k) % GROUP] = ref[...]


def apply(parts, j, x):
    face = x.shape[0]
    at = slice(j * face, (j + 1) * face)
    return dot(parts[0, at, :], x) + dot(parts[1, at, :], x)


def total_kernel(own, got1, got2, got3, after, out, held):
    gathered((own, got1, got2, got3), held)
    total = unpack(held[GROUP - 1].astype(F32))
    for j in range(GROUP - 1):
        total = total + apply(after, j, unpack(held[j].astype(F32)).astype(BF16))
    out[...] = pack(total).astype(BF16)


def plane_total(shifts, after):
    half, columns = shifts[0].shape
    return call(
        total_kernel,
        "plane_total",
        [IN_VMEM] * (GROUP + 1),
        shape(half, columns),
        [pltpu.VMEM((GROUP, half, columns), BF16)],
        2 * after.size * columns,
        2 * after.size,
    )(*shifts, after)


def local_kernel(own, got1, got2, got3, within, out, held):
    gathered((own, got1, got2, got3), held)
    face = out.shape[0] // (GROUP - 1)
    first, second, third = (unpack(held[j].astype(F32)) for j in range(GROUP - 1))
    out[0:face] = first
    out[face : 2 * face] = second + apply(within, 0, first.astype(BF16))
    out[2 * face :] = third + apply(within, 1, second.astype(BF16)) + apply(within, 2, first.astype(BF16))


def plane_local(shifts, within):
    half, columns = shifts[0].shape
    return call(
        local_kernel,
        "plane_local",
        [IN_VMEM] * (GROUP + 1),
        shape((GROUP - 1) * 2 * half, columns, dtype=F32),
        [pltpu.VMEM((GROUP, half, columns), BF16)],
        2 * within.size * columns,
        2 * within.size,
    )(*shifts, within)


def entering_kernel(count, *refs):
    below, maps = refs[:count], refs[count : 2 * count - 1]
    upto, local, own, send1, send2, send3, held = refs[2 * count - 1 :]
    base = unpack(below[-1][...].astype(F32))
    for k in range(count - 2, -1, -1):
        high, low = two_parts(base)
        base = unpack(below[k][...].astype(F32)) + dot(maps[k][...], high) + dot(maps[k][...], low)
    high, low = two_parts(base)
    face = base.shape[0]
    held[0] = pack(base)
    for j in range(1, GROUP):
        at = slice((j - 1) * face, j * face)
        held[j] = pack(local[at, :] + dot(upto[0, at, :], high) + dot(upto[0, at, :], low) + dot(upto[1, at, :], high))
    here = place()
    for k, out in enumerate((own, send1, send2, send3)):
        out[...] = held[(here + k) % GROUP].astype(BF16)


def entering(below, maps, upto, local):
    half, columns = below[0].shape
    count = len(below)
    quarter = shape(half, columns)
    return call(
        functools.partial(entering_kernel, count),
        "entering",
        [IN_VMEM] * (2 * count + 1),
        [quarter] * GROUP,
        [pltpu.VMEM((GROUP, half, columns), F32)],
        3 * upto.size * columns,
        2 * upto.size + 4 * local.size,
    )(*below, *maps, upto, local)


def waves_kernel(own, got1, got2, got3, prop, image, out, held):
    gathered((own, got1, got2, got3), held)
    split = GROUP // prop.shape[0]
    for e in range(prop.shape[0]):
        near, far = held[e * split].astype(F32), held[e * split + 1].astype(F32)
        left = left_lanes(near)
        top = jnp.where(left, near, swap_lanes(far))
        low = jnp.where(left, swap_lanes(near), far)
        incoming = jnp.concatenate([top, low], axis=0).astype(BF16)
        out[e] = (dot(prop[e], incoming) + image[e]).astype(BF16)


def final_waves(arrived, prop, image):
    half, columns = arrived[0].shape
    return call(
        waves_kernel,
        "waves",
        [IN_VMEM] * (GROUP + 2),
        shape(*image.shape),
        [pltpu.VMEM((GROUP, half, columns), BF16)],
        2 * prop.size * columns,
        2 * prop.size + 6 * image.size,
    )(*arrived, prop, image)


def plane_shift(sections, k):
    return [(s, s // GROUP * GROUP + (s % GROUP + k) % GROUP) for s in range(sections)]


def up_shift(sections, k):
    return [(s, s + GROUP * k) for s in range(sections - GROUP * k)]


def in_plane(items, sections):
    return [lax.ppermute(item, "sec", plane_shift(sections, k)) for k, item in enumerate(items, 1)]


def spread(packed):
    half = packed.shape[1] // 2
    return jnp.concatenate([packed[:, :half], packed[:, half:]], axis=0)


def gather_below(total_map, total, sections):
    planes = sections // GROUP
    if planes <= 4:
        maps = [lax.ppermute(total_map, "sec", up_shift(sections, k)) for k in range(1, planes - 1)]
        below = [lax.ppermute(total, "sec", up_shift(sections, k)) for k in range(1, planes)]
        return below, maps
    shift = lax.ppermute(spread(total).astype(F32), "sec", up_shift(sections, 1))
    joined = lax.ppermute(total_map, "sec", up_shift(sections, 1))
    stride = 1
    while stride < planes:
        other = lax.ppermute(shift, "sec", up_shift(sections, stride))
        other_map = lax.ppermute(joined, "sec", up_shift(sections, stride))
        shift = shift + dot_wide(joined, other)
        joined = dot_wide(joined, other_map)
        stride *= 2
    half = shift.shape[0] // 2
    return [jnp.concatenate([shift[:half], shift[half:]], axis=1)], []


def per_device(green, injected, coupling, pattern, owner, pair_blocks):
    sections = lax.axis_size("sec")
    here = lax.axis_index("sec") % GROUP
    green, inject = green[0], injected[0]
    energies = green.shape[0]
    face = coupling.shape[2]
    split = GROUP // energies

    outgoing = outgoing_pairs(owner[:, 0], pair_blocks, green, inject, sections)
    received = lax.all_to_all(outgoing, "sec", split_axis=0, concat_axis=0, tiled=True)

    face_map, couple = face_maps(pattern[0], green, coupling[0])
    sent = [lax.dynamic_index_in_dim(face_map, (here + k) % GROUP // split, 0, False) for k in range(1, GROUP)]
    total_dtype = BF16 if sections // GROUP <= 4 else F32
    total_map, after, within, upto = chain(face_map, in_plane(sent, sections), total_dtype)
    prop = product(green, couple, BF16, "prop")

    source, own, *quarters = placed_source(received, inject, green, face)
    shifts = [own] + in_plane(quarters, sections)
    total = plane_total(shifts, after)
    below, maps = gather_below(total_map, total, sections)
    local = plane_local(shifts, within)
    own, *inner = entering(below, maps, upto, local)
    arrived = [own] + in_plane(inner, sections)
    image = product(green, source, F32, "image")
    return final_waves(arrived, prop, image)[None]


def solution(mesh):
    in_specs = (
        P("sec", "grp", None, None),
        P("sec", "grp", None, None),
        P("sec", None, None),
        P("sec", None, None),
        P("sec", None),
        P("sec", None),
    )
    out_specs = P("sec", "grp", None, None)
    return jax.shard_map(
        per_device, mesh=mesh, in_specs=in_specs, out_specs=out_specs, check_vma=False
    )
```

```python
import functools

import jax
import jax.numpy as jnp
from jax import lax
from jax.experimental import pallas as pl
from jax.experimental.pallas import tpu as pltpu
from jax.sharding import PartitionSpec as P

BLK = 32
CAP = 2
GROUP = 4
HEAD = 16

HIGH = lax.Precision.HIGHEST
F32 = jnp.float32
BF16 = jnp.bfloat16
VMEM_SMALL = 16 * 1024 * 1024
VMEM_LARGE = 60000000
VMEM_WHOLE = 63400000

IN_VMEM = pl.BlockSpec(memory_space=pltpu.VMEM)
IN_SMEM = pl.BlockSpec(memory_space=pltpu.SMEM)
IN_HBM = pl.BlockSpec(memory_space=pltpu.HBM)
IN_PLACE = pl.BlockSpec(memory_space=pl.ANY)


def shape(*dims, dtype=BF16):
    return jax.ShapeDtypeStruct(dims, dtype)


def call(body, name, ins, outs, scratch, flops, moved, vmem=VMEM_SMALL):
    return pl.pallas_call(
        body,
        name=name,
        in_specs=ins,
        out_shape=outs,
        out_specs=jax.tree.map(lambda _: IN_VMEM, outs),
        scratch_shapes=scratch,
        compiler_params=pltpu.CompilerParams(vmem_limit_bytes=vmem),
        cost_estimate=pl.CostEstimate(flops=flops, bytes_accessed=moved, transcendentals=0),
    )


def place():
    return lax.axis_index("sec") % GROUP


def dot(a, b):
    return jnp.dot(a, b, preferred_element_type=F32)


def dot_wide(a, b):
    return jnp.dot(a, b, precision=HIGH, preferred_element_type=F32)


def two_parts(x):
    high = x.astype(BF16)
    return high, (x - high.astype(F32)).astype(BF16)


def left_lanes(x):
    return lax.broadcasted_iota(jnp.int32, x.shape, 1) < x.shape[1] // 2


def swap_lanes(x):
    return pltpu.roll(x, x.shape[1] // 2, 1)


def pack(tall):
    half = tall.shape[0] // 2
    top, low = tall[:half], tall[half:]
    return jnp.where(left_lanes(top), top, swap_lanes(low))


def unpack(packed):
    return jnp.concatenate([packed, swap_lanes(packed)], axis=0)


def copies(green, held, sem, rows, steps):
    energies = green.shape[0]
    size = rows.size // steps
    out = []
    for e in range(energies):
        for c in range(steps):
            src = green.at[e, pl.ds(rows.start + c * size, size)]
            out.append((e, c * size, pltpu.make_async_copy(src, held.at[e, pl.ds(c * size, size)], sem.at[e, c])))
    return size, out


def gathered(refs, held):
    here = place()
    for k, ref in enumerate(refs):
        held[(here + GROUP - k) % GROUP] = ref[...]


def pairs_kernel(owner_in, blocks_in, green, inject_in, out, owner, blocks, inject, held, full, slot_of, counts, sem, side):
    energies, orbitals, _ = green.shape
    sections = out.shape[0]
    count = owner.shape[0]
    lists = [
        pltpu.make_async_copy(owner_in, owner, side.at[0]),
        pltpu.make_async_copy(blocks_in, blocks, side.at[1]),
    ]
    columns = pltpu.make_async_copy(inject_in, inject, side.at[2])
    size, moves = copies(green, held, sem, pl.ds(0, orbitals), sem.shape[1])
    for move in (*lists, columns):
        move.start()
    for _, _, move in moves:
        move.start()
    rows = CAP * energies * BLK
    lane = lax.broadcasted_iota(jnp.int32, (HEAD, out.shape[2]), 1)
    none = jnp.where(lane < CAP, -1.0, 0.0).astype(BF16)

    def blank(d, _):
        counts[d] = 0
        out[d, :rows, :] = jnp.zeros((rows, out.shape[2]), BF16)
        out[d, rows : rows + HEAD, :] = none
        return 0

    lax.fori_loop(0, sections, blank, 0)
    for move in lists:
        move.wait()

    def rank(q, _):
        d = owner[q]
        r = counts[d]
        counts[d] = r + 1
        slot_of[q] = r
        head = out[d, rows : rows + HEAD, :].astype(F32)
        head = jnp.where(lane == r, blocks[1, q].astype(F32), head)
        out[d, rows : rows + HEAD, :] = head.astype(BF16)
        return 0

    lax.fori_loop(0, count, rank, 0)
    columns.wait()
    for e, first, move in moves:
        move.wait()
        full[e, first : first + size, :] = dot(held[e, first : first + size, :], inject[e]).astype(BF16)

    def fill(q, _):
        d, r = owner[q], slot_of[q]
        first = pl.multiple_of(blocks[0, q] * BLK, BLK)
        for e in range(energies):
            to = pl.multiple_of((r * energies + e) * BLK, BLK)
            out[d, pl.ds(to, BLK), :] = full[e, pl.ds(first, BLK), :]
        return 0

    lax.fori_loop(0, count, fill, 0, unroll=4)


def outgoing_pairs(owner, blocks, green, inject, sections):
    energies, orbitals, _ = green.shape
    columns = inject.shape[2]
    steps = 4
    return call(
        pairs_kernel,
        "pairs",
        [IN_HBM] * 4,
        shape(sections, CAP * energies * BLK + HEAD, columns),
        [
            pltpu.SMEM(owner.shape, jnp.int32),
            pltpu.SMEM(blocks.shape, jnp.int32),
            pltpu.VMEM(inject.shape, BF16),
            pltpu.VMEM(green.shape, BF16),
            pltpu.VMEM(inject.shape, BF16),
            pltpu.SMEM(owner.shape, jnp.int32),
            pltpu.SMEM((sections,), jnp.int32),
            pltpu.SemaphoreType.DMA((energies, steps)),
            pltpu.SemaphoreType.DMA((3,)),
        ],
        2 * energies * orbitals * orbitals * columns,
        2 * green.size,
        VMEM_WHOLE,
    )(owner, blocks, green, inject)


def maps_kernel(pattern_in, green, coupling_in, couple, own, send1, send2, send3, pattern, coupling, held, maps, sem, side):
    energies, orbitals, _ = green.shape
    face = coupling.shape[1]
    size, moves = copies(green, held, sem, pl.ds(orbitals - face, face), sem.shape[1])
    tiles = pltpu.make_async_copy(pattern_in, pattern, side.at[0])
    whole = pltpu.make_async_copy(coupling_in, coupling, side.at[1])
    tiles.start()
    whole.start()
    for _, _, move in moves:
        move.start()
    tiles.wait()
    whole.wait()
    high, wide = orbitals // pattern.shape[1], face // pattern.shape[0]
    for i in range(pattern.shape[1]):
        for j in range(pattern.shape[0]):
            at = (slice(i * high, (i + 1) * high), slice(j * wide, (j + 1) * wide))
            tile = coupling[at]
            couple[at] = jnp.where(pattern[j, i] == 1, tile, jnp.zeros_like(tile))
    for e, first, move in moves:
        move.wait()
        maps[e, first : first + size, :] = dot(held[e, first : first + size, :], couple[...])
    here = place()
    split = GROUP // energies
    for k, out in enumerate((own, send1, send2, send3)):
        out[...] = maps[(here + k) % GROUP // split]


def face_maps(pattern, green, coupling):
    energies, orbitals, _ = green.shape
    face = coupling.shape[1]
    square = shape(face, face, dtype=F32)
    return call(
        maps_kernel,
        "face_maps",
        [IN_HBM] * 3,
        [shape(orbitals, face)] + [square] * GROUP,
        [
            pltpu.SMEM(pattern.shape, jnp.int32),
            pltpu.VMEM(coupling.shape, BF16),
            pltpu.VMEM((energies, face, orbitals), BF16),
            pltpu.VMEM((energies, face, face), F32),
            pltpu.SemaphoreType.DMA((energies, 1)),
            pltpu.SemaphoreType.DMA((2,)),
        ],
        2 * energies * face * orbitals * face,
        2 * energies * face * orbitals,
        VMEM_WHOLE,
    )(pattern, green, coupling)


def product_kernel(green, right, out, held, sem):
    orbitals = green.shape[1]
    size, moves = copies(green, held, sem, pl.ds(0, orbitals), sem.shape[1])
    for _, _, move in moves:
        move.start()
    for e, first, move in moves:
        move.wait()
        factor = right[e] if len(right.shape) == 3 else right[...]
        out[e, first : first + size, :] = dot(held[e, first : first + size, :], factor).astype(out.dtype)


def product(green, right, dtype, name):
    energies, orbitals, _ = green.shape
    wide = right.shape[-1]
    return call(
        product_kernel,
        name,
        [IN_HBM, IN_VMEM],
        shape(energies, orbitals, wide, dtype=dtype),
        [pltpu.VMEM(green.shape, BF16), pltpu.SemaphoreType.DMA((energies, 4))],
        2 * energies * orbitals * orbitals * wide,
        2 * green.size,
        VMEM_LARGE,
    )(green, right)


def chain_kernel(own, got1, got2, got3, total_out, after_out, within_out, upto_out, maps):
    gathered((own, got1, got2, got3), maps)
    first, second, third, fourth = (two_parts(maps[j]) for j in range(GROUP))
    face = own.shape[0]

    def times(a, b):
        return dot(a[0], b[0]) + (dot(a[0], b[1]) + dot(a[1], b[0]))

    upto2 = two_parts(times(second, first))
    upto3 = two_parts(times(third, upto2))
    after1 = two_parts(times(fourth, third))
    after0 = two_parts(times(after1, second))
    total_out[...] = times(fourth, upto3).astype(total_out.dtype)
    for out, items in (
        (after_out, (after0, after1, fourth)),
        (within_out, (second, third, two_parts(times(third, second)))),
        (upto_out, (first, upto2, upto3)),
    ):
        for j, (high, low) in enumerate(items):
            out[0, j * face : (j + 1) * face, :] = high
            out[1, j * face : (j + 1) * face, :] = low


def chain(maps, total_dtype):
    face = maps[0].shape[0]
    stack = shape(2, (GROUP - 1) * face, face)
    return call(
        chain_kernel,
        "chain_maps",
        [IN_VMEM] * GROUP,
        [shape(face, face, dtype=total_dtype), stack, stack, stack],
        [pltpu.VMEM((GROUP, face, face), F32)],
        2 * 6 * 3 * face**3,
        4 * 10 * face * face,
    )(*maps)


def source_kernel(received, inject_in, green, _prop, _map, source, own, send1, send2, send3, held, inject, total, heads, targets, quarters, sem, head_sem, side):
    energies, orbitals, columns = inject.shape
    columns_in = pltpu.make_async_copy(inject_in, inject, side)
    columns_in.start()
    sections = received.shape[0]
    face = held.shape[1]
    size, moves = copies(green, held, sem, pl.ds(orbitals - face, face), sem.shape[1])
    for _, _, move in moves:
        move.start()
    rows = CAP * energies * BLK

    def read(s, _):
        block = received[s, rows : rows + HEAD, :].astype(F32)
        heads[pl.ds(s, 1), :] = block[:1].astype(jnp.int32)
        return 0

    lax.fori_loop(0, sections, read, 0, unroll=min(sections, 8))
    fetch = pltpu.make_async_copy(heads, targets, head_sem)
    fetch.start()
    columns_in.wait()
    total[...] = inject[...].astype(F32)
    fetch.wait()

    def add(s, _):
        for r in range(CAP):
            first = pl.multiple_of(jnp.maximum(targets[s, r], 0) * BLK, BLK)
            for e in range(energies):
                item = received[s, (r * energies + e) * BLK : (r * energies + e + 1) * BLK, :]
                total[e, pl.ds(first, BLK), :] += item.astype(F32)
        return 0

    lax.fori_loop(0, sections, add, 0, unroll=2)
    split = GROUP // energies
    for e in range(energies):
        source[e] = total[e].astype(BF16)
    for e, first, move in moves:
        move.wait()
        tall = dot(held[e], source[e])
        quarters[e * split] = pack(tall)
        half = face // 2
        quarters[e * split + 1] = jnp.where(left_lanes(tall[:half]), swap_lanes(tall[:half]), tall[half:])
    here = place()
    for k, out in enumerate((own, send1, send2, send3)):
        out[...] = quarters[(here + k) % GROUP].astype(BF16)


def placed_source(received, inject, green, face, ready):
    energies, orbitals, columns = inject.shape
    sections = received.shape[0]
    quarter = shape(face // 2, columns)
    return call(
        source_kernel,
        "source_and_face",
        [IN_VMEM, IN_HBM, IN_HBM, IN_PLACE, IN_PLACE],
        [shape(*inject.shape), quarter, quarter, quarter, quarter],
        [
            pltpu.VMEM((energies, face, orbitals), BF16),
            pltpu.VMEM(inject.shape, BF16),
            pltpu.VMEM(inject.shape, F32),
            pltpu.VMEM((sections, columns), jnp.int32),
            pltpu.SMEM((sections, columns), jnp.int32),
            pltpu.VMEM((GROUP, face // 2, columns), F32),
            pltpu.SemaphoreType.DMA((energies, 1)),
            pltpu.SemaphoreType.DMA,
            pltpu.SemaphoreType.DMA,
        ],
        2 * energies * face * orbitals * columns,
        2 * energies * face * orbitals + 2 * received.size,
        VMEM_LARGE,
    )(received, inject, green, *ready)


def apply(parts, j, x):
    face = x.shape[0]
    at = slice(j * face, (j + 1) * face)
    return dot(parts[0, at, :], x) + dot(parts[1, at, :], x)


def total_kernel(own, got1, got2, got3, after, out, held):
    gathered((own, got1, got2, got3), held)
    total = unpack(held[GROUP - 1].astype(F32))
    for j in range(GROUP - 1):
        total = total + apply(after, j, unpack(held[j].astype(F32)).astype(BF16))
    out[...] = pack(total).astype(BF16)


def plane_total(shifts, after):
    half, columns = shifts[0].shape
    return call(
        total_kernel,
        "plane_total",
        [IN_VMEM] * (GROUP + 1),
        shape(half, columns),
        [pltpu.VMEM((GROUP, half, columns), BF16)],
        2 * after.size * columns,
        2 * after.size,
    )(*shifts, after)


def local_kernel(own, got1, got2, got3, within, out, held):
    gathered((own, got1, got2, got3), held)
    face = out.shape[0] // (GROUP - 1)
    first, second, third = (unpack(held[j].astype(F32)) for j in range(GROUP - 1))
    out[0:face] = first
    out[face : 2 * face] = second + apply(within, 0, first.astype(BF16))
    out[2 * face :] = third + apply(within, 1, second.astype(BF16)) + apply(within, 2, first.astype(BF16))


def plane_local(shifts, within):
    half, columns = shifts[0].shape
    return call(
        local_kernel,
        "plane_local",
        [IN_VMEM] * (GROUP + 1),
        shape((GROUP - 1) * 2 * half, columns, dtype=F32),
        [pltpu.VMEM((GROUP, half, columns), BF16)],
        2 * within.size * columns,
        2 * within.size,
    )(*shifts, within)


def entering_kernel(count, *refs):
    below, maps = refs[:count], refs[count : 2 * count - 1]
    upto, local, _image, own, send1, send2, send3, held = refs[2 * count - 1 :]
    base = unpack(below[-1][...].astype(F32))
    for k in range(count - 2, -1, -1):
        high, low = two_parts(base)
        base = unpack(below[k][...].astype(F32)) + dot(maps[k][...], high) + dot(maps[k][...], low)
    high, low = two_parts(base)
    face = base.shape[0]
    held[0] = pack(base)
    for j in range(1, GROUP):
        at = slice((j - 1) * face, j * face)
        held[j] = pack(local[at, :] + dot(upto[0, at, :], high) + dot(upto[0, at, :], low) + dot(upto[1, at, :], high))
    here = place()
    for k, out in enumerate((own, send1, send2, send3)):
        out[...] = held[(here + k) % GROUP].astype(BF16)


def entering(below, maps, upto, local, ready):
    half, columns = below[0].shape
    count = len(below)
    quarter = shape(half, columns)
    return call(
        functools.partial(entering_kernel, count),
        "entering",
        [IN_VMEM] * (2 * count + 1) + [IN_PLACE],
        [quarter] * GROUP,
        [pltpu.VMEM((GROUP, half, columns), F32)],
        3 * upto.size * columns,
        2 * upto.size + 4 * local.size,
    )(*below, *maps, upto, local, ready)


def waves_kernel(own, got1, got2, got3, prop, image, out, held):
    gathered((own, got1, got2, got3), held)
    split = GROUP // prop.shape[0]
    for e in range(prop.shape[0]):
        near, far = held[e * split].astype(F32), held[e * split + 1].astype(F32)
        left = left_lanes(near)
        top = jnp.where(left, near, swap_lanes(far))
        low = jnp.where(left, swap_lanes(near), far)
        incoming = jnp.concatenate([top, low], axis=0).astype(BF16)
        out[e] = (dot(prop[e], incoming) + image[e]).astype(BF16)


def final_waves(arrived, prop, image):
    half, columns = arrived[0].shape
    return call(
        waves_kernel,
        "waves",
        [IN_VMEM] * (GROUP + 2),
        shape(*image.shape),
        [pltpu.VMEM((GROUP, half, columns), BF16)],
        2 * prop.size * columns,
        2 * prop.size + 6 * image.size,
    )(*arrived, prop, image)


def plane_shift(sections, k):
    return [(s, s // GROUP * GROUP + (s % GROUP + k) % GROUP) for s in range(sections)]


def up_shift(sections, k):
    return [(s, s + GROUP * k) for s in range(sections - GROUP * k)]


def in_plane(items, sections):
    return [lax.ppermute(item, "sec", plane_shift(sections, k)) for k, item in enumerate(items, 1)]


def spread(packed):
    half = packed.shape[1] // 2
    return jnp.concatenate([packed[:, :half], packed[:, half:]], axis=0)


def gather_below(total_map, total, sections):
    planes = sections // GROUP
    if planes <= 4:
        maps = [lax.ppermute(total_map, "sec", up_shift(sections, k)) for k in range(1, planes - 1)]
        below = [lax.ppermute(total, "sec", up_shift(sections, k)) for k in range(1, planes)]
        return below, maps
    shift = lax.ppermute(spread(total).astype(F32), "sec", up_shift(sections, 1))
    joined = lax.ppermute(total_map, "sec", up_shift(sections, 1))
    stride = 1
    while stride < planes:
        other = lax.ppermute(shift, "sec", up_shift(sections, stride))
        other_map = lax.ppermute(joined, "sec", up_shift(sections, stride))
        shift = shift + dot_wide(joined, other)
        joined = dot_wide(joined, other_map)
        stride *= 2
    half = shift.shape[0] // 2
    return [jnp.concatenate([shift[:half], shift[half:]], axis=1)], []


def per_device(green, injected, coupling, pattern, owner, pair_blocks):
    sections = lax.axis_size("sec")
    green, inject = green[0], injected[0]
    face = coupling.shape[2]

    outgoing = outgoing_pairs(owner[:, 0], pair_blocks.T, green, inject, sections)
    received = lax.all_to_all(outgoing, "sec", split_axis=0, concat_axis=0, tiled=True)

    couple, own_map, *sent = face_maps(pattern[0].T, green, coupling[0])
    total_dtype = BF16 if sections // GROUP <= 4 else F32
    total_map, after, within, upto = chain([own_map] + in_plane(sent, sections), total_dtype)
    prop = product(green, couple, BF16, "prop")

    source, own, *quarters = placed_source(received, inject, green, face, (prop, total_map))
    shifts = [own] + in_plane(quarters, sections)
    total = plane_total(shifts, after)
    below, maps = gather_below(total_map, total, sections)
    local = plane_local(shifts, within)
    image = product(green, source, F32, "image")
    own, *inner = entering(below, maps, upto, local, image)
    arrived = [own] + in_plane(inner, sections)
    return final_waves(arrived, prop, image)[None]


def solution(mesh):
    in_specs = (
        P("sec", "grp", None, None),
        P("sec", "grp", None, None),
        P("sec", None, None),
        P("sec", None, None),
        P("sec", None),
        P("sec", None),
    )
    out_specs = P("sec", "grp", None, None)
    return jax.shard_map(
        per_device, mesh=mesh, in_specs=in_specs, out_specs=out_specs, check_vma=False
    )
```

```python
import functools

import jax
import jax.numpy as jnp
from jax import lax
from jax.experimental import pallas as pl
from jax.experimental.pallas import tpu as pltpu
from jax.sharding import PartitionSpec as P

BLK = 32
CAP = 2
GROUP = 4
HEAD = 16
CORES = 2

HIGH = lax.Precision.HIGHEST
F32 = jnp.float32
BF16 = jnp.bfloat16
VMEM_BYTES = 16 * 1024 * 1024

IN_VMEM = pl.BlockSpec(memory_space=pltpu.VMEM)
IN_SMEM = pl.BlockSpec(memory_space=pltpu.SMEM)
IN_PLACE = pl.BlockSpec(memory_space=pl.ANY)


def shape(*dims, dtype=BF16):
    return jax.ShapeDtypeStruct(dims, dtype)


def call(body, name, ins, outs, scratch, flops, moved):
    return pl.pallas_call(
        body,
        name=name,
        in_specs=ins,
        out_shape=outs,
        out_specs=jax.tree.map(lambda _: IN_VMEM, outs),
        scratch_shapes=scratch,
        compiler_params=pltpu.CompilerParams(vmem_limit_bytes=VMEM_BYTES),
        cost_estimate=pl.CostEstimate(flops=flops, bytes_accessed=moved, transcendentals=0),
    )


def place():
    return lax.axis_index("sec") % GROUP


def dot(a, b):
    return jnp.dot(a, b, preferred_element_type=F32)


def dot_wide(a, b):
    return jnp.dot(a, b, precision=HIGH, preferred_element_type=F32)


def two_parts(x):
    high = x.astype(BF16)
    return high, (x - high.astype(F32)).astype(BF16)


def left_lanes(x):
    return lax.broadcasted_iota(jnp.int32, x.shape, 1) < x.shape[1] // 2


def swap_lanes(x):
    return pltpu.roll(x, x.shape[1] // 2, 1)


def pack(tall):
    half = tall.shape[0] // 2
    top, low = tall[:half], tall[half:]
    return jnp.where(left_lanes(top), top, swap_lanes(low))


def unpack(packed):
    return jnp.concatenate([packed, swap_lanes(packed)], axis=0)


def pairs_kernel(owner, blocks, green, inject, out, full, slot_of, counts):
    energies = green.shape[0]
    sections = out.shape[0]
    count = owner.shape[0]
    rows = CAP * energies * BLK
    lane = lax.broadcasted_iota(jnp.int32, (HEAD, out.shape[2]), 1)
    none = jnp.where(lane < CAP, -1.0, 0.0).astype(BF16)

    def blank(d, _):
        counts[d] = 0
        out[d, :rows, :] = jnp.zeros((rows, out.shape[2]), BF16)
        out[d, rows : rows + HEAD, :] = none
        return 0

    lax.fori_loop(0, sections, blank, 0)

    def rank(q, _):
        d = owner[q]
        r = counts[d]
        counts[d] = r + 1
        slot_of[q] = r
        head = out[d, rows : rows + HEAD, :].astype(F32)
        head = jnp.where(lane == r, blocks[1, q].astype(F32), head)
        out[d, rows : rows + HEAD, :] = head.astype(BF16)
        return 0

    lax.fori_loop(0, count, rank, 0)
    for e in range(energies):
        full[e] = dot(green[e], inject[e]).astype(BF16)

    def fill(q, _):
        d, r = owner[q], slot_of[q]
        first = pl.multiple_of(blocks[0, q] * BLK, BLK)
        for e in range(energies):
            to = pl.multiple_of((r * energies + e) * BLK, BLK)
            out[d, pl.ds(to, BLK), :] = full[e, pl.ds(first, BLK), :]
        return 0

    lax.fori_loop(0, count, fill, 0, unroll=4)


def outgoing_pairs(owner, blocks, green, inject, sections):
    energies, orbitals, _ = green.shape
    columns = inject.shape[2]
    return call(
        pairs_kernel,
        "pairs",
        [IN_SMEM, IN_SMEM, IN_VMEM, IN_VMEM],
        shape(sections, CAP * energies * BLK + HEAD, columns),
        [
            pltpu.VMEM(inject.shape, BF16),
            pltpu.SMEM(owner.shape, jnp.int32),
            pltpu.SMEM((sections,), jnp.int32),
        ],
        2 * energies * orbitals * orbitals * columns,
        2 * green.size,
    )(owner, blocks, green, inject)


def maps_kernel(pattern, green, coupling, couple, own, other, maps):
    energies, orbitals, _ = green.shape
    face = coupling.shape[1]
    high, wide = orbitals // pattern.shape[1], face // pattern.shape[0]
    for i in range(pattern.shape[1]):
        for j in range(pattern.shape[0]):
            at = (slice(i * high, (i + 1) * high), slice(j * wide, (j + 1) * wide))
            tile = coupling[at]
            couple[at] = jnp.where(pattern[j, i] == 1, tile, jnp.zeros_like(tile))
    for e in range(energies):
        maps[e] = dot(green[e, orbitals - face :, :], couple[...])
    mine = place() // CORES
    own[...] = maps[mine]
    other[...] = maps[1 - mine]


def face_maps(pattern, green, coupling):
    energies, orbitals, _ = green.shape
    face = coupling.shape[1]
    square = shape(face, face, dtype=F32)
    return call(
        maps_kernel,
        "face_maps",
        [IN_SMEM, IN_VMEM, IN_VMEM],
        [shape(orbitals, face), square, square],
        [pltpu.VMEM((energies, face, face), F32)],
        2 * energies * face * orbitals * face,
        2 * energies * face * orbitals,
    )(pattern, green, coupling)


def product_kernel(green, right, out):
    for e in range(green.shape[0]):
        factor = right[e] if len(right.shape) == 3 else right[...]
        out[e] = dot(green[e], factor).astype(out.dtype)


def product(green, right, dtype, name):
    energies, orbitals, _ = green.shape
    wide = right.shape[-1]
    return call(
        product_kernel,
        name,
        [IN_VMEM, IN_VMEM],
        shape(energies, orbitals, wide, dtype=dtype),
        [],
        2 * energies * orbitals * orbitals * wide,
        2 * green.size,
    )(green, right)


def chain_kernel(own, near, across, far, _prop, total_out, after_out, within_out, upto_out, maps):
    here = place()
    opposite = (here + CORES) % GROUP
    for j, ref in ((here, own), (here ^ 1, near), (opposite, across), (opposite ^ 1, far)):
        maps[j] = ref[...]
    first, second, third, fourth = (two_parts(maps[j]) for j in range(GROUP))
    face = own.shape[0]

    def times(a, b):
        return dot(a[0], b[0]) + (dot(a[0], b[1]) + dot(a[1], b[0]))

    upto2 = two_parts(times(second, first))
    upto3 = two_parts(times(third, upto2))
    after1 = two_parts(times(fourth, third))
    after0 = two_parts(times(after1, second))
    total_out[...] = times(fourth, upto3).astype(total_out.dtype)
    for out, items in (
        (after_out, (after0, after1, fourth)),
        (within_out, (second, third, two_parts(times(third, second)))),
        (upto_out, (first, upto2, upto3)),
    ):
        for j, (high, low) in enumerate(items):
            out[0, j * face : (j + 1) * face, :] = high
            out[1, j * face : (j + 1) * face, :] = low


def chain(maps, total_dtype, ready):
    face = maps[0].shape[0]
    stack = shape(2, (GROUP - 1) * face, face)
    return call(
        chain_kernel,
        "chain_maps",
        [IN_VMEM] * GROUP + [IN_PLACE],
        [shape(face, face, dtype=total_dtype), stack, stack, stack],
        [pltpu.VMEM((GROUP, face, face), F32)],
        2 * 6 * 3 * face**3,
        4 * 10 * face * face,
    )(*maps, ready)


def source_kernel(received, inject, green, _map, source, quarters, total, heads, targets, sem):
    energies, orbitals, columns = inject.shape
    sections = received.shape[0]
    half = quarters.shape[1]
    rows = CAP * energies * BLK

    def read(s, _):
        block = received[s, rows : rows + HEAD, :].astype(F32)
        heads[pl.ds(s, 1), :] = block[:1].astype(jnp.int32)
        return 0

    lax.fori_loop(0, sections, read, 0, unroll=min(sections, 8))
    fetch = pltpu.make_async_copy(heads, targets, sem)
    fetch.start()
    total[...] = inject[...].astype(F32)
    fetch.wait()

    def add(s, _):
        for r in range(CAP):
            first = pl.multiple_of(jnp.maximum(targets[s, r], 0) * BLK, BLK)
            for e in range(energies):
                item = received[s, (r * energies + e) * BLK : (r * energies + e + 1) * BLK, :]
                total[e, pl.ds(first, BLK), :] += item.astype(F32)
        return 0

    lax.fori_loop(0, sections, add, 0, unroll=2)
    split = GROUP // energies
    for e in range(energies):
        source[e] = total[e].astype(BF16)
        tall = dot(green[e, orbitals - 2 * half :, :], source[e])
        quarters[e * split] = pack(tall).astype(BF16)
        second = jnp.where(left_lanes(tall[:half]), swap_lanes(tall[:half]), tall[half:])
        quarters[e * split + 1] = second.astype(BF16)


def placed_source(received, inject, green, face, ready):
    energies, orbitals, columns = inject.shape
    sections = received.shape[0]
    return call(
        source_kernel,
        "source_and_face",
        [IN_VMEM, IN_VMEM, IN_VMEM, IN_PLACE],
        [shape(*inject.shape), shape(GROUP, face // 2, columns)],
        [
            pltpu.VMEM(inject.shape, F32),
            pltpu.VMEM((sections, columns), jnp.int32),
            pltpu.SMEM((sections, columns), jnp.int32),
            pltpu.SemaphoreType.DMA,
        ],
        2 * energies * face * orbitals * columns,
        2 * energies * face * orbitals + 2 * received.size,
    )(received, inject, green, ready)


def apply(parts, j, x):
    face = x.shape[0]
    at = slice(j * face, (j + 1) * face)
    return dot(parts[0, at, :], x) + dot(parts[1, at, :], x)


def total_kernel(shifts, after, out):
    total = unpack(shifts[GROUP - 1].astype(F32))
    for j in range(GROUP - 1):
        total = total + apply(after, j, unpack(shifts[j].astype(F32)).astype(BF16))
    packed = pack(total).astype(BF16)
    for k in range(out.shape[0]):
        out[k] = packed


def plane_total(shifts, after, times):
    _, half, columns = shifts.shape
    return call(
        total_kernel,
        "plane_total",
        [IN_VMEM] * 2,
        shape(times, half, columns),
        [],
        2 * after.size * columns,
        2 * after.size,
    )(shifts, after)


def local_kernel(shifts, within, out):
    face = out.shape[0] // (GROUP - 1)
    first, second, third = (unpack(shifts[j].astype(F32)) for j in range(GROUP - 1))
    out[0:face] = first
    out[face : 2 * face] = second + apply(within, 0, first.astype(BF16))
    out[2 * face :] = third + apply(within, 1, second.astype(BF16)) + apply(within, 2, first.astype(BF16))


def plane_local(shifts, within):
    _, half, columns = shifts.shape
    return call(
        local_kernel,
        "plane_local",
        [IN_VMEM] * 2,
        shape((GROUP - 1) * 2 * half, columns, dtype=F32),
        [],
        2 * within.size * columns,
        2 * within.size,
    )(shifts, within)


def entering_kernel(below, *refs):
    maps, (upto, local, _image, out) = refs[:-4], refs[-4:]
    planes = below.shape[0]
    plane = lax.axis_index("sec") // GROUP

    def total_of(k):
        if planes == 1:
            return unpack(below[0].astype(F32))
        item = below[jnp.maximum(plane - k, 0)].astype(F32)
        return unpack(jnp.where(plane >= k, item, 0.0))

    base = total_of(planes - 1)
    for k in range(planes - 2, 0, -1):
        high, low = two_parts(base)
        base = total_of(k) + dot(maps[k - 1][...], high) + dot(maps[k - 1][...], low)
    high, low = two_parts(base)
    face = base.shape[0]
    out[0] = pack(base).astype(BF16)
    for j in range(1, GROUP):
        at = slice((j - 1) * face, j * face)
        state = local[at, :] + dot(upto[0, at, :], high) + dot(upto[0, at, :], low) + dot(upto[1, at, :], high)
        out[j] = pack(state).astype(BF16)


def entering(below, maps, upto, local, ready):
    _, half, columns = below.shape
    return call(
        entering_kernel,
        "entering",
        [IN_VMEM] * (3 + len(maps)) + [IN_PLACE],
        shape(GROUP, half, columns),
        [],
        3 * upto.size * columns,
        2 * upto.size + 4 * local.size,
    )(below, *maps, upto, local, ready)


def waves_kernel(arrived, prop, image, out):
    split = GROUP // prop.shape[0]
    for e in range(prop.shape[0]):
        near, far = arrived[e * split].astype(F32), arrived[e * split + 1].astype(F32)
        left = left_lanes(near)
        top = jnp.where(left, near, swap_lanes(far))
        low = jnp.where(left, swap_lanes(near), far)
        incoming = jnp.concatenate([top, low], axis=0).astype(BF16)
        out[e] = (dot(prop[e], incoming) + image[e]).astype(BF16)


def final_waves(arrived, prop, image):
    return call(
        waves_kernel,
        "waves",
        [IN_VMEM] * 3,
        shape(*image.shape),
        [],
        2 * prop.size * arrived.shape[2],
        2 * prop.size + 6 * image.size,
    )(arrived, prop, image)


def in_plane(sections, move):
    return [(s, s // GROUP * GROUP + move(s % GROUP)) for s in range(sections)]


def exchange(items, groups):
    return lax.all_to_all(items, "sec", split_axis=0, concat_axis=0, axis_index_groups=groups, tiled=True)


def plane_groups(sections):
    return [[p * GROUP + i for i in range(GROUP)] for p in range(sections // GROUP)]


def upward_groups(sections):
    return [list(range(i, sections, GROUP)) for i in range(GROUP)]


def up_shift(sections, k):
    return [(s, s + GROUP * k) for s in range(sections - GROUP * k)]


def spread(packed):
    half = packed.shape[1] // 2
    return jnp.concatenate([packed[:, :half], packed[:, half:]], axis=0)


def scan_below(total_map, total, sections):
    planes = sections // GROUP
    shift = lax.ppermute(spread(total).astype(F32), "sec", up_shift(sections, 1))
    joined = lax.ppermute(total_map, "sec", up_shift(sections, 1))
    stride = 1
    while stride < planes:
        other = lax.ppermute(shift, "sec", up_shift(sections, stride))
        other_map = lax.ppermute(joined, "sec", up_shift(sections, stride))
        shift = shift + dot_wide(joined, other)
        joined = dot_wide(joined, other_map)
        stride *= 2
    half = shift.shape[0] // 2
    return jnp.concatenate([shift[:half], shift[half:]], axis=1)[None]


def per_device(green, injected, coupling, pattern, owner, pair_blocks):
    sections = lax.axis_size("sec")
    green, inject = green[0], injected[0]
    face = coupling.shape[2]

    outgoing = outgoing_pairs(owner[:, 0], pair_blocks.T, green, inject, sections)
    received = lax.all_to_all(outgoing, "sec", split_axis=0, concat_axis=0, tiled=True)

    couple, own_map, other_map = face_maps(pattern[0].T, green, coupling[0])
    across = lax.ppermute(other_map, "sec", in_plane(sections, lambda i: (i + CORES) % GROUP))
    near = lax.ppermute(own_map, "sec", in_plane(sections, lambda i: i ^ 1))
    prop = product(green, couple, BF16, "prop")
    far = lax.ppermute(across, "sec", in_plane(sections, lambda i: i ^ 1))
    planes = sections // GROUP
    few = planes <= 4
    total_map, after, within, upto = chain([own_map, near, across, far], BF16 if few else F32, prop)
    maps = [lax.ppermute(total_map, "sec", up_shift(sections, k)) for k in range(1, planes - 1)] if few else []

    source, quarters = placed_source(received, inject, green, face, total_map)
    shifts = exchange(quarters, plane_groups(sections))
    total = plane_total(shifts, after, planes if few else 1)
    below = exchange(total, upward_groups(sections)) if few else scan_below(total_map, total[0], sections)
    local = plane_local(shifts, within)
    image = product(green, source, F32, "image")
    arrived = exchange(entering(below, maps, upto, local, image), plane_groups(sections))
    return final_waves(arrived, prop, image)[None]


def solution(mesh):
    in_specs = (
        P("sec", "grp", None, None),
        P("sec", "grp", None, None),
        P("sec", None, None),
        P("sec", None, None),
        P("sec", None),
        P("sec", None),
    )
    out_specs = P("sec", "grp", None, None)
    return jax.shard_map(
        per_device, mesh=mesh, in_specs=in_specs, out_specs=out_specs, check_vma=False
    )
```

```python
import functools

import jax
import jax.numpy as jnp
from jax import lax
from jax.experimental import pallas as pl
from jax.experimental.pallas import tpu as pltpu
from jax.sharding import PartitionSpec as P

BLK = 32
CAP = 2
GROUP = 4
HEAD = 16
CORES = 2

HIGH = lax.Precision.HIGHEST
F32 = jnp.float32
BF16 = jnp.bfloat16
VMEM_SMALL = 16 * 1024 * 1024
VMEM_WHOLE = 63400000

IN_VMEM = pl.BlockSpec(memory_space=pltpu.VMEM)
IN_SMEM = pl.BlockSpec(memory_space=pltpu.SMEM)
IN_HBM = pl.BlockSpec(memory_space=pltpu.HBM)
IN_PLACE = pl.BlockSpec(memory_space=pl.ANY)


def shape(*dims, dtype=BF16):
    return jax.ShapeDtypeStruct(dims, dtype)


def call(body, name, ins, outs, scratch, flops, moved, vmem=VMEM_SMALL):
    return pl.pallas_call(
        body,
        name=name,
        in_specs=ins,
        out_shape=outs,
        out_specs=jax.tree.map(lambda _: IN_VMEM, outs),
        scratch_shapes=scratch,
        compiler_params=pltpu.CompilerParams(vmem_limit_bytes=vmem),
        cost_estimate=pl.CostEstimate(flops=flops, bytes_accessed=moved, transcendentals=0),
    )


def place():
    return lax.axis_index("sec") % GROUP


def partners():
    here = place()
    across = (here + CORES) % GROUP
    return here, here ^ 1, across, across ^ 1


def dot(a, b):
    return jnp.dot(a, b, preferred_element_type=F32)


def dot_wide(a, b):
    return jnp.dot(a, b, precision=HIGH, preferred_element_type=F32)


def two_parts(x):
    high = x.astype(BF16)
    return high, (x - high.astype(F32)).astype(BF16)


def left_lanes(x):
    return lax.broadcasted_iota(jnp.int32, x.shape, 1) < x.shape[1] // 2


def swap_lanes(x):
    return pltpu.roll(x, x.shape[1] // 2, 1)


def pack(tall):
    half = tall.shape[0] // 2
    top, low = tall[:half], tall[half:]
    return jnp.where(left_lanes(top), top, swap_lanes(low))


def unpack(packed):
    return jnp.concatenate([packed, swap_lanes(packed)], axis=0)


def copies(green, held, sem, first, rows):
    energies, steps = sem.shape
    size = rows // steps
    out = []
    for e in range(energies):
        for c in range(steps):
            at = pl.ds(c * size, size)
            move = pltpu.make_async_copy(green.at[e, pl.ds(first + c * size, size)], held.at[e, at], sem.at[e, c])
            move.start(priority=(e * steps + c) % 2)
            out.append((e, slice(c * size, (c + 1) * size), move))
    return out


def pairs_kernel(owner_in, blocks_in, green, inject_in, out, owner, blocks, inject, held, full, slot_of, counts, sem, side):
    energies, orbitals, _ = green.shape
    sections = out.shape[0]
    count = owner.shape[0]
    lists = [
        pltpu.make_async_copy(owner_in, owner, side.at[0]),
        pltpu.make_async_copy(blocks_in, blocks, side.at[1]),
    ]
    columns = pltpu.make_async_copy(inject_in, inject, side.at[2])
    for move in lists:
        move.start()
    columns.start(priority=1)
    moves = copies(green, held, sem, 0, orbitals)
    rows = CAP * energies * BLK
    lane = lax.broadcasted_iota(jnp.int32, (HEAD, out.shape[2]), 1)
    none = jnp.where(lane < CAP, -1.0, 0.0).astype(BF16)

    def blank(d, _):
        counts[d] = 0
        out[d, :rows, :] = jnp.zeros((rows, out.shape[2]), BF16)
        out[d, rows : rows + HEAD, :] = none
        return 0

    lax.fori_loop(0, sections, blank, 0)
    for move in lists:
        move.wait()

    def rank(q, _):
        d = owner[q]
        r = counts[d]
        counts[d] = r + 1
        slot_of[q] = r
        head = out[d, rows : rows + HEAD, :].astype(F32)
        head = jnp.where(lane == r, blocks[1, q].astype(F32), head)
        out[d, rows : rows + HEAD, :] = head.astype(BF16)
        return 0

    lax.fori_loop(0, count, rank, 0)
    columns.wait()
    for e, at, move in moves:
        move.wait()
        full[e, at, :] = dot(held[e, at, :], inject[e]).astype(BF16)

    def fill(q, _):
        d, r = owner[q], slot_of[q]
        first = pl.multiple_of(blocks[0, q] * BLK, BLK)
        for e in range(energies):
            to = pl.multiple_of((r * energies + e) * BLK, BLK)
            out[d, pl.ds(to, BLK), :] = full[e, pl.ds(first, BLK), :]
        return 0

    lax.fori_loop(0, count, fill, 0, unroll=4)


def outgoing_pairs(owner, blocks, green, inject, sections):
    energies, orbitals, _ = green.shape
    columns = inject.shape[2]
    steps = 4
    return call(
        pairs_kernel,
        "pairs",
        [IN_HBM] * 4,
        shape(sections, CAP * energies * BLK + HEAD, columns),
        [
            pltpu.SMEM(owner.shape, jnp.int32),
            pltpu.SMEM(blocks.shape, jnp.int32),
            pltpu.VMEM(inject.shape, BF16),
            pltpu.VMEM(green.shape, BF16),
            pltpu.VMEM(inject.shape, BF16),
            pltpu.SMEM(owner.shape, jnp.int32),
            pltpu.SMEM((sections,), jnp.int32),
            pltpu.SemaphoreType.DMA((energies, steps)),
            pltpu.SemaphoreType.DMA((3,)),
        ],
        2 * energies * orbitals * orbitals * columns,
        2 * green.size,
        VMEM_WHOLE,
    )(owner, blocks, green, inject)


def maps_kernel(pattern_in, green, coupling_in, couple, own, other, held, pattern, coupling, maps, sem, side):
    energies, orbitals, _ = green.shape
    face = coupling.shape[1]
    tiles = pltpu.make_async_copy(pattern_in, pattern, side.at[0])
    whole = pltpu.make_async_copy(coupling_in, coupling, side.at[1])
    tiles.start()
    whole.start()
    moves = copies(green, held, sem, orbitals - face, face)
    tiles.wait()
    whole.wait()
    high, wide = orbitals // pattern.shape[1], face // pattern.shape[0]
    for i in range(pattern.shape[1]):
        for j in range(pattern.shape[0]):
            at = (slice(i * high, (i + 1) * high), slice(j * wide, (j + 1) * wide))
            tile = coupling[at]
            couple[at] = jnp.where(pattern[j, i] == 1, tile, jnp.zeros_like(tile))
    for e, at, move in moves:
        move.wait()
        maps[e, at, :] = dot(held[e, at, :], couple[...])
    mine = place() // CORES
    own[...] = maps[mine]
    other[...] = maps[1 - mine]


def face_maps(pattern, green, coupling):
    energies, orbitals, _ = green.shape
    face = coupling.shape[1]
    square = shape(face, face, dtype=F32)
    return call(
        maps_kernel,
        "face_maps",
        [IN_HBM] * 3,
        [shape(orbitals, face), square, square, shape(energies, face, orbitals)],
        [
            pltpu.SMEM(pattern.shape, jnp.int32),
            pltpu.VMEM(coupling.shape, BF16),
            pltpu.VMEM((energies, face, face), F32),
            pltpu.SemaphoreType.DMA((energies, 1)),
            pltpu.SemaphoreType.DMA((2,)),
        ],
        2 * energies * face * orbitals * face,
        2 * energies * face * orbitals,
        VMEM_WHOLE,
    )(pattern, green, coupling)


def prop_kernel(green, couple, out, held, sem):
    for e, at, move in copies(green, held, sem, 0, green.shape[1]):
        move.wait()
        out[e, at, :] = dot(held[e, at, :], couple[...]).astype(BF16)


def propagator(green, couple):
    energies, orbitals, _ = green.shape
    face = couple.shape[1]
    return call(
        prop_kernel,
        "prop",
        [IN_HBM, IN_VMEM],
        shape(energies, orbitals, face),
        [pltpu.VMEM(green.shape, BF16), pltpu.SemaphoreType.DMA((energies, 4))],
        2 * energies * orbitals * orbitals * face,
        2 * green.size,
        VMEM_WHOLE,
    )(green, couple)


def image_kernel(green, source, out):
    for e in range(green.shape[0]):
        out[e] = dot(green[e], source[e])


def images(green, source):
    return call(
        image_kernel,
        "image",
        [IN_VMEM] * 2,
        shape(*source.shape, dtype=F32),
        [],
        2 * green.size * source.shape[2],
        2 * green.size,
    )(green, source)


def times(a, b):
    return dot(a[0], b[0]) + (dot(a[0], b[1]) + dot(a[1], b[0]))


def chain_kernel(own, near, across, far, _tie, total_out, parts, maps):
    collect((own, near, across, far), maps)
    split = [two_parts(maps[j]) for j in range(GROUP)]
    lower, upper = two_parts(times(split[1], split[0])), two_parts(times(split[3], split[2]))
    total_out[...] = times(upper, lower).astype(total_out.dtype)
    for j, (high, low) in enumerate(split):
        parts[0, j] = high
        parts[1, j] = low


def chain(maps, total_dtype, tie):
    face = maps[0].shape[0]
    return call(
        chain_kernel,
        "chain_maps",
        [IN_VMEM] * GROUP + [IN_PLACE],
        [shape(face, face, dtype=total_dtype), shape(2, GROUP, face, face)],
        [pltpu.VMEM((GROUP, face, face), F32)],
        2 * 3 * 3 * face**3,
        4 * 10 * face * face,
    )(*maps, tie)


def source_kernel(received, inject, face_rows, _prop, source, own, near, across, far, quarters, total, heads, targets, sem):
    energies, orbitals, columns = inject.shape
    sections = received.shape[0]
    half = quarters.shape[1]
    rows = CAP * energies * BLK

    def read(s, _):
        block = received[s, rows : rows + HEAD, :].astype(F32)
        heads[pl.ds(s, 1), :] = block[:1].astype(jnp.int32)
        return 0

    lax.fori_loop(0, sections, read, 0, unroll=min(sections, 8))
    fetch = pltpu.make_async_copy(heads, targets, sem)
    fetch.start()
    total[...] = inject[...].astype(F32)
    fetch.wait()

    def add(s, _):
        for r in range(CAP):
            first = pl.multiple_of(jnp.maximum(targets[s, r], 0) * BLK, BLK)
            for e in range(energies):
                item = received[s, (r * energies + e) * BLK : (r * energies + e + 1) * BLK, :]
                total[e, pl.ds(first, BLK), :] += item.astype(F32)
        return 0

    lax.fori_loop(0, sections, add, 0, unroll=2)
    split = GROUP // energies
    for e in range(energies):
        source[e] = total[e].astype(BF16)
        tall = dot(face_rows[e], source[e])
        quarters[e * split] = pack(tall)
        second = jnp.where(left_lanes(tall[:half]), swap_lanes(tall[:half]), tall[half:])
        quarters[e * split + 1] = second
    deal(quarters, (own, near, across, far))


def placed_source(received, inject, face_rows, ready):
    face = face_rows.shape[1]
    energies, orbitals, columns = inject.shape
    sections = received.shape[0]
    return call(
        source_kernel,
        "source_and_face",
        [IN_VMEM, IN_VMEM, IN_VMEM, IN_PLACE],
        [shape(*inject.shape)] + [shape(face // 2, columns)] * GROUP,
        [
            pltpu.VMEM((GROUP, face // 2, columns), F32),
            pltpu.VMEM(inject.shape, F32),
            pltpu.VMEM((sections, columns), jnp.int32),
            pltpu.SMEM((sections, columns), jnp.int32),
            pltpu.SemaphoreType.DMA,
        ],
        2 * energies * face * orbitals * columns,
        2 * energies * face * orbitals + 2 * received.size,
    )(received, inject, face_rows, ready)


def deal(items, outs):
    for out, at in zip(outs, partners()):
        out[...] = items[at].astype(out.dtype)


def collect(refs, held):
    for ref, at in zip(refs, partners()):
        held[at] = ref[...]


def step(parts, j, shift, state):
    return unpack(shift.astype(F32)) + times((parts[0, j], parts[1, j]), two_parts(state))


def total_kernel(own, near, across, far, parts, out, shifts):
    collect((own, near, across, far), shifts)
    state = unpack(shifts[0].astype(F32))
    for j in range(1, GROUP):
        state = step(parts, j, shifts[j], state)
    out[...] = pack(state).astype(BF16)


def plane_total(shifts, parts):
    half, columns = shifts[0].shape
    return call(
        total_kernel,
        "plane_total",
        [IN_VMEM] * (GROUP + 1),
        shape(half, columns),
        [pltpu.VMEM((GROUP, half, columns), BF16)],
        3 * parts.size * columns,
        2 * parts.size,
    )(*shifts, parts)


def entering_kernel(count, *refs):
    below, maps = refs[:count], refs[count : 2 * count - 1]
    parts, _image = refs[2 * count - 1 : 2 * count + 1]
    arrived, out = refs[2 * count + 1 : 2 * count + 1 + GROUP], refs[2 * count + 1 + GROUP : -2]
    shifts, held = refs[-2:]
    collect(arrived, shifts)
    state = unpack(below[-1][...].astype(F32))
    for k in range(count - 2, -1, -1):
        high, low = two_parts(state)
        state = unpack(below[k][...].astype(F32)) + dot(maps[k][...], high) + dot(maps[k][...], low)
    held[0] = pack(state)
    for j in range(1, GROUP):
        state = step(parts, j - 1, shifts[j - 1], state)
        held[j] = pack(state)
    deal(held, out)


def entering(below, maps, parts, shifts, tie):
    half, columns = below[0].shape
    count = len(below)
    return call(
        functools.partial(entering_kernel, count),
        "entering",
        [IN_VMEM] * (2 * count) + [IN_PLACE] + [IN_VMEM] * GROUP,
        [shape(half, columns)] * GROUP,
        [pltpu.VMEM((GROUP, half, columns), BF16), pltpu.VMEM((GROUP, half, columns), F32)],
        4 * parts.size * columns,
        2 * parts.size,
    )(*below, *maps, parts, tie, *shifts)


def waves_kernel(own, near, across, far, prop, image, out, arrived):
    collect((own, near, across, far), arrived)
    split = GROUP // prop.shape[0]
    for e in range(prop.shape[0]):
        near, far = arrived[e * split].astype(F32), arrived[e * split + 1].astype(F32)
        left = left_lanes(near)
        top = jnp.where(left, near, swap_lanes(far))
        low = jnp.where(left, swap_lanes(near), far)
        incoming = jnp.concatenate([top, low], axis=0).astype(BF16)
        out[e] = (dot(prop[e], incoming) + image[e]).astype(BF16)


def final_waves(arrived, prop, image):
    half, columns = arrived[0].shape
    return call(
        waves_kernel,
        "waves",
        [IN_VMEM] * (GROUP + 2),
        shape(*image.shape),
        [pltpu.VMEM((GROUP, half, columns), BF16)],
        2 * prop.size * columns,
        2 * prop.size + 6 * image.size,
    )(*arrived, prop, image)


def to_near(item, sections):
    return lax.ppermute(item, "sec", [(s, s ^ 1) for s in range(sections)])


def to_across(item, sections):
    return lax.ppermute(item, "sec", [(s, s // GROUP * GROUP + (s % GROUP + CORES) % GROUP) for s in range(sections)])


def to_far(item, sections):
    return lax.ppermute(item, "sec", [(s, s // GROUP * GROUP + (s % GROUP + CORES) % GROUP ^ 1) for s in range(sections)])


def exchange(own, near, across, far, sections):
    across, far = to_across(across, sections), to_far(far, sections)
    return [own, to_near(near, sections), across, far]


def up_shift(sections, k):
    return [(s, s + GROUP * k) for s in range(sections - GROUP * k)]


def spread(packed):
    half = packed.shape[1] // 2
    return jnp.concatenate([packed[:, :half], packed[:, half:]], axis=0)


def gather_below(total_map, total, sections):
    planes = sections // GROUP
    if planes <= 4:
        below = [lax.ppermute(total, "sec", up_shift(sections, k)) for k in range(1, planes)]
        maps = [lax.ppermute(total_map, "sec", up_shift(sections, k)) for k in range(1, planes - 1)]
        return below, maps
    shift = lax.ppermute(spread(total).astype(F32), "sec", up_shift(sections, 1))
    joined = lax.ppermute(total_map, "sec", up_shift(sections, 1))
    stride = 1
    while stride < planes:
        other = lax.ppermute(shift, "sec", up_shift(sections, stride))
        other_map = lax.ppermute(joined, "sec", up_shift(sections, stride))
        shift = shift + dot_wide(joined, other)
        joined = dot_wide(joined, other_map)
        stride *= 2
    half = shift.shape[0] // 2
    return [jnp.concatenate([shift[:half], shift[half:]], axis=1)], []


def per_device(green, injected, coupling, pattern, owner, pair_blocks):
    sections = lax.axis_size("sec")
    green, inject = green[0], injected[0]

    outgoing = outgoing_pairs(owner[:, 0], pair_blocks.T, green, inject, sections)
    received = lax.all_to_all(outgoing, "sec", split_axis=0, concat_axis=0, tiled=True)

    couple, own_map, other_map, face_rows = face_maps(pattern[0].T, green, coupling[0])
    across = to_across(other_map, sections)
    near = to_near(own_map, sections)
    prop = propagator(green, couple)
    far = to_near(across, sections)

    source, *quarters = placed_source(received, inject, face_rows, prop)
    total_dtype = BF16 if sections // GROUP <= 4 else F32
    shifts = exchange(*quarters, sections)
    total_map, parts = chain([own_map, near, across, far], total_dtype, shifts[1])
    below, maps = gather_below(total_map, plane_total(shifts, parts), sections)
    image = images(green, source)
    arrived = exchange(*entering(below, maps, parts, shifts, image), sections)
    return final_waves(arrived, prop, image)[None]


def solution(mesh):
    in_specs = (
        P("sec", "grp", None, None),
        P("sec", "grp", None, None),
        P("sec", None, None),
        P("sec", None, None),
        P("sec", None),
        P("sec", None),
    )
    out_specs = P("sec", "grp", None, None)
    return jax.shard_map(
        per_device, mesh=mesh, in_specs=in_specs, out_specs=out_specs, check_vma=False
    )
```

```python
import functools

import jax
import jax.numpy as jnp
from jax import lax
from jax.experimental import pallas as pl
from jax.experimental.pallas import tpu as pltpu
from jax.sharding import PartitionSpec as P

BLK = 32
CAP = 2
GROUP = 4
HEAD = 16
CORES = 2

HIGH = lax.Precision.HIGHEST
F32 = jnp.float32
BF16 = jnp.bfloat16
VMEM_SMALL = 16 * 1024 * 1024
VMEM_WHOLE = 63400000

IN_VMEM = pl.BlockSpec(memory_space=pltpu.VMEM)
IN_SMEM = pl.BlockSpec(memory_space=pltpu.SMEM)
IN_HBM = pl.BlockSpec(memory_space=pltpu.HBM)
IN_PLACE = pl.BlockSpec(memory_space=pl.ANY)


def shape(*dims, dtype=BF16):
    return jax.ShapeDtypeStruct(dims, dtype)


def call(body, name, ins, outs, scratch, flops, moved, vmem=VMEM_SMALL):
    return pl.pallas_call(
        body,
        name=name,
        in_specs=ins,
        out_shape=outs,
        out_specs=jax.tree.map(lambda _: IN_VMEM, outs),
        scratch_shapes=scratch,
        compiler_params=pltpu.CompilerParams(vmem_limit_bytes=vmem),
        cost_estimate=pl.CostEstimate(flops=flops, bytes_accessed=moved, transcendentals=0),
    )


def place():
    return lax.axis_index("sec") % GROUP


def partners():
    here = place()
    across = (here + CORES) % GROUP
    return here, here ^ 1, across, across ^ 1


def dot(a, b):
    return jnp.dot(a, b, preferred_element_type=F32)


def dot_wide(a, b):
    return jnp.dot(a, b, precision=HIGH, preferred_element_type=F32)


def two_parts(x):
    high = x.astype(BF16)
    return high, (x - high.astype(F32)).astype(BF16)


def left_lanes(x):
    return lax.broadcasted_iota(jnp.int32, x.shape, 1) < x.shape[1] // 2


def swap_lanes(x):
    return pltpu.roll(x, x.shape[1] // 2, 1)


def pack(tall):
    half = tall.shape[0] // 2
    top, low = tall[:half], tall[half:]
    return jnp.where(left_lanes(top), top, swap_lanes(low))


def unpack(packed):
    return jnp.concatenate([packed, swap_lanes(packed)], axis=0)


def fetch(green, held, sem):
    moves = [pltpu.make_async_copy(green.at[e], held.at[e], sem.at[e]) for e in range(green.shape[0])]
    for move in moves:
        move.start()
    return moves


def mask_tiles(pattern, coupling):
    high, wide = coupling.shape[0] // pattern.shape[1], coupling.shape[1] // pattern.shape[0]
    for i in range(pattern.shape[1]):
        for j in range(pattern.shape[0]):
            at = (slice(i * high, (i + 1) * high), slice(j * wide, (j + 1) * wide))
            tile = coupling[at]
            coupling[at] = jnp.where(pattern[j, i] == 1, tile, jnp.zeros_like(tile))


def first_kernel(
    owner_in, blocks_in, pattern_in, green, inject_in, coupling_in, out, own, other,
    owner, blocks, pattern, inject, coupling, held, full, maps, slot_of, counts, sem, side,
):
    energies, orbitals, _ = green.shape
    sections = out.shape[0]
    count = owner.shape[0]
    face = coupling.shape[1]
    small = [
        pltpu.make_async_copy(src, dst, side.at[k])
        for k, (src, dst) in enumerate(
            ((owner_in, owner), (blocks_in, blocks), (pattern_in, pattern), (inject_in, inject), (coupling_in, coupling))
        )
    ]
    for move in small:
        move.start()
    moves = fetch(green, held, sem)
    rows = CAP * energies * BLK
    lane = lax.broadcasted_iota(jnp.int32, (HEAD, out.shape[2]), 1)
    none = jnp.where(lane < CAP, -1.0, 0.0).astype(BF16)

    def blank(d, _):
        counts[d] = 0
        out[d, :rows, :] = jnp.zeros((rows, out.shape[2]), BF16)
        out[d, rows : rows + HEAD, :] = none
        return 0

    lax.fori_loop(0, sections, blank, 0)
    for move in small:
        move.wait()

    def rank(q, _):
        d = owner[q]
        r = counts[d]
        counts[d] = r + 1
        slot_of[q] = r
        head = out[d, rows : rows + HEAD, :].astype(F32)
        head = jnp.where(lane == r, blocks[1, q].astype(F32), head)
        out[d, rows : rows + HEAD, :] = head.astype(BF16)
        return 0

    lax.fori_loop(0, count, rank, 0)
    mask_tiles(pattern, coupling)
    for e, move in enumerate(moves):
        move.wait()
        full[e] = dot(held[e], inject[e]).astype(BF16)
        maps[e] = dot(held[e, orbitals - face :, :], coupling[...])

        def fill(q, _):
            first = pl.multiple_of(blocks[0, q] * BLK, BLK)
            to = pl.multiple_of((slot_of[q] * energies + e) * BLK, BLK)
            out[owner[q], pl.ds(to, BLK), :] = full[e, pl.ds(first, BLK), :]
            return 0

        lax.fori_loop(0, count, fill, 0, unroll=4)
    mine = place() // CORES
    own[...] = maps[mine]
    other[...] = maps[1 - mine]


def pairs_and_maps(owner, blocks, pattern, green, inject, coupling, sections):
    energies, orbitals, _ = green.shape
    columns, face = inject.shape[2], coupling.shape[1]
    square = shape(face, face, dtype=F32)
    return call(
        first_kernel,
        "pairs_and_maps",
        [IN_HBM] * 6,
        [shape(sections, CAP * energies * BLK + HEAD, columns), square, square],
        [
            pltpu.SMEM(owner.shape, jnp.int32),
            pltpu.SMEM(blocks.shape, jnp.int32),
            pltpu.SMEM(pattern.shape, jnp.int32),
            pltpu.VMEM(inject.shape, BF16),
            pltpu.VMEM(coupling.shape, BF16),
            pltpu.VMEM(green.shape, BF16),
            pltpu.VMEM(inject.shape, BF16),
            pltpu.VMEM((energies, face, face), F32),
            pltpu.SMEM(owner.shape, jnp.int32),
            pltpu.SMEM((sections,), jnp.int32),
            pltpu.SemaphoreType.DMA((energies,)),
            pltpu.SemaphoreType.DMA((5,)),
        ],
        2 * green.size * (columns + face // 4),
        2 * green.size,
        VMEM_WHOLE,
    )(owner, blocks, pattern, green, inject, coupling)


def prop_kernel(pattern_in, green, coupling_in, _tie, out, face_rows, pattern, coupling, held, sem, side):
    energies, orbitals, _ = green.shape
    face = coupling.shape[1]
    tiles = pltpu.make_async_copy(pattern_in, pattern, side.at[0])
    whole = pltpu.make_async_copy(coupling_in, coupling, side.at[1])
    tiles.start()
    whole.start()
    moves = fetch(green, held, sem)
    tiles.wait()
    whole.wait()
    mask_tiles(pattern, coupling)
    for e, move in enumerate(moves):
        move.wait()
        out[e] = dot(held[e], coupling[...]).astype(BF16)
        face_rows[e] = held[e, orbitals - face :, :]


def propagator(pattern, green, coupling, tie):
    energies, orbitals, _ = green.shape
    face = coupling.shape[1]
    return call(
        prop_kernel,
        "prop",
        [IN_HBM] * 3 + [IN_PLACE],
        [shape(energies, orbitals, face), shape(energies, face, orbitals)],
        [
            pltpu.SMEM(pattern.shape, jnp.int32),
            pltpu.VMEM(coupling.shape, BF16),
            pltpu.VMEM(green.shape, BF16),
            pltpu.SemaphoreType.DMA((energies,)),
            pltpu.SemaphoreType.DMA((2,)),
        ],
        2 * green.size * face,
        2 * green.size,
        VMEM_WHOLE,
    )(pattern, green, coupling, tie)


def image_kernel(green, source, out):
    for e in range(green.shape[0]):
        out[e] = dot(green[e], source[e])


def images(green, source):
    return call(
        image_kernel,
        "image",
        [IN_VMEM] * 2,
        shape(*source.shape, dtype=F32),
        [],
        2 * green.size * source.shape[2],
        2 * green.size,
    )(green, source)


def times(a, b):
    return dot(a[0], b[0]) + (dot(a[0], b[1]) + dot(a[1], b[0]))


def chain_kernel(own, near, across, far, total_out, parts, maps, total):
    collect((own, near, across, far), maps)
    split = [two_parts(maps[j]) for j in range(GROUP)]
    lower, upper = two_parts(times(split[1], split[0])), two_parts(times(split[3], split[2]))
    total[...] = times(upper, lower)
    rows = total_out.shape[0]
    core = place() % CORES if rows < total.shape[0] else 0
    total_out[...] = total[pl.ds(pl.multiple_of(core * rows, rows), rows), :].astype(total_out.dtype)
    for j, (high, low) in enumerate(split):
        parts[0, j] = high
        parts[1, j] = low


def chain(maps, few):
    face = maps[0].shape[0]
    total = shape(face // CORES, face) if few else shape(face, face, dtype=F32)
    return call(
        chain_kernel,
        "chain_maps",
        [IN_VMEM] * GROUP,
        [total, shape(2, GROUP, face, face)],
        [pltpu.VMEM((GROUP, face, face), F32), pltpu.VMEM((face, face), F32)],
        2 * 3 * 3 * face**3,
        4 * 10 * face * face,
    )(*maps)


def source_kernel(received, inject, face_rows, _map, source, own, near, across, far, quarters, total, heads, targets, sem):
    energies, orbitals, columns = inject.shape
    sections = received.shape[0]
    half = quarters.shape[1]
    rows = CAP * energies * BLK

    def read(s, _):
        block = received[s, rows : rows + HEAD, :].astype(F32)
        heads[pl.ds(s, 1), :] = block[:1].astype(jnp.int32)
        return 0

    lax.fori_loop(0, sections, read, 0, unroll=min(sections, 8))
    fetch = pltpu.make_async_copy(heads, targets, sem)
    fetch.start()
    total[...] = inject[...].astype(F32)
    fetch.wait()

    def add(s, _):
        for r in range(CAP):
            first = pl.multiple_of(jnp.maximum(targets[s, r], 0) * BLK, BLK)
            for e in range(energies):
                item = received[s, (r * energies + e) * BLK : (r * energies + e + 1) * BLK, :]
                total[e, pl.ds(first, BLK), :] += item.astype(F32)
        return 0

    lax.fori_loop(0, sections, add, 0, unroll=2)
    split = GROUP // energies
    for e in range(energies):
        source[e] = total[e].astype(BF16)
        tall = dot(face_rows[e], source[e])
        quarters[e * split] = pack(tall)
        second = jnp.where(left_lanes(tall[:half]), swap_lanes(tall[:half]), tall[half:])
        quarters[e * split + 1] = second
    deal(quarters, (own, near, across, far))


def placed_source(received, inject, face_rows, ready):
    face = face_rows.shape[1]
    energies, orbitals, columns = inject.shape
    sections = received.shape[0]
    return call(
        source_kernel,
        "source_and_face",
        [IN_VMEM, IN_VMEM, IN_VMEM, IN_PLACE],
        [shape(*inject.shape)] + [shape(face // 2, columns)] * GROUP,
        [
            pltpu.VMEM((GROUP, face // 2, columns), F32),
            pltpu.VMEM(inject.shape, F32),
            pltpu.VMEM((sections, columns), jnp.int32),
            pltpu.SMEM((sections, columns), jnp.int32),
            pltpu.SemaphoreType.DMA,
        ],
        2 * energies * face * orbitals * columns,
        2 * energies * face * orbitals + 2 * received.size,
    )(received, inject, face_rows, ready)


def deal(items, outs):
    for out, at in zip(outs, partners()):
        out[...] = items[at].astype(out.dtype)


def collect(refs, held):
    for ref, at in zip(refs, partners()):
        held[at] = ref[...]


def step(parts, j, shift, state):
    return unpack(shift.astype(F32)) + times((parts[0, j], parts[1, j]), two_parts(state))


def total_kernel(own, near, across, far, parts, out, shifts):
    collect((own, near, across, far), shifts)
    state = unpack(shifts[0].astype(F32))
    for j in range(1, GROUP):
        state = step(parts, j, shifts[j], state)
    out[...] = pack(state).astype(BF16)


def plane_total(shifts, parts):
    half, columns = shifts[0].shape
    return call(
        total_kernel,
        "plane_total",
        [IN_VMEM] * (GROUP + 1),
        shape(half, columns),
        [pltpu.VMEM((GROUP, half, columns), BF16)],
        3 * parts.size * columns,
        2 * parts.size,
    )(*shifts, parts)


def entering_kernel(count, *refs):
    below, maps = refs[:count], refs[count : 3 * count - 2]
    parts, _image = refs[3 * count - 2 : 3 * count]
    arrived, out = refs[3 * count : 3 * count + GROUP], refs[3 * count + GROUP : -2]
    shifts, held = refs[-2:]
    collect(arrived, shifts)
    first_core = place() % CORES == 0
    state = unpack(below[-1][...].astype(F32))
    for k in range(count - 2, -1, -1):
        high, low = two_parts(state)
        mine, other = (dot(half[...], high) + dot(half[...], low) for half in maps[2 * k : 2 * k + 2])
        top, bottom = jnp.where(first_core, mine, other), jnp.where(first_core, other, mine)
        state = unpack(below[k][...].astype(F32)) + jnp.concatenate([top, bottom], axis=0)
    held[0] = pack(state)
    for j in range(1, GROUP):
        state = step(parts, j - 1, shifts[j - 1], state)
        held[j] = pack(state)
    deal(held, out)


def entering(below, maps, parts, shifts, tie):
    half, columns = below[0].shape
    count = len(below)
    return call(
        functools.partial(entering_kernel, count),
        "entering",
        [IN_VMEM] * (3 * count - 1) + [IN_PLACE] + [IN_VMEM] * GROUP,
        [shape(half, columns)] * GROUP,
        [pltpu.VMEM((GROUP, half, columns), BF16), pltpu.VMEM((GROUP, half, columns), F32)],
        4 * parts.size * columns,
        2 * parts.size,
    )(*below, *maps, parts, tie, *shifts)


def waves_kernel(own, near, across, far, prop, image, out, arrived):
    collect((own, near, across, far), arrived)
    split = GROUP // prop.shape[0]
    for e in range(prop.shape[0]):
        near, far = arrived[e * split].astype(F32), arrived[e * split + 1].astype(F32)
        left = left_lanes(near)
        top = jnp.where(left, near, swap_lanes(far))
        low = jnp.where(left, swap_lanes(near), far)
        incoming = jnp.concatenate([top, low], axis=0).astype(BF16)
        out[e] = (dot(prop[e], incoming) + image[e]).astype(BF16)


def final_waves(arrived, prop, image):
    half, columns = arrived[0].shape
    return call(
        waves_kernel,
        "waves",
        [IN_VMEM] * (GROUP + 2),
        shape(*image.shape),
        [pltpu.VMEM((GROUP, half, columns), BF16)],
        2 * prop.size * columns,
        2 * prop.size + 6 * image.size,
    )(*arrived, prop, image)


def to_near(item, sections):
    return lax.ppermute(item, "sec", [(s, s ^ 1) for s in range(sections)])


def to_across(item, sections):
    return lax.ppermute(item, "sec", [(s, s // GROUP * GROUP + (s % GROUP + CORES) % GROUP) for s in range(sections)])


def to_far(item, sections):
    return lax.ppermute(item, "sec", [(s, s // GROUP * GROUP + (s % GROUP + CORES) % GROUP ^ 1) for s in range(sections)])


def exchange(own, near, across, far, sections):
    across, far = to_across(across, sections), to_far(far, sections)
    return [own, to_near(near, sections), across, far]


def up_shift(sections, k):
    return [(s, s + GROUP * k) for s in range(sections - GROUP * k)]


def spread(packed):
    half = packed.shape[1] // 2
    return jnp.concatenate([packed[:, :half], packed[:, half:]], axis=0)


def maps_below(total_map, sections):
    out = []
    for k in range(1, sections // GROUP - 1):
        half = lax.ppermute(total_map, "sec", up_shift(sections, k))
        out += [half, to_near(half, sections)]
    return out


def totals_below(total, sections):
    return [lax.ppermute(total, "sec", up_shift(sections, k)) for k in range(1, sections // GROUP)]


def scan_below(total_map, total, sections):
    shift = lax.ppermute(spread(total).astype(F32), "sec", up_shift(sections, 1))
    joined = lax.ppermute(total_map, "sec", up_shift(sections, 1))
    stride = 1
    while stride < sections // GROUP:
        other = lax.ppermute(shift, "sec", up_shift(sections, stride))
        other_map = lax.ppermute(joined, "sec", up_shift(sections, stride))
        shift = shift + dot_wide(joined, other)
        joined = dot_wide(joined, other_map)
        stride *= 2
    half = shift.shape[0] // 2
    return [jnp.concatenate([shift[:half], shift[half:]], axis=1)]


def per_device(green, injected, coupling, pattern, owner, pair_blocks):
    sections = lax.axis_size("sec")
    green, inject = green[0], injected[0]

    coupling, tiles = coupling[0], pattern[0].T
    outgoing, own_map, other_map = pairs_and_maps(
        owner[:, 0], pair_blocks.T, tiles, green, inject, coupling, sections
    )
    across = to_across(other_map, sections)
    near = to_near(own_map, sections)
    far = to_near(across, sections)
    received = lax.all_to_all(outgoing, "sec", split_axis=0, concat_axis=0, tiled=True)

    few = sections // GROUP <= 4
    total_map, parts = chain([own_map, near, across, far], few)
    maps = maps_below(total_map, sections) if few else []
    prop, face_rows = propagator(tiles, green, coupling, total_map)

    source, *quarters = placed_source(received, inject, face_rows, total_map)
    shifts = exchange(*quarters, sections)
    total = plane_total(shifts, parts)
    below = totals_below(total, sections) if few else scan_below(total_map, total, sections)
    image = images(green, source)
    arrived = exchange(*entering(below, maps, parts, shifts, image), sections)
    return final_waves(arrived, prop, image)[None]


def solution(mesh):
    in_specs = (
        P("sec", "grp", None, None),
        P("sec", "grp", None, None),
        P("sec", None, None),
        P("sec", None, None),
        P("sec", None),
        P("sec", None),
    )
    out_specs = P("sec", "grp", None, None)
    return jax.shard_map(
        per_device, mesh=mesh, in_specs=in_specs, out_specs=out_specs, check_vma=False
    )
```

```python
import functools

import jax
import jax.numpy as jnp
from jax import lax
from jax.experimental import pallas as pl
from jax.experimental.pallas import tpu as pltpu
from jax.sharding import PartitionSpec as P

BLK = 32
CAP = 2
GROUP = 4
HEAD = 16
CORES = 2

HIGH = lax.Precision.HIGHEST
F32 = jnp.float32
BF16 = jnp.bfloat16
VMEM_SMALL = 16 * 1024 * 1024
VMEM_WHOLE = 63400000
PEAK = 1.15e9

IN_VMEM = pl.BlockSpec(memory_space=pltpu.VMEM)
IN_SMEM = pl.BlockSpec(memory_space=pltpu.SMEM)
IN_HBM = pl.BlockSpec(memory_space=pltpu.HBM)
IN_PLACE = pl.BlockSpec(memory_space=pl.ANY)


def shape(*dims, dtype=BF16):
    return jax.ShapeDtypeStruct(dims, dtype)


def call(body, name, ins, outs, scratch, micros, vmem=VMEM_SMALL, aliases=None):
    places = list(range(len(outs))) if isinstance(outs, list) else 0
    return pl.pallas_call(
        body,
        name=name,
        in_specs=ins,
        out_shape=outs,
        out_specs=jax.tree.map(lambda k: IN_PLACE if k in (aliases or {}).values() else IN_VMEM, places),
        input_output_aliases=aliases or {},
        scratch_shapes=scratch,
        compiler_params=pltpu.CompilerParams(vmem_limit_bytes=vmem),
        cost_estimate=pl.CostEstimate(flops=int(micros * PEAK), bytes_accessed=0, transcendentals=0),
    )


def place():
    return lax.axis_index("sec") % GROUP


def partners():
    here = place()
    across = (here + CORES) % GROUP
    return here, here ^ 1, across, across ^ 1


def dot(a, b):
    return jnp.dot(a, b, preferred_element_type=F32)


def dot_wide(a, b):
    return jnp.dot(a, b, precision=HIGH, preferred_element_type=F32)


def two_parts(x):
    high = x.astype(BF16)
    return high, (x - high.astype(F32)).astype(BF16)


def left_lanes(x):
    return lax.broadcasted_iota(jnp.int32, x.shape, 1) < x.shape[1] // 2


def swap_lanes(x):
    return pltpu.roll(x, x.shape[1] // 2, 1)


def pack(tall):
    half = tall.shape[0] // 2
    top, low = tall[:half], tall[half:]
    return jnp.where(left_lanes(top), top, swap_lanes(low))


def unpack(packed):
    return jnp.concatenate([packed, swap_lanes(packed)], axis=0)


def fetch(green, held, sem):
    moves = [pltpu.make_async_copy(green.at[e], held.at[e], sem.at[e]) for e in range(green.shape[0])]
    for move in moves:
        move.start()
    return moves


def mask_tiles(pattern, coupling):
    high, wide = coupling.shape[0] // pattern.shape[1], coupling.shape[1] // pattern.shape[0]
    for i in range(pattern.shape[1]):
        for j in range(pattern.shape[0]):
            at = (slice(i * high, (i + 1) * high), slice(j * wide, (j + 1) * wide))
            tile = coupling[at]
            coupling[at] = jnp.where(pattern[j, i] == 1, tile, jnp.zeros_like(tile))


def first_kernel(
    owner_in, blocks_in, pattern_in, green, inject_in, coupling_in, out, own, other,
    owner, blocks, pattern, inject, coupling, held, full, maps, slot_of, counts, sem, side,
):
    energies, orbitals, _ = green.shape
    sections = out.shape[0]
    count = owner.shape[0]
    face = coupling.shape[1]
    small = [
        pltpu.make_async_copy(src, dst, side.at[k])
        for k, (src, dst) in enumerate(
            ((owner_in, owner), (blocks_in, blocks), (pattern_in, pattern), (inject_in, inject), (coupling_in, coupling))
        )
    ]
    for move in small:
        move.start()
    moves = fetch(green, held, sem)
    rows = CAP * energies * BLK
    lane = lax.broadcasted_iota(jnp.int32, (HEAD, out.shape[2]), 1)
    none = jnp.where(lane < CAP, -1.0, 0.0).astype(BF16)

    def blank(d, _):
        counts[d] = 0
        out[d, :rows, :] = jnp.zeros((rows, out.shape[2]), BF16)
        out[d, rows : rows + HEAD, :] = none
        return 0

    lax.fori_loop(0, sections, blank, 0)
    for move in small:
        move.wait()

    def rank(q, _):
        d = owner[q]
        r = counts[d]
        counts[d] = r + 1
        slot_of[q] = r
        head = out[d, rows : rows + HEAD, :].astype(F32)
        head = jnp.where(lane == r, blocks[1, q].astype(F32), head)
        out[d, rows : rows + HEAD, :] = head.astype(BF16)
        return 0

    lax.fori_loop(0, count, rank, 0)
    mask_tiles(pattern, coupling)
    for e, move in enumerate(moves):
        move.wait()
        full[e] = dot(held[e], inject[e]).astype(BF16)
        maps[e] = dot(held[e, orbitals - face :, :], coupling[...])

        def fill(q, _):
            first = pl.multiple_of(blocks[0, q] * BLK, BLK)
            to = pl.multiple_of((slot_of[q] * energies + e) * BLK, BLK)
            out[owner[q], pl.ds(to, BLK), :] = full[e, pl.ds(first, BLK), :]
            return 0

        lax.fori_loop(0, count, fill, 0, unroll=4)
    mine = place() // CORES
    own[...] = maps[mine]
    other[...] = maps[1 - mine]


def pairs_and_maps(owner, blocks, pattern, green, inject, coupling, sections):
    energies, orbitals, _ = green.shape
    columns, face = inject.shape[2], coupling.shape[1]
    square = shape(face, face, dtype=F32)
    return call(
        first_kernel,
        "pairs_and_maps",
        [IN_HBM] * 6,
        [shape(sections, CAP * energies * BLK + HEAD, columns), square, square],
        [
            pltpu.SMEM(owner.shape, jnp.int32),
            pltpu.SMEM(blocks.shape, jnp.int32),
            pltpu.SMEM(pattern.shape, jnp.int32),
            pltpu.VMEM(inject.shape, BF16),
            pltpu.VMEM(coupling.shape, BF16),
            pltpu.VMEM(green.shape, BF16),
            pltpu.VMEM(inject.shape, BF16),
            pltpu.VMEM((energies, face, face), F32),
            pltpu.SMEM(owner.shape, jnp.int32),
            pltpu.SMEM((sections,), jnp.int32),
            pltpu.SemaphoreType.DMA((energies,)),
            pltpu.SemaphoreType.DMA((5,)),
        ],
        5.6,
        VMEM_WHOLE,
    )(owner, blocks, pattern, green, inject, coupling)


def prop_kernel(pattern, green, coupling, out, face_rows, couple):
    energies, orbitals, _ = green.shape
    face = couple.shape[1]
    couple[...] = coupling[...]
    mask_tiles(pattern, couple)
    for e in range(energies):
        out[e] = dot(green[e], couple[...]).astype(BF16)
        face_rows[e] = green[e, orbitals - face :, :]


def propagator(pattern, green, coupling):
    energies, orbitals, _ = green.shape
    face = coupling.shape[1]
    return call(
        prop_kernel,
        "prop",
        [IN_SMEM, IN_VMEM, IN_VMEM],
        [shape(energies, orbitals, face), shape(energies, face, orbitals)],
        [pltpu.VMEM(coupling.shape, BF16)],
        1.6,
    )(pattern, green, coupling)


def image_kernel(green, source, out):
    for e in range(green.shape[0]):
        out[e] = dot(green[e], source[e])


def images(green, source):
    return call(
        image_kernel,
        "image",
        [IN_VMEM] * 2,
        shape(*source.shape, dtype=F32),
        [],
        1.2,
    )(green, source)


def times(a, b):
    return dot(a[0], b[0]) + (dot(a[0], b[1]) + dot(a[1], b[0]))


def chain_kernel(own, near, across, far, total_out, whole, parts, maps, total):
    collect((own, near, across, far), maps)
    split = [two_parts(maps[j]) for j in range(GROUP)]
    lower, upper = two_parts(times(split[1], split[0])), two_parts(times(split[3], split[2]))
    total[...] = times(upper, lower)
    whole[0], whole[1] = two_parts(total[...])
    rows = total_out.shape[0]
    core = place() % CORES if rows < total.shape[0] else 0
    total_out[...] = total[pl.ds(pl.multiple_of(core * rows, rows), rows), :].astype(total_out.dtype)
    for j, (high, low) in enumerate(split):
        parts[0, j] = high
        parts[1, j] = low


def chain(maps, few):
    face = maps[0].shape[0]
    total = shape(face // CORES, face) if few else shape(face, face, dtype=F32)
    return call(
        chain_kernel,
        "chain_maps",
        [IN_VMEM] * GROUP,
        [total, shape(2, face, face), shape(2, GROUP, face, face)],
        [pltpu.VMEM((GROUP, face, face), F32), pltpu.VMEM((face, face), F32)],
        0.9,
    )(*maps)


def source_kernel(received, inject, face_rows, _map, source, own, near, across, far, _same_map, quarters, total, heads, targets, sem):
    energies, orbitals, columns = inject.shape
    sections = received.shape[0]
    half = quarters.shape[1]
    rows = CAP * energies * BLK

    def read(s, _):
        block = received[s, rows : rows + HEAD, :].astype(F32)
        heads[pl.ds(s, 1), :] = block[:1].astype(jnp.int32)
        return 0

    lax.fori_loop(0, sections, read, 0, unroll=min(sections, 8))
    fetch = pltpu.make_async_copy(heads, targets, sem)
    fetch.start()
    total[...] = inject[...].astype(F32)
    fetch.wait()

    def add(s, _):
        for r in range(CAP):
            first = pl.multiple_of(jnp.maximum(targets[s, r], 0) * BLK, BLK)
            for e in range(energies):
                item = received[s, (r * energies + e) * BLK : (r * energies + e + 1) * BLK, :]
                total[e, pl.ds(first, BLK), :] += item.astype(F32)
        return 0

    lax.fori_loop(0, sections, add, 0, unroll=2)
    split = GROUP // energies
    for e in range(energies):
        source[e] = total[e].astype(BF16)
        tall = dot(face_rows[e], source[e])
        quarters[e * split] = pack(tall)
        second = jnp.where(left_lanes(tall[:half]), swap_lanes(tall[:half]), tall[half:])
        quarters[e * split + 1] = second
    deal(quarters, (own, near, across, far))


def placed_source(received, inject, face_rows, passed):
    face = face_rows.shape[1]
    energies, orbitals, columns = inject.shape
    sections = received.shape[0]
    return call(
        source_kernel,
        "source_and_face",
        [IN_VMEM, IN_VMEM, IN_VMEM, IN_PLACE],
        [shape(*inject.shape)] + [shape(face // 2, columns)] * GROUP + [shape(*passed.shape, dtype=passed.dtype)],
        [
            pltpu.VMEM((GROUP, face // 2, columns), F32),
            pltpu.VMEM(inject.shape, F32),
            pltpu.VMEM((sections, columns), jnp.int32),
            pltpu.SMEM((sections, columns), jnp.int32),
            pltpu.SemaphoreType.DMA,
        ],
        1.4,
        aliases={3: 1 + GROUP},
    )(received, inject, face_rows, passed)


def deal(items, outs):
    for out, at in zip(outs, partners()):
        out[...] = items[at].astype(out.dtype)


def collect(refs, held):
    for ref, at in zip(refs, partners()):
        held[at] = ref[...]


def step(parts, j, shift, state):
    return unpack(shift.astype(F32)) + times((parts[0, j], parts[1, j]), two_parts(state))


def total_kernel(own, near, across, far, parts, _map, out, _same_map, shifts):
    collect((own, near, across, far), shifts)
    state = unpack(shifts[0].astype(F32))
    for j in range(1, GROUP):
        state = step(parts, j, shifts[j], state)
    out[...] = pack(state).astype(BF16)


def plane_total(shifts, parts, passed):
    half, columns = shifts[0].shape
    return call(
        total_kernel,
        "plane_total",
        [IN_VMEM] * (GROUP + 1) + [IN_PLACE],
        [shape(half, columns), shape(*passed.shape, dtype=passed.dtype)],
        [pltpu.VMEM((GROUP, half, columns), BF16)],
        0.9,
        aliases={GROUP + 1: 1},
    )(*shifts, parts, passed)


def pair_kernel(total, below, whole, out):
    state = unpack(below[...].astype(F32))
    state = unpack(total[...].astype(F32)) + times((whole[0], whole[1]), two_parts(state))
    out[...] = pack(state).astype(BF16)


def pair_total(total, below, whole):
    return call(pair_kernel, "pair_total", [IN_VMEM] * 3, shape(*total.shape), [], 0.5)(total, below, whole)


def entering_kernel(below, second, mine_map, other_map, parts, _image, *refs):
    arrived, out = refs[:GROUP], refs[GROUP : 2 * GROUP]
    shifts, held = refs[2 * GROUP :]
    collect(arrived, shifts)
    twice = unpack(second[...].astype(F32)).astype(BF16)
    mine, other = dot(mine_map[...], twice), dot(other_map[...], twice)
    first_core = place() % CORES == 0
    top, bottom = jnp.where(first_core, mine, other), jnp.where(first_core, other, mine)
    state = unpack(below[...].astype(F32)) + jnp.concatenate([top, bottom], axis=0)
    sweep_plane(state, parts, shifts, held, out)


def sweep_plane(state, parts, shifts, held, out):
    held[0] = pack(state)
    for j in range(1, GROUP):
        state = step(parts, j - 1, shifts[j - 1], state)
        held[j] = pack(state)
    deal(held, out)


def entering(below, second, maps, parts, shifts, tie):
    half, columns = below.shape
    return call(
        entering_kernel,
        "entering",
        [IN_VMEM] * 5 + [IN_PLACE] + [IN_VMEM] * GROUP,
        [shape(half, columns)] * GROUP,
        [pltpu.VMEM((GROUP, half, columns), BF16), pltpu.VMEM((GROUP, half, columns), F32)],
        1.4,
    )(below, second, *maps, parts, tie, *shifts)


def entering_from_kernel(base, parts, *refs):
    shifts, held = refs[2 * GROUP :]
    collect(refs[:GROUP], shifts)
    sweep_plane(unpack(base[...]), parts, shifts, held, refs[GROUP : 2 * GROUP])


def entering_from(base, parts, shifts):
    half, columns = base.shape
    return call(
        entering_from_kernel,
        "entering",
        [IN_VMEM] * (2 + GROUP),
        [shape(half, columns)] * GROUP,
        [pltpu.VMEM((GROUP, half, columns), BF16), pltpu.VMEM((GROUP, half, columns), F32)],
        1.4,
    )(base, parts, *shifts)


def waves_kernel(own, near, across, far, prop, image, out, arrived):
    collect((own, near, across, far), arrived)
    split = GROUP // prop.shape[0]
    for e in range(prop.shape[0]):
        near, far = arrived[e * split].astype(F32), arrived[e * split + 1].astype(F32)
        left = left_lanes(near)
        top = jnp.where(left, near, swap_lanes(far))
        low = jnp.where(left, swap_lanes(near), far)
        incoming = jnp.concatenate([top, low], axis=0).astype(BF16)
        out[e] = (dot(prop[e], incoming) + image[e]).astype(BF16)


def final_waves(arrived, prop, image):
    half, columns = arrived[0].shape
    return call(
        waves_kernel,
        "waves",
        [IN_VMEM] * (GROUP + 2),
        shape(*image.shape),
        [pltpu.VMEM((GROUP, half, columns), BF16)],
        1.3,
    )(*arrived, prop, image)


def to_near(item, sections):
    return lax.ppermute(item, "sec", [(s, s ^ 1) for s in range(sections)])


def to_across(item, sections):
    return lax.ppermute(item, "sec", [(s, s // GROUP * GROUP + (s % GROUP + CORES) % GROUP) for s in range(sections)])


def to_far(item, sections):
    return lax.ppermute(item, "sec", [(s, s // GROUP * GROUP + (s % GROUP + CORES) % GROUP ^ 1) for s in range(sections)])


def exchange(own, near, across, far, sections):
    across, far = to_across(across, sections), to_far(far, sections)
    return [own, to_near(near, sections), across, far]


def up_shift(sections, k):
    return [(s, s + GROUP * k) for s in range(sections - GROUP * k)]


def spread(packed):
    half = packed.shape[1] // 2
    return jnp.concatenate([packed[:, :half], packed[:, half:]], axis=0)


def upward(item, k, sections):
    return lax.ppermute(item, "sec", up_shift(sections, k))


def scan_below(total_map, total, sections):
    shift = lax.ppermute(spread(total).astype(F32), "sec", up_shift(sections, 1))
    joined = lax.ppermute(total_map, "sec", up_shift(sections, 1))
    stride = 1
    while stride < sections // GROUP:
        other = lax.ppermute(shift, "sec", up_shift(sections, stride))
        other_map = lax.ppermute(joined, "sec", up_shift(sections, stride))
        shift = shift + dot_wide(joined, other)
        joined = dot_wide(joined, other_map)
        stride *= 2
    half = shift.shape[0] // 2
    return jnp.concatenate([shift[:half], shift[half:]], axis=1)


def per_device(green, injected, coupling, pattern, owner, pair_blocks):
    sections = lax.axis_size("sec")
    green, inject = green[0], injected[0]

    coupling, tiles = coupling[0], pattern[0].T
    outgoing, own_map, other_map = pairs_and_maps(
        owner[:, 0], pair_blocks.T, tiles, green, inject, coupling, sections
    )
    across = to_across(other_map, sections)
    near = to_near(own_map, sections)
    received = lax.all_to_all(outgoing, "sec", split_axis=0, concat_axis=0, tiled=True)
    prop, face_rows = propagator(tiles, green, coupling)

    source, *quarters, across = placed_source(received, inject, face_rows, across)
    shifts = exchange(*quarters, sections)
    far = to_near(across, sections)
    few = sections // GROUP <= 4
    total_map, whole, parts = chain([own_map, near, across, far], few)
    total, total_map = plane_total(shifts, parts, total_map)
    image = images(green, source)
    if few:
        below = upward(total, 1, sections)
        map_below = upward(total_map, 1, sections)
        second = upward(pair_total(total, below, whole), 2, sections)
        maps = (map_below, to_near(map_below, sections))
        entered = entering(below, second, maps, parts, shifts, image)
    else:
        entered = entering_from(scan_below(total_map, total, sections), parts, shifts)
    arrived = exchange(*entered, sections)
    return final_waves(arrived, prop, image)[None]


def solution(mesh):
    in_specs = (
        P("sec", "grp", None, None),
        P("sec", "grp", None, None),
        P("sec", None, None),
        P("sec", None, None),
        P("sec", None),
        P("sec", None),
    )
    out_specs = P("sec", "grp", None, None)
    return jax.shard_map(
        per_device, mesh=mesh, in_specs=in_specs, out_specs=out_specs, check_vma=False
    )
```

```python
import functools

import jax
import jax.numpy as jnp
from jax import lax
from jax.experimental import pallas as pl
from jax.experimental.pallas import tpu as pltpu
from jax.sharding import PartitionSpec as P

BLK = 32
CAP = 2
GROUP = 4
HEAD = 16
CORES = 2

HIGH = lax.Precision.HIGHEST
F32 = jnp.float32
BF16 = jnp.bfloat16
VMEM_SMALL = 16 * 1024 * 1024
VMEM_MOST = 60500000
VMEM_WHOLE = 63400000
PEAK = 1.15e9

IN_VMEM = pl.BlockSpec(memory_space=pltpu.VMEM)
IN_SMEM = pl.BlockSpec(memory_space=pltpu.SMEM)
IN_HBM = pl.BlockSpec(memory_space=pltpu.HBM)
IN_PLACE = pl.BlockSpec(memory_space=pl.ANY)


def shape(*dims, dtype=BF16):
    return jax.ShapeDtypeStruct(dims, dtype)


def call(body, name, ins, outs, scratch, micros, vmem=VMEM_SMALL, aliases=None):
    places = list(range(len(outs))) if isinstance(outs, list) else 0
    return pl.pallas_call(
        body,
        name=name,
        in_specs=ins,
        out_shape=outs,
        out_specs=jax.tree.map(lambda k: IN_PLACE if k in (aliases or {}).values() else IN_VMEM, places),
        input_output_aliases=aliases or {},
        scratch_shapes=scratch,
        compiler_params=pltpu.CompilerParams(vmem_limit_bytes=vmem),
        cost_estimate=pl.CostEstimate(flops=int(micros * PEAK), bytes_accessed=0, transcendentals=0),
    )


def place():
    return lax.axis_index("sec") % GROUP


def partners():
    here = place()
    across = (here + CORES) % GROUP
    return here, here ^ 1, across, across ^ 1


def dot(a, b):
    return jnp.dot(a, b, preferred_element_type=F32)


def dot_wide(a, b):
    return jnp.dot(a, b, precision=HIGH, preferred_element_type=F32)


def two_parts(x):
    high = x.astype(BF16)
    return high, (x - high.astype(F32)).astype(BF16)


def left_lanes(x):
    return lax.broadcasted_iota(jnp.int32, x.shape, 1) < x.shape[1] // 2


def swap_lanes(x):
    return pltpu.roll(x, x.shape[1] // 2, 1)


def pack(tall):
    half = tall.shape[0] // 2
    top, low = tall[:half], tall[half:]
    return jnp.where(left_lanes(top), top, swap_lanes(low))


def unpack(packed):
    return jnp.concatenate([packed, swap_lanes(packed)], axis=0)


def fetch(green, held, sem):
    moves = [pltpu.make_async_copy(green.at[e], held.at[e], sem.at[e]) for e in range(green.shape[0])]
    for move in moves:
        move.start()
    return moves


def mask_tiles(pattern, coupling):
    high, wide = coupling.shape[0] // pattern.shape[1], coupling.shape[1] // pattern.shape[0]
    for i in range(pattern.shape[1]):
        for j in range(pattern.shape[0]):
            at = (slice(i * high, (i + 1) * high), slice(j * wide, (j + 1) * wide))
            tile = coupling[at]
            coupling[at] = jnp.where(pattern[j, i] == 1, tile, jnp.zeros_like(tile))


def first_kernel(
    owner_in, blocks_in, pattern_in, green, inject_in, coupling_in, out, own, other,
    owner, blocks, pattern, inject, coupling, held, full, maps, slot_of, counts, sem, side,
):
    energies, orbitals, _ = green.shape
    sections = out.shape[0]
    count = owner.shape[0]
    face = coupling.shape[1]
    small = [
        pltpu.make_async_copy(src, dst, side.at[k])
        for k, (src, dst) in enumerate(
            ((owner_in, owner), (blocks_in, blocks), (pattern_in, pattern), (inject_in, inject), (coupling_in, coupling))
        )
    ]
    for move in small:
        move.start()
    moves = fetch(green, held, sem)
    rows = CAP * energies * BLK
    lane = lax.broadcasted_iota(jnp.int32, (HEAD, out.shape[2]), 1)
    none = jnp.where(lane < CAP, -1.0, 0.0).astype(BF16)

    def blank(d, _):
        counts[d] = 0
        out[d, :rows, :] = jnp.zeros((rows, out.shape[2]), BF16)
        out[d, rows : rows + HEAD, :] = none
        return 0

    lax.fori_loop(0, sections, blank, 0)
    for move in small:
        move.wait()

    def rank(q, _):
        d = owner[q]
        r = counts[d]
        counts[d] = r + 1
        slot_of[q] = r
        head = out[d, rows : rows + HEAD, :].astype(F32)
        head = jnp.where(lane == r, blocks[1, q].astype(F32), head)
        out[d, rows : rows + HEAD, :] = head.astype(BF16)
        return 0

    lax.fori_loop(0, count, rank, 0)
    mask_tiles(pattern, coupling)
    for e, move in enumerate(moves):
        move.wait()
        full[e] = dot(held[e], inject[e]).astype(BF16)
        maps[e] = dot(held[e, orbitals - face :, :], coupling[...])

        def fill(q, _):
            first = pl.multiple_of(blocks[0, q] * BLK, BLK)
            to = pl.multiple_of((slot_of[q] * energies + e) * BLK, BLK)
            out[owner[q], pl.ds(to, BLK), :] = full[e, pl.ds(first, BLK), :]
            return 0

        lax.fori_loop(0, count, fill, 0, unroll=4)
    mine = place() // CORES
    own[...] = maps[mine]
    other[...] = maps[1 - mine]


def pairs_and_maps(owner, blocks, pattern, green, inject, coupling, sections):
    energies, orbitals, _ = green.shape
    columns, face = inject.shape[2], coupling.shape[1]
    square = shape(face, face, dtype=F32)
    return call(
        first_kernel,
        "pairs_and_maps",
        [IN_HBM] * 6,
        [shape(sections, CAP * energies * BLK + HEAD, columns), square, square],
        [
            pltpu.SMEM(owner.shape, jnp.int32),
            pltpu.SMEM(blocks.shape, jnp.int32),
            pltpu.SMEM(pattern.shape, jnp.int32),
            pltpu.VMEM(inject.shape, BF16),
            pltpu.VMEM(coupling.shape, BF16),
            pltpu.VMEM(green.shape, BF16),
            pltpu.VMEM(inject.shape, BF16),
            pltpu.VMEM((energies, face, face), F32),
            pltpu.SMEM(owner.shape, jnp.int32),
            pltpu.SMEM((sections,), jnp.int32),
            pltpu.SemaphoreType.DMA((energies,)),
            pltpu.SemaphoreType.DMA((5,)),
        ],
        5.6,
        VMEM_WHOLE,
    )(owner, blocks, pattern, green, inject, coupling)


def prop_kernel(pattern_in, green, coupling_in, out, pattern, coupling, held, sem, side):
    tiles = pltpu.make_async_copy(pattern_in, pattern, side.at[0])
    whole = pltpu.make_async_copy(coupling_in, coupling, side.at[1])
    tiles.start()
    whole.start()
    moves = fetch(green, held, sem)
    tiles.wait()
    whole.wait()
    mask_tiles(pattern, coupling)
    for e, move in enumerate(moves):
        move.wait()
        out[e] = dot(held[e], coupling[...]).astype(BF16)


def propagator(pattern, green, coupling):
    energies, orbitals, _ = green.shape
    return call(
        prop_kernel,
        "prop",
        [IN_HBM] * 3,
        shape(energies, orbitals, coupling.shape[1]),
        [
            pltpu.SMEM(pattern.shape, jnp.int32),
            pltpu.VMEM(coupling.shape, BF16),
            pltpu.VMEM(green.shape, BF16),
            pltpu.SemaphoreType.DMA((energies,)),
            pltpu.SemaphoreType.DMA((2,)),
        ],
        5.0,
        VMEM_WHOLE,
    )(pattern, green, coupling)


def rows_kernel(green, out, sem):
    face = out.shape[1]
    moves = [
        pltpu.make_async_copy(green.at[e, pl.ds(green.shape[1] - face, face)], out.at[e], sem.at[e])
        for e in range(green.shape[0])
    ]
    for move in moves:
        move.start()
    for move in moves:
        move.wait()


def face_rows_of(green, face):
    energies, _, orbitals = green.shape
    return call(
        rows_kernel,
        "face_rows",
        [IN_HBM],
        shape(energies, face, orbitals),
        [pltpu.SemaphoreType.DMA((energies,))],
        1.5,
        VMEM_MOST,
    )(green)


def image_kernel(green, source, out):
    for e in range(green.shape[0]):
        out[e] = dot(green[e], source[e])


def images(green, source):
    return call(
        image_kernel,
        "image",
        [IN_VMEM] * 2,
        shape(*source.shape, dtype=F32),
        [],
        1.2,
    )(green, source)


def times(a, b):
    return dot(a[0], b[0]) + (dot(a[0], b[1]) + dot(a[1], b[0]))


def chain_kernel(own, near, across, far, total_out, parts, maps, total):
    collect((own, near, across, far), maps)
    split = [two_parts(maps[j]) for j in range(GROUP)]
    lower, upper = two_parts(times(split[1], split[0])), two_parts(times(split[3], split[2]))
    total[...] = times(upper, lower)
    rows = total_out.shape[0]
    core = place() % CORES if rows < total.shape[0] else 0
    total_out[...] = total[pl.ds(pl.multiple_of(core * rows, rows), rows), :].astype(total_out.dtype)
    for j, (high, low) in enumerate(split):
        parts[0, j] = high
        parts[1, j] = low


def chain(maps, few):
    face = maps[0].shape[0]
    total = shape(face // CORES, face) if few else shape(face, face, dtype=F32)
    return call(
        chain_kernel,
        "chain_maps",
        [IN_VMEM] * GROUP,
        [total, shape(2, GROUP, face, face)],
        [pltpu.VMEM((GROUP, face, face), F32), pltpu.VMEM((face, face), F32)],
        0.9,
    )(*maps)


def source_kernel(received, inject, face_rows, _prop, _map, source, own, near, across, far, _same_map, quarters, total, heads, targets, sem):
    energies, orbitals, columns = inject.shape
    sections = received.shape[0]
    half = quarters.shape[1]
    rows = CAP * energies * BLK

    def read(s, _):
        block = received[s, rows : rows + HEAD, :].astype(F32)
        heads[pl.ds(s, 1), :] = block[:1].astype(jnp.int32)
        return 0

    lax.fori_loop(0, sections, read, 0, unroll=min(sections, 8))
    fetch = pltpu.make_async_copy(heads, targets, sem)
    fetch.start()
    total[...] = inject[...].astype(F32)
    fetch.wait()

    def add(s, _):
        for r in range(CAP):
            first = pl.multiple_of(jnp.maximum(targets[s, r], 0) * BLK, BLK)
            for e in range(energies):
                item = received[s, (r * energies + e) * BLK : (r * energies + e + 1) * BLK, :]
                total[e, pl.ds(first, BLK), :] += item.astype(F32)
        return 0

    lax.fori_loop(0, sections, add, 0, unroll=2)
    split = GROUP // energies
    for e in range(energies):
        source[e] = total[e].astype(BF16)
        tall = dot(face_rows[e], source[e])
        quarters[e * split] = pack(tall)
        second = jnp.where(left_lanes(tall[:half]), swap_lanes(tall[:half]), tall[half:])
        quarters[e * split + 1] = second
    deal(quarters, (own, near, across, far))


def placed_source(received, inject, face_rows, prop, passed):
    face = face_rows.shape[1]
    energies, orbitals, columns = inject.shape
    sections = received.shape[0]
    return call(
        source_kernel,
        "source_and_face",
        [IN_VMEM, IN_VMEM, IN_VMEM, IN_PLACE, IN_PLACE],
        [shape(*inject.shape)] + [shape(face // 2, columns)] * GROUP + [shape(*passed.shape, dtype=passed.dtype)],
        [
            pltpu.VMEM((GROUP, face // 2, columns), F32),
            pltpu.VMEM(inject.shape, F32),
            pltpu.VMEM((sections, columns), jnp.int32),
            pltpu.SMEM((sections, columns), jnp.int32),
            pltpu.SemaphoreType.DMA,
        ],
        1.4,
        aliases={4: 1 + GROUP},
    )(received, inject, face_rows, prop, passed)


def deal(items, outs):
    for out, at in zip(outs, partners()):
        out[...] = items[at].astype(out.dtype)


def collect(refs, held):
    for ref, at in zip(refs, partners()):
        held[at] = ref[...]


def step(parts, j, shift, state):
    return unpack(shift.astype(F32)) + times((parts[0, j], parts[1, j]), two_parts(state))


def total_kernel(own, near, across, far, parts, out, shifts):
    collect((own, near, across, far), shifts)
    state = unpack(shifts[0].astype(F32))
    for j in range(1, GROUP):
        state = step(parts, j, shifts[j], state)
    out[...] = pack(state).astype(BF16)


def plane_total(shifts, parts):
    half, columns = shifts[0].shape
    return call(
        total_kernel,
        "plane_total",
        [IN_VMEM] * (GROUP + 1),
        shape(half, columns),
        [pltpu.VMEM((GROUP, half, columns), BF16)],
        0.9,
    )(*shifts, parts)


def entering_kernel(count, *refs):
    below, maps = refs[:count], refs[count : 3 * count - 2]
    parts, _image = refs[3 * count - 2 : 3 * count]
    arrived, out = refs[3 * count : 3 * count + GROUP], refs[3 * count + GROUP : -2]
    shifts, held = refs[-2:]
    collect(arrived, shifts)
    first_core = place() % CORES == 0
    state = unpack(below[-1][...].astype(F32))
    for k in range(count - 2, -1, -1):
        high, low = two_parts(state)
        mine, other = (dot(half[...], high) + dot(half[...], low) for half in maps[2 * k : 2 * k + 2])
        top, bottom = jnp.where(first_core, mine, other), jnp.where(first_core, other, mine)
        state = unpack(below[k][...].astype(F32)) + jnp.concatenate([top, bottom], axis=0)
    sweep_plane(state, parts, shifts, held, out)


def sweep_plane(state, parts, shifts, held, out):
    held[0] = pack(state)
    for j in range(1, GROUP):
        state = step(parts, j - 1, shifts[j - 1], state)
        held[j] = pack(state)
    deal(held, out)


def entering(below, maps, parts, shifts, tie):
    half, columns = below[0].shape
    count = len(below)
    return call(
        functools.partial(entering_kernel, count),
        "entering",
        [IN_VMEM] * (3 * count - 1) + [IN_PLACE] + [IN_VMEM] * GROUP,
        [shape(half, columns)] * GROUP,
        [pltpu.VMEM((GROUP, half, columns), BF16), pltpu.VMEM((GROUP, half, columns), F32)],
        1.4,
    )(*below, *maps, parts, tie, *shifts)


def entering_from_kernel(base, parts, *refs):
    shifts, held = refs[2 * GROUP :]
    collect(refs[:GROUP], shifts)
    sweep_plane(unpack(base[...]), parts, shifts, held, refs[GROUP : 2 * GROUP])


def entering_from(base, parts, shifts):
    half, columns = base.shape
    return call(
        entering_from_kernel,
        "entering",
        [IN_VMEM] * (2 + GROUP),
        [shape(half, columns)] * GROUP,
        [pltpu.VMEM((GROUP, half, columns), BF16), pltpu.VMEM((GROUP, half, columns), F32)],
        1.4,
    )(base, parts, *shifts)


def waves_kernel(own, near, across, far, prop, image, out, arrived):
    collect((own, near, across, far), arrived)
    split = GROUP // prop.shape[0]
    for e in range(prop.shape[0]):
        near, far = arrived[e * split].astype(F32), arrived[e * split + 1].astype(F32)
        left = left_lanes(near)
        top = jnp.where(left, near, swap_lanes(far))
        low = jnp.where(left, swap_lanes(near), far)
        incoming = jnp.concatenate([top, low], axis=0).astype(BF16)
        out[e] = (dot(prop[e], incoming) + image[e]).astype(BF16)


def final_waves(arrived, prop, image):
    half, columns = arrived[0].shape
    return call(
        waves_kernel,
        "waves",
        [IN_VMEM] * (GROUP + 2),
        shape(*image.shape),
        [pltpu.VMEM((GROUP, half, columns), BF16)],
        1.3,
    )(*arrived, prop, image)


def to_near(item, sections):
    return lax.ppermute(item, "sec", [(s, s ^ 1) for s in range(sections)])


def to_across(item, sections):
    return lax.ppermute(item, "sec", [(s, s // GROUP * GROUP + (s % GROUP + CORES) % GROUP) for s in range(sections)])


def to_far(item, sections):
    return lax.ppermute(item, "sec", [(s, s // GROUP * GROUP + (s % GROUP + CORES) % GROUP ^ 1) for s in range(sections)])


def exchange(own, near, across, far, sections):
    across, far = to_across(across, sections), to_far(far, sections)
    return [own, to_near(near, sections), across, far]


def up_shift(sections, k):
    return [(s, s + GROUP * k) for s in range(sections - GROUP * k)]


def spread(packed):
    half = packed.shape[1] // 2
    return jnp.concatenate([packed[:, :half], packed[:, half:]], axis=0)


def upward(item, k, sections):
    return lax.ppermute(item, "sec", up_shift(sections, k))


def scan_below(total_map, total, sections):
    shift = lax.ppermute(spread(total).astype(F32), "sec", up_shift(sections, 1))
    joined = lax.ppermute(total_map, "sec", up_shift(sections, 1))
    stride = 1
    while stride < sections // GROUP:
        other = lax.ppermute(shift, "sec", up_shift(sections, stride))
        other_map = lax.ppermute(joined, "sec", up_shift(sections, stride))
        shift = shift + dot_wide(joined, other)
        joined = dot_wide(joined, other_map)
        stride *= 2
    half = shift.shape[0] // 2
    return jnp.concatenate([shift[:half], shift[half:]], axis=1)


def per_device(green, injected, coupling, pattern, owner, pair_blocks):
    sections = lax.axis_size("sec")
    green, inject = green[0], injected[0]

    coupling, tiles = coupling[0], pattern[0].T
    outgoing, own_map, other_map = pairs_and_maps(
        owner[:, 0], pair_blocks.T, tiles, green, inject, coupling, sections
    )
    across = to_across(other_map, sections)
    near = to_near(own_map, sections)
    received = lax.all_to_all(outgoing, "sec", split_axis=0, concat_axis=0, tiled=True)
    prop = propagator(tiles, green, coupling)
    face_rows = face_rows_of(green, coupling.shape[1])

    source, *quarters, across = placed_source(received, inject, face_rows, prop, across)
    shifts = exchange(*quarters, sections)
    far = to_near(across, sections)
    planes = sections // GROUP
    total_map, parts = chain([own_map, near, across, far], planes <= 4)
    image = images(green, source)
    if planes <= 4:
        halves = [upward(total_map, k, sections) for k in range(1, planes - 1)]
        maps = [half for mine in halves for half in (mine, to_near(mine, sections))]
        total = plane_total(shifts, parts)
        below = [upward(total, k, sections) for k in range(1, planes)]
        entered = entering(below, maps, parts, shifts, image)
    else:
        total = plane_total(shifts, parts)
        entered = entering_from(scan_below(total_map, total, sections), parts, shifts)
    arrived = exchange(*entered, sections)
    return final_waves(arrived, prop, image)[None]


def solution(mesh):
    in_specs = (
        P("sec", "grp", None, None),
        P("sec", "grp", None, None),
        P("sec", None, None),
        P("sec", None, None),
        P("sec", None),
        P("sec", None),
    )
    out_specs = P("sec", "grp", None, None)
    return jax.shard_map(
        per_device, mesh=mesh, in_specs=in_specs, out_specs=out_specs, check_vma=False
    )
```

```python
import functools

import jax
import jax.numpy as jnp
from jax import lax
from jax.experimental import pallas as pl
from jax.experimental.pallas import tpu as pltpu
from jax.sharding import PartitionSpec as P

BLK = 32
CAP = 2
GROUP = 4
HEAD = 16
CORES = 2

HIGH = lax.Precision.HIGHEST
F32 = jnp.float32
BF16 = jnp.bfloat16
VMEM_SMALL = 16 * 1024 * 1024
VMEM_MOST = 60500000
VMEM_WHOLE = 63400000
PEAK = 1.15e9

IN_VMEM = pl.BlockSpec(memory_space=pltpu.VMEM)
IN_SMEM = pl.BlockSpec(memory_space=pltpu.SMEM)
IN_HBM = pl.BlockSpec(memory_space=pltpu.HBM)
IN_PLACE = pl.BlockSpec(memory_space=pl.ANY)


def shape(*dims, dtype=BF16):
    return jax.ShapeDtypeStruct(dims, dtype)


def call(body, name, ins, outs, scratch, micros, vmem=VMEM_SMALL, aliases=None):
    places = list(range(len(outs))) if isinstance(outs, list) else 0
    return pl.pallas_call(
        body,
        name=name,
        in_specs=ins,
        out_shape=outs,
        out_specs=jax.tree.map(lambda k: IN_PLACE if k in (aliases or {}).values() else IN_VMEM, places),
        input_output_aliases=aliases or {},
        scratch_shapes=scratch,
        compiler_params=pltpu.CompilerParams(vmem_limit_bytes=vmem),
        cost_estimate=pl.CostEstimate(flops=int(micros * PEAK), bytes_accessed=0, transcendentals=0),
    )


def place():
    return lax.axis_index("sec") % GROUP


def partners():
    here = place()
    across = (here + CORES) % GROUP
    return here, here ^ 1, across, across ^ 1


def dot(a, b):
    return jnp.dot(a, b, preferred_element_type=F32)


def dot_wide(a, b):
    return jnp.dot(a, b, precision=HIGH, preferred_element_type=F32)


def two_parts(x):
    high = x.astype(BF16)
    return high, (x - high.astype(F32)).astype(BF16)


def left_lanes(x):
    return lax.broadcasted_iota(jnp.int32, x.shape, 1) < x.shape[1] // 2


def swap_lanes(x):
    return pltpu.roll(x, x.shape[1] // 2, 1)


def pack(tall):
    half = tall.shape[0] // 2
    top, low = tall[:half], tall[half:]
    return jnp.where(left_lanes(top), top, swap_lanes(low))


def unpack(packed):
    return jnp.concatenate([packed, swap_lanes(packed)], axis=0)


def mask_tiles(pattern, coupling):
    high, wide = coupling.shape[0] // pattern.shape[1], coupling.shape[1] // pattern.shape[0]
    for i in range(pattern.shape[1]):
        for j in range(pattern.shape[0]):
            at = (slice(i * high, (i + 1) * high), slice(j * wide, (j + 1) * wide))
            tile = coupling[at]
            coupling[at] = jnp.where(pattern[j, i] == 1, tile, jnp.zeros_like(tile))


def pairs_kernel(owner_in, blocks_in, green, inject_in, out, owner, blocks, inject, held, product, slot_of, counts, sem, side):
    energies, orbitals, _ = green.shape
    sections = out.shape[0]
    count = owner.shape[0]
    named = held.shape[1] < orbitals
    small = [
        pltpu.make_async_copy(src, dst, side.at[k])
        for k, (src, dst) in enumerate(((owner_in, owner), (blocks_in, blocks), (inject_in, inject)))
    ]
    for move in small:
        move.start()

    def copy_of(e, q):
        first = pl.multiple_of(blocks[0, q] * BLK, BLK)
        to = pl.multiple_of(q * BLK, BLK)
        return pltpu.make_async_copy(green.at[e, pl.ds(first, BLK)], held.at[e, pl.ds(to, BLK)], sem.at[e])

    def whole(e):
        return pltpu.make_async_copy(green.at[e], held.at[e], sem.at[e])

    if not named:
        for e in range(energies):
            whole(e).start()
    for move in small[:2]:
        move.wait()
    if named:
        for e in range(energies):
            lax.fori_loop(0, count, lambda q, _, e=e: copy_of(e, q).start(), None, unroll=4)
    rows = CAP * energies * BLK
    lane = lax.broadcasted_iota(jnp.int32, (HEAD, out.shape[2]), 1)
    none = jnp.where(lane < CAP, -1.0, 0.0).astype(BF16)

    def blank(d, _):
        counts[d] = 0
        out[d, :rows, :] = jnp.zeros((rows, out.shape[2]), BF16)
        out[d, rows : rows + HEAD, :] = none
        return 0

    lax.fori_loop(0, sections, blank, 0)

    def rank(q, _):
        d = owner[q]
        r = counts[d]
        counts[d] = r + 1
        slot_of[q] = r
        head = out[d, rows : rows + HEAD, :].astype(F32)
        head = jnp.where(lane == r, blocks[1, q].astype(F32), head)
        out[d, rows : rows + HEAD, :] = head.astype(BF16)
        return 0

    lax.fori_loop(0, count, rank, 0)
    small[2].wait()
    for e in range(energies):
        whole_held = pltpu.make_async_copy(green.at[e, pl.ds(0, held.shape[1])], held.at[e], sem.at[e])
        whole_held.wait()
        product[...] = dot(held[e], inject[e]).astype(BF16)

        def fill(q, _):
            first = pl.multiple_of((q if named else blocks[0, q]) * BLK, BLK)
            to = pl.multiple_of((slot_of[q] * energies + e) * BLK, BLK)
            out[owner[q], pl.ds(to, BLK), :] = product[pl.ds(first, BLK), :]
            return 0

        lax.fori_loop(0, count, fill, 0, unroll=4)


def outgoing_pairs(owner, blocks, green, inject, sections):
    energies, orbitals, _ = green.shape
    columns = inject.shape[2]
    rows = min(orbitals, owner.shape[0] * BLK)
    return call(
        pairs_kernel,
        "pairs",
        [IN_HBM] * 4,
        shape(sections, CAP * energies * BLK + HEAD, columns),
        [
            pltpu.SMEM(owner.shape, jnp.int32),
            pltpu.SMEM(blocks.shape, jnp.int32),
            pltpu.VMEM(inject.shape, BF16),
            pltpu.VMEM((energies, rows, orbitals), BF16),
            pltpu.VMEM((rows, columns), BF16),
            pltpu.SMEM(owner.shape, jnp.int32),
            pltpu.SMEM((sections,), jnp.int32),
            pltpu.SemaphoreType.DMA((energies,)),
            pltpu.SemaphoreType.DMA((3,)),
        ],
        4.0,
        VMEM_WHOLE,
    )(owner, blocks, green, inject)


def maps_kernel(pattern, green, coupling, couple, own, other, maps):
    energies, orbitals, _ = green.shape
    face = coupling.shape[1]
    couple[...] = coupling[...]
    mask_tiles(pattern, couple)
    for e in range(energies):
        maps[e] = dot(green[e, orbitals - face :, :], couple[...])
    mine = place() // CORES
    own[...] = maps[mine]
    other[...] = maps[1 - mine]


def face_maps(pattern, green, coupling):
    orbitals, face = coupling.shape
    square = shape(face, face, dtype=F32)
    return call(
        maps_kernel,
        "face_maps",
        [IN_SMEM, IN_VMEM, IN_VMEM],
        [shape(orbitals, face), square, square],
        [pltpu.VMEM((green.shape[0], face, face), F32)],
        1.1,
    )(pattern, green, coupling)


def prop_kernel(green, couple, out):
    for e in range(green.shape[0]):
        out[e] = dot(green[e], couple[...]).astype(BF16)


def propagator(green, couple):
    energies, orbitals, _ = green.shape
    return call(
        prop_kernel,
        "prop",
        [IN_VMEM, IN_VMEM],
        shape(energies, orbitals, couple.shape[1]),
        [],
        1.3,
    )(green, couple)


def image_kernel(green, source, out):
    for e in range(green.shape[0]):
        out[e] = dot(green[e], source[e])


def images(green, source):
    return call(
        image_kernel,
        "image",
        [IN_VMEM] * 2,
        shape(*source.shape, dtype=F32),
        [],
        1.2,
    )(green, source)


def times(a, b):
    return dot(a[0], b[0]) + (dot(a[0], b[1]) + dot(a[1], b[0]))


def chain_kernel(own, near, across, far, total_out, parts, maps, total):
    collect((own, near, across, far), maps)
    split = [two_parts(maps[j]) for j in range(GROUP)]
    lower, upper = two_parts(times(split[1], split[0])), two_parts(times(split[3], split[2]))
    total[...] = times(upper, lower)
    rows = total_out.shape[0]
    core = place() % CORES if rows < total.shape[0] else 0
    total_out[...] = total[pl.ds(pl.multiple_of(core * rows, rows), rows), :].astype(total_out.dtype)
    for j, (high, low) in enumerate(split):
        parts[0, j] = high
        parts[1, j] = low


def chain(maps, few):
    face = maps[0].shape[0]
    total = shape(face // CORES, face) if few else shape(face, face, dtype=F32)
    return call(
        chain_kernel,
        "chain_maps",
        [IN_VMEM] * GROUP,
        [total, shape(2, GROUP, face, face)],
        [pltpu.VMEM((GROUP, face, face), F32), pltpu.VMEM((face, face), F32)],
        0.9,
    )(*maps)


def source_kernel(
    received, inject, green, _prop, _map, source, own, near, across, far, _same_map, face_rows, quarters, total, heads, targets, sem, rows_sem
):
    energies, orbitals, columns = inject.shape
    face = face_rows.shape[1]
    moves = [
        pltpu.make_async_copy(green.at[e, pl.ds(orbitals - face, face)], face_rows.at[e], rows_sem.at[e])
        for e in range(energies)
    ]
    for move in moves:
        move.start()
    sections = received.shape[0]
    half = quarters.shape[1]
    rows = CAP * energies * BLK

    def read(s, _):
        block = received[s, rows : rows + HEAD, :].astype(F32)
        heads[pl.ds(s, 1), :] = block[:1].astype(jnp.int32)
        return 0

    lax.fori_loop(0, sections, read, 0, unroll=min(sections, 8))
    fetch = pltpu.make_async_copy(heads, targets, sem)
    fetch.start()
    total[...] = inject[...].astype(F32)
    fetch.wait()

    def add(s, _):
        for r in range(CAP):
            first = pl.multiple_of(jnp.maximum(targets[s, r], 0) * BLK, BLK)
            for e in range(energies):
                item = received[s, (r * energies + e) * BLK : (r * energies + e + 1) * BLK, :]
                total[e, pl.ds(first, BLK), :] += item.astype(F32)
        return 0

    lax.fori_loop(0, sections, add, 0, unroll=2)
    split = GROUP // energies
    for e in range(energies):
        source[e] = total[e].astype(BF16)
        moves[e].wait()
        tall = dot(face_rows[e], source[e])
        quarters[e * split] = pack(tall)
        second = jnp.where(left_lanes(tall[:half]), swap_lanes(tall[:half]), tall[half:])
        quarters[e * split + 1] = second
    deal(quarters, (own, near, across, far))


def placed_source(received, inject, green, prop, passed):
    face = passed.shape[0]
    energies, orbitals, columns = inject.shape
    sections = received.shape[0]
    return call(
        source_kernel,
        "source_and_face",
        [IN_VMEM, IN_VMEM, IN_HBM, IN_PLACE, IN_PLACE],
        [shape(*inject.shape)] + [shape(face // 2, columns)] * GROUP + [shape(*passed.shape, dtype=passed.dtype)],
        [
            pltpu.VMEM((energies, face, orbitals), BF16),
            pltpu.VMEM((GROUP, face // 2, columns), F32),
            pltpu.VMEM(inject.shape, F32),
            pltpu.VMEM((sections, columns), jnp.int32),
            pltpu.SMEM((sections, columns), jnp.int32),
            pltpu.SemaphoreType.DMA,
            pltpu.SemaphoreType.DMA((energies,)),
        ],
        1.8,
        VMEM_MOST,
        aliases={4: 1 + GROUP},
    )(received, inject, green, prop, passed)


def deal(items, outs):
    for out, at in zip(outs, partners()):
        out[...] = items[at].astype(out.dtype)


def collect(refs, held):
    for ref, at in zip(refs, partners()):
        held[at] = ref[...]


def step(parts, j, shift, state):
    return unpack(shift.astype(F32)) + times((parts[0, j], parts[1, j]), two_parts(state))


def total_kernel(own, near, across, far, parts, out, shifts):
    collect((own, near, across, far), shifts)
    state = unpack(shifts[0].astype(F32))
    for j in range(1, GROUP):
        state = step(parts, j, shifts[j], state)
    out[...] = pack(state).astype(BF16)


def plane_total(shifts, parts):
    half, columns = shifts[0].shape
    return call(
        total_kernel,
        "plane_total",
        [IN_VMEM] * (GROUP + 1),
        shape(half, columns),
        [pltpu.VMEM((GROUP, half, columns), BF16)],
        0.9,
    )(*shifts, parts)


def entering_kernel(count, *refs):
    below, maps = refs[:count], refs[count : 3 * count - 2]
    parts, _image = refs[3 * count - 2 : 3 * count]
    arrived, out = refs[3 * count : 3 * count + GROUP], refs[3 * count + GROUP : -2]
    shifts, held = refs[-2:]
    collect(arrived, shifts)
    first_core = place() % CORES == 0
    state = unpack(below[-1][...].astype(F32))
    for k in range(count - 2, -1, -1):
        high, low = two_parts(state)
        mine, other = (dot(half[...], high) + dot(half[...], low) for half in maps[2 * k : 2 * k + 2])
        top, bottom = jnp.where(first_core, mine, other), jnp.where(first_core, other, mine)
        state = unpack(below[k][...].astype(F32)) + jnp.concatenate([top, bottom], axis=0)
    sweep_plane(state, parts, shifts, held, out)


def sweep_plane(state, parts, shifts, held, out):
    held[0] = pack(state)
    for j in range(1, GROUP):
        state = step(parts, j - 1, shifts[j - 1], state)
        held[j] = pack(state)
    deal(held, out)


def entering(below, maps, parts, shifts, tie):
    half, columns = below[0].shape
    count = len(below)
    return call(
        functools.partial(entering_kernel, count),
        "entering",
        [IN_VMEM] * (3 * count - 1) + [IN_PLACE] + [IN_VMEM] * GROUP,
        [shape(half, columns)] * GROUP,
        [pltpu.VMEM((GROUP, half, columns), BF16), pltpu.VMEM((GROUP, half, columns), F32)],
        1.4,
    )(*below, *maps, parts, tie, *shifts)


def entering_from_kernel(base, parts, *refs):
    shifts, held = refs[2 * GROUP :]
    collect(refs[:GROUP], shifts)
    sweep_plane(unpack(base[...]), parts, shifts, held, refs[GROUP : 2 * GROUP])


def entering_from(base, parts, shifts):
    half, columns = base.shape
    return call(
        entering_from_kernel,
        "entering",
        [IN_VMEM] * (2 + GROUP),
        [shape(half, columns)] * GROUP,
        [pltpu.VMEM((GROUP, half, columns), BF16), pltpu.VMEM((GROUP, half, columns), F32)],
        1.4,
    )(base, parts, *shifts)


def waves_kernel(own, near, across, far, prop, image, out, arrived):
    collect((own, near, across, far), arrived)
    split = GROUP // prop.shape[0]
    for e in range(prop.shape[0]):
        near, far = arrived[e * split].astype(F32), arrived[e * split + 1].astype(F32)
        left = left_lanes(near)
        top = jnp.where(left, near, swap_lanes(far))
        low = jnp.where(left, swap_lanes(near), far)
        incoming = jnp.concatenate([top, low], axis=0).astype(BF16)
        out[e] = (dot(prop[e], incoming) + image[e]).astype(BF16)


def final_waves(arrived, prop, image):
    half, columns = arrived[0].shape
    return call(
        waves_kernel,
        "waves",
        [IN_VMEM] * (GROUP + 2),
        shape(*image.shape),
        [pltpu.VMEM((GROUP, half, columns), BF16)],
        1.3,
    )(*arrived, prop, image)


def to_near(item, sections):
    return lax.ppermute(item, "sec", [(s, s ^ 1) for s in range(sections)])


def to_across(item, sections):
    return lax.ppermute(item, "sec", [(s, s // GROUP * GROUP + (s % GROUP + CORES) % GROUP) for s in range(sections)])


def to_far(item, sections):
    return lax.ppermute(item, "sec", [(s, s // GROUP * GROUP + (s % GROUP + CORES) % GROUP ^ 1) for s in range(sections)])


def exchange(own, near, across, far, sections):
    across, far = to_across(across, sections), to_far(far, sections)
    return [own, to_near(near, sections), across, far]


def up_shift(sections, k):
    return [(s, s + GROUP * k) for s in range(sections - GROUP * k)]


def spread(packed):
    half = packed.shape[1] // 2
    return jnp.concatenate([packed[:, :half], packed[:, half:]], axis=0)


def upward(item, k, sections):
    return lax.ppermute(item, "sec", up_shift(sections, k))


def scan_below(total_map, total, sections):
    shift = lax.ppermute(spread(total).astype(F32), "sec", up_shift(sections, 1))
    joined = lax.ppermute(total_map, "sec", up_shift(sections, 1))
    stride = 1
    while stride < sections // GROUP:
        other = lax.ppermute(shift, "sec", up_shift(sections, stride))
        other_map = lax.ppermute(joined, "sec", up_shift(sections, stride))
        shift = shift + dot_wide(joined, other)
        joined = dot_wide(joined, other_map)
        stride *= 2
    half = shift.shape[0] // 2
    return jnp.concatenate([shift[:half], shift[half:]], axis=1)


def per_device(green, injected, coupling, pattern, owner, pair_blocks):
    sections = lax.axis_size("sec")
    green, inject = green[0], injected[0]

    coupling, tiles = coupling[0], pattern[0].T
    outgoing = outgoing_pairs(owner[:, 0], pair_blocks.T, green, inject, sections)
    received = lax.all_to_all(outgoing, "sec", split_axis=0, concat_axis=0, tiled=True)

    couple, own_map, other_map = face_maps(tiles, green, coupling)
    across = to_across(other_map, sections)
    near = to_near(own_map, sections)
    prop = propagator(green, couple)

    source, *quarters, across = placed_source(received, inject, green, prop, across)
    shifts = exchange(*quarters, sections)
    far = to_near(across, sections)
    planes = sections // GROUP
    total_map, parts = chain([own_map, near, across, far], planes <= 4)
    image = images(green, source)
    if planes <= 4:
        halves = [upward(total_map, k, sections) for k in range(1, planes - 1)]
        maps = [half for mine in halves for half in (mine, to_near(mine, sections))]
        total = plane_total(shifts, parts)
        below = [upward(total, k, sections) for k in range(1, planes)]
        entered = entering(below, maps, parts, shifts, image)
    else:
        total = plane_total(shifts, parts)
        entered = entering_from(scan_below(total_map, total, sections), parts, shifts)
    arrived = exchange(*entered, sections)
    return final_waves(arrived, prop, image)[None]


def solution(mesh):
    in_specs = (
        P("sec", "grp", None, None),
        P("sec", "grp", None, None),
        P("sec", None, None),
        P("sec", None, None),
        P("sec", None),
        P("sec", None),
    )
    out_specs = P("sec", "grp", None, None)
    return jax.shard_map(
        per_device, mesh=mesh, in_specs=in_specs, out_specs=out_specs, check_vma=False
    )
```

```python
import functools

import jax
import jax.numpy as jnp
from jax import lax
from jax.experimental import pallas as pl
from jax.experimental.pallas import tpu as pltpu
from jax.sharding import PartitionSpec as P

BLK = 32
CAP = 2
GROUP = 4
HEAD = 16
CORES = 2

HIGH = lax.Precision.HIGHEST
F32 = jnp.float32
BF16 = jnp.bfloat16
VMEM_SMALL = 16 * 1024 * 1024
VMEM_WHOLE = 63400000
PEAK = 1.15e9

IN_VMEM = pl.BlockSpec(memory_space=pltpu.VMEM)
IN_SMEM = pl.BlockSpec(memory_space=pltpu.SMEM)
IN_HBM = pl.BlockSpec(memory_space=pltpu.HBM)
IN_PLACE = pl.BlockSpec(memory_space=pl.ANY)


def shape(*dims, dtype=BF16):
    return jax.ShapeDtypeStruct(dims, dtype)


def call(body, name, ins, outs, scratch, micros, vmem=VMEM_SMALL, aliases=None):
    places = list(range(len(outs))) if isinstance(outs, list) else 0
    return pl.pallas_call(
        body,
        name=name,
        in_specs=ins,
        out_shape=outs,
        out_specs=jax.tree.map(lambda k: IN_PLACE if k in (aliases or {}).values() else IN_VMEM, places),
        input_output_aliases=aliases or {},
        scratch_shapes=scratch,
        compiler_params=pltpu.CompilerParams(vmem_limit_bytes=vmem),
        cost_estimate=pl.CostEstimate(flops=int(micros * PEAK), bytes_accessed=0, transcendentals=0),
    )


def place():
    return lax.axis_index("sec") % GROUP


def partners():
    here = place()
    across = (here + CORES) % GROUP
    return here, here ^ 1, across, across ^ 1


def dot(a, b):
    return jnp.dot(a, b, preferred_element_type=F32)


def dot_wide(a, b):
    return jnp.dot(a, b, precision=HIGH, preferred_element_type=F32)


def two_parts(x):
    high = x.astype(BF16)
    return high, (x - high.astype(F32)).astype(BF16)


def left_lanes(x):
    return lax.broadcasted_iota(jnp.int32, x.shape, 1) < x.shape[1] // 2


def swap_lanes(x):
    return pltpu.roll(x, x.shape[1] // 2, 1)


def pack(tall):
    half = tall.shape[0] // 2
    top, low = tall[:half], tall[half:]
    return jnp.where(left_lanes(top), top, swap_lanes(low))


def unpack(packed):
    return jnp.concatenate([packed, swap_lanes(packed)], axis=0)


def mask_tiles(pattern, coupling):
    high, wide = coupling.shape[0] // pattern.shape[1], coupling.shape[1] // pattern.shape[0]
    for i in range(pattern.shape[1]):
        for j in range(pattern.shape[0]):
            at = (slice(i * high, (i + 1) * high), slice(j * wide, (j + 1) * wide))
            tile = coupling[at]
            coupling[at] = jnp.where(pattern[j, i] == 1, tile, jnp.zeros_like(tile))


def pairs_kernel(owner_in, blocks_in, green, inject_in, out, owner, blocks, inject, held, product, slot_of, counts, sem, side):
    energies, orbitals, _ = green.shape
    sections = out.shape[0]
    count = owner.shape[0]
    named = held.shape[1] < orbitals
    small = [
        pltpu.make_async_copy(src, dst, side.at[k])
        for k, (src, dst) in enumerate(((owner_in, owner), (blocks_in, blocks), (inject_in, inject)))
    ]
    for move in small:
        move.start()

    def copy_of(e, q):
        first = pl.multiple_of(blocks[0, q] * BLK, BLK)
        to = pl.multiple_of(q * BLK, BLK)
        return pltpu.make_async_copy(green.at[e, pl.ds(first, BLK)], held.at[e, pl.ds(to, BLK)], sem.at[e])

    def whole(e):
        return pltpu.make_async_copy(green.at[e], held.at[e], sem.at[e])

    if not named:
        for e in range(energies):
            whole(e).start()
    for move in small[:2]:
        move.wait()
    if named:
        for e in range(energies):
            lax.fori_loop(0, count, lambda q, _, e=e: copy_of(e, q).start(), None, unroll=4)
    rows = CAP * energies * BLK
    lane = lax.broadcasted_iota(jnp.int32, (HEAD, out.shape[2]), 1)
    none = jnp.where(lane < CAP, -1.0, 0.0).astype(BF16)

    def blank(d, _):
        counts[d] = 0
        out[d, :rows, :] = jnp.zeros((rows, out.shape[2]), BF16)
        out[d, rows : rows + HEAD, :] = none
        return 0

    lax.fori_loop(0, sections, blank, 0)

    def rank(q, _):
        d = owner[q]
        r = counts[d]
        counts[d] = r + 1
        slot_of[q] = r
        head = out[d, rows : rows + HEAD, :].astype(F32)
        head = jnp.where(lane == r, blocks[1, q].astype(F32), head)
        out[d, rows : rows + HEAD, :] = head.astype(BF16)
        return 0

    lax.fori_loop(0, count, rank, 0)
    small[2].wait()
    for e in range(energies):
        whole_held = pltpu.make_async_copy(green.at[e, pl.ds(0, held.shape[1])], held.at[e], sem.at[e])
        whole_held.wait()
        product[...] = dot(held[e], inject[e]).astype(BF16)

        def fill(q, _):
            first = pl.multiple_of((q if named else blocks[0, q]) * BLK, BLK)
            to = pl.multiple_of((slot_of[q] * energies + e) * BLK, BLK)
            out[owner[q], pl.ds(to, BLK), :] = product[pl.ds(first, BLK), :]
            return 0

        lax.fori_loop(0, count, fill, 0, unroll=4)


def outgoing_pairs(owner, blocks, green, inject, sections):
    energies, orbitals, _ = green.shape
    columns = inject.shape[2]
    rows = min(orbitals, owner.shape[0] * BLK)
    return call(
        pairs_kernel,
        "pairs",
        [IN_HBM] * 4,
        shape(sections, CAP * energies * BLK + HEAD, columns),
        [
            pltpu.SMEM(owner.shape, jnp.int32),
            pltpu.SMEM(blocks.shape, jnp.int32),
            pltpu.VMEM(inject.shape, BF16),
            pltpu.VMEM((energies, rows, orbitals), BF16),
            pltpu.VMEM((rows, columns), BF16),
            pltpu.SMEM(owner.shape, jnp.int32),
            pltpu.SMEM((sections,), jnp.int32),
            pltpu.SemaphoreType.DMA((energies,)),
            pltpu.SemaphoreType.DMA((3,)),
        ],
        4.0,
        VMEM_WHOLE,
    )(owner, blocks, green, inject)


def maps_kernel(pattern, green, coupling, own, other, face_rows, couple, maps):
    energies, orbitals, _ = green.shape
    face = coupling.shape[1]
    couple[...] = coupling[...]
    mask_tiles(pattern, couple)
    for e in range(energies):
        rows = green[e, orbitals - face :, :]
        face_rows[e] = rows
        maps[e] = dot(rows, couple[...])
    mine = place() // CORES
    own[...] = maps[mine]
    other[...] = maps[1 - mine]


def face_maps(pattern, green, coupling):
    orbitals, face = coupling.shape
    square = shape(face, face, dtype=F32)
    return call(
        maps_kernel,
        "face_maps",
        [IN_SMEM, IN_VMEM, IN_VMEM],
        [square, square, shape(green.shape[0], face, orbitals)],
        [pltpu.VMEM(coupling.shape, BF16), pltpu.VMEM((green.shape[0], face, face), F32)],
        1.2,
    )(pattern, green, coupling)


def products_kernel(pattern, green, coupling, source, image, prop, couple):
    couple[...] = coupling[...]
    mask_tiles(pattern, couple)
    for e in range(green.shape[0]):
        image[e] = dot(green[e], source[e])
        prop[e] = dot(green[e], couple[...]).astype(BF16)


def products(pattern, green, coupling, source):
    energies, orbitals, _ = green.shape
    return call(
        products_kernel,
        "image_and_prop",
        [IN_SMEM] + [IN_VMEM] * 3,
        [shape(*source.shape, dtype=F32), shape(energies, orbitals, coupling.shape[1])],
        [pltpu.VMEM(coupling.shape, BF16)],
        2.4,
    )(pattern, green, coupling, source)


def times(a, b):
    return dot(a[0], b[0]) + (dot(a[0], b[1]) + dot(a[1], b[0]))


def chain_kernel(own, near, across, far, total_out, parts, maps):
    collect((own, near, across, far), maps)
    split = [two_parts(maps[j]) for j in range(GROUP)]
    lower, upper = two_parts(times(split[1], split[0])), two_parts(times(split[3], split[2]))
    total_out[...] = times(upper, lower).astype(total_out.dtype)
    for j, (high, low) in enumerate(split):
        parts[0, j] = high
        parts[1, j] = low


def chain(maps, dtype):
    face = maps[0].shape[0]
    return call(
        chain_kernel,
        "chain_maps",
        [IN_VMEM] * GROUP,
        [shape(face, face, dtype=dtype), shape(2, GROUP, face, face)],
        [pltpu.VMEM((GROUP, face, face), F32)],
        0.9,
    )(*maps)


def source_kernel(received, inject, face_rows, _map, source, own, near, across, far, _same_map, quarters, total, heads, targets, sem):
    energies, orbitals, columns = inject.shape
    sections = received.shape[0]
    half = quarters.shape[1]
    rows = CAP * energies * BLK

    def read(s, _):
        block = received[s, rows : rows + HEAD, :].astype(F32)
        heads[pl.ds(s, 1), :] = block[:1].astype(jnp.int32)
        return 0

    lax.fori_loop(0, sections, read, 0, unroll=min(sections, 8))
    fetch = pltpu.make_async_copy(heads, targets, sem)
    fetch.start()
    total[...] = inject[...].astype(F32)
    fetch.wait()

    def add(s, _):
        for r in range(CAP):
            first = pl.multiple_of(jnp.maximum(targets[s, r], 0) * BLK, BLK)
            for e in range(energies):
                item = received[s, (r * energies + e) * BLK : (r * energies + e + 1) * BLK, :]
                total[e, pl.ds(first, BLK), :] += item.astype(F32)
        return 0

    lax.fori_loop(0, sections, add, 0, unroll=2)
    split = GROUP // energies
    for e in range(energies):
        source[e] = total[e].astype(BF16)
        tall = dot(face_rows[e], source[e])
        quarters[e * split] = pack(tall)
        second = jnp.where(left_lanes(tall[:half]), swap_lanes(tall[:half]), tall[half:])
        quarters[e * split + 1] = second
    deal(quarters, (own, near, across, far))


def placed_source(received, inject, face_rows, passed):
    face = face_rows.shape[1]
    energies, orbitals, columns = inject.shape
    sections = received.shape[0]
    return call(
        source_kernel,
        "source_and_face",
        [IN_VMEM, IN_VMEM, IN_VMEM, IN_PLACE],
        [shape(*inject.shape)] + [shape(face // 2, columns)] * GROUP + [shape(*passed.shape, dtype=passed.dtype)],
        [
            pltpu.VMEM((GROUP, face // 2, columns), F32),
            pltpu.VMEM(inject.shape, F32),
            pltpu.VMEM((sections, columns), jnp.int32),
            pltpu.SMEM((sections, columns), jnp.int32),
            pltpu.SemaphoreType.DMA,
        ],
        1.4,
        aliases={3: 1 + GROUP},
    )(received, inject, face_rows, passed)


def deal(items, outs):
    for out, at in zip(outs, partners()):
        out[...] = items[at].astype(out.dtype)


def collect(refs, held):
    for ref, at in zip(refs, partners()):
        held[at] = ref[...]


def step(parts, j, shift, state):
    return unpack(shift.astype(F32)) + times((parts[0, j], parts[1, j]), two_parts(state))


def total_kernel(own, near, across, far, parts, out, shifts):
    collect((own, near, across, far), shifts)
    state = unpack(shifts[0].astype(F32))
    for j in range(1, GROUP):
        state = step(parts, j, shifts[j], state)
    out[...] = pack(state).astype(BF16)


def plane_total(shifts, parts):
    half, columns = shifts[0].shape
    return call(
        total_kernel,
        "plane_total",
        [IN_VMEM] * (GROUP + 1),
        shape(half, columns),
        [pltpu.VMEM((GROUP, half, columns), BF16)],
        3.0,
    )(*shifts, parts)


def entering_kernel(first, second, third, got, other, parts, _image, *refs):
    arrived, out = refs[:GROUP], refs[GROUP : 2 * GROUP]
    shifts, held = refs[2 * GROUP :]
    collect(arrived, shifts)
    first_core = place() % CORES == 0
    state = unpack(third[...].astype(F32))
    for below, (one, two) in ((second, (other, got)), (first, (got, other))):
        factor = jnp.where(first_core, one[...], two[...])
        high, low = two_parts(state)
        state = unpack(below[...].astype(F32)) + dot(factor, high) + dot(factor, low)
    sweep_plane(state, parts, shifts, held, out)


def sweep_plane(state, parts, shifts, held, out):
    held[0] = pack(state)
    for j in range(1, GROUP):
        state = step(parts, j - 1, shifts[j - 1], state)
        held[j] = pack(state)
    deal(held, out)


def entering(below, maps, parts, shifts, tie):
    half, columns = below[0].shape
    return call(
        entering_kernel,
        "entering",
        [IN_VMEM] * 6 + [IN_PLACE] + [IN_VMEM] * GROUP,
        [shape(half, columns)] * GROUP,
        [pltpu.VMEM((GROUP, half, columns), BF16), pltpu.VMEM((GROUP, half, columns), F32)],
        1.4,
    )(*below, *maps, parts, tie, *shifts)


def entering_from_kernel(base, parts, *refs):
    shifts, held = refs[2 * GROUP :]
    collect(refs[:GROUP], shifts)
    sweep_plane(unpack(base[...]), parts, shifts, held, refs[GROUP : 2 * GROUP])


def entering_from(base, parts, shifts):
    half, columns = base.shape
    return call(
        entering_from_kernel,
        "entering",
        [IN_VMEM] * (2 + GROUP),
        [shape(half, columns)] * GROUP,
        [pltpu.VMEM((GROUP, half, columns), BF16), pltpu.VMEM((GROUP, half, columns), F32)],
        1.4,
    )(base, parts, *shifts)


def waves_kernel(own, near, across, far, prop, image, out, arrived):
    collect((own, near, across, far), arrived)
    split = GROUP // prop.shape[0]
    for e in range(prop.shape[0]):
        near, far = arrived[e * split].astype(F32), arrived[e * split + 1].astype(F32)
        left = left_lanes(near)
        top = jnp.where(left, near, swap_lanes(far))
        low = jnp.where(left, swap_lanes(near), far)
        incoming = jnp.concatenate([top, low], axis=0).astype(BF16)
        out[e] = (dot(prop[e], incoming) + image[e]).astype(BF16)


def final_waves(arrived, prop, image):
    half, columns = arrived[0].shape
    return call(
        waves_kernel,
        "waves",
        [IN_VMEM] * (GROUP + 2),
        shape(*image.shape),
        [pltpu.VMEM((GROUP, half, columns), BF16)],
        1.3,
    )(*arrived, prop, image)


def to_near(item, sections):
    return lax.ppermute(item, "sec", [(s, s ^ 1) for s in range(sections)])


def to_across(item, sections):
    return lax.ppermute(item, "sec", [(s, s // GROUP * GROUP + (s % GROUP + CORES) % GROUP) for s in range(sections)])


def to_far(item, sections):
    return lax.ppermute(item, "sec", [(s, s // GROUP * GROUP + (s % GROUP + CORES) % GROUP ^ 1) for s in range(sections)])


def exchange(own, near, across, far, sections):
    across, far = to_across(across, sections), to_far(far, sections)
    return [own, to_near(near, sections), across, far]


def up_shift(sections, k):
    return [(s, s + GROUP * k) for s in range(sections - GROUP * k)]


def spread(packed):
    half = packed.shape[1] // 2
    return jnp.concatenate([packed[:, :half], packed[:, half:]], axis=0)


def maps_up(total_map, sections):
    pairs = []
    for i in range(GROUP):
        if i % CORES == 0:
            pairs += [(GROUP + i, 2 * GROUP + i), (2 * GROUP + i, 3 * GROUP + i)]
        else:
            pairs += [(GROUP + i, 3 * GROUP + i)]
    got = lax.ppermute(total_map, "sec", pairs)
    return got, to_near(got, sections)


def upward(item, k, sections):
    return lax.ppermute(item, "sec", up_shift(sections, k))


def scan_below(total_map, total, sections):
    shift = lax.ppermute(spread(total).astype(F32), "sec", up_shift(sections, 1))
    joined = lax.ppermute(total_map, "sec", up_shift(sections, 1))
    stride = 1
    while stride < sections // GROUP:
        other = lax.ppermute(shift, "sec", up_shift(sections, stride))
        other_map = lax.ppermute(joined, "sec", up_shift(sections, stride))
        shift = shift + dot_wide(joined, other)
        joined = dot_wide(joined, other_map)
        stride *= 2
    half = shift.shape[0] // 2
    return jnp.concatenate([shift[:half], shift[half:]], axis=1)


def per_device(green, injected, coupling, pattern, owner, pair_blocks):
    sections = lax.axis_size("sec")
    green, inject = green[0], injected[0]

    coupling, tiles = coupling[0], pattern[0].T
    outgoing = outgoing_pairs(owner[:, 0], pair_blocks.T, green, inject, sections)
    received = lax.all_to_all(outgoing, "sec", split_axis=0, concat_axis=0, tiled=True)

    own_map, other_map, face_rows = face_maps(tiles, green, coupling)
    across = to_across(other_map, sections)
    near = to_near(own_map, sections)

    source, *quarters, across = placed_source(received, inject, face_rows, across)
    shifts = exchange(*quarters, sections)
    far = to_near(across, sections)
    four = sections // GROUP == 4
    total_map, parts = chain([own_map, near, across, far], BF16 if four else F32)
    image, prop = products(tiles, green, coupling, source)
    if four:
        maps = maps_up(total_map, sections)
        total = plane_total(shifts, parts)
        below = [upward(total, k, sections) for k in range(1, 4)]
        entered = entering(below, maps, parts, shifts, image)
    else:
        total = plane_total(shifts, parts)
        entered = entering_from(scan_below(total_map, total, sections), parts, shifts)
    arrived = exchange(*entered, sections)
    return final_waves(arrived, prop, image)[None]


def solution(mesh):
    in_specs = (
        P("sec", "grp", None, None),
        P("sec", "grp", None, None),
        P("sec", None, None),
        P("sec", None, None),
        P("sec", None),
        P("sec", None),
    )
    out_specs = P("sec", "grp", None, None)
    return jax.shard_map(
        per_device, mesh=mesh, in_specs=in_specs, out_specs=out_specs, check_vma=False
    )
```

```python
import functools

import jax
import jax.numpy as jnp
from jax import lax
from jax.experimental import pallas as pl
from jax.experimental.pallas import tpu as pltpu
from jax.sharding import PartitionSpec as P

BLK = 32
CAP = 2
GROUP = 4
HEAD = 16
CORES = 2

HIGH = lax.Precision.HIGHEST
F32 = jnp.float32
BF16 = jnp.bfloat16
VMEM_SMALL = 16 * 1024 * 1024
VMEM_WHOLE = 63400000
PEAK = 1.15e9

IN_VMEM = pl.BlockSpec(memory_space=pltpu.VMEM)
IN_SMEM = pl.BlockSpec(memory_space=pltpu.SMEM)
IN_HBM = pl.BlockSpec(memory_space=pltpu.HBM)
IN_PLACE = pl.BlockSpec(memory_space=pl.ANY)


def shape(*dims, dtype=BF16):
    return jax.ShapeDtypeStruct(dims, dtype)


def call(body, name, ins, outs, scratch, micros, vmem=VMEM_SMALL, aliases=None):
    places = list(range(len(outs))) if isinstance(outs, list) else 0
    return pl.pallas_call(
        body,
        name=name,
        in_specs=ins,
        out_shape=outs,
        out_specs=jax.tree.map(lambda k: IN_PLACE if k in (aliases or {}).values() else IN_VMEM, places),
        input_output_aliases=aliases or {},
        scratch_shapes=scratch,
        compiler_params=pltpu.CompilerParams(vmem_limit_bytes=vmem),
        cost_estimate=pl.CostEstimate(flops=int(micros * PEAK), bytes_accessed=0, transcendentals=0),
    )


def place():
    return lax.axis_index("sec") % GROUP


def partners():
    here = place()
    across = (here + CORES) % GROUP
    return here, here ^ 1, across, across ^ 1


def dot(a, b):
    return jnp.dot(a, b, preferred_element_type=F32)


def dot_wide(a, b):
    return jnp.dot(a, b, precision=HIGH, preferred_element_type=F32)


def two_parts(x):
    high = x.astype(BF16)
    return high, (x - high.astype(F32)).astype(BF16)


def left_lanes(x):
    return lax.broadcasted_iota(jnp.int32, x.shape, 1) < x.shape[1] // 2


def swap_lanes(x):
    return pltpu.roll(x, x.shape[1] // 2, 1)


def pack(tall):
    half = tall.shape[0] // 2
    top, low = tall[:half], tall[half:]
    return jnp.where(left_lanes(top), top, swap_lanes(low))


def unpack(packed):
    return jnp.concatenate([packed, swap_lanes(packed)], axis=0)


def mask_tiles(pattern, coupling):
    high, wide = coupling.shape[0] // pattern.shape[1], coupling.shape[1] // pattern.shape[0]
    for i in range(pattern.shape[1]):
        for j in range(pattern.shape[0]):
            at = (slice(i * high, (i + 1) * high), slice(j * wide, (j + 1) * wide))
            tile = coupling[at]
            coupling[at] = jnp.where(pattern[j, i] == 1, tile, jnp.zeros_like(tile))


def pairs_kernel(owner_in, blocks_in, green, inject_in, out, owner, blocks, inject, held, product, slot_of, counts, sem, side):
    energies, orbitals, _ = green.shape
    sections = out.shape[0]
    count = owner.shape[0]
    named = held.shape[1] < orbitals
    small = [
        pltpu.make_async_copy(src, dst, side.at[k])
        for k, (src, dst) in enumerate(((owner_in, owner), (blocks_in, blocks), (inject_in, inject)))
    ]
    for move in small:
        move.start()

    def copy_of(e, q):
        first = pl.multiple_of(blocks[0, q] * BLK, BLK)
        to = pl.multiple_of(q * BLK, BLK)
        return pltpu.make_async_copy(green.at[e, pl.ds(first, BLK)], held.at[e, pl.ds(to, BLK)], sem.at[e])

    def whole(e):
        return pltpu.make_async_copy(green.at[e], held.at[e], sem.at[e])

    if not named:
        for e in range(energies):
            whole(e).start()
    for move in small[:2]:
        move.wait()
    if named:
        for e in range(energies):
            lax.fori_loop(0, count, lambda q, _, e=e: copy_of(e, q).start(), None, unroll=4)
    rows = CAP * energies * BLK
    lane = lax.broadcasted_iota(jnp.int32, (HEAD, out.shape[2]), 1)
    none = jnp.where(lane < CAP, -1.0, 0.0).astype(BF16)

    def blank(d, _):
        counts[d] = 0
        out[d, :rows, :] = jnp.zeros((rows, out.shape[2]), BF16)
        out[d, rows : rows + HEAD, :] = none
        return 0

    lax.fori_loop(0, sections, blank, 0)

    def rank(q, _):
        d = owner[q]
        r = counts[d]
        counts[d] = r + 1
        slot_of[q] = r
        head = out[d, rows : rows + HEAD, :].astype(F32)
        head = jnp.where(lane == r, blocks[1, q].astype(F32), head)
        out[d, rows : rows + HEAD, :] = head.astype(BF16)
        return 0

    lax.fori_loop(0, count, rank, 0)
    small[2].wait()
    for e in range(energies):
        whole_held = pltpu.make_async_copy(green.at[e, pl.ds(0, held.shape[1])], held.at[e], sem.at[e])
        whole_held.wait()
        product[...] = dot(held[e], inject[e]).astype(BF16)

        def fill(q, _):
            first = pl.multiple_of((q if named else blocks[0, q]) * BLK, BLK)
            to = pl.multiple_of((slot_of[q] * energies + e) * BLK, BLK)
            out[owner[q], pl.ds(to, BLK), :] = product[pl.ds(first, BLK), :]
            return 0

        lax.fori_loop(0, count, fill, 0, unroll=4)


def outgoing_pairs(owner, blocks, green, inject, sections):
    energies, orbitals, _ = green.shape
    columns = inject.shape[2]
    rows = min(orbitals, owner.shape[0] * BLK)
    return call(
        pairs_kernel,
        "pairs",
        [IN_HBM] * 4,
        shape(sections, CAP * energies * BLK + HEAD, columns),
        [
            pltpu.SMEM(owner.shape, jnp.int32),
            pltpu.SMEM(blocks.shape, jnp.int32),
            pltpu.VMEM(inject.shape, BF16),
            pltpu.VMEM((energies, rows, orbitals), BF16),
            pltpu.VMEM((rows, columns), BF16),
            pltpu.SMEM(owner.shape, jnp.int32),
            pltpu.SMEM((sections,), jnp.int32),
            pltpu.SemaphoreType.DMA((energies,)),
            pltpu.SemaphoreType.DMA((3,)),
        ],
        4.0,
        VMEM_WHOLE,
    )(owner, blocks, green, inject)


def maps_kernel(pattern, green, coupling, _token, own, other, face_rows, couple, maps):
    energies, orbitals, _ = green.shape
    face = coupling.shape[1]
    couple[...] = coupling[...]
    mask_tiles(pattern, couple)
    for e in range(energies):
        rows = green[e, orbitals - face :, :]
        face_rows[e] = rows
        maps[e] = dot(rows, couple[...])
    mine = place() // CORES
    own[...] = maps[mine]
    other[...] = maps[1 - mine]


def face_maps(pattern, green, coupling, token):
    orbitals, face = coupling.shape
    square = shape(face, face, dtype=F32)
    return call(
        maps_kernel,
        "face_maps",
        [IN_SMEM, IN_VMEM, IN_VMEM, IN_PLACE],
        [square, square, shape(green.shape[0], face, orbitals)],
        [pltpu.VMEM(coupling.shape, BF16), pltpu.VMEM((green.shape[0], face, face), F32)],
        1.2,
    )(pattern, green, coupling, token)


def fetch(green, held, sem):
    moves = [pltpu.make_async_copy(green.at[e], held.at[e], sem.at[e]) for e in range(green.shape[0])]
    for move in moves:
        move.start()
    return moves


def prop_kernel(pattern_in, green, coupling_in, out, token, pattern, coupling, held, sem, side):
    token[...] = jnp.zeros_like(token)
    tiles = pltpu.make_async_copy(pattern_in, pattern, side.at[0])
    whole = pltpu.make_async_copy(coupling_in, coupling, side.at[1])
    tiles.start()
    whole.start()
    moves = fetch(green, held, sem)
    tiles.wait()
    whole.wait()
    mask_tiles(pattern, coupling)
    for e, move in enumerate(moves):
        move.wait()
        out[e] = dot(held[e], coupling[...]).astype(BF16)


def propagator(pattern, green, coupling):
    energies, orbitals, _ = green.shape
    return call(
        prop_kernel,
        "prop",
        [IN_HBM] * 3,
        [shape(energies, orbitals, coupling.shape[1]), shape(8, 128, dtype=F32)],
        [
            pltpu.SMEM(pattern.shape, jnp.int32),
            pltpu.VMEM(coupling.shape, BF16),
            pltpu.VMEM(green.shape, BF16),
            pltpu.SemaphoreType.DMA((energies,)),
            pltpu.SemaphoreType.DMA((2,)),
        ],
        5.0,
        VMEM_WHOLE,
    )(pattern, green, coupling)


def image_kernel(green, source, out):
    for e in range(green.shape[0]):
        out[e] = dot(green[e], source[e])


def images(green, source):
    return call(image_kernel, "image", [IN_VMEM] * 2, shape(*source.shape, dtype=F32), [], 1.2)(green, source)


def times(a, b):
    return dot(a[0], b[0]) + (dot(a[0], b[1]) + dot(a[1], b[0]))


def chain_kernel(own, near, across, far, _image, total_out, parts, maps):
    collect((own, near, across, far), maps)
    split = [two_parts(maps[j]) for j in range(GROUP)]
    lower, upper = two_parts(times(split[1], split[0])), two_parts(times(split[3], split[2]))
    total_out[...] = times(upper, lower).astype(total_out.dtype)
    for j, (high, low) in enumerate(split):
        parts[0, j] = high
        parts[1, j] = low


def chain(maps, dtype, tie):
    face = maps[0].shape[0]
    return call(
        chain_kernel,
        "chain_maps",
        [IN_VMEM] * GROUP + [IN_PLACE],
        [shape(face, face, dtype=dtype), shape(2, GROUP, face, face)],
        [pltpu.VMEM((GROUP, face, face), F32)],
        0.9,
    )(*maps, tie)


def source_kernel(received, inject, face_rows, _map, source, own, near, across, far, _same_map, quarters, total, heads, targets, sem):
    energies, orbitals, columns = inject.shape
    sections = received.shape[0]
    half = quarters.shape[1]
    rows = CAP * energies * BLK

    def read(s, _):
        block = received[s, rows : rows + HEAD, :].astype(F32)
        heads[pl.ds(s, 1), :] = block[:1].astype(jnp.int32)
        return 0

    lax.fori_loop(0, sections, read, 0, unroll=min(sections, 8))
    fetch = pltpu.make_async_copy(heads, targets, sem)
    fetch.start()
    total[...] = inject[...].astype(F32)
    fetch.wait()

    def add(s, _):
        for r in range(CAP):
            first = pl.multiple_of(jnp.maximum(targets[s, r], 0) * BLK, BLK)
            for e in range(energies):
                item = received[s, (r * energies + e) * BLK : (r * energies + e + 1) * BLK, :]
                total[e, pl.ds(first, BLK), :] += item.astype(F32)
        return 0

    lax.fori_loop(0, sections, add, 0, unroll=2)
    split = GROUP // energies
    for e in range(energies):
        source[e] = total[e].astype(BF16)
        tall = dot(face_rows[e], source[e])
        quarters[e * split] = pack(tall)
        second = jnp.where(left_lanes(tall[:half]), swap_lanes(tall[:half]), tall[half:])
        quarters[e * split + 1] = second
    for out, at in zip((own, near, across, far), partners()):
        out[...] = quarters[at].astype(BF16)


def placed_source(received, inject, face_rows, passed):
    face = face_rows.shape[1]
    energies, orbitals, columns = inject.shape
    sections = received.shape[0]
    return call(
        source_kernel,
        "source_and_face",
        [IN_VMEM, IN_VMEM, IN_VMEM, IN_PLACE],
        [shape(*inject.shape)] + [shape(face // 2, columns)] * GROUP + [shape(*passed.shape, dtype=passed.dtype)],
        [
            pltpu.VMEM((GROUP, face // 2, columns), F32),
            pltpu.VMEM(inject.shape, F32),
            pltpu.VMEM((sections, columns), jnp.int32),
            pltpu.SMEM((sections, columns), jnp.int32),
            pltpu.SemaphoreType.DMA,
        ],
        1.4,
        aliases={3: 1 + GROUP},
    )(received, inject, face_rows, passed)


def collect(refs, held):
    for ref, at in zip(refs, partners()):
        held[at] = ref[...]


def step(parts, j, shift, state):
    return unpack(shift.astype(F32)) + times((parts[0, j], parts[1, j]), two_parts(state))


def total_kernel(own, near, across, far, parts, out, local, shifts):
    collect((own, near, across, far), shifts)
    state = unpack(shifts[0].astype(F32))
    for j in range(1, GROUP):
        local[j - 1] = state
        state = step(parts, j, shifts[j], state)
    out[...] = pack(state).astype(BF16)


def plane_total(shifts, parts):
    half, columns = shifts[0].shape
    return call(
        total_kernel,
        "plane_total",
        [IN_VMEM] * (GROUP + 1),
        [shape(half, columns), shape(GROUP - 1, 2 * half, columns, dtype=F32)],
        [pltpu.VMEM((GROUP, half, columns), BF16)],
        3.0,
    )(*shifts, parts)


def upto_kernel(parts, _total, out):
    maps = (parts[0, 0], parts[1, 0])
    for j in range(1, GROUP - 1):
        maps = two_parts(times((parts[0, j], parts[1, j]), maps))
        out[0, j - 1], out[1, j - 1] = maps


def maps_upto(parts, tie):
    _, _, face, _ = parts.shape
    return call(
        upto_kernel, "maps_upto", [IN_VMEM, IN_PLACE], shape(2, GROUP - 2, face, face), [], 3.0
    )(parts, tie)


def sweep_plane(state, parts, upto, local, out):
    two = two_parts(state)
    held = [pack(state)]
    for j in range(1, GROUP):
        maps = (parts[0, 0], parts[1, 0]) if j == 1 else (upto[0, j - 2], upto[1, j - 2])
        held.append(pack(local[j - 1] + times(maps, two)))
    own, near, across, work = out
    for j, item in enumerate(held):
        work[j] = item
    here, at_near, at_across, at_far = partners()
    own[...] = work[here].astype(BF16)
    near[...] = work[at_near].astype(BF16)
    across[0] = work[at_across].astype(BF16)
    across[1] = work[at_far].astype(BF16)


def entering_kernel(first, second, third, got, other, parts, upto, local, *out):
    first_core = place() % CORES == 0
    state = unpack(third[...].astype(F32))
    for below, (one, two) in ((second, (other, got)), (first, (got, other))):
        factor = jnp.where(first_core, one[...], two[...])
        high, low = two_parts(state)
        state = unpack(below[...].astype(F32)) + dot(factor, high) + dot(factor, low)
    sweep_plane(state, parts, upto, local, out)


def entering_from_kernel(base, parts, upto, local, *out):
    sweep_plane(unpack(base[...]), parts, upto, local, out)


def entering(body, args):
    half, columns = args[0].shape
    return call(
        body,
        "entering",
        [IN_VMEM] * len(args),
        [shape(half, columns), shape(half, columns), shape(CORES, half, columns)],
        [pltpu.VMEM((GROUP, half, columns), F32)],
        1.4,
    )(*args)


def waves_kernel(own, near, across, far, prop, image, out, arrived):
    for at, item in zip(partners(), (own[...], near[...], across[0], far[1])):
        arrived[at] = item
    split = GROUP // prop.shape[0]
    for e in range(prop.shape[0]):
        near, far = arrived[e * split].astype(F32), arrived[e * split + 1].astype(F32)
        left = left_lanes(near)
        top = jnp.where(left, near, swap_lanes(far))
        low = jnp.where(left, swap_lanes(near), far)
        incoming = jnp.concatenate([top, low], axis=0).astype(BF16)
        out[e] = (dot(prop[e], incoming) + image[e]).astype(BF16)


def final_waves(arrived, prop, image):
    half, columns = arrived[0].shape
    return call(
        waves_kernel,
        "waves",
        [IN_VMEM] * (GROUP + 2),
        shape(*image.shape),
        [pltpu.VMEM((GROUP, half, columns), BF16)],
        1.3,
    )(*arrived, prop, image)


def to_near(item, sections):
    return lax.ppermute(item, "sec", [(s, s ^ 1) for s in range(sections)])


def to_across(item, sections):
    return lax.ppermute(item, "sec", [(s, s // GROUP * GROUP + (s % GROUP + CORES) % GROUP) for s in range(sections)])


def to_far(item, sections):
    return lax.ppermute(item, "sec", [(s, s // GROUP * GROUP + (s % GROUP + CORES) % GROUP ^ 1) for s in range(sections)])


def exchange(own, near, across, far, sections):
    across, far = to_across(across, sections), to_far(far, sections)
    return [own, to_near(near, sections), across, far]


def exchange_by_chip(own, near, across, sections):
    across = to_across(across, sections)
    return [own, to_near(near, sections), across, to_near(across, sections)]


def up_shift(sections, k):
    return [(s, s + GROUP * k) for s in range(sections - GROUP * k)]


def spread(packed):
    half = packed.shape[1] // 2
    return jnp.concatenate([packed[:, :half], packed[:, half:]], axis=0)


def maps_up(total_map, sections):
    pairs = []
    for i in range(GROUP):
        if i % CORES == 0:
            pairs += [(GROUP + i, 2 * GROUP + i), (2 * GROUP + i, 3 * GROUP + i)]
        else:
            pairs += [(GROUP + i, 3 * GROUP + i)]
    got = lax.ppermute(total_map, "sec", pairs)
    return got, to_near(got, sections)


def upward(item, k, sections):
    return lax.ppermute(item, "sec", up_shift(sections, k))


def scan_below(total_map, total, sections):
    shift = lax.ppermute(spread(total).astype(F32), "sec", up_shift(sections, 1))
    joined = lax.ppermute(total_map, "sec", up_shift(sections, 1))
    stride = 1
    while stride < sections // GROUP:
        other = lax.ppermute(shift, "sec", up_shift(sections, stride))
        other_map = lax.ppermute(joined, "sec", up_shift(sections, stride))
        shift = shift + dot_wide(joined, other)
        joined = dot_wide(joined, other_map)
        stride *= 2
    half = shift.shape[0] // 2
    return jnp.concatenate([shift[:half], shift[half:]], axis=1)


def per_device(green, injected, coupling, pattern, owner, pair_blocks):
    sections = lax.axis_size("sec")
    green, inject = green[0], injected[0]

    coupling, tiles = coupling[0], pattern[0].T
    outgoing = outgoing_pairs(owner[:, 0], pair_blocks.T, green, inject, sections)
    received = lax.all_to_all(outgoing, "sec", split_axis=0, concat_axis=0, tiled=True)

    prop, token = propagator(tiles, green, coupling)
    own_map, other_map, face_rows = face_maps(tiles, green, coupling, token)
    across = to_across(other_map, sections)
    near = to_near(own_map, sections)

    source, *quarters, across = placed_source(received, inject, face_rows, across)
    shifts = exchange(*quarters, sections)
    far = to_near(across, sections)
    image = images(green, source)
    four = sections // GROUP == 4
    total_map, parts = chain([own_map, near, across, far], BF16 if four else F32, image)
    maps = maps_up(total_map, sections) if four else []
    total, local = plane_total(shifts, parts)
    upto = maps_upto(parts, total)
    if four:
        below = [upward(total, k, sections) for k in range(1, 4)]
        entered = entering(entering_kernel, (*below, *maps, parts, upto, local))
    else:
        base = scan_below(total_map, total, sections)
        entered = entering(entering_from_kernel, (base, parts, upto, local))
    arrived = exchange_by_chip(*entered, sections)
    return final_waves(arrived, prop, image)[None]


def solution(mesh):
    in_specs = (
        P("sec", "grp", None, None),
        P("sec", "grp", None, None),
        P("sec", None, None),
        P("sec", None, None),
        P("sec", None),
        P("sec", None),
    )
    out_specs = P("sec", "grp", None, None)
    return jax.shard_map(
        per_device, mesh=mesh, in_specs=in_specs, out_specs=out_specs, check_vma=False
    )
```

```python
import functools

import jax
import jax.numpy as jnp
from jax import lax
from jax.experimental import pallas as pl
from jax.experimental.pallas import tpu as pltpu
from jax.sharding import PartitionSpec as P

BLK = 32
CAP = 2
GROUP = 4
HEAD = 16
CORES = 2

HIGH = lax.Precision.HIGHEST
F32 = jnp.float32
BF16 = jnp.bfloat16
VMEM_SMALL = 16 * 1024 * 1024
VMEM_MOST = 61900000
VMEM_WHOLE = 63400000
PEAK = 1.15e9

IN_VMEM = pl.BlockSpec(memory_space=pltpu.VMEM)
IN_SMEM = pl.BlockSpec(memory_space=pltpu.SMEM)
IN_HBM = pl.BlockSpec(memory_space=pltpu.HBM)
IN_PLACE = pl.BlockSpec(memory_space=pl.ANY)


def shape(*dims, dtype=BF16):
    return jax.ShapeDtypeStruct(dims, dtype)


def call(body, name, ins, outs, scratch, micros, vmem=VMEM_SMALL, aliases=None):
    places = list(range(len(outs))) if isinstance(outs, list) else 0
    return pl.pallas_call(
        body,
        name=name,
        in_specs=ins,
        out_shape=outs,
        out_specs=jax.tree.map(lambda k: IN_PLACE if k in (aliases or {}).values() else IN_VMEM, places),
        input_output_aliases=aliases or {},
        scratch_shapes=scratch,
        compiler_params=pltpu.CompilerParams(vmem_limit_bytes=vmem),
        cost_estimate=pl.CostEstimate(flops=int(micros * PEAK), bytes_accessed=0, transcendentals=0),
    )


def place():
    return lax.axis_index("sec") % GROUP


def partners():
    here = place()
    across = (here + CORES) % GROUP
    return here, here ^ 1, across, across ^ 1


def dot(a, b):
    return jnp.dot(a, b, preferred_element_type=F32)


def dot_wide(a, b):
    return jnp.dot(a, b, precision=HIGH, preferred_element_type=F32)


def two_parts(x):
    high = x.astype(BF16)
    return high, (x - high.astype(F32)).astype(BF16)


def left_lanes(x):
    return lax.broadcasted_iota(jnp.int32, x.shape, 1) < x.shape[1] // 2


def swap_lanes(x):
    return pltpu.roll(x, x.shape[1] // 2, 1)


def pack(tall):
    half = tall.shape[0] // 2
    top, low = tall[:half], tall[half:]
    return jnp.where(left_lanes(top), top, swap_lanes(low))


def unpack(packed):
    return jnp.concatenate([packed, swap_lanes(packed)], axis=0)


def mask_tiles(pattern, coupling):
    high, wide = coupling.shape[0] // pattern.shape[1], coupling.shape[1] // pattern.shape[0]
    for i in range(pattern.shape[1]):
        for j in range(pattern.shape[0]):
            at = (slice(i * high, (i + 1) * high), slice(j * wide, (j + 1) * wide))
            tile = coupling[at]
            coupling[at] = jnp.where(pattern[j, i] == 1, tile, jnp.zeros_like(tile))


def pairs_kernel(owner_in, blocks_in, green, inject_in, out, owner, blocks, inject, held, product, slot_of, counts, sem, side):
    energies, orbitals, _ = green.shape
    sections = out.shape[0]
    count = owner.shape[0]
    named = held.shape[1] < orbitals
    small = [
        pltpu.make_async_copy(src, dst, side.at[k])
        for k, (src, dst) in enumerate(((owner_in, owner), (blocks_in, blocks), (inject_in, inject)))
    ]
    for move in small:
        move.start()

    def copy_of(e, q):
        first = pl.multiple_of(blocks[0, q] * BLK, BLK)
        to = pl.multiple_of(q * BLK, BLK)
        return pltpu.make_async_copy(green.at[e, pl.ds(first, BLK)], held.at[e, pl.ds(to, BLK)], sem.at[e])

    def whole(e):
        return pltpu.make_async_copy(green.at[e], held.at[e], sem.at[e])

    if not named:
        for e in range(energies):
            whole(e).start()
    for move in small[:2]:
        move.wait()
    if named:
        for e in range(energies):
            lax.fori_loop(0, count, lambda q, _, e=e: copy_of(e, q).start(), None, unroll=4)
    rows = CAP * energies * BLK
    lane = lax.broadcasted_iota(jnp.int32, (HEAD, out.shape[2]), 1)
    none = jnp.where(lane < CAP, -1.0, 0.0).astype(BF16)

    def blank(d, _):
        counts[d] = 0
        out[d, :rows, :] = jnp.zeros((rows, out.shape[2]), BF16)
        out[d, rows : rows + HEAD, :] = none
        return 0

    lax.fori_loop(0, sections, blank, 0)

    def rank(q, _):
        d = owner[q]
        r = counts[d]
        counts[d] = r + 1
        slot_of[q] = r
        head = out[d, rows : rows + HEAD, :].astype(F32)
        head = jnp.where(lane == r, blocks[1, q].astype(F32), head)
        out[d, rows : rows + HEAD, :] = head.astype(BF16)
        return 0

    lax.fori_loop(0, count, rank, 0)
    small[2].wait()
    for e in range(energies):
        whole_held = pltpu.make_async_copy(green.at[e, pl.ds(0, held.shape[1])], held.at[e], sem.at[e])
        whole_held.wait()
        product[...] = dot(held[e], inject[e]).astype(BF16)

        def fill(q, _):
            first = pl.multiple_of((q if named else blocks[0, q]) * BLK, BLK)
            to = pl.multiple_of((slot_of[q] * energies + e) * BLK, BLK)
            out[owner[q], pl.ds(to, BLK), :] = product[pl.ds(first, BLK), :]
            return 0

        lax.fori_loop(0, count, fill, 0, unroll=4)


def outgoing_pairs(owner, blocks, green, inject, sections):
    energies, orbitals, _ = green.shape
    columns = inject.shape[2]
    rows = min(orbitals, owner.shape[0] * BLK)
    return call(
        pairs_kernel,
        "pairs",
        [IN_HBM] * 4,
        shape(sections, CAP * energies * BLK + HEAD, columns),
        [
            pltpu.SMEM(owner.shape, jnp.int32),
            pltpu.SMEM(blocks.shape, jnp.int32),
            pltpu.VMEM(inject.shape, BF16),
            pltpu.VMEM((energies, rows, orbitals), BF16),
            pltpu.VMEM((rows, columns), BF16),
            pltpu.SMEM(owner.shape, jnp.int32),
            pltpu.SMEM((sections,), jnp.int32),
            pltpu.SemaphoreType.DMA((energies,)),
            pltpu.SemaphoreType.DMA((3,)),
        ],
        4.0,
        VMEM_WHOLE,
    )(owner, blocks, green, inject)


def maps_kernel(pattern, green, coupling, own, other, face_rows, couple, maps):
    energies, orbitals, _ = green.shape
    face = coupling.shape[1]
    couple[...] = coupling[...]
    mask_tiles(pattern, couple)
    for e in range(energies):
        rows = green[e, orbitals - face :, :]
        face_rows[e] = rows
        maps[e] = dot(rows, couple[...])
    mine = place() // CORES
    own[...] = maps[mine]
    other[...] = maps[1 - mine]


def face_maps(pattern, green, coupling):
    orbitals, face = coupling.shape
    square = shape(face, face, dtype=F32)
    return call(
        maps_kernel,
        "face_maps",
        [IN_SMEM, IN_VMEM, IN_VMEM],
        [square, square, shape(green.shape[0], face, orbitals)],
        [pltpu.VMEM(coupling.shape, BF16), pltpu.VMEM((green.shape[0], face, face), F32)],
        1.2,
    )(pattern, green, coupling)


def fetch(green, held, sem):
    moves = [pltpu.make_async_copy(green.at[e], held.at[e], sem.at[e]) for e in range(green.shape[0])]
    for move in moves:
        move.start()
    return moves


def prop_kernel(pattern_in, green, coupling_in, _rows, out, _same_rows, pattern, coupling, held, sem, side):
    tiles = pltpu.make_async_copy(pattern_in, pattern, side.at[0])
    whole = pltpu.make_async_copy(coupling_in, coupling, side.at[1])
    tiles.start()
    whole.start()
    moves = fetch(green, held, sem)
    tiles.wait()
    whole.wait()
    mask_tiles(pattern, coupling)
    for e, move in enumerate(moves):
        move.wait()
        out[e] = dot(held[e], coupling[...]).astype(BF16)


def propagator(pattern, green, coupling, passed):
    energies, orbitals, _ = green.shape
    return call(
        prop_kernel,
        "prop",
        [IN_HBM] * 3 + [IN_PLACE],
        [shape(energies, orbitals, coupling.shape[1]), shape(*passed.shape)],
        [
            pltpu.SMEM(pattern.shape, jnp.int32),
            pltpu.VMEM(coupling.shape, BF16),
            pltpu.VMEM(green.shape, BF16),
            pltpu.SemaphoreType.DMA((energies,)),
            pltpu.SemaphoreType.DMA((2,)),
        ],
        5.0,
        VMEM_MOST,
        aliases={3: 1},
    )(pattern, green, coupling, passed)


def image_kernel(green, source, out):
    for e in range(green.shape[0]):
        out[e] = dot(green[e], source[e])


def images(green, source):
    return call(image_kernel, "image", [IN_VMEM] * 2, shape(*source.shape, dtype=F32), [], 1.2)(green, source)


def times(a, b):
    return dot(a[0], b[0]) + (dot(a[0], b[1]) + dot(a[1], b[0]))


def chain_kernel(own, near, across, far, _image, total_out, parts, maps):
    collect((own, near, across, far), maps)
    split = [two_parts(maps[j]) for j in range(GROUP)]
    lower, upper = two_parts(times(split[1], split[0])), two_parts(times(split[3], split[2]))
    total_out[...] = times(upper, lower).astype(total_out.dtype)
    for j, (high, low) in enumerate(split):
        parts[0, j] = high
        parts[1, j] = low


def chain(maps, dtype, tie):
    face = maps[0].shape[0]
    return call(
        chain_kernel,
        "chain_maps",
        [IN_VMEM] * GROUP + [IN_PLACE],
        [shape(face, face, dtype=dtype), shape(2, GROUP, face, face)],
        [pltpu.VMEM((GROUP, face, face), F32)],
        0.9,
    )(*maps, tie)


def source_kernel(received, inject, face_rows, _map, source, own, near, across, far, _same_map, quarters, total, heads, targets, sem):
    energies, orbitals, columns = inject.shape
    sections = received.shape[0]
    half = quarters.shape[1]
    rows = CAP * energies * BLK

    def read(s, _):
        block = received[s, rows : rows + HEAD, :].astype(F32)
        heads[pl.ds(s, 1), :] = block[:1].astype(jnp.int32)
        return 0

    lax.fori_loop(0, sections, read, 0, unroll=min(sections, 8))
    fetch = pltpu.make_async_copy(heads, targets, sem)
    fetch.start()
    total[...] = inject[...].astype(F32)
    fetch.wait()

    def add(s, _):
        for r in range(CAP):
            first = pl.multiple_of(jnp.maximum(targets[s, r], 0) * BLK, BLK)
            for e in range(energies):
                item = received[s, (r * energies + e) * BLK : (r * energies + e + 1) * BLK, :]
                total[e, pl.ds(first, BLK), :] += item.astype(F32)
        return 0

    lax.fori_loop(0, sections, add, 0, unroll=2)
    split = GROUP // energies
    for e in range(energies):
        source[e] = total[e].astype(BF16)
        tall = dot(face_rows[e], source[e])
        quarters[e * split] = pack(tall)
        second = jnp.where(left_lanes(tall[:half]), swap_lanes(tall[:half]), tall[half:])
        quarters[e * split + 1] = second
    for out, at in zip((own, near, across, far), partners()):
        out[...] = quarters[at].astype(BF16)


def placed_source(received, inject, face_rows, passed):
    face = face_rows.shape[1]
    energies, orbitals, columns = inject.shape
    sections = received.shape[0]
    return call(
        source_kernel,
        "source_and_face",
        [IN_VMEM, IN_VMEM, IN_VMEM, IN_PLACE],
        [shape(*inject.shape)] + [shape(face // 2, columns)] * GROUP + [shape(*passed.shape, dtype=passed.dtype)],
        [
            pltpu.VMEM((GROUP, face // 2, columns), F32),
            pltpu.VMEM(inject.shape, F32),
            pltpu.VMEM((sections, columns), jnp.int32),
            pltpu.SMEM((sections, columns), jnp.int32),
            pltpu.SemaphoreType.DMA,
        ],
        1.4,
        aliases={3: 1 + GROUP},
    )(received, inject, face_rows, passed)


def collect(refs, held):
    for ref, at in zip(refs, partners()):
        held[at] = ref[...]


def step(parts, j, shift, state):
    return unpack(shift.astype(F32)) + times((parts[0, j], parts[1, j]), two_parts(state))


def total_kernel(own, near, across, far, parts, out, local, shifts):
    collect((own, near, across, far), shifts)
    state = unpack(shifts[0].astype(F32))
    for j in range(1, GROUP):
        local[j - 1] = state
        state = step(parts, j, shifts[j], state)
    out[...] = pack(state).astype(BF16)


def plane_total(shifts, parts):
    half, columns = shifts[0].shape
    return call(
        total_kernel,
        "plane_total",
        [IN_VMEM] * (GROUP + 1),
        [shape(half, columns), shape(GROUP - 1, 2 * half, columns, dtype=F32)],
        [pltpu.VMEM((GROUP, half, columns), BF16)],
        3.0,
    )(*shifts, parts)


def upto_kernel(parts, _total, out):
    maps = (parts[0, 0], parts[1, 0])
    for j in range(1, GROUP - 1):
        maps = two_parts(times((parts[0, j], parts[1, j]), maps))
        out[0, j - 1], out[1, j - 1] = maps


def maps_upto(parts, tie):
    _, _, face, _ = parts.shape
    return call(
        upto_kernel, "maps_upto", [IN_VMEM, IN_PLACE], shape(2, GROUP - 2, face, face), [], 3.0
    )(parts, tie)


def sweep_plane(state, parts, upto, local, out):
    two = two_parts(state)
    held = [pack(state)]
    for j in range(1, GROUP):
        maps = (parts[0, 0], parts[1, 0]) if j == 1 else (upto[0, j - 2], upto[1, j - 2])
        held.append(pack(local[j - 1] + times(maps, two)))
    work = out[GROUP]
    for j, item in enumerate(held):
        work[j] = item
    for ref, at in zip(out, partners()):
        ref[...] = work[at].astype(BF16)


def entering_kernel(first, second, third, got, other, parts, upto, local, *out):
    first_core = place() % CORES == 0
    state = unpack(third[...].astype(F32))
    for below, (one, two) in ((second, (other, got)), (first, (got, other))):
        factor = jnp.where(first_core, one[...], two[...])
        high, low = two_parts(state)
        state = unpack(below[...].astype(F32)) + dot(factor, high) + dot(factor, low)
    sweep_plane(state, parts, upto, local, out)


def entering_from_kernel(base, parts, upto, local, *out):
    sweep_plane(unpack(base[...]), parts, upto, local, out)


def entering(body, args):
    half, columns = args[0].shape
    return call(
        body,
        "entering",
        [IN_VMEM] * len(args),
        [shape(half, columns)] * GROUP,
        [pltpu.VMEM((GROUP, half, columns), F32)],
        1.4,
    )(*args)


def waves_kernel(own, near, across, far, prop, image, out, arrived):
    collect((own, near, across, far), arrived)
    split = GROUP // prop.shape[0]
    for e in range(prop.shape[0]):
        near, far = arrived[e * split].astype(F32), arrived[e * split + 1].astype(F32)
        left = left_lanes(near)
        top = jnp.where(left, near, swap_lanes(far))
        low = jnp.where(left, swap_lanes(near), far)
        incoming = jnp.concatenate([top, low], axis=0).astype(BF16)
        out[e] = (dot(prop[e], incoming) + image[e]).astype(BF16)


def final_waves(arrived, prop, image):
    half, columns = arrived[0].shape
    return call(
        waves_kernel,
        "waves",
        [IN_VMEM] * (GROUP + 2),
        shape(*image.shape),
        [pltpu.VMEM((GROUP, half, columns), BF16)],
        1.3,
    )(*arrived, prop, image)


def to_near(item, sections):
    return lax.ppermute(item, "sec", [(s, s ^ 1) for s in range(sections)])


def to_across(item, sections):
    return lax.ppermute(item, "sec", [(s, s // GROUP * GROUP + (s % GROUP + CORES) % GROUP) for s in range(sections)])


def to_far(item, sections):
    return lax.ppermute(item, "sec", [(s, s // GROUP * GROUP + (s % GROUP + CORES) % GROUP ^ 1) for s in range(sections)])


def exchange(own, near, across, far, sections):
    across, far = to_across(across, sections), to_far(far, sections)
    return [own, to_near(near, sections), across, far]


def up_shift(sections, k):
    return [(s, s + GROUP * k) for s in range(sections - GROUP * k)]


def spread(packed):
    half = packed.shape[1] // 2
    return jnp.concatenate([packed[:, :half], packed[:, half:]], axis=0)


def maps_up(total_map, sections):
    pairs = []
    for i in range(GROUP):
        if i % CORES == 0:
            pairs += [(GROUP + i, 2 * GROUP + i), (2 * GROUP + i, 3 * GROUP + i)]
        else:
            pairs += [(GROUP + i, 3 * GROUP + i)]
    got = lax.ppermute(total_map, "sec", pairs)
    return got, to_near(got, sections)


def upward(item, k, sections):
    return lax.ppermute(item, "sec", up_shift(sections, k))


def scan_below(total_map, total, sections):
    shift = lax.ppermute(spread(total).astype(F32), "sec", up_shift(sections, 1))
    joined = lax.ppermute(total_map, "sec", up_shift(sections, 1))
    stride = 1
    while stride < sections // GROUP:
        other = lax.ppermute(shift, "sec", up_shift(sections, stride))
        other_map = lax.ppermute(joined, "sec", up_shift(sections, stride))
        shift = shift + dot_wide(joined, other)
        joined = dot_wide(joined, other_map)
        stride *= 2
    half = shift.shape[0] // 2
    return jnp.concatenate([shift[:half], shift[half:]], axis=1)


def per_device(green, injected, coupling, pattern, owner, pair_blocks):
    sections = lax.axis_size("sec")
    green, inject = green[0], injected[0]

    coupling, tiles = coupling[0], pattern[0].T
    outgoing = outgoing_pairs(owner[:, 0], pair_blocks.T, green, inject, sections)
    received = lax.all_to_all(outgoing, "sec", split_axis=0, concat_axis=0, tiled=True)

    own_map, other_map, face_rows = face_maps(tiles, green, coupling)
    across = to_across(other_map, sections)
    near = to_near(own_map, sections)
    prop, face_rows = propagator(tiles, green, coupling, face_rows)

    source, *quarters, across = placed_source(received, inject, face_rows, across)
    shifts = exchange(*quarters, sections)
    far = to_near(across, sections)
    image = images(green, source)
    four = sections // GROUP == 4
    total_map, parts = chain([own_map, near, across, far], BF16 if four else F32, image)
    maps = maps_up(total_map, sections) if four else []
    total, local = plane_total(shifts, parts)
    upto = maps_upto(parts, total)
    if four:
        below = [upward(total, k, sections) for k in range(1, 4)]
        entered = entering(entering_kernel, (*below, *maps, parts, upto, local))
    else:
        base = scan_below(total_map, total, sections)
        entered = entering(entering_from_kernel, (base, parts, upto, local))
    arrived = exchange(*entered, sections)
    return final_waves(arrived, prop, image)[None]


def solution(mesh):
    in_specs = (
        P("sec", "grp", None, None),
        P("sec", "grp", None, None),
        P("sec", None, None),
        P("sec", None, None),
        P("sec", None),
        P("sec", None),
    )
    out_specs = P("sec", "grp", None, None)
    return jax.shard_map(
        per_device, mesh=mesh, in_specs=in_specs, out_specs=out_specs, check_vma=False
    )
```

```python
import functools

import jax
import jax.numpy as jnp
from jax import lax
from jax.experimental import pallas as pl
from jax.experimental.pallas import tpu as pltpu
from jax.sharding import PartitionSpec as P

BLK = 32
CAP = 2
GROUP = 4
HEAD = 16
CORES = 2

HIGH = lax.Precision.HIGHEST
F32 = jnp.float32
BF16 = jnp.bfloat16
VMEM_SMALL = 16 * 1024 * 1024
VMEM_WHOLE = 63400000
PEAK = 1.15e9

IN_VMEM = pl.BlockSpec(memory_space=pltpu.VMEM)
IN_SMEM = pl.BlockSpec(memory_space=pltpu.SMEM)
IN_HBM = pl.BlockSpec(memory_space=pltpu.HBM)
IN_PLACE = pl.BlockSpec(memory_space=pl.ANY)


def shape(*dims, dtype=BF16):
    return jax.ShapeDtypeStruct(dims, dtype)


def call(body, name, ins, outs, scratch, micros, vmem=VMEM_SMALL, aliases=None):
    places = list(range(len(outs))) if isinstance(outs, list) else 0
    return pl.pallas_call(
        body,
        name=name,
        in_specs=ins,
        out_shape=outs,
        out_specs=jax.tree.map(lambda k: IN_PLACE if k in (aliases or {}).values() else IN_VMEM, places),
        input_output_aliases=aliases or {},
        scratch_shapes=scratch,
        compiler_params=pltpu.CompilerParams(vmem_limit_bytes=vmem),
        cost_estimate=pl.CostEstimate(flops=int(micros * PEAK), bytes_accessed=0, transcendentals=0),
    )


def place():
    return lax.axis_index("sec") % GROUP


def partners():
    here = place()
    across = (here + CORES) % GROUP
    return here, here ^ 1, across, across ^ 1


def dot(a, b):
    return jnp.dot(a, b, preferred_element_type=F32)


def dot_wide(a, b):
    return jnp.dot(a, b, precision=HIGH, preferred_element_type=F32)


def two_parts(x):
    high = x.astype(BF16)
    return high, (x - high.astype(F32)).astype(BF16)


def left_lanes(x):
    return lax.broadcasted_iota(jnp.int32, x.shape, 1) < x.shape[1] // 2


def swap_lanes(x):
    return pltpu.roll(x, x.shape[1] // 2, 1)


def pack(tall):
    half = tall.shape[0] // 2
    top, low = tall[:half], tall[half:]
    return jnp.where(left_lanes(top), top, swap_lanes(low))


def unpack(packed):
    return jnp.concatenate([packed, swap_lanes(packed)], axis=0)


def mask_tiles(pattern, coupling):
    high, wide = coupling.shape[0] // pattern.shape[1], coupling.shape[1] // pattern.shape[0]
    for i in range(pattern.shape[1]):
        for j in range(pattern.shape[0]):
            at = (slice(i * high, (i + 1) * high), slice(j * wide, (j + 1) * wide))
            tile = coupling[at]
            coupling[at] = jnp.where(pattern[j, i] == 1, tile, jnp.zeros_like(tile))


def pairs_kernel(owner_in, blocks_in, green, inject_in, out, owner, blocks, inject, held, product, slot_of, counts, sem, side):
    energies, orbitals, _ = green.shape
    sections = out.shape[0]
    count = owner.shape[0]
    named = held.shape[1] < orbitals
    small = [
        pltpu.make_async_copy(src, dst, side.at[k])
        for k, (src, dst) in enumerate(((owner_in, owner), (blocks_in, blocks), (inject_in, inject)))
    ]
    for move in small:
        move.start()

    def copy_of(e, q):
        first = pl.multiple_of(blocks[0, q] * BLK, BLK)
        to = pl.multiple_of(q * BLK, BLK)
        return pltpu.make_async_copy(green.at[e, pl.ds(first, BLK)], held.at[e, pl.ds(to, BLK)], sem.at[e])

    def whole(e):
        return pltpu.make_async_copy(green.at[e], held.at[e], sem.at[e])

    if not named:
        for e in range(energies):
            whole(e).start()
    for move in small[:2]:
        move.wait()
    if named:
        for e in range(energies):
            lax.fori_loop(0, count, lambda q, _, e=e: copy_of(e, q).start(), None, unroll=4)
    rows = CAP * energies * BLK
    lane = lax.broadcasted_iota(jnp.int32, (HEAD, out.shape[2]), 1)
    none = jnp.where(lane < CAP, -1.0, 0.0).astype(BF16)

    def blank(d, _):
        counts[d] = 0
        out[d, :rows, :] = jnp.zeros((rows, out.shape[2]), BF16)
        out[d, rows : rows + HEAD, :] = none
        return 0

    lax.fori_loop(0, sections, blank, 0)

    def rank(q, _):
        d = owner[q]
        r = counts[d]
        counts[d] = r + 1
        slot_of[q] = r
        head = out[d, rows : rows + HEAD, :].astype(F32)
        head = jnp.where(lane == r, blocks[1, q].astype(F32), head)
        out[d, rows : rows + HEAD, :] = head.astype(BF16)
        return 0

    lax.fori_loop(0, count, rank, 0)
    small[2].wait()
    for e in range(energies):
        whole_held = pltpu.make_async_copy(green.at[e, pl.ds(0, held.shape[1])], held.at[e], sem.at[e])
        whole_held.wait()
        product[...] = dot(held[e], inject[e]).astype(BF16)

        def fill(q, _):
            first = pl.multiple_of((q if named else blocks[0, q]) * BLK, BLK)
            to = pl.multiple_of((slot_of[q] * energies + e) * BLK, BLK)
            out[owner[q], pl.ds(to, BLK), :] = product[pl.ds(first, BLK), :]
            return 0

        lax.fori_loop(0, count, fill, 0, unroll=4)


def outgoing_pairs(owner, blocks, green, inject, sections):
    energies, orbitals, _ = green.shape
    columns = inject.shape[2]
    rows = min(orbitals, owner.shape[0] * BLK)
    return call(
        pairs_kernel,
        "pairs",
        [IN_HBM] * 4,
        shape(sections, CAP * energies * BLK + HEAD, columns),
        [
            pltpu.SMEM(owner.shape, jnp.int32),
            pltpu.SMEM(blocks.shape, jnp.int32),
            pltpu.VMEM(inject.shape, BF16),
            pltpu.VMEM((energies, rows, orbitals), BF16),
            pltpu.VMEM((rows, columns), BF16),
            pltpu.SMEM(owner.shape, jnp.int32),
            pltpu.SMEM((sections,), jnp.int32),
            pltpu.SemaphoreType.DMA((energies,)),
            pltpu.SemaphoreType.DMA((3,)),
        ],
        4.0,
        VMEM_WHOLE,
    )(owner, blocks, green, inject)


def maps_kernel(pattern, green, coupling, own, other, face_rows, couple, maps):
    energies, orbitals, _ = green.shape
    face = coupling.shape[1]
    couple[...] = coupling[...]
    mask_tiles(pattern, couple)
    for e in range(energies):
        rows = green[e, orbitals - face :, :]
        face_rows[e] = rows
        maps[e] = dot(rows, couple[...])
    mine = place() // CORES
    own[...] = maps[mine]
    other[...] = maps[1 - mine]


def face_maps(pattern, green, coupling):
    orbitals, face = coupling.shape
    square = shape(face, face, dtype=F32)
    return call(
        maps_kernel,
        "face_maps",
        [IN_SMEM, IN_VMEM, IN_VMEM],
        [square, square, shape(green.shape[0], face, orbitals)],
        [pltpu.VMEM(coupling.shape, BF16), pltpu.VMEM((green.shape[0], face, face), F32)],
        1.2,
    )(pattern, green, coupling)


def prop_kernel(pattern, green, coupling, _tie, out, couple):
    couple[...] = coupling[...]
    mask_tiles(pattern, couple)
    for e in range(green.shape[0]):
        out[e] = dot(green[e], couple[...]).astype(BF16)


def propagator(pattern, green, coupling, tie):
    energies, orbitals, _ = green.shape
    return call(
        prop_kernel,
        "prop",
        [IN_SMEM, IN_VMEM, IN_VMEM, IN_PLACE],
        shape(energies, orbitals, coupling.shape[1]),
        [pltpu.VMEM(coupling.shape, BF16)],
        1.5,
    )(pattern, green, coupling, tie)


def image_kernel(green, source, out):
    for e in range(green.shape[0]):
        out[e] = dot(green[e], source[e])


def images(green, source):
    return call(image_kernel, "image", [IN_VMEM] * 2, shape(*source.shape, dtype=F32), [], 1.2)(green, source)


def times(a, b):
    return dot(a[0], b[0]) + (dot(a[0], b[1]) + dot(a[1], b[0]))


def chain_kernel(own, near, across, far, _image, total_out, parts, maps):
    collect((own, near, across, far), maps)
    split = [two_parts(maps[j]) for j in range(GROUP)]
    lower, upper = two_parts(times(split[1], split[0])), two_parts(times(split[3], split[2]))
    total_out[...] = times(upper, lower).astype(total_out.dtype)
    for j, (high, low) in enumerate(split):
        parts[0, j] = high
        parts[1, j] = low


def chain(maps, dtype, tie):
    face = maps[0].shape[0]
    return call(
        chain_kernel,
        "chain_maps",
        [IN_VMEM] * GROUP + [IN_PLACE],
        [shape(face, face, dtype=dtype), shape(2, GROUP, face, face)],
        [pltpu.VMEM((GROUP, face, face), F32)],
        0.9,
    )(*maps, tie)


def source_kernel(received, inject, face_rows, _map, source, own, near, across, far, _same_map, quarters, total, heads, targets, sem):
    energies, orbitals, columns = inject.shape
    sections = received.shape[0]
    half = quarters.shape[1]
    rows = CAP * energies * BLK

    def read(s, _):
        block = received[s, rows : rows + HEAD, :].astype(F32)
        heads[pl.ds(s, 1), :] = block[:1].astype(jnp.int32)
        return 0

    lax.fori_loop(0, sections, read, 0, unroll=min(sections, 8))
    fetch = pltpu.make_async_copy(heads, targets, sem)
    fetch.start()
    total[...] = inject[...].astype(F32)
    fetch.wait()

    def add(s, _):
        for r in range(CAP):
            first = pl.multiple_of(jnp.maximum(targets[s, r], 0) * BLK, BLK)
            for e in range(energies):
                item = received[s, (r * energies + e) * BLK : (r * energies + e + 1) * BLK, :]
                total[e, pl.ds(first, BLK), :] += item.astype(F32)
        return 0

    lax.fori_loop(0, sections, add, 0, unroll=2)
    split = GROUP // energies
    for e in range(energies):
        source[e] = total[e].astype(BF16)
        tall = dot(face_rows[e], source[e])
        quarters[e * split] = pack(tall)
        second = jnp.where(left_lanes(tall[:half]), swap_lanes(tall[:half]), tall[half:])
        quarters[e * split + 1] = second
    for out, at in zip((own, near, across, far), partners()):
        out[...] = quarters[at].astype(BF16)


def placed_source(received, inject, face_rows, passed):
    face = face_rows.shape[1]
    energies, orbitals, columns = inject.shape
    sections = received.shape[0]
    return call(
        source_kernel,
        "source_and_face",
        [IN_VMEM, IN_VMEM, IN_VMEM, IN_PLACE],
        [shape(*inject.shape)] + [shape(face // 2, columns)] * GROUP + [shape(*passed.shape, dtype=passed.dtype)],
        [
            pltpu.VMEM((GROUP, face // 2, columns), F32),
            pltpu.VMEM(inject.shape, F32),
            pltpu.VMEM((sections, columns), jnp.int32),
            pltpu.SMEM((sections, columns), jnp.int32),
            pltpu.SemaphoreType.DMA,
        ],
        1.4,
        aliases={3: 1 + GROUP},
    )(received, inject, face_rows, passed)


def collect(refs, held):
    for ref, at in zip(refs, partners()):
        held[at] = ref[...]


def step(parts, j, shift, state):
    return unpack(shift.astype(F32)) + times((parts[0, j], parts[1, j]), two_parts(state))


def total_kernel(own, near, across, far, parts, out, local, shifts):
    collect((own, near, across, far), shifts)
    state = unpack(shifts[0].astype(F32))
    for j in range(1, GROUP):
        local[j - 1] = state
        state = step(parts, j, shifts[j], state)
    out[...] = pack(state).astype(BF16)


def plane_total(shifts, parts):
    half, columns = shifts[0].shape
    return call(
        total_kernel,
        "plane_total",
        [IN_VMEM] * (GROUP + 1),
        [shape(half, columns), shape(GROUP - 1, 2 * half, columns, dtype=F32)],
        [pltpu.VMEM((GROUP, half, columns), BF16)],
        3.0,
    )(*shifts, parts)


def upto_kernel(parts, _total, out):
    maps = (parts[0, 0], parts[1, 0])
    for j in range(1, GROUP - 1):
        maps = two_parts(times((parts[0, j], parts[1, j]), maps))
        out[0, j - 1], out[1, j - 1] = maps


def maps_upto(parts, tie):
    _, _, face, _ = parts.shape
    return call(
        upto_kernel, "maps_upto", [IN_VMEM, IN_PLACE], shape(2, GROUP - 2, face, face), [], 3.0
    )(parts, tie)


def sweep_plane(state, parts, upto, local, out):
    two = two_parts(state)
    held = [pack(state)]
    for j in range(1, GROUP):
        maps = (parts[0, 0], parts[1, 0]) if j == 1 else (upto[0, j - 2], upto[1, j - 2])
        held.append(pack(local[j - 1] + times(maps, two)))
    work = out[GROUP]
    for j, item in enumerate(held):
        work[j] = item
    for ref, at in zip(out, partners()):
        ref[...] = work[at].astype(BF16)


def entering_kernel(first, second, third, got, other, parts, upto, local, *out):
    first_core = place() % CORES == 0
    state = unpack(third[...].astype(F32))
    for below, (one, two) in ((second, (other, got)), (first, (got, other))):
        factor = jnp.where(first_core, one[...], two[...])
        high, low = two_parts(state)
        state = unpack(below[...].astype(F32)) + dot(factor, high) + dot(factor, low)
    sweep_plane(state, parts, upto, local, out)


def entering_from_kernel(base, parts, upto, local, *out):
    sweep_plane(unpack(base[...]), parts, upto, local, out)


def entering(body, args):
    half, columns = args[0].shape
    return call(
        body,
        "entering",
        [IN_VMEM] * len(args),
        [shape(half, columns)] * GROUP,
        [pltpu.VMEM((GROUP, half, columns), F32)],
        1.4,
    )(*args)


def waves_kernel(own, near, across, far, prop, image, out, arrived):
    collect((own, near, across, far), arrived)
    split = GROUP // prop.shape[0]
    for e in range(prop.shape[0]):
        near, far = arrived[e * split].astype(F32), arrived[e * split + 1].astype(F32)
        left = left_lanes(near)
        top = jnp.where(left, near, swap_lanes(far))
        low = jnp.where(left, swap_lanes(near), far)
        incoming = jnp.concatenate([top, low], axis=0).astype(BF16)
        out[e] = (dot(prop[e], incoming) + image[e]).astype(BF16)


def final_waves(arrived, prop, image):
    half, columns = arrived[0].shape
    return call(
        waves_kernel,
        "waves",
        [IN_VMEM] * (GROUP + 2),
        shape(*image.shape),
        [pltpu.VMEM((GROUP, half, columns), BF16)],
        1.3,
    )(*arrived, prop, image)


def to_near(item, sections):
    return lax.ppermute(item, "sec", [(s, s ^ 1) for s in range(sections)])


def to_across(item, sections):
    return lax.ppermute(item, "sec", [(s, s // GROUP * GROUP + (s % GROUP + CORES) % GROUP) for s in range(sections)])


def to_far(item, sections):
    return lax.ppermute(item, "sec", [(s, s // GROUP * GROUP + (s % GROUP + CORES) % GROUP ^ 1) for s in range(sections)])


def exchange(own, near, across, far, sections):
    across, far = to_across(across, sections), to_far(far, sections)
    return [own, to_near(near, sections), across, far]


def up_shift(sections, k):
    return [(s, s + GROUP * k) for s in range(sections - GROUP * k)]


def spread(packed):
    half = packed.shape[1] // 2
    return jnp.concatenate([packed[:, :half], packed[:, half:]], axis=0)


def maps_up(total_map, sections):
    pairs = []
    for i in range(GROUP):
        if i % CORES == 0:
            pairs += [(GROUP + i, 2 * GROUP + i), (2 * GROUP + i, 3 * GROUP + i)]
        else:
            pairs += [(GROUP + i, 3 * GROUP + i)]
    got = lax.ppermute(total_map, "sec", pairs)
    return got, to_near(got, sections)


def upward(item, k, sections):
    return lax.ppermute(item, "sec", up_shift(sections, k))


def scan_below(total_map, total, sections):
    shift = lax.ppermute(spread(total).astype(F32), "sec", up_shift(sections, 1))
    joined = lax.ppermute(total_map, "sec", up_shift(sections, 1))
    stride = 1
    while stride < sections // GROUP:
        other = lax.ppermute(shift, "sec", up_shift(sections, stride))
        other_map = lax.ppermute(joined, "sec", up_shift(sections, stride))
        shift = shift + dot_wide(joined, other)
        joined = dot_wide(joined, other_map)
        stride *= 2
    half = shift.shape[0] // 2
    return jnp.concatenate([shift[:half], shift[half:]], axis=1)


def per_device(green, injected, coupling, pattern, owner, pair_blocks):
    sections = lax.axis_size("sec")
    green, inject = green[0], injected[0]

    coupling, tiles = coupling[0], pattern[0].T
    outgoing = outgoing_pairs(owner[:, 0], pair_blocks.T, green, inject, sections)
    received = lax.all_to_all(outgoing, "sec", split_axis=0, concat_axis=0, tiled=True)

    own_map, other_map, face_rows = face_maps(tiles, green, coupling)
    across = to_across(other_map, sections)
    near = to_near(own_map, sections)

    source, *quarters, across = placed_source(received, inject, face_rows, across)
    shifts = exchange(*quarters, sections)
    far = to_near(across, sections)
    image = images(green, source)
    four = sections // GROUP == 4
    total_map, parts = chain([own_map, near, across, far], BF16 if four else F32, image)
    maps = maps_up(total_map, sections) if four else []
    total, local = plane_total(shifts, parts)
    upto = maps_upto(parts, total)
    if four:
        below = [upward(total, k, sections) for k in range(1, 4)]
        entered = entering(entering_kernel, (*below, *maps, parts, upto, local))
    else:
        base = scan_below(total_map, total, sections)
        entered = entering(entering_from_kernel, (base, parts, upto, local))
    arrived = exchange(*entered, sections)
    prop = propagator(tiles, green, coupling, entered[0])
    return final_waves(arrived, prop, image)[None]


def solution(mesh):
    in_specs = (
        P("sec", "grp", None, None),
        P("sec", "grp", None, None),
        P("sec", None, None),
        P("sec", None, None),
        P("sec", None),
        P("sec", None),
    )
    out_specs = P("sec", "grp", None, None)
    return jax.shard_map(
        per_device, mesh=mesh, in_specs=in_specs, out_specs=out_specs, check_vma=False
    )
```

```python
import functools

import jax
import jax.numpy as jnp
from jax import lax
from jax.experimental import pallas as pl
from jax.experimental.pallas import tpu as pltpu
from jax.sharding import PartitionSpec as P

BLK = 32
CAP = 2
GROUP = 4
HEAD = 8
CORES = 2

HIGH = lax.Precision.HIGHEST
F32 = jnp.float32
BF16 = jnp.bfloat16
VMEM_SMALL = 16 * 1024 * 1024
VMEM_WHOLE = 63400000
PEAK = 1.15e9

IN_VMEM = pl.BlockSpec(memory_space=pltpu.VMEM)
IN_SMEM = pl.BlockSpec(memory_space=pltpu.SMEM)
IN_HBM = pl.BlockSpec(memory_space=pltpu.HBM)
IN_PLACE = pl.BlockSpec(memory_space=pl.ANY)


def shape(*dims, dtype=BF16):
    return jax.ShapeDtypeStruct(dims, dtype)


def call(body, name, ins, outs, scratch, micros, vmem=VMEM_SMALL, aliases=None):
    places = list(range(len(outs))) if isinstance(outs, list) else 0
    return pl.pallas_call(
        body,
        name=name,
        in_specs=ins,
        out_shape=outs,
        out_specs=jax.tree.map(lambda k: IN_PLACE if k in (aliases or {}).values() else IN_VMEM, places),
        input_output_aliases=aliases or {},
        scratch_shapes=scratch,
        compiler_params=pltpu.CompilerParams(vmem_limit_bytes=vmem),
        cost_estimate=pl.CostEstimate(flops=int(micros * PEAK), bytes_accessed=0, transcendentals=0),
    )


def place():
    return lax.axis_index("sec") % GROUP


def partners():
    here = place()
    across = (here + CORES) % GROUP
    return here, here ^ 1, across, across ^ 1


def dot(a, b):
    return jnp.dot(a, b, preferred_element_type=F32)


def dot_wide(a, b):
    return jnp.dot(a, b, precision=HIGH, preferred_element_type=F32)


def two_parts(x):
    high = x.astype(BF16)
    return high, (x - high.astype(F32)).astype(BF16)


def left_lanes(x):
    return lax.broadcasted_iota(jnp.int32, x.shape, 1) < x.shape[1] // 2


def swap_lanes(x):
    return pltpu.roll(x, x.shape[1] // 2, 1)


def pack(tall):
    half = tall.shape[0] // 2
    top, low = tall[:half], tall[half:]
    return jnp.where(left_lanes(top), top, swap_lanes(low))


def unpack(packed):
    return jnp.concatenate([packed, swap_lanes(packed)], axis=0)


def mask_tiles(pattern, coupling):
    high, wide = coupling.shape[0] // pattern.shape[1], coupling.shape[1] // pattern.shape[0]
    for i in range(pattern.shape[1]):
        for j in range(pattern.shape[0]):
            at = (slice(i * high, (i + 1) * high), slice(j * wide, (j + 1) * wide))
            tile = coupling[at]
            coupling[at] = jnp.where(pattern[j, i] == 1, tile, jnp.zeros_like(tile))


def pairs_kernel(owner_in, blocks_in, green, inject_in, out, owner, blocks, inject, held, product, slot_of, counts, sem, side):
    energies, orbitals, _ = green.shape
    sections = out.shape[0]
    count = owner.shape[0]
    named = held.shape[1] < orbitals
    small = [
        pltpu.make_async_copy(src, dst, side.at[k])
        for k, (src, dst) in enumerate(((owner_in, owner), (blocks_in, blocks), (inject_in, inject)))
    ]
    for move in small:
        move.start()

    def copy_of(e, q):
        first = pl.multiple_of(blocks[0, q] * BLK, BLK)
        to = pl.multiple_of(q * BLK, BLK)
        return pltpu.make_async_copy(green.at[e, pl.ds(first, BLK)], held.at[e, pl.ds(to, BLK)], sem.at[e])

    def whole(e):
        return pltpu.make_async_copy(green.at[e], held.at[e], sem.at[e])

    if not named:
        for e in range(energies):
            whole(e).start()
    for move in small[:2]:
        move.wait()
    if named:
        for e in range(energies):
            lax.fori_loop(0, count, lambda q, _, e=e: copy_of(e, q).start(), None, unroll=4)
    rows = CAP * energies * BLK
    lane = lax.broadcasted_iota(jnp.int32, (HEAD, out.shape[2]), 1)
    none = jnp.where(lane < CAP, -1.0, 0.0).astype(BF16)

    def blank(d, _):
        counts[d] = 0
        out[d, :rows, :] = jnp.zeros((rows, out.shape[2]), BF16)
        out[d, rows : rows + HEAD, :] = none
        return 0

    lax.fori_loop(0, sections, blank, 0)

    def rank(q, _):
        d = owner[q]
        r = counts[d]
        counts[d] = r + 1
        slot_of[q] = r
        head = out[d, rows : rows + HEAD, :].astype(F32)
        head = jnp.where(lane == r, blocks[1, q].astype(F32), head)
        out[d, rows : rows + HEAD, :] = head.astype(BF16)
        return 0

    lax.fori_loop(0, count, rank, 0)
    small[2].wait()
    for e in range(energies):
        whole_held = pltpu.make_async_copy(green.at[e, pl.ds(0, held.shape[1])], held.at[e], sem.at[e])
        whole_held.wait()
        product[...] = dot(held[e], inject[e]).astype(BF16)

        def fill(q, _):
            first = pl.multiple_of((q if named else blocks[0, q]) * BLK, BLK)
            to = pl.multiple_of((slot_of[q] * energies + e) * BLK, BLK)
            out[owner[q], pl.ds(to, BLK), :] = product[pl.ds(first, BLK), :]
            return 0

        lax.fori_loop(0, count, fill, 0, unroll=4)


def outgoing_pairs(owner, blocks, green, inject, sections):
    energies, orbitals, _ = green.shape
    columns = inject.shape[2]
    rows = min(orbitals, owner.shape[0] * BLK)
    return call(
        pairs_kernel,
        "pairs",
        [IN_HBM] * 4,
        shape(sections, CAP * energies * BLK + HEAD, columns),
        [
            pltpu.SMEM(owner.shape, jnp.int32),
            pltpu.SMEM(blocks.shape, jnp.int32),
            pltpu.VMEM(inject.shape, BF16),
            pltpu.VMEM((energies, rows, orbitals), BF16),
            pltpu.VMEM((rows, columns), BF16),
            pltpu.SMEM(owner.shape, jnp.int32),
            pltpu.SMEM((sections,), jnp.int32),
            pltpu.SemaphoreType.DMA((energies,)),
            pltpu.SemaphoreType.DMA((3,)),
        ],
        4.0,
        VMEM_WHOLE,
    )(owner, blocks, green, inject)


def maps_kernel(pattern, green, coupling, own, other, face_rows, couple, maps):
    energies, orbitals, _ = green.shape
    face = coupling.shape[1]
    couple[...] = coupling[...]
    mask_tiles(pattern, couple)
    for e in range(energies):
        rows = green[e, orbitals - face :, :]
        face_rows[e] = rows
        maps[e] = dot(rows, couple[...])
    mine = place() // CORES
    own[...] = maps[mine]
    other[...] = maps[1 - mine]


def face_maps(pattern, green, coupling):
    orbitals, face = coupling.shape
    square = shape(face, face, dtype=F32)
    return call(
        maps_kernel,
        "face_maps",
        [IN_SMEM, IN_VMEM, IN_VMEM],
        [square, square, shape(green.shape[0], face, orbitals)],
        [pltpu.VMEM(coupling.shape, BF16), pltpu.VMEM((green.shape[0], face, face), F32)],
        1.2,
    )(pattern, green, coupling)


def prop_kernel(pattern, green, coupling, _tie, out, couple):
    couple[...] = coupling[...]
    mask_tiles(pattern, couple)
    for e in range(green.shape[0]):
        out[e] = dot(green[e], couple[...]).astype(BF16)


def propagator(pattern, green, coupling, tie):
    energies, orbitals, _ = green.shape
    return call(
        prop_kernel,
        "prop",
        [IN_SMEM, IN_VMEM, IN_VMEM, IN_PLACE],
        shape(energies, orbitals, coupling.shape[1]),
        [pltpu.VMEM(coupling.shape, BF16)],
        1.5,
    )(pattern, green, coupling, tie)


def image_kernel(green, source, _tie, out):
    for e in range(green.shape[0]):
        out[e] = dot(green[e], source[e])


def images(green, source, tie):
    return call(
        image_kernel, "image", [IN_VMEM] * 2 + [IN_PLACE], shape(*source.shape, dtype=F32), [], 1.2
    )(green, source, tie)


def times(a, b):
    return dot(a[0], b[0]) + (dot(a[0], b[1]) + dot(a[1], b[0]))


def chain_kernel(own, near, across, far, total_out, parts, maps):
    collect((own, near, across, far), maps)
    split = [two_parts(maps[j]) for j in range(GROUP)]
    lower, upper = two_parts(times(split[1], split[0])), two_parts(times(split[3], split[2]))
    total_out[...] = times(upper, lower).astype(total_out.dtype)
    for j, (high, low) in enumerate(split):
        parts[0, j] = high
        parts[1, j] = low


def chain(maps, dtype):
    face = maps[0].shape[0]
    return call(
        chain_kernel,
        "chain_maps",
        [IN_VMEM] * GROUP,
        [shape(face, face, dtype=dtype), shape(2, GROUP, face, face)],
        [pltpu.VMEM((GROUP, face, face), F32)],
        0.9,
    )(*maps)


def source_kernel(received, inject, face_rows, _map, source, own, near, across, far, _same_map, quarters, total, heads, targets, sem):
    energies, orbitals, columns = inject.shape
    sections = received.shape[0]
    half = quarters.shape[1]
    rows = CAP * energies * BLK

    def read(s, _):
        block = received[s, rows : rows + HEAD, :].astype(F32)
        heads[pl.ds(s, 1), :] = block[:1].astype(jnp.int32)
        return 0

    lax.fori_loop(0, sections, read, 0, unroll=min(sections, 8))
    fetch = pltpu.make_async_copy(heads, targets, sem)
    fetch.start()
    total[...] = inject[...].astype(F32)
    fetch.wait()

    def add(s, _):
        for r in range(CAP):
            first = pl.multiple_of(jnp.maximum(targets[s, r], 0) * BLK, BLK)
            for e in range(energies):
                item = received[s, (r * energies + e) * BLK : (r * energies + e + 1) * BLK, :]
                total[e, pl.ds(first, BLK), :] += item.astype(F32)
        return 0

    lax.fori_loop(0, sections, add, 0, unroll=2)
    split = GROUP // energies
    for e in range(energies):
        source[e] = total[e].astype(BF16)
        tall = dot(face_rows[e], source[e])
        quarters[e * split] = pack(tall)
        second = jnp.where(left_lanes(tall[:half]), swap_lanes(tall[:half]), tall[half:])
        quarters[e * split + 1] = second
    for out, at in zip((own, near, across, far), partners()):
        out[...] = quarters[at].astype(BF16)


def placed_source(received, inject, face_rows, passed):
    face = face_rows.shape[1]
    energies, orbitals, columns = inject.shape
    sections = received.shape[0]
    return call(
        source_kernel,
        "source_and_face",
        [IN_VMEM, IN_VMEM, IN_VMEM, IN_PLACE],
        [shape(*inject.shape)] + [shape(face // 2, columns)] * GROUP + [shape(*passed.shape, dtype=passed.dtype)],
        [
            pltpu.VMEM((GROUP, face // 2, columns), F32),
            pltpu.VMEM(inject.shape, F32),
            pltpu.VMEM((sections, columns), jnp.int32),
            pltpu.SMEM((sections, columns), jnp.int32),
            pltpu.SemaphoreType.DMA,
        ],
        1.4,
        aliases={3: 1 + GROUP},
    )(received, inject, face_rows, passed)


def collect(refs, held):
    for ref, at in zip(refs, partners()):
        held[at] = ref[...]


def step(parts, j, shift, state):
    return unpack(shift.astype(F32)) + times((parts[0, j], parts[1, j]), two_parts(state))


def total_kernel(own, near, across, far, parts, out, local, shifts):
    collect((own, near, across, far), shifts)
    state = unpack(shifts[0].astype(F32))
    for j in range(1, GROUP):
        local[j - 1] = state
        state = step(parts, j, shifts[j], state)
    out[...] = pack(state).astype(BF16)


def plane_total(shifts, parts):
    half, columns = shifts[0].shape
    return call(
        total_kernel,
        "plane_total",
        [IN_VMEM] * (GROUP + 1),
        [shape(half, columns), shape(GROUP - 1, 2 * half, columns, dtype=F32)],
        [pltpu.VMEM((GROUP, half, columns), BF16)],
        3.0,
    )(*shifts, parts)


def upto_kernel(parts, _total, out):
    maps = (parts[0, 0], parts[1, 0])
    for j in range(1, GROUP - 1):
        maps = two_parts(times((parts[0, j], parts[1, j]), maps))
        out[0, j - 1], out[1, j - 1] = maps


def maps_upto(parts, tie):
    _, _, face, _ = parts.shape
    return call(
        upto_kernel, "maps_upto", [IN_VMEM, IN_PLACE], shape(2, GROUP - 2, face, face), [], 3.0
    )(parts, tie)


def sweep_plane(state, parts, upto, local, out):
    two = two_parts(state)
    held = [pack(state)]
    for j in range(1, GROUP):
        maps = (parts[0, 0], parts[1, 0]) if j == 1 else (upto[0, j - 2], upto[1, j - 2])
        held.append(pack(local[j - 1] + times(maps, two)))
    work = out[GROUP]
    for j, item in enumerate(held):
        work[j] = item
    for ref, at in zip(out, partners()):
        ref[...] = work[at].astype(BF16)


def entering_kernel(_image, first, second, third, got, other, parts, upto, local, *out):
    first_core = place() % CORES == 0
    state = unpack(third[...].astype(F32))
    for below, (one, two) in ((second, (other, got)), (first, (got, other))):
        factor = jnp.where(first_core, one[...], two[...])
        high, low = two_parts(state)
        state = unpack(below[...].astype(F32)) + dot(factor, high) + dot(factor, low)
    sweep_plane(state, parts, upto, local, out)


def entering_from_kernel(_image, base, parts, upto, local, *out):
    sweep_plane(unpack(base[...]), parts, upto, local, out)


def entering(body, tie, args):
    half, columns = args[0].shape
    return call(
        body,
        "entering",
        [IN_PLACE] + [IN_VMEM] * len(args),
        [shape(half, columns)] * GROUP,
        [pltpu.VMEM((GROUP, half, columns), F32)],
        1.4,
    )(tie, *args)


def waves_kernel(own, near, across, far, prop, image, out, arrived):
    collect((own, near, across, far), arrived)
    split = GROUP // prop.shape[0]
    for e in range(prop.shape[0]):
        near, far = arrived[e * split].astype(F32), arrived[e * split + 1].astype(F32)
        left = left_lanes(near)
        top = jnp.where(left, near, swap_lanes(far))
        low = jnp.where(left, swap_lanes(near), far)
        incoming = jnp.concatenate([top, low], axis=0).astype(BF16)
        out[e] = (dot(prop[e], incoming) + image[e]).astype(BF16)


def final_waves(arrived, prop, image):
    half, columns = arrived[0].shape
    return call(
        waves_kernel,
        "waves",
        [IN_VMEM] * (GROUP + 2),
        shape(*image.shape),
        [pltpu.VMEM((GROUP, half, columns), BF16)],
        1.3,
    )(*arrived, prop, image)


def to_near(item, sections):
    return lax.ppermute(item, "sec", [(s, s ^ 1) for s in range(sections)])


def to_across(item, sections):
    return lax.ppermute(item, "sec", [(s, s // GROUP * GROUP + (s % GROUP + CORES) % GROUP) for s in range(sections)])


def to_far(item, sections):
    return lax.ppermute(item, "sec", [(s, s // GROUP * GROUP + (s % GROUP + CORES) % GROUP ^ 1) for s in range(sections)])


def exchange(own, near, across, far, sections):
    across, far = to_across(across, sections), to_far(far, sections)
    return [own, to_near(near, sections), across, far]


def up_shift(sections, k):
    return [(s, s + GROUP * k) for s in range(sections - GROUP * k)]


def spread(packed):
    half = packed.shape[1] // 2
    return jnp.concatenate([packed[:, :half], packed[:, half:]], axis=0)


def maps_up(total_map, sections):
    pairs = []
    for i in range(GROUP):
        if i % CORES == 0:
            pairs += [(GROUP + i, 2 * GROUP + i), (2 * GROUP + i, 3 * GROUP + i)]
        else:
            pairs += [(GROUP + i, 3 * GROUP + i)]
    got = lax.ppermute(total_map, "sec", pairs)
    return got, to_near(got, sections)


def upward(item, k, sections):
    return lax.ppermute(item, "sec", up_shift(sections, k))


def scan_below(total_map, total, sections):
    shift = lax.ppermute(spread(total).astype(F32), "sec", up_shift(sections, 1))
    joined = lax.ppermute(total_map, "sec", up_shift(sections, 1))
    stride = 1
    while stride < sections // GROUP:
        other = lax.ppermute(shift, "sec", up_shift(sections, stride))
        other_map = lax.ppermute(joined, "sec", up_shift(sections, stride))
        shift = shift + dot_wide(joined, other)
        joined = dot_wide(joined, other_map)
        stride *= 2
    half = shift.shape[0] // 2
    return jnp.concatenate([shift[:half], shift[half:]], axis=1)


def per_device(green, injected, coupling, pattern, owner, pair_blocks):
    sections = lax.axis_size("sec")
    green, inject = green[0], injected[0]

    coupling, tiles = coupling[0], pattern[0].T
    outgoing = outgoing_pairs(owner[:, 0], pair_blocks.T, green, inject, sections)
    received = lax.all_to_all(outgoing, "sec", split_axis=0, concat_axis=0, tiled=True)

    own_map, other_map, face_rows = face_maps(tiles, green, coupling)
    across = to_across(other_map, sections)
    near = to_near(own_map, sections)

    source, *quarters, across = placed_source(received, inject, face_rows, across)
    shifts = exchange(*quarters, sections)
    far = to_near(across, sections)
    four = sections // GROUP == 4
    total_map, parts = chain([own_map, near, across, far], BF16 if four else F32)
    maps = maps_up(total_map, sections) if four else []
    total, local = plane_total(shifts, parts)
    upto = maps_upto(parts, total)
    image = images(green, source, total)
    if four:
        below = [upward(total, k, sections) for k in range(1, 4)]
        entered = entering(entering_kernel, image, (*below, *maps, parts, upto, local))
    else:
        base = scan_below(total_map, total, sections)
        entered = entering(entering_from_kernel, image, (base, parts, upto, local))
    arrived = exchange(*entered, sections)
    prop = propagator(tiles, green, coupling, entered[0])
    return final_waves(arrived, prop, image)[None]


def solution(mesh):
    in_specs = (
        P("sec", "grp", None, None),
        P("sec", "grp", None, None),
        P("sec", None, None),
        P("sec", None, None),
        P("sec", None),
        P("sec", None),
    )
    out_specs = P("sec", "grp", None, None)
    return jax.shard_map(
        per_device, mesh=mesh, in_specs=in_specs, out_specs=out_specs, check_vma=False
    )
```

```python
import functools

import jax
import jax.numpy as jnp
from jax import lax
from jax.experimental import pallas as pl
from jax.experimental.pallas import tpu as pltpu
from jax.sharding import PartitionSpec as P

BLK = 32
CAP = 2
GROUP = 4
HEAD = 8
CORES = 2

HIGH = lax.Precision.HIGHEST
F32 = jnp.float32
BF16 = jnp.bfloat16
VMEM_SMALL = 16 * 1024 * 1024
VMEM_WHOLE = 63400000
PEAK = 1.15e9

IN_VMEM = pl.BlockSpec(memory_space=pltpu.VMEM)
IN_SMEM = pl.BlockSpec(memory_space=pltpu.SMEM)
IN_HBM = pl.BlockSpec(memory_space=pltpu.HBM)
IN_PLACE = pl.BlockSpec(memory_space=pl.ANY)


def shape(*dims, dtype=BF16):
    return jax.ShapeDtypeStruct(dims, dtype)


def call(body, name, ins, outs, scratch, micros, vmem=VMEM_SMALL, aliases=None):
    places = list(range(len(outs))) if isinstance(outs, list) else 0
    return pl.pallas_call(
        body,
        name=name,
        in_specs=ins,
        out_shape=outs,
        out_specs=jax.tree.map(lambda k: IN_PLACE if k in (aliases or {}).values() else IN_VMEM, places),
        input_output_aliases=aliases or {},
        scratch_shapes=scratch,
        compiler_params=pltpu.CompilerParams(vmem_limit_bytes=vmem),
        cost_estimate=pl.CostEstimate(flops=int(micros * PEAK), bytes_accessed=0, transcendentals=0),
    )


def place():
    return lax.axis_index("sec") % GROUP


def partners():
    here = place()
    across = (here + CORES) % GROUP
    return here, here ^ 1, across, across ^ 1


def dot(a, b):
    return jnp.dot(a, b, preferred_element_type=F32)


def dot_wide(a, b):
    return jnp.dot(a, b, precision=HIGH, preferred_element_type=F32)


def two_parts(x):
    high = x.astype(BF16)
    return high, (x - high.astype(F32)).astype(BF16)


def left_lanes(x):
    return lax.broadcasted_iota(jnp.int32, x.shape, 1) < x.shape[1] // 2


def swap_lanes(x):
    return pltpu.roll(x, x.shape[1] // 2, 1)


def pack(tall):
    half = tall.shape[0] // 2
    top, low = tall[:half], tall[half:]
    return jnp.where(left_lanes(top), top, swap_lanes(low))


def unpack(packed):
    return jnp.concatenate([packed, swap_lanes(packed)], axis=0)


def mask_tiles(pattern, coupling):
    high, wide = coupling.shape[0] // pattern.shape[1], coupling.shape[1] // pattern.shape[0]
    for i in range(pattern.shape[1]):
        for j in range(pattern.shape[0]):
            at = (slice(i * high, (i + 1) * high), slice(j * wide, (j + 1) * wide))
            tile = coupling[at]
            coupling[at] = jnp.where(pattern[j, i] == 1, tile, jnp.zeros_like(tile))


def pairs_kernel(owner_in, blocks_in, green, inject_in, out, owner, blocks, inject, held, product, slot_of, counts, sem, side):
    energies, orbitals, _ = green.shape
    sections = out.shape[0]
    count = owner.shape[0]
    named = held.shape[1] < orbitals
    small = [
        pltpu.make_async_copy(src, dst, side.at[k])
        for k, (src, dst) in enumerate(((owner_in, owner), (blocks_in, blocks), (inject_in, inject)))
    ]
    for move in small:
        move.start()

    def copy_of(e, q):
        first = pl.multiple_of(blocks[0, q] * BLK, BLK)
        to = pl.multiple_of(q * BLK, BLK)
        return pltpu.make_async_copy(green.at[e, pl.ds(first, BLK)], held.at[e, pl.ds(to, BLK)], sem.at[e])

    def whole(e):
        return pltpu.make_async_copy(green.at[e], held.at[e], sem.at[e])

    if not named:
        for e in range(energies):
            whole(e).start()
    for move in small[:2]:
        move.wait()
    if named:
        for e in range(energies):
            lax.fori_loop(0, count, lambda q, _, e=e: copy_of(e, q).start(), None, unroll=4)
    rows = CAP * energies * BLK
    lane = lax.broadcasted_iota(jnp.int32, (HEAD, out.shape[2]), 1)
    none = jnp.where(lane < CAP, -1.0, 0.0).astype(BF16)

    def blank(d, _):
        counts[d] = 0
        out[d, :rows, :] = jnp.zeros((rows, out.shape[2]), BF16)
        out[d, rows : rows + HEAD, :] = none
        return 0

    lax.fori_loop(0, sections, blank, 0)

    def rank(q, _):
        d = owner[q]
        r = counts[d]
        counts[d] = r + 1
        slot_of[q] = r
        head = out[d, rows : rows + HEAD, :].astype(F32)
        head = jnp.where(lane == r, blocks[1, q].astype(F32), head)
        out[d, rows : rows + HEAD, :] = head.astype(BF16)
        return 0

    lax.fori_loop(0, count, rank, 0)
    small[2].wait()
    for e in range(energies):
        whole_held = pltpu.make_async_copy(green.at[e, pl.ds(0, held.shape[1])], held.at[e], sem.at[e])
        whole_held.wait()
        product[...] = dot(held[e], inject[e]).astype(BF16)

        def fill(q, _):
            first = pl.multiple_of((q if named else blocks[0, q]) * BLK, BLK)
            to = pl.multiple_of((slot_of[q] * energies + e) * BLK, BLK)
            out[owner[q], pl.ds(to, BLK), :] = product[pl.ds(first, BLK), :]
            return 0

        lax.fori_loop(0, count, fill, 0, unroll=4)


def outgoing_pairs(owner, blocks, green, inject, sections):
    energies, orbitals, _ = green.shape
    columns = inject.shape[2]
    rows = min(orbitals, owner.shape[0] * BLK)
    return call(
        pairs_kernel,
        "pairs",
        [IN_HBM] * 4,
        shape(sections, CAP * energies * BLK + HEAD, columns),
        [
            pltpu.SMEM(owner.shape, jnp.int32),
            pltpu.SMEM(blocks.shape, jnp.int32),
            pltpu.VMEM(inject.shape, BF16),
            pltpu.VMEM((energies, rows, orbitals), BF16),
            pltpu.VMEM((rows, columns), BF16),
            pltpu.SMEM(owner.shape, jnp.int32),
            pltpu.SMEM((sections,), jnp.int32),
            pltpu.SemaphoreType.DMA((energies,)),
            pltpu.SemaphoreType.DMA((3,)),
        ],
        4.0,
        VMEM_WHOLE,
    )(owner, blocks, green, inject)


def maps_kernel(pattern, green, coupling, own, other, face_rows, couple, maps):
    energies, orbitals, _ = green.shape
    face = coupling.shape[1]
    couple[...] = coupling[...]
    mask_tiles(pattern, couple)
    for e in range(energies):
        rows = green[e, orbitals - face :, :]
        face_rows[e] = rows
        maps[e] = dot(rows, couple[...])
    mine = place() // CORES
    own[...] = maps[mine]
    other[...] = maps[1 - mine]


def face_maps(pattern, green, coupling):
    orbitals, face = coupling.shape
    square = shape(face, face, dtype=F32)
    return call(
        maps_kernel,
        "face_maps",
        [IN_SMEM, IN_VMEM, IN_VMEM],
        [square, square, shape(green.shape[0], face, orbitals)],
        [pltpu.VMEM(coupling.shape, BF16), pltpu.VMEM((green.shape[0], face, face), F32)],
        1.2,
    )(pattern, green, coupling)


def prop_kernel(pattern, green, coupling, _tie, out, couple):
    couple[...] = coupling[...]
    mask_tiles(pattern, couple)
    for e in range(green.shape[0]):
        out[e] = dot(green[e], couple[...]).astype(BF16)


def propagator(pattern, green, coupling, tie):
    energies, orbitals, _ = green.shape
    return call(
        prop_kernel,
        "prop",
        [IN_SMEM, IN_VMEM, IN_VMEM, IN_PLACE],
        shape(energies, orbitals, coupling.shape[1]),
        [pltpu.VMEM(coupling.shape, BF16)],
        1.5,
    )(pattern, green, coupling, tie)


def image_kernel(green, source, _tie, out):
    for e in range(green.shape[0]):
        out[e] = dot(green[e], source[e])


def images(green, source, tie):
    return call(
        image_kernel, "image", [IN_VMEM] * 2 + [IN_PLACE], shape(*source.shape, dtype=F32), [], 1.2
    )(green, source, tie)


def times(a, b):
    return dot(a[0], b[0]) + (dot(a[0], b[1]) + dot(a[1], b[0]))


def chain_kernel(own, near, across, far, total_out, sent_out, parts, maps):
    collect((own, near, across, far), maps)
    split = [two_parts(maps[j]) for j in range(GROUP)]
    lower, upper = two_parts(times(split[1], split[0])), two_parts(times(split[3], split[2]))
    total = times(upper, lower)
    total_out[...] = total
    sent_out[...] = total.astype(BF16)
    for j, (high, low) in enumerate(split):
        parts[0, j] = high
        parts[1, j] = low


def chain(maps):
    face = maps[0].shape[0]
    return call(
        chain_kernel,
        "chain_maps",
        [IN_VMEM] * GROUP,
        [shape(face, face, dtype=F32), shape(face, face), shape(2, GROUP, face, face)],
        [pltpu.VMEM((GROUP, face, face), F32)],
        0.9,
    )(*maps)


def source_kernel(received, inject, face_rows, _map, source, own, near, across, far, _same_map, quarters, total, heads, targets, sem):
    energies, orbitals, columns = inject.shape
    sections = received.shape[0]
    half = quarters.shape[1]
    rows = CAP * energies * BLK

    def read(s, _):
        block = received[s, rows : rows + HEAD, :].astype(F32)
        heads[pl.ds(s, 1), :] = block[:1].astype(jnp.int32)
        return 0

    lax.fori_loop(0, sections, read, 0, unroll=min(sections, 8))
    fetch = pltpu.make_async_copy(heads, targets, sem)
    fetch.start()
    total[...] = inject[...].astype(F32)
    fetch.wait()

    def add(s, _):
        for r in range(CAP):
            first = pl.multiple_of(jnp.maximum(targets[s, r], 0) * BLK, BLK)
            for e in range(energies):
                item = received[s, (r * energies + e) * BLK : (r * energies + e + 1) * BLK, :]
                total[e, pl.ds(first, BLK), :] += item.astype(F32)
        return 0

    lax.fori_loop(0, sections, add, 0, unroll=2)
    split = GROUP // energies
    for e in range(energies):
        source[e] = total[e].astype(BF16)
        tall = dot(face_rows[e], source[e])
        quarters[e * split] = pack(tall)
        second = jnp.where(left_lanes(tall[:half]), swap_lanes(tall[:half]), tall[half:])
        quarters[e * split + 1] = second
    for out, at in zip((own, near, across, far), partners()):
        out[...] = quarters[at].astype(BF16)


def placed_source(received, inject, face_rows, passed):
    face = face_rows.shape[1]
    energies, orbitals, columns = inject.shape
    sections = received.shape[0]
    return call(
        source_kernel,
        "source_and_face",
        [IN_VMEM, IN_VMEM, IN_VMEM, IN_PLACE],
        [shape(*inject.shape)] + [shape(face // 2, columns)] * GROUP + [shape(*passed.shape, dtype=passed.dtype)],
        [
            pltpu.VMEM((GROUP, face // 2, columns), F32),
            pltpu.VMEM(inject.shape, F32),
            pltpu.VMEM((sections, columns), jnp.int32),
            pltpu.SMEM((sections, columns), jnp.int32),
            pltpu.SemaphoreType.DMA,
        ],
        1.4,
        aliases={3: 1 + GROUP},
    )(received, inject, face_rows, passed)


def collect(refs, held):
    for ref, at in zip(refs, partners()):
        held[at] = ref[...]


def step(parts, j, shift, state):
    return unpack(shift.astype(F32)) + times((parts[0, j], parts[1, j]), two_parts(state))


def total_kernel(own, near, across, far, parts, out, local, shifts):
    collect((own, near, across, far), shifts)
    state = unpack(shifts[0].astype(F32))
    for j in range(1, GROUP):
        local[j - 1] = state
        state = step(parts, j, shifts[j], state)
    out[...] = pack(state).astype(BF16)


def plane_total(shifts, parts):
    half, columns = shifts[0].shape
    return call(
        total_kernel,
        "plane_total",
        [IN_VMEM] * (GROUP + 1),
        [shape(half, columns), shape(GROUP - 1, 2 * half, columns, dtype=F32)],
        [pltpu.VMEM((GROUP, half, columns), BF16)],
        3.0,
    )(*shifts, parts)


def upto_kernel(parts, _total, out):
    maps = (parts[0, 0], parts[1, 0])
    for j in range(1, GROUP - 1):
        maps = two_parts(times((parts[0, j], parts[1, j]), maps))
        out[0, j - 1], out[1, j - 1] = maps


def maps_upto(parts, tie):
    _, _, face, _ = parts.shape
    return call(
        upto_kernel, "maps_upto", [IN_VMEM, IN_PLACE], shape(2, GROUP - 2, face, face), [], 3.0
    )(parts, tie)


def sweep_plane(state, parts, upto, local, out):
    two = two_parts(state)
    held = [pack(state)]
    for j in range(1, GROUP):
        maps = (parts[0, 0], parts[1, 0]) if j == 1 else (upto[0, j - 2], upto[1, j - 2])
        held.append(pack(local[j - 1] + times(maps, two)))
    work = out[GROUP]
    for j, item in enumerate(held):
        work[j] = item
    for ref, at in zip(out, partners()):
        ref[...] = work[at].astype(BF16)


def pair_kernel(total, below, whole, _image, out):
    state = unpack(total[...].astype(F32)) + times(two_parts(whole[...]), two_parts(unpack(below[...].astype(F32))))
    out[...] = pack(state).astype(BF16)


def pair_total(total, below, whole, tie):
    return call(
        pair_kernel, "pair_total", [IN_VMEM] * 3 + [IN_PLACE], shape(*total.shape), [], 0.5
    )(total, below, whole, tie)


def entering_kernel(_image, below, first, second, got, parts, upto, local, *out):
    high, low = two_parts(unpack(second[...].astype(F32)))
    state = unpack(below[...].astype(F32) + first[...].astype(F32)) + dot(got[...], high) + dot(got[...], low)
    sweep_plane(state, parts, upto, local, out)


def entering_from_kernel(_image, base, parts, upto, local, *out):
    sweep_plane(unpack(base[...]), parts, upto, local, out)


def entering(body, tie, args):
    half, columns = args[0].shape
    return call(
        body,
        "entering",
        [IN_PLACE] + [IN_VMEM] * len(args),
        [shape(half, columns)] * GROUP,
        [pltpu.VMEM((GROUP, half, columns), F32)],
        1.4,
    )(tie, *args)


def waves_kernel(own, near, across, far, prop, image, out, arrived):
    collect((own, near, across, far), arrived)
    split = GROUP // prop.shape[0]
    for e in range(prop.shape[0]):
        near, far = arrived[e * split].astype(F32), arrived[e * split + 1].astype(F32)
        left = left_lanes(near)
        top = jnp.where(left, near, swap_lanes(far))
        low = jnp.where(left, swap_lanes(near), far)
        incoming = jnp.concatenate([top, low], axis=0).astype(BF16)
        out[e] = (dot(prop[e], incoming) + image[e]).astype(BF16)


def final_waves(arrived, prop, image):
    half, columns = arrived[0].shape
    return call(
        waves_kernel,
        "waves",
        [IN_VMEM] * (GROUP + 2),
        shape(*image.shape),
        [pltpu.VMEM((GROUP, half, columns), BF16)],
        1.3,
    )(*arrived, prop, image)


def to_near(item, sections):
    return lax.ppermute(item, "sec", [(s, s ^ 1) for s in range(sections)])


def to_across(item, sections):
    return lax.ppermute(item, "sec", [(s, s // GROUP * GROUP + (s % GROUP + CORES) % GROUP) for s in range(sections)])


def to_far(item, sections):
    return lax.ppermute(item, "sec", [(s, s // GROUP * GROUP + (s % GROUP + CORES) % GROUP ^ 1) for s in range(sections)])


def exchange(own, near, across, far, sections):
    across, far = to_across(across, sections), to_far(far, sections)
    return [own, to_near(near, sections), across, far]


def up_shift(sections, k):
    return [(s, s + GROUP * k) for s in range(sections - GROUP * k)]


def spread(packed):
    half = packed.shape[1] // 2
    return jnp.concatenate([packed[:, :half], packed[:, half:]], axis=0)


def between(item, *planes):
    pairs = [(p * GROUP + i, q * GROUP + i) for p, q in planes for i in range(GROUP)]
    return lax.ppermute(item, "sec", pairs)


def scan_below(total_map, total, sections):
    shift = lax.ppermute(spread(total).astype(F32), "sec", up_shift(sections, 1))
    joined = lax.ppermute(total_map, "sec", up_shift(sections, 1))
    stride = 1
    while stride < sections // GROUP:
        other = lax.ppermute(shift, "sec", up_shift(sections, stride))
        other_map = lax.ppermute(joined, "sec", up_shift(sections, stride))
        shift = shift + dot_wide(joined, other)
        joined = dot_wide(joined, other_map)
        stride *= 2
    half = shift.shape[0] // 2
    return jnp.concatenate([shift[:half], shift[half:]], axis=1)


def per_device(green, injected, coupling, pattern, owner, pair_blocks):
    sections = lax.axis_size("sec")
    green, inject = green[0], injected[0]

    coupling, tiles = coupling[0], pattern[0].T
    outgoing = outgoing_pairs(owner[:, 0], pair_blocks.T, green, inject, sections)
    received = lax.all_to_all(outgoing, "sec", split_axis=0, concat_axis=0, tiled=True)

    own_map, other_map, face_rows = face_maps(tiles, green, coupling)
    across = to_across(other_map, sections)
    near = to_near(own_map, sections)

    source, *quarters, across = placed_source(received, inject, face_rows, across)
    shifts = exchange(*quarters, sections)
    far = to_near(across, sections)
    four = sections // GROUP == 4
    whole, sent, parts = chain([own_map, near, across, far])
    got = between(sent, (2, 3)) if four else None
    total, local = plane_total(shifts, parts)
    upto = maps_upto(parts, total)
    image = images(green, source, total)
    if four:
        below = between(total, (0, 1), (2, 3))
        pair = pair_total(total, below, whole, image)
        first, second = between(pair, (1, 2)), between(pair, (1, 3))
        entered = entering(entering_kernel, image, (below, first, second, got, parts, upto, local))
    else:
        base = scan_below(whole, total, sections)
        entered = entering(entering_from_kernel, image, (base, parts, upto, local))
    arrived = exchange(*entered, sections)
    prop = propagator(tiles, green, coupling, entered[0])
    return final_waves(arrived, prop, image)[None]


def solution(mesh):
    in_specs = (
        P("sec", "grp", None, None),
        P("sec", "grp", None, None),
        P("sec", None, None),
        P("sec", None, None),
        P("sec", None),
        P("sec", None),
    )
    out_specs = P("sec", "grp", None, None)
    return jax.shard_map(
        per_device, mesh=mesh, in_specs=in_specs, out_specs=out_specs, check_vma=False
    )
```

```python
import functools

import jax
import jax.numpy as jnp
from jax import lax
from jax.experimental import pallas as pl
from jax.experimental.pallas import tpu as pltpu
from jax.sharding import PartitionSpec as P

BLK = 32
CAP = 2
GROUP = 4
HEAD = 8
CORES = 2

HIGH = lax.Precision.HIGHEST
F32 = jnp.float32
BF16 = jnp.bfloat16
VMEM_SMALL = 16 * 1024 * 1024
VMEM_WHOLE = 63400000
PEAK = 1.15e9

IN_VMEM = pl.BlockSpec(memory_space=pltpu.VMEM)
IN_SMEM = pl.BlockSpec(memory_space=pltpu.SMEM)
IN_HBM = pl.BlockSpec(memory_space=pltpu.HBM)
IN_PLACE = pl.BlockSpec(memory_space=pl.ANY)


def shape(*dims, dtype=BF16):
    return jax.ShapeDtypeStruct(dims, dtype)


def call(body, name, ins, outs, scratch, micros, vmem=VMEM_SMALL, aliases=None):
    places = list(range(len(outs))) if isinstance(outs, list) else 0
    return pl.pallas_call(
        body,
        name=name,
        in_specs=ins,
        out_shape=outs,
        out_specs=jax.tree.map(lambda k: IN_PLACE if k in (aliases or {}).values() else IN_VMEM, places),
        input_output_aliases=aliases or {},
        scratch_shapes=scratch,
        compiler_params=pltpu.CompilerParams(vmem_limit_bytes=vmem),
        cost_estimate=pl.CostEstimate(flops=int(micros * PEAK), bytes_accessed=0, transcendentals=0),
    )


def place():
    return lax.axis_index("sec") % GROUP


def partners():
    here = place()
    across = (here + CORES) % GROUP
    return here, here ^ 1, across, across ^ 1


def dot(a, b):
    return jnp.dot(a, b, preferred_element_type=F32)


def dot_wide(a, b):
    return jnp.dot(a, b, precision=HIGH, preferred_element_type=F32)


def two_parts(x):
    high = x.astype(BF16)
    return high, (x - high.astype(F32)).astype(BF16)


def left_lanes(x):
    return lax.broadcasted_iota(jnp.int32, x.shape, 1) < x.shape[1] // 2


def swap_lanes(x):
    return pltpu.roll(x, x.shape[1] // 2, 1)


def pack(tall):
    half = tall.shape[0] // 2
    top, low = tall[:half], tall[half:]
    return jnp.where(left_lanes(top), top, swap_lanes(low))


def unpack(packed):
    return jnp.concatenate([packed, swap_lanes(packed)], axis=0)


def mask_tiles(pattern, coupling):
    high, wide = coupling.shape[0] // pattern.shape[1], coupling.shape[1] // pattern.shape[0]
    for i in range(pattern.shape[1]):
        for j in range(pattern.shape[0]):
            at = (slice(i * high, (i + 1) * high), slice(j * wide, (j + 1) * wide))
            tile = coupling[at]
            coupling[at] = jnp.where(pattern[j, i] == 1, tile, jnp.zeros_like(tile))


def pairs_kernel(owner_in, blocks_in, green, inject_in, out, owner, blocks, inject, held, product, slot_of, counts, sem, side):
    energies, orbitals, _ = green.shape
    sections = out.shape[0]
    count = owner.shape[0]
    named = held.shape[1] < orbitals
    small = [
        pltpu.make_async_copy(src, dst, side.at[k])
        for k, (src, dst) in enumerate(((owner_in, owner), (blocks_in, blocks), (inject_in, inject)))
    ]
    for move in small:
        move.start()

    def copy_of(e, q):
        first = pl.multiple_of(blocks[0, q] * BLK, BLK)
        to = pl.multiple_of(q * BLK, BLK)
        return pltpu.make_async_copy(green.at[e, pl.ds(first, BLK)], held.at[e, pl.ds(to, BLK)], sem.at[e])

    def whole(e):
        return pltpu.make_async_copy(green.at[e], held.at[e], sem.at[e])

    if not named:
        for e in range(energies):
            whole(e).start()
    for move in small[:2]:
        move.wait()
    if named:
        for e in range(energies):
            lax.fori_loop(0, count, lambda q, _, e=e: copy_of(e, q).start(), None, unroll=4)
    rows = CAP * energies * BLK
    lane = lax.broadcasted_iota(jnp.int32, (HEAD, out.shape[2]), 1)
    none = jnp.where(lane < CAP, -1.0, 0.0).astype(BF16)

    def blank(d, _):
        counts[d] = 0
        out[d, :rows, :] = jnp.zeros((rows, out.shape[2]), BF16)
        out[d, rows : rows + HEAD, :] = none
        return 0

    lax.fori_loop(0, sections, blank, 0)

    def rank(q, _):
        d = owner[q]
        r = counts[d]
        counts[d] = r + 1
        slot_of[q] = r
        head = out[d, rows : rows + HEAD, :].astype(F32)
        head = jnp.where(lane == r, blocks[1, q].astype(F32), head)
        out[d, rows : rows + HEAD, :] = head.astype(BF16)
        return 0

    lax.fori_loop(0, count, rank, 0)
    small[2].wait()
    for e in range(energies):
        whole_held = pltpu.make_async_copy(green.at[e, pl.ds(0, held.shape[1])], held.at[e], sem.at[e])
        whole_held.wait()
        product[...] = dot(held[e], inject[e]).astype(BF16)

        def fill(q, _):
            first = pl.multiple_of((q if named else blocks[0, q]) * BLK, BLK)
            to = pl.multiple_of((slot_of[q] * energies + e) * BLK, BLK)
            out[owner[q], pl.ds(to, BLK), :] = product[pl.ds(first, BLK), :]
            return 0

        lax.fori_loop(0, count, fill, 0, unroll=4)


def outgoing_pairs(owner, blocks, green, inject, sections):
    energies, orbitals, _ = green.shape
    columns = inject.shape[2]
    rows = min(orbitals, owner.shape[0] * BLK)
    return call(
        pairs_kernel,
        "pairs",
        [IN_HBM] * 4,
        shape(sections, CAP * energies * BLK + HEAD, columns),
        [
            pltpu.SMEM(owner.shape, jnp.int32),
            pltpu.SMEM(blocks.shape, jnp.int32),
            pltpu.VMEM(inject.shape, BF16),
            pltpu.VMEM((energies, rows, orbitals), BF16),
            pltpu.VMEM((rows, columns), BF16),
            pltpu.SMEM(owner.shape, jnp.int32),
            pltpu.SMEM((sections,), jnp.int32),
            pltpu.SemaphoreType.DMA((energies,)),
            pltpu.SemaphoreType.DMA((3,)),
        ],
        4.0,
        VMEM_WHOLE,
    )(owner, blocks, green, inject)


def maps_kernel(pattern, green, coupling, own, other, face_rows, couple, maps):
    energies, orbitals, _ = green.shape
    face = coupling.shape[1]
    couple[...] = coupling[...]
    mask_tiles(pattern, couple)
    for e in range(energies):
        rows = green[e, orbitals - face :, :]
        face_rows[e] = rows
        maps[e] = dot(rows, couple[...])
    mine = place() // CORES
    own[...] = maps[mine]
    other[...] = maps[1 - mine]


def face_maps(pattern, green, coupling):
    orbitals, face = coupling.shape
    square = shape(face, face, dtype=F32)
    return call(
        maps_kernel,
        "face_maps",
        [IN_SMEM, IN_VMEM, IN_VMEM],
        [square, square, shape(green.shape[0], face, orbitals)],
        [pltpu.VMEM(coupling.shape, BF16), pltpu.VMEM((green.shape[0], face, face), F32)],
        1.2,
    )(pattern, green, coupling)


def prop_kernel(pattern, green, coupling, _tie, out, couple):
    couple[...] = coupling[...]
    mask_tiles(pattern, couple)
    for e in range(green.shape[0]):
        out[e] = dot(green[e], couple[...]).astype(BF16)


def propagator(pattern, green, coupling, tie):
    energies, orbitals, _ = green.shape
    return call(
        prop_kernel,
        "prop",
        [IN_SMEM, IN_VMEM, IN_VMEM, IN_PLACE],
        shape(energies, orbitals, coupling.shape[1]),
        [pltpu.VMEM(coupling.shape, BF16)],
        1.5,
    )(pattern, green, coupling, tie)


def image_kernel(green, source, _tie, out):
    for e in range(green.shape[0]):
        out[e] = dot(green[e], source[e])


def images(green, source, tie):
    return call(
        image_kernel, "image", [IN_VMEM] * 2 + [IN_PLACE], shape(*source.shape, dtype=F32), [], 1.2
    )(green, source, tie)


def times(a, b):
    return dot(a[0], b[0]) + (dot(a[0], b[1]) + dot(a[1], b[0]))


def chain_kernel(own, near, across, far, total_out, sent_out, parts, maps):
    collect((own, near, across, far), maps)
    split = [two_parts(maps[j]) for j in range(GROUP)]
    lower, upper = two_parts(times(split[1], split[0])), two_parts(times(split[3], split[2]))
    total = times(upper, lower)
    total_out[...] = total
    sent_out[...] = total.astype(BF16)
    for j, (high, low) in enumerate(split):
        parts[0, j] = high
        parts[1, j] = low


def chain(maps):
    face = maps[0].shape[0]
    return call(
        chain_kernel,
        "chain_maps",
        [IN_VMEM] * GROUP,
        [shape(face, face, dtype=F32), shape(face, face), shape(2, GROUP, face, face)],
        [pltpu.VMEM((GROUP, face, face), F32)],
        0.9,
    )(*maps)


def source_kernel(received, inject, face_rows, _map, source, own, near, across, far, _same_map, quarters, total, heads, targets, sem):
    energies, orbitals, columns = inject.shape
    sections = received.shape[0]
    half = quarters.shape[1]
    rows = CAP * energies * BLK

    def read(s, _):
        block = received[s, rows : rows + HEAD, :].astype(F32)
        heads[pl.ds(s, 1), :] = block[:1].astype(jnp.int32)
        return 0

    lax.fori_loop(0, sections, read, 0, unroll=min(sections, 8))
    fetch = pltpu.make_async_copy(heads, targets, sem)
    fetch.start()
    total[...] = inject[...].astype(F32)
    fetch.wait()

    def add(s, _):
        for r in range(CAP):
            first = pl.multiple_of(jnp.maximum(targets[s, r], 0) * BLK, BLK)
            for e in range(energies):
                item = received[s, (r * energies + e) * BLK : (r * energies + e + 1) * BLK, :]
                total[e, pl.ds(first, BLK), :] += item.astype(F32)
        return 0

    lax.fori_loop(0, sections, add, 0, unroll=2)
    split = GROUP // energies
    for e in range(energies):
        source[e] = total[e].astype(BF16)
        tall = dot(face_rows[e], source[e])
        quarters[e * split] = pack(tall)
        second = jnp.where(left_lanes(tall[:half]), swap_lanes(tall[:half]), tall[half:])
        quarters[e * split + 1] = second
    for out, at in zip((own, near, across, far), partners()):
        out[...] = quarters[at].astype(BF16)


def placed_source(received, inject, face_rows, passed):
    face = face_rows.shape[1]
    energies, orbitals, columns = inject.shape
    sections = received.shape[0]
    return call(
        source_kernel,
        "source_and_face",
        [IN_VMEM, IN_VMEM, IN_VMEM, IN_PLACE],
        [shape(*inject.shape)] + [shape(face // 2, columns)] * GROUP + [shape(*passed.shape, dtype=passed.dtype)],
        [
            pltpu.VMEM((GROUP, face // 2, columns), F32),
            pltpu.VMEM(inject.shape, F32),
            pltpu.VMEM((sections, columns), jnp.int32),
            pltpu.SMEM((sections, columns), jnp.int32),
            pltpu.SemaphoreType.DMA,
        ],
        1.4,
        aliases={3: 1 + GROUP},
    )(received, inject, face_rows, passed)


def collect(refs, held):
    for ref, at in zip(refs, partners()):
        held[at] = ref[...]


def step(parts, j, shift, state):
    return unpack(shift.astype(F32)) + times((parts[0, j], parts[1, j]), two_parts(state))


def total_kernel(own, near, across, far, parts, out, local, shifts):
    collect((own, near, across, far), shifts)
    state = unpack(shifts[0].astype(F32))
    for j in range(1, GROUP):
        local[j - 1] = state
        state = step(parts, j, shifts[j], state)
    out[...] = pack(state).astype(BF16)


def plane_total(shifts, parts):
    half, columns = shifts[0].shape
    return call(
        total_kernel,
        "plane_total",
        [IN_VMEM] * (GROUP + 1),
        [shape(half, columns), shape(GROUP - 1, 2 * half, columns, dtype=F32)],
        [pltpu.VMEM((GROUP, half, columns), BF16)],
        3.0,
    )(*shifts, parts)


def upto_kernel(parts, _total, out):
    maps = (parts[0, 0], parts[1, 0])
    for j in range(1, GROUP - 1):
        maps = two_parts(times((parts[0, j], parts[1, j]), maps))
        out[0, j - 1], out[1, j - 1] = maps


def maps_upto(parts, tie):
    _, _, face, _ = parts.shape
    return call(
        upto_kernel, "maps_upto", [IN_VMEM, IN_PLACE], shape(2, GROUP - 2, face, face), [], 3.0
    )(parts, tie)


def sweep_plane(state, parts, upto, local, out):
    two = two_parts(state)
    held = [pack(state)]
    for j in range(1, GROUP):
        maps = (parts[0, 0], parts[1, 0]) if j == 1 else (upto[0, j - 2], upto[1, j - 2])
        held.append(pack(local[j - 1] + times(maps, two)))
    work = out[GROUP]
    for j, item in enumerate(held):
        work[j] = item
    for ref, at in zip(out, partners()):
        ref[...] = work[at].astype(BF16)


def pair_kernel(total, below, whole, _image, _upto, out):
    state = unpack(total[...].astype(F32)) + times(two_parts(whole[...]), two_parts(unpack(below[...].astype(F32))))
    out[...] = pack(state).astype(BF16)


def pair_total(total, below, whole, *ties):
    return call(
        pair_kernel, "pair_total", [IN_VMEM] * 3 + [IN_PLACE] * 2, shape(*total.shape), [], 0.5
    )(total, below, whole, *ties)


def entering_kernel(_image, below, first, second, got, parts, upto, local, *out):
    high, low = two_parts(unpack(second[...].astype(F32)))
    state = unpack(below[...].astype(F32) + first[...].astype(F32)) + dot(got[...], high) + dot(got[...], low)
    sweep_plane(state, parts, upto, local, out)


def entering_from_kernel(_image, base, parts, upto, local, *out):
    sweep_plane(unpack(base[...]), parts, upto, local, out)


def entering(body, tie, args):
    half, columns = args[0].shape
    return call(
        body,
        "entering",
        [IN_PLACE] + [IN_VMEM] * len(args),
        [shape(half, columns)] * GROUP,
        [pltpu.VMEM((GROUP, half, columns), F32)],
        1.4,
    )(tie, *args)


def waves_kernel(own, near, across, far, prop, image, out, arrived):
    collect((own, near, across, far), arrived)
    split = GROUP // prop.shape[0]
    for e in range(prop.shape[0]):
        near, far = arrived[e * split].astype(F32), arrived[e * split + 1].astype(F32)
        left = left_lanes(near)
        top = jnp.where(left, near, swap_lanes(far))
        low = jnp.where(left, swap_lanes(near), far)
        incoming = jnp.concatenate([top, low], axis=0).astype(BF16)
        out[e] = (dot(prop[e], incoming) + image[e]).astype(BF16)


def final_waves(arrived, prop, image):
    half, columns = arrived[0].shape
    return call(
        waves_kernel,
        "waves",
        [IN_VMEM] * (GROUP + 2),
        shape(*image.shape),
        [pltpu.VMEM((GROUP, half, columns), BF16)],
        1.3,
    )(*arrived, prop, image)


def to_near(item, sections):
    return lax.ppermute(item, "sec", [(s, s ^ 1) for s in range(sections)])


def to_across(item, sections):
    return lax.ppermute(item, "sec", [(s, s // GROUP * GROUP + (s % GROUP + CORES) % GROUP) for s in range(sections)])


def to_far(item, sections):
    return lax.ppermute(item, "sec", [(s, s // GROUP * GROUP + (s % GROUP + CORES) % GROUP ^ 1) for s in range(sections)])


def exchange(own, near, across, far, sections):
    across, far = to_across(across, sections), to_far(far, sections)
    return [own, to_near(near, sections), across, far]


def up_shift(sections, k):
    return [(s, s + GROUP * k) for s in range(sections - GROUP * k)]


def spread(packed):
    half = packed.shape[1] // 2
    return jnp.concatenate([packed[:, :half], packed[:, half:]], axis=0)


def between(item, *planes):
    pairs = [(p * GROUP + i, q * GROUP + i) for p, q in planes for i in range(GROUP)]
    return lax.ppermute(item, "sec", pairs)


def scan_below(total_map, total, sections):
    shift = lax.ppermute(spread(total).astype(F32), "sec", up_shift(sections, 1))
    joined = lax.ppermute(total_map, "sec", up_shift(sections, 1))
    stride = 1
    while stride < sections // GROUP:
        other = lax.ppermute(shift, "sec", up_shift(sections, stride))
        other_map = lax.ppermute(joined, "sec", up_shift(sections, stride))
        shift = shift + dot_wide(joined, other)
        joined = dot_wide(joined, other_map)
        stride *= 2
    half = shift.shape[0] // 2
    return jnp.concatenate([shift[:half], shift[half:]], axis=1)


def per_device(green, injected, coupling, pattern, owner, pair_blocks):
    sections = lax.axis_size("sec")
    green, inject = green[0], injected[0]

    coupling, tiles = coupling[0], pattern[0].T
    outgoing = outgoing_pairs(owner[:, 0], pair_blocks.T, green, inject, sections)
    received = lax.all_to_all(outgoing, "sec", split_axis=0, concat_axis=0, tiled=True)

    own_map, other_map, face_rows = face_maps(tiles, green, coupling)
    across = to_across(other_map, sections)
    near = to_near(own_map, sections)

    source, *quarters, across = placed_source(received, inject, face_rows, across)
    shifts = exchange(*quarters, sections)
    far = to_near(across, sections)
    four = sections // GROUP == 4
    whole, sent, parts = chain([own_map, near, across, far])
    got = between(sent, (2, 3)) if four else None
    total, local = plane_total(shifts, parts)
    upto = maps_upto(parts, total)
    image = images(green, source, total)
    if four:
        below = between(total, (0, 1))
        pair = pair_total(total, below, whole, image, upto)
        first, second = between(pair, (1, 2), (2, 3)), between(pair, (1, 3))
        entered = entering(entering_kernel, image, (below, first, second, got, parts, upto, local))
    else:
        base = scan_below(whole, total, sections)
        entered = entering(entering_from_kernel, image, (base, parts, upto, local))
    arrived = exchange(*entered, sections)
    prop = propagator(tiles, green, coupling, entered[0])
    return final_waves(arrived, prop, image)[None]


def solution(mesh):
    in_specs = (
        P("sec", "grp", None, None),
        P("sec", "grp", None, None),
        P("sec", None, None),
        P("sec", None, None),
        P("sec", None),
        P("sec", None),
    )
    out_specs = P("sec", "grp", None, None)
    return jax.shard_map(
        per_device, mesh=mesh, in_specs=in_specs, out_specs=out_specs, check_vma=False
    )
```

```python
import functools

import jax
import jax.numpy as jnp
from jax import lax
from jax.experimental import pallas as pl
from jax.experimental.pallas import tpu as pltpu
from jax.sharding import PartitionSpec as P

BLK = 32
CAP = 2
GROUP = 4
HEAD = 8
CORES = 2

HIGH = lax.Precision.HIGHEST
F32 = jnp.float32
BF16 = jnp.bfloat16
VMEM_SMALL = 16 * 1024 * 1024
VMEM_WHOLE = 63400000
PEAK = 1.15e9

IN_VMEM = pl.BlockSpec(memory_space=pltpu.VMEM)
IN_SMEM = pl.BlockSpec(memory_space=pltpu.SMEM)
IN_HBM = pl.BlockSpec(memory_space=pltpu.HBM)
IN_PLACE = pl.BlockSpec(memory_space=pl.ANY)


def shape(*dims, dtype=BF16):
    return jax.ShapeDtypeStruct(dims, dtype)


def call(body, name, ins, outs, scratch, micros, vmem=VMEM_SMALL, aliases=None):
    places = list(range(len(outs))) if isinstance(outs, list) else 0
    return pl.pallas_call(
        body,
        name=name,
        in_specs=ins,
        out_shape=outs,
        out_specs=jax.tree.map(lambda k: IN_PLACE if k in (aliases or {}).values() else IN_VMEM, places),
        input_output_aliases=aliases or {},
        scratch_shapes=scratch,
        compiler_params=pltpu.CompilerParams(vmem_limit_bytes=vmem),
        cost_estimate=pl.CostEstimate(flops=int(micros * PEAK), bytes_accessed=0, transcendentals=0),
    )


def place():
    return lax.axis_index("sec") % GROUP


def partners():
    here = place()
    across = (here + CORES) % GROUP
    return here, here ^ 1, across, across ^ 1


def dot(a, b):
    return jnp.dot(a, b, preferred_element_type=F32)


def dot_wide(a, b):
    return jnp.dot(a, b, precision=HIGH, preferred_element_type=F32)


def two_parts(x):
    high = x.astype(BF16)
    return high, (x - high.astype(F32)).astype(BF16)


def left_lanes(x):
    return lax.broadcasted_iota(jnp.int32, x.shape, 1) < x.shape[1] // 2


def swap_lanes(x):
    return pltpu.roll(x, x.shape[1] // 2, 1)


def pack(tall):
    half = tall.shape[0] // 2
    top, low = tall[:half], tall[half:]
    return jnp.where(left_lanes(top), top, swap_lanes(low))


def unpack(packed):
    return jnp.concatenate([packed, swap_lanes(packed)], axis=0)


def mask_tiles(pattern, coupling):
    high, wide = coupling.shape[0] // pattern.shape[1], coupling.shape[1] // pattern.shape[0]
    for i in range(pattern.shape[1]):
        for j in range(pattern.shape[0]):
            at = (slice(i * high, (i + 1) * high), slice(j * wide, (j + 1) * wide))
            tile = coupling[at]
            coupling[at] = jnp.where(pattern[j, i] == 1, tile, jnp.zeros_like(tile))


def pairs_kernel(owner_in, blocks_in, green, inject_in, out, owner, blocks, inject, held, product, slot_of, counts, sem, side):
    energies, orbitals, _ = green.shape
    sections = out.shape[0]
    count = owner.shape[0]
    named = held.shape[1] < orbitals
    small = [
        pltpu.make_async_copy(src, dst, side.at[k])
        for k, (src, dst) in enumerate(((owner_in, owner), (blocks_in, blocks), (inject_in, inject)))
    ]
    for move in small:
        move.start()

    def copy_of(e, q):
        first = pl.multiple_of(blocks[0, q] * BLK, BLK)
        to = pl.multiple_of(q * BLK, BLK)
        return pltpu.make_async_copy(green.at[e, pl.ds(first, BLK)], held.at[e, pl.ds(to, BLK)], sem.at[e])

    def whole(e):
        return pltpu.make_async_copy(green.at[e], held.at[e], sem.at[e])

    if not named:
        for e in range(energies):
            whole(e).start()
    for move in small[:2]:
        move.wait()
    if named:
        for e in range(energies):
            lax.fori_loop(0, count, lambda q, _, e=e: copy_of(e, q).start(), None, unroll=4)
    rows = CAP * energies * BLK
    lane = lax.broadcasted_iota(jnp.int32, (HEAD, out.shape[2]), 1)
    none = jnp.where(lane < CAP, -1.0, 0.0).astype(BF16)

    def blank(d, _):
        counts[d] = 0
        out[d, :rows, :] = jnp.zeros((rows, out.shape[2]), BF16)
        out[d, rows : rows + HEAD, :] = none
        return 0

    lax.fori_loop(0, sections, blank, 0)

    def rank(q, _):
        d = owner[q]
        r = counts[d]
        counts[d] = r + 1
        slot_of[q] = r
        head = out[d, rows : rows + HEAD, :].astype(F32)
        head = jnp.where(lane == r, blocks[1, q].astype(F32), head)
        out[d, rows : rows + HEAD, :] = head.astype(BF16)
        return 0

    lax.fori_loop(0, count, rank, 0)
    small[2].wait()
    for e in range(energies):
        whole_held = pltpu.make_async_copy(green.at[e, pl.ds(0, held.shape[1])], held.at[e], sem.at[e])
        whole_held.wait()
        product[...] = dot(held[e], inject[e]).astype(BF16)

        def fill(q, _):
            first = pl.multiple_of((q if named else blocks[0, q]) * BLK, BLK)
            to = pl.multiple_of((slot_of[q] * energies + e) * BLK, BLK)
            out[owner[q], pl.ds(to, BLK), :] = product[pl.ds(first, BLK), :]
            return 0

        lax.fori_loop(0, count, fill, 0, unroll=4)


def outgoing_pairs(owner, blocks, green, inject, sections):
    energies, orbitals, _ = green.shape
    columns = inject.shape[2]
    rows = min(orbitals, owner.shape[0] * BLK)
    return call(
        pairs_kernel,
        "pairs",
        [IN_HBM] * 4,
        shape(sections, CAP * energies * BLK + HEAD, columns),
        [
            pltpu.SMEM(owner.shape, jnp.int32),
            pltpu.SMEM(blocks.shape, jnp.int32),
            pltpu.VMEM(inject.shape, BF16),
            pltpu.VMEM((energies, rows, orbitals), BF16),
            pltpu.VMEM((rows, columns), BF16),
            pltpu.SMEM(owner.shape, jnp.int32),
            pltpu.SMEM((sections,), jnp.int32),
            pltpu.SemaphoreType.DMA((energies,)),
            pltpu.SemaphoreType.DMA((3,)),
        ],
        4.0,
        VMEM_WHOLE,
    )(owner, blocks, green, inject)


def maps_kernel(pattern, green, coupling, own, other, face_rows, couple, maps):
    energies, orbitals, _ = green.shape
    face = coupling.shape[1]
    couple[...] = coupling[...]
    mask_tiles(pattern, couple)
    for e in range(energies):
        rows = green[e, orbitals - face :, :]
        face_rows[e] = rows
        maps[e] = dot(rows, couple[...])
    mine = place() // CORES
    own[...] = maps[mine]
    other[...] = maps[1 - mine]


def face_maps(pattern, green, coupling):
    orbitals, face = coupling.shape
    square = shape(face, face, dtype=F32)
    return call(
        maps_kernel,
        "face_maps",
        [IN_SMEM, IN_VMEM, IN_VMEM],
        [square, square, shape(green.shape[0], face, orbitals)],
        [pltpu.VMEM(coupling.shape, BF16), pltpu.VMEM((green.shape[0], face, face), F32)],
        1.2,
    )(pattern, green, coupling)


def prop_kernel(pattern, green, coupling, _tie, out, couple):
    couple[...] = coupling[...]
    mask_tiles(pattern, couple)
    for e in range(green.shape[0]):
        out[e] = dot(green[e], couple[...]).astype(BF16)


def propagator(pattern, green, coupling, tie):
    energies, orbitals, _ = green.shape
    return call(
        prop_kernel,
        "prop",
        [IN_SMEM, IN_VMEM, IN_VMEM, IN_PLACE],
        shape(energies, orbitals, coupling.shape[1]),
        [pltpu.VMEM(coupling.shape, BF16)],
        1.5,
    )(pattern, green, coupling, tie)


def times(a, b):
    return dot(a[0], b[0]) + (dot(a[0], b[1]) + dot(a[1], b[0]))


def chain_kernel(own, near, across, far, _tie, total_out, sent_out, parts, maps):
    collect((own, near, across, far), maps)
    split = [two_parts(maps[j]) for j in range(GROUP)]
    lower, upper = two_parts(times(split[1], split[0])), two_parts(times(split[3], split[2]))
    total = times(upper, lower)
    total_out[...] = total
    sent_out[...] = total.astype(BF16)
    for j, (high, low) in enumerate(split):
        parts[0, j] = high
        parts[1, j] = low


def chain(maps, tie):
    face = maps[0].shape[0]
    return call(
        chain_kernel,
        "chain_maps",
        [IN_VMEM] * GROUP + [IN_PLACE],
        [shape(face, face, dtype=F32), shape(face, face), shape(2, GROUP, face, face)],
        [pltpu.VMEM((GROUP, face, face), F32)],
        0.9,
    )(*maps, tie)


def source_kernel(received, inject, face_rows, source, own, near, across, far, quarters, total, heads, targets, sem):
    energies, orbitals, columns = inject.shape
    sections = received.shape[0]
    half = quarters.shape[1]
    rows = CAP * energies * BLK

    def read(s, _):
        block = received[s, rows : rows + HEAD, :].astype(F32)
        heads[pl.ds(s, 1), :] = block[:1].astype(jnp.int32)
        return 0

    lax.fori_loop(0, sections, read, 0, unroll=min(sections, 8))
    fetch = pltpu.make_async_copy(heads, targets, sem)
    fetch.start()
    total[...] = inject[...].astype(F32)
    fetch.wait()

    def add(s, _):
        for r in range(CAP):
            first = pl.multiple_of(jnp.maximum(targets[s, r], 0) * BLK, BLK)
            for e in range(energies):
                item = received[s, (r * energies + e) * BLK : (r * energies + e + 1) * BLK, :]
                total[e, pl.ds(first, BLK), :] += item.astype(F32)
        return 0

    lax.fori_loop(0, sections, add, 0, unroll=2)
    split = GROUP // energies
    for e in range(energies):
        source[e] = total[e].astype(BF16)
        tall = dot(face_rows[e], source[e])
        quarters[e * split] = pack(tall)
        second = jnp.where(left_lanes(tall[:half]), swap_lanes(tall[:half]), tall[half:])
        quarters[e * split + 1] = second
    for out, at in zip((own, near, across, far), partners()):
        out[...] = quarters[at].astype(BF16)


def placed_source(received, inject, face_rows):
    face = face_rows.shape[1]
    energies, orbitals, columns = inject.shape
    sections = received.shape[0]
    return call(
        source_kernel,
        "source_and_face",
        [IN_VMEM, IN_VMEM, IN_VMEM],
        [shape(*inject.shape)] + [shape(face // 2, columns)] * GROUP,
        [
            pltpu.VMEM((GROUP, face // 2, columns), F32),
            pltpu.VMEM(inject.shape, F32),
            pltpu.VMEM((sections, columns), jnp.int32),
            pltpu.SMEM((sections, columns), jnp.int32),
            pltpu.SemaphoreType.DMA,
        ],
        1.4,
    )(received, inject, face_rows)


def collect(refs, held):
    for ref, at in zip(refs, partners()):
        held[at] = ref[...]


def step(parts, j, shift, state):
    return unpack(shift.astype(F32)) + times((parts[0, j], parts[1, j]), two_parts(state))


def total_kernel(own, near, across, far, parts, out, local, shifts):
    collect((own, near, across, far), shifts)
    state = unpack(shifts[0].astype(F32))
    for j in range(1, GROUP):
        local[j - 1] = state
        state = step(parts, j, shifts[j], state)
    out[...] = pack(state).astype(BF16)


def plane_total(shifts, parts):
    half, columns = shifts[0].shape
    return call(
        total_kernel,
        "plane_total",
        [IN_VMEM] * (GROUP + 1),
        [shape(half, columns), shape(GROUP - 1, 2 * half, columns, dtype=F32)],
        [pltpu.VMEM((GROUP, half, columns), BF16)],
        3.0,
    )(*shifts, parts)


def work_kernel(early, *refs):
    green, source, parts, _tie = refs[:4]
    held, (image, upto) = refs[4:-2], refs[-2:]
    low_plane = lax.axis_index("sec") // GROUP < 2

    @pl.when(low_plane if early else jnp.logical_not(low_plane))
    def _():
        for e in range(green.shape[0]):
            image[e] = dot(green[e], source[e])
        maps = (parts[0, 0], parts[1, 0])
        for j in range(1, GROUP - 1):
            maps = two_parts(times((parts[0, j], parts[1, j]), maps))
            upto[0, j - 1], upto[1, j - 1] = maps

    if held:

        @pl.when(low_plane)
        def _():
            image[...] = held[0][...]
            upto[...] = held[1][...]


def image_and_maps(green, source, parts, tie, held=()):
    _, _, face, _ = parts.shape
    return call(
        functools.partial(work_kernel, not held),
        "image_and_maps",
        [IN_VMEM] * 3 + [IN_PLACE] + [IN_VMEM] * len(held),
        [shape(*source.shape, dtype=F32), shape(2, GROUP - 2, face, face)],
        [],
        2.0,
    )(green, source, parts, tie, *held)


def sweep_plane(state, parts, upto, local, out):
    two = two_parts(state)
    held = [pack(state)]
    for j in range(1, GROUP):
        maps = (parts[0, 0], parts[1, 0]) if j == 1 else (upto[0, j - 2], upto[1, j - 2])
        held.append(pack(local[j - 1] + times(maps, two)))
    work = out[GROUP]
    for j, item in enumerate(held):
        work[j] = item
    for ref, at in zip(out, partners()):
        ref[...] = work[at].astype(BF16)


def pair_kernel(total, below, whole, _image, _upto, out):
    state = unpack(total[...].astype(F32)) + times(two_parts(whole[...]), two_parts(unpack(below[...].astype(F32))))
    out[...] = pack(state).astype(BF16)


def pair_total(total, below, whole, *ties):
    return call(
        pair_kernel, "pair_total", [IN_VMEM] * 3 + [IN_PLACE] * 2, shape(*total.shape), [], 0.5
    )(total, below, whole, *ties)


def entering_kernel(below, first, second, got, parts, upto, local, *out):
    high, low = two_parts(unpack(second[...].astype(F32)))
    state = unpack(below[...].astype(F32) + first[...].astype(F32)) + dot(got[...], high) + dot(got[...], low)
    sweep_plane(state, parts, upto, local, out)


def entering_from_kernel(base, parts, upto, local, *out):
    sweep_plane(unpack(base[...]), parts, upto, local, out)


def entering(body, args):
    half, columns = args[0].shape
    return call(
        body,
        "entering",
        [IN_VMEM] * len(args),
        [shape(half, columns)] * GROUP,
        [pltpu.VMEM((GROUP, half, columns), F32)],
        1.4,
    )(*args)


def waves_kernel(own, near, across, far, prop, image, out, arrived):
    collect((own, near, across, far), arrived)
    split = GROUP // prop.shape[0]
    for e in range(prop.shape[0]):
        near, far = arrived[e * split].astype(F32), arrived[e * split + 1].astype(F32)
        left = left_lanes(near)
        top = jnp.where(left, near, swap_lanes(far))
        low = jnp.where(left, swap_lanes(near), far)
        incoming = jnp.concatenate([top, low], axis=0).astype(BF16)
        out[e] = (dot(prop[e], incoming) + image[e]).astype(BF16)


def final_waves(arrived, prop, image):
    half, columns = arrived[0].shape
    return call(
        waves_kernel,
        "waves",
        [IN_VMEM] * (GROUP + 2),
        shape(*image.shape),
        [pltpu.VMEM((GROUP, half, columns), BF16)],
        1.3,
    )(*arrived, prop, image)


def to_near(item, sections):
    return lax.ppermute(item, "sec", [(s, s ^ 1) for s in range(sections)])


def to_across(item, sections):
    return lax.ppermute(item, "sec", [(s, s // GROUP * GROUP + (s % GROUP + CORES) % GROUP) for s in range(sections)])


def to_far(item, sections):
    return lax.ppermute(item, "sec", [(s, s // GROUP * GROUP + (s % GROUP + CORES) % GROUP ^ 1) for s in range(sections)])


def exchange(own, near, across, far, sections):
    across, far = to_across(across, sections), to_far(far, sections)
    return [own, to_near(near, sections), across, far]


def up_shift(sections, k):
    return [(s, s + GROUP * k) for s in range(sections - GROUP * k)]


def spread(packed):
    half = packed.shape[1] // 2
    return jnp.concatenate([packed[:, :half], packed[:, half:]], axis=0)


def between(item, *planes):
    pairs = [(p * GROUP + i, q * GROUP + i) for p, q in planes for i in range(GROUP)]
    return lax.ppermute(item, "sec", pairs)


def scan_below(total_map, total, sections):
    shift = lax.ppermute(spread(total).astype(F32), "sec", up_shift(sections, 1))
    joined = lax.ppermute(total_map, "sec", up_shift(sections, 1))
    stride = 1
    while stride < sections // GROUP:
        other = lax.ppermute(shift, "sec", up_shift(sections, stride))
        other_map = lax.ppermute(joined, "sec", up_shift(sections, stride))
        shift = shift + dot_wide(joined, other)
        joined = dot_wide(joined, other_map)
        stride *= 2
    half = shift.shape[0] // 2
    return jnp.concatenate([shift[:half], shift[half:]], axis=1)


def per_device(green, injected, coupling, pattern, owner, pair_blocks):
    sections = lax.axis_size("sec")
    green, inject = green[0], injected[0]

    coupling, tiles = coupling[0], pattern[0].T
    outgoing = outgoing_pairs(owner[:, 0], pair_blocks.T, green, inject, sections)
    received = lax.all_to_all(outgoing, "sec", split_axis=0, concat_axis=0, tiled=True)

    own_map, other_map, face_rows = face_maps(tiles, green, coupling)
    across = to_across(other_map, sections)
    near = to_near(own_map, sections)

    far = to_near(across, sections)

    source, *quarters = placed_source(received, inject, face_rows)
    shifts = exchange(*quarters, sections)
    four = sections // GROUP == 4
    whole, sent, parts = chain([own_map, near, across, far], quarters[0])
    got = between(sent, (2, 3)) if four else None
    total, local = plane_total(shifts, parts)
    early = image_and_maps(green, source, parts, total)
    if four:
        below = between(total, (0, 1))
        pair = pair_total(total, below, whole, *early)
        second, first = between(pair, (1, 3)), between(pair, (1, 2), (2, 3))
        image, upto = image_and_maps(green, source, parts, pair, early)
        entered = entering(entering_kernel, (below, first, second, got, parts, upto, local))
    else:
        base = scan_below(whole, total, sections)
        image, upto = image_and_maps(green, source, parts, base, early)
        entered = entering(entering_from_kernel, (base, parts, upto, local))
    arrived = exchange(*entered, sections)
    prop = propagator(tiles, green, coupling, entered[0])
    return final_waves(arrived, prop, image)[None]


def solution(mesh):
    in_specs = (
        P("sec", "grp", None, None),
        P("sec", "grp", None, None),
        P("sec", None, None),
        P("sec", None, None),
        P("sec", None),
        P("sec", None),
    )
    out_specs = P("sec", "grp", None, None)
    return jax.shard_map(
        per_device, mesh=mesh, in_specs=in_specs, out_specs=out_specs, check_vma=False
    )
```

```python
import functools

import jax
import jax.numpy as jnp
from jax import lax
from jax.experimental import pallas as pl
from jax.experimental.pallas import tpu as pltpu
from jax.sharding import PartitionSpec as P

BLK = 32
CAP = 2
GROUP = 4
HEAD = 8
CORES = 2

HIGH = lax.Precision.HIGHEST
F32 = jnp.float32
BF16 = jnp.bfloat16
VMEM_SMALL = 16 * 1024 * 1024
VMEM_WHOLE = 63400000
PEAK = 1.15e9

IN_VMEM = pl.BlockSpec(memory_space=pltpu.VMEM)
IN_SMEM = pl.BlockSpec(memory_space=pltpu.SMEM)
IN_HBM = pl.BlockSpec(memory_space=pltpu.HBM)
IN_PLACE = pl.BlockSpec(memory_space=pl.ANY)


def shape(*dims, dtype=BF16):
    return jax.ShapeDtypeStruct(dims, dtype)


def call(body, name, ins, outs, scratch, micros, vmem=VMEM_SMALL, aliases=None):
    places = list(range(len(outs))) if isinstance(outs, list) else 0
    return pl.pallas_call(
        body,
        name=name,
        in_specs=ins,
        out_shape=outs,
        out_specs=jax.tree.map(lambda k: IN_PLACE if k in (aliases or {}).values() else IN_VMEM, places),
        input_output_aliases=aliases or {},
        scratch_shapes=scratch,
        compiler_params=pltpu.CompilerParams(vmem_limit_bytes=vmem),
        cost_estimate=pl.CostEstimate(flops=int(micros * PEAK), bytes_accessed=0, transcendentals=0),
    )


def place():
    return lax.axis_index("sec") % GROUP


def partners():
    here = place()
    across = (here + CORES) % GROUP
    return here, here ^ 1, across, across ^ 1


def dot(a, b):
    return jnp.dot(a, b, preferred_element_type=F32)


def dot_wide(a, b):
    return jnp.dot(a, b, precision=HIGH, preferred_element_type=F32)


def two_parts(x):
    high = x.astype(BF16)
    return high, (x - high.astype(F32)).astype(BF16)


def left_lanes(x):
    return lax.broadcasted_iota(jnp.int32, x.shape, 1) < x.shape[1] // 2


def swap_lanes(x):
    return pltpu.roll(x, x.shape[1] // 2, 1)


def pack(tall):
    half = tall.shape[0] // 2
    top, low = tall[:half], tall[half:]
    return jnp.where(left_lanes(top), top, swap_lanes(low))


def unpack(packed):
    return jnp.concatenate([packed, swap_lanes(packed)], axis=0)


def mask_tiles(pattern, coupling):
    high, wide = coupling.shape[0] // pattern.shape[1], coupling.shape[1] // pattern.shape[0]
    for i in range(pattern.shape[1]):
        for j in range(pattern.shape[0]):
            at = (slice(i * high, (i + 1) * high), slice(j * wide, (j + 1) * wide))
            tile = coupling[at]
            coupling[at] = jnp.where(pattern[j, i] == 1, tile, jnp.zeros_like(tile))


def pairs_kernel(owner_in, blocks_in, green, inject_in, out, owner, blocks, inject, held, product, slot_of, counts, sem, side):
    energies, orbitals, _ = green.shape
    sections = out.shape[0]
    count = owner.shape[0]
    named = held.shape[1] < orbitals
    small = [
        pltpu.make_async_copy(src, dst, side.at[k])
        for k, (src, dst) in enumerate(((owner_in, owner), (blocks_in, blocks), (inject_in, inject)))
    ]
    for move in small:
        move.start()

    def copy_of(e, q):
        first = pl.multiple_of(blocks[0, q] * BLK, BLK)
        to = pl.multiple_of(q * BLK, BLK)
        return pltpu.make_async_copy(green.at[e, pl.ds(first, BLK)], held.at[e, pl.ds(to, BLK)], sem.at[e])

    def whole(e):
        return pltpu.make_async_copy(green.at[e], held.at[e], sem.at[e])

    if not named:
        for e in range(energies):
            whole(e).start()
    for move in small[:2]:
        move.wait()
    if named:
        for e in range(energies):
            lax.fori_loop(0, count, lambda q, _, e=e: copy_of(e, q).start(), None, unroll=4)
    rows = CAP * energies * BLK
    lane = lax.broadcasted_iota(jnp.int32, (HEAD, out.shape[2]), 1)
    none = jnp.where(lane < CAP, -1.0, 0.0).astype(BF16)

    def blank(d, _):
        counts[d] = 0
        out[d, :rows, :] = jnp.zeros((rows, out.shape[2]), BF16)
        out[d, rows : rows + HEAD, :] = none
        return 0

    lax.fori_loop(0, sections, blank, 0)

    def rank(q, _):
        d = owner[q]
        r = counts[d]
        counts[d] = r + 1
        slot_of[q] = r
        head = out[d, rows : rows + HEAD, :].astype(F32)
        head = jnp.where(lane == r, blocks[1, q].astype(F32), head)
        out[d, rows : rows + HEAD, :] = head.astype(BF16)
        return 0

    lax.fori_loop(0, count, rank, 0)
    small[2].wait()
    for e in range(energies):
        whole_held = pltpu.make_async_copy(green.at[e, pl.ds(0, held.shape[1])], held.at[e], sem.at[e])
        whole_held.wait()
        product[...] = dot(held[e], inject[e]).astype(BF16)

        def fill(q, _):
            first = pl.multiple_of((q if named else blocks[0, q]) * BLK, BLK)
            to = pl.multiple_of((slot_of[q] * energies + e) * BLK, BLK)
            out[owner[q], pl.ds(to, BLK), :] = product[pl.ds(first, BLK), :]
            return 0

        lax.fori_loop(0, count, fill, 0, unroll=4)


def outgoing_pairs(owner, blocks, green, inject, sections):
    energies, orbitals, _ = green.shape
    columns = inject.shape[2]
    rows = min(orbitals, owner.shape[0] * BLK)
    return call(
        pairs_kernel,
        "pairs",
        [IN_HBM] * 4,
        shape(sections, CAP * energies * BLK + HEAD, columns),
        [
            pltpu.SMEM(owner.shape, jnp.int32),
            pltpu.SMEM(blocks.shape, jnp.int32),
            pltpu.VMEM(inject.shape, BF16),
            pltpu.VMEM((energies, rows, orbitals), BF16),
            pltpu.VMEM((rows, columns), BF16),
            pltpu.SMEM(owner.shape, jnp.int32),
            pltpu.SMEM((sections,), jnp.int32),
            pltpu.SemaphoreType.DMA((energies,)),
            pltpu.SemaphoreType.DMA((3,)),
        ],
        4.0,
        VMEM_WHOLE,
    )(owner, blocks, green, inject)


def maps_kernel(pattern, green, coupling, own, other, face_rows, couple, maps):
    energies, orbitals, _ = green.shape
    face = coupling.shape[1]
    couple[...] = coupling[...]
    mask_tiles(pattern, couple)
    for e in range(energies):
        rows = green[e, orbitals - face :, :]
        face_rows[e] = rows
        maps[e] = dot(rows, couple[...])
    mine = place() // CORES
    own[...] = maps[mine]
    other[...] = maps[1 - mine]


def face_maps(pattern, green, coupling):
    orbitals, face = coupling.shape
    square = shape(face, face, dtype=F32)
    return call(
        maps_kernel,
        "face_maps",
        [IN_SMEM, IN_VMEM, IN_VMEM],
        [square, square, shape(green.shape[0], face, orbitals)],
        [pltpu.VMEM(coupling.shape, BF16), pltpu.VMEM((green.shape[0], face, face), F32)],
        1.2,
    )(pattern, green, coupling)


def prop_kernel(pattern, green, coupling, _tie, out, couple):
    couple[...] = coupling[...]
    mask_tiles(pattern, couple)
    for e in range(green.shape[0]):
        out[e] = dot(green[e], couple[...]).astype(BF16)


def propagator(pattern, green, coupling, tie):
    energies, orbitals, _ = green.shape
    return call(
        prop_kernel,
        "prop",
        [IN_SMEM, IN_VMEM, IN_VMEM, IN_PLACE],
        shape(energies, orbitals, coupling.shape[1]),
        [pltpu.VMEM(coupling.shape, BF16)],
        1.5,
    )(pattern, green, coupling, tie)


def times(a, b):
    return dot(a[0], b[0]) + (dot(a[0], b[1]) + dot(a[1], b[0]))


def chain_kernel(own, near, across, far, total_out, sent_out, parts, maps):
    collect((own, near, across, far), maps)
    split = [two_parts(maps[j]) for j in range(GROUP)]
    lower, upper = two_parts(times(split[1], split[0])), two_parts(times(split[3], split[2]))
    total = times(upper, lower)
    total_out[...] = total
    sent_out[...] = total.astype(BF16)
    for j, (high, low) in enumerate(split):
        parts[0, j] = high
        parts[1, j] = low


def chain(maps):
    face = maps[0].shape[0]
    return call(
        chain_kernel,
        "chain_maps",
        [IN_VMEM] * GROUP,
        [shape(face, face, dtype=F32), shape(face, face), shape(2, GROUP, face, face)],
        [pltpu.VMEM((GROUP, face, face), F32)],
        0.9,
    )(*maps)


def source_kernel(received, inject, face_rows, _map, source, own, near, across, far, _same_map, quarters, total, heads, targets, sem):
    energies, orbitals, columns = inject.shape
    sections = received.shape[0]
    half = quarters.shape[1]
    rows = CAP * energies * BLK

    def read(s, _):
        block = received[s, rows : rows + HEAD, :].astype(F32)
        heads[pl.ds(s, 1), :] = block[:1].astype(jnp.int32)
        return 0

    lax.fori_loop(0, sections, read, 0, unroll=min(sections, 8))
    fetch = pltpu.make_async_copy(heads, targets, sem)
    fetch.start()
    total[...] = inject[...].astype(F32)
    fetch.wait()

    def add(s, _):
        for r in range(CAP):
            first = pl.multiple_of(jnp.maximum(targets[s, r], 0) * BLK, BLK)
            for e in range(energies):
                item = received[s, (r * energies + e) * BLK : (r * energies + e + 1) * BLK, :]
                total[e, pl.ds(first, BLK), :] += item.astype(F32)
        return 0

    lax.fori_loop(0, sections, add, 0, unroll=2)
    split = GROUP // energies
    for e in range(energies):
        source[e] = total[e].astype(BF16)
        tall = dot(face_rows[e], source[e])
        quarters[e * split] = pack(tall)
        second = jnp.where(left_lanes(tall[:half]), swap_lanes(tall[:half]), tall[half:])
        quarters[e * split + 1] = second
    for out, at in zip((own, near, across, far), partners()):
        out[...] = quarters[at].astype(BF16)


def placed_source(received, inject, face_rows, passed):
    face = face_rows.shape[1]
    energies, orbitals, columns = inject.shape
    sections = received.shape[0]
    return call(
        source_kernel,
        "source_and_face",
        [IN_VMEM, IN_VMEM, IN_VMEM, IN_PLACE],
        [shape(*inject.shape)] + [shape(face // 2, columns)] * GROUP + [shape(*passed.shape, dtype=F32)],
        [
            pltpu.VMEM((GROUP, face // 2, columns), F32),
            pltpu.VMEM(inject.shape, F32),
            pltpu.VMEM((sections, columns), jnp.int32),
            pltpu.SMEM((sections, columns), jnp.int32),
            pltpu.SemaphoreType.DMA,
        ],
        1.4,
        aliases={3: 1 + GROUP},
    )(received, inject, face_rows, passed)


def collect(refs, held):
    for ref, at in zip(refs, partners()):
        held[at] = ref[...]


def step(parts, j, shift, state):
    return unpack(shift.astype(F32)) + times((parts[0, j], parts[1, j]), two_parts(state))


def total_kernel(own, near, across, far, parts, out, local, shifts):
    collect((own, near, across, far), shifts)
    state = unpack(shifts[0].astype(F32))
    for j in range(1, GROUP):
        local[j - 1] = state
        state = step(parts, j, shifts[j], state)
    out[...] = pack(state).astype(BF16)


def plane_total(shifts, parts):
    half, columns = shifts[0].shape
    return call(
        total_kernel,
        "plane_total",
        [IN_VMEM] * (GROUP + 1),
        [shape(half, columns), shape(GROUP - 1, 2 * half, columns, dtype=F32)],
        [pltpu.VMEM((GROUP, half, columns), BF16)],
        3.0,
    )(*shifts, parts)


def work_kernel(early, *refs):
    green, source, parts, _tie = refs[:4]
    held, (image, upto) = refs[4:-2], refs[-2:]
    low_plane = lax.axis_index("sec") // GROUP < 2

    @pl.when(low_plane if early else jnp.logical_not(low_plane))
    def _():
        for e in range(green.shape[0]):
            image[e] = dot(green[e], source[e])
        maps = (parts[0, 0], parts[1, 0])
        for j in range(1, GROUP - 1):
            maps = two_parts(times((parts[0, j], parts[1, j]), maps))
            upto[0, j - 1], upto[1, j - 1] = maps

    if held:

        @pl.when(low_plane)
        def _():
            image[...] = held[0][...]
            upto[...] = held[1][...]


def image_and_maps(green, source, parts, tie, held=()):
    _, _, face, _ = parts.shape
    return call(
        functools.partial(work_kernel, not held),
        "image_and_maps",
        [IN_VMEM] * 3 + [IN_PLACE] + [IN_VMEM] * len(held),
        [shape(*source.shape, dtype=F32), shape(2, GROUP - 2, face, face)],
        [],
        2.0,
    )(green, source, parts, tie, *held)


def sweep_plane(state, parts, upto, local, out):
    two = two_parts(state)
    held = [pack(state)]
    for j in range(1, GROUP):
        maps = (parts[0, 0], parts[1, 0]) if j == 1 else (upto[0, j - 2], upto[1, j - 2])
        held.append(pack(local[j - 1] + times(maps, two)))
    work = out[GROUP]
    for j, item in enumerate(held):
        work[j] = item
    for ref, at in zip(out, partners()):
        ref[...] = work[at].astype(BF16)


def pair_kernel(total, below, whole, _image, _upto, out):
    state = unpack(total[...].astype(F32)) + times(two_parts(whole[...]), two_parts(unpack(below[...].astype(F32))))
    out[...] = pack(state).astype(BF16)


def pair_total(total, below, whole, *ties):
    return call(
        pair_kernel, "pair_total", [IN_VMEM] * 3 + [IN_PLACE] * 2, shape(*total.shape), [], 0.5
    )(total, below, whole, *ties)


def entering_kernel(below, second, first, got, parts, upto, local, *out):
    high, low = two_parts(unpack(second[...].astype(F32)))
    state = unpack(below[...].astype(F32) + first[...].astype(F32)) + dot(got[...], high) + dot(got[...], low)
    sweep_plane(state, parts, upto, local, out)


def entering_from_kernel(base, parts, upto, local, *out):
    sweep_plane(unpack(base[...]), parts, upto, local, out)


def entering(body, args):
    half, columns = args[0].shape
    return call(
        body,
        "entering",
        [IN_VMEM] * len(args),
        [shape(half, columns)] * GROUP,
        [pltpu.VMEM((GROUP, half, columns), F32)],
        1.4,
    )(*args)


def waves_kernel(own, near, across, far, prop, image, out, arrived):
    collect((own, near, across, far), arrived)
    split = GROUP // prop.shape[0]
    for e in range(prop.shape[0]):
        near, far = arrived[e * split].astype(F32), arrived[e * split + 1].astype(F32)
        left = left_lanes(near)
        top = jnp.where(left, near, swap_lanes(far))
        low = jnp.where(left, swap_lanes(near), far)
        incoming = jnp.concatenate([top, low], axis=0).astype(BF16)
        out[e] = (dot(prop[e], incoming) + image[e]).astype(BF16)


def final_waves(arrived, prop, image):
    half, columns = arrived[0].shape
    return call(
        waves_kernel,
        "waves",
        [IN_VMEM] * (GROUP + 2),
        shape(*image.shape),
        [pltpu.VMEM((GROUP, half, columns), BF16)],
        1.3,
    )(*arrived, prop, image)


def to_near(item, sections):
    return lax.ppermute(item, "sec", [(s, s ^ 1) for s in range(sections)])


def to_across(item, sections):
    return lax.ppermute(item, "sec", [(s, s // GROUP * GROUP + (s % GROUP + CORES) % GROUP) for s in range(sections)])


def to_far(item, sections):
    return lax.ppermute(item, "sec", [(s, s // GROUP * GROUP + (s % GROUP + CORES) % GROUP ^ 1) for s in range(sections)])


def exchange(own, near, across, far, sections):
    across, far = to_across(across, sections), to_far(far, sections)
    return [own, to_near(near, sections), across, far]


def up_shift(sections, k):
    return [(s, s + GROUP * k) for s in range(sections - GROUP * k)]


def spread(packed):
    half = packed.shape[1] // 2
    return jnp.concatenate([packed[:, :half], packed[:, half:]], axis=0)


def between(item, *planes):
    pairs = [(p * GROUP + i, q * GROUP + i) for p, q in planes for i in range(GROUP)]
    return lax.ppermute(item, "sec", pairs)


def scan_below(total_map, total, sections):
    shift = lax.ppermute(spread(total).astype(F32), "sec", up_shift(sections, 1))
    joined = lax.ppermute(total_map, "sec", up_shift(sections, 1))
    stride = 1
    while stride < sections // GROUP:
        other = lax.ppermute(shift, "sec", up_shift(sections, stride))
        other_map = lax.ppermute(joined, "sec", up_shift(sections, stride))
        shift = shift + dot_wide(joined, other)
        joined = dot_wide(joined, other_map)
        stride *= 2
    half = shift.shape[0] // 2
    return jnp.concatenate([shift[:half], shift[half:]], axis=1)


def per_device(green, injected, coupling, pattern, owner, pair_blocks):
    sections = lax.axis_size("sec")
    green, inject = green[0], injected[0]

    coupling, tiles = coupling[0], pattern[0].T
    outgoing = outgoing_pairs(owner[:, 0], pair_blocks.T, green, inject, sections)
    received = lax.all_to_all(outgoing, "sec", split_axis=0, concat_axis=0, tiled=True)

    own_map, other_map, face_rows = face_maps(tiles, green, coupling)
    across = to_across(other_map, sections)
    near = to_near(own_map, sections)

    source, *quarters, across = placed_source(received, inject, face_rows, across)
    shifts = exchange(*quarters, sections)
    far = to_near(across, sections)
    four = sections // GROUP == 4
    whole, sent, parts = chain([own_map, near, across, far])
    got = between(sent, (2, 3)) if four else None
    total, local = plane_total(shifts, parts)
    early = image_and_maps(green, source, parts, total)
    if four:
        below = between(total, (0, 1))
        pair = pair_total(total, below, whole, *early)
        second, first = between(pair, (1, 3)), between(pair, (1, 2), (2, 3))
        image, upto = image_and_maps(green, source, parts, pair, early)
        entered = entering(entering_kernel, (below, second, first, got, parts, upto, local))
    else:
        base = scan_below(whole, total, sections)
        image, upto = image_and_maps(green, source, parts, base, early)
        entered = entering(entering_from_kernel, (base, parts, upto, local))
    arrived = exchange(*entered, sections)
    prop = propagator(tiles, green, coupling, entered[0])
    return final_waves(arrived, prop, image)[None]


def solution(mesh):
    in_specs = (
        P("sec", "grp", None, None),
        P("sec", "grp", None, None),
        P("sec", None, None),
        P("sec", None, None),
        P("sec", None),
        P("sec", None),
    )
    out_specs = P("sec", "grp", None, None)
    return jax.shard_map(
        per_device, mesh=mesh, in_specs=in_specs, out_specs=out_specs, check_vma=False
    )
```

```python
import functools

import jax
import jax.numpy as jnp
from jax import lax
from jax.experimental import pallas as pl
from jax.experimental.pallas import tpu as pltpu
from jax.sharding import PartitionSpec as P

BLK = 32
CAP = 2
GROUP = 4
HEAD = 8
CORES = 2

HIGH = lax.Precision.HIGHEST
F32 = jnp.float32
BF16 = jnp.bfloat16
VMEM_SMALL = 16 * 1024 * 1024
VMEM_WHOLE = 63400000
PEAK = 1.15e9

IN_VMEM = pl.BlockSpec(memory_space=pltpu.VMEM)
IN_SMEM = pl.BlockSpec(memory_space=pltpu.SMEM)
IN_HBM = pl.BlockSpec(memory_space=pltpu.HBM)
IN_PLACE = pl.BlockSpec(memory_space=pl.ANY)


def shape(*dims, dtype=BF16):
    return jax.ShapeDtypeStruct(dims, dtype)


def call(body, name, ins, outs, scratch, micros, vmem=VMEM_SMALL, aliases=None):
    places = list(range(len(outs))) if isinstance(outs, list) else 0
    return pl.pallas_call(
        body,
        name=name,
        in_specs=ins,
        out_shape=outs,
        out_specs=jax.tree.map(lambda k: IN_PLACE if k in (aliases or {}).values() else IN_VMEM, places),
        input_output_aliases=aliases or {},
        scratch_shapes=scratch,
        compiler_params=pltpu.CompilerParams(vmem_limit_bytes=vmem),
        cost_estimate=pl.CostEstimate(flops=int(micros * PEAK), bytes_accessed=0, transcendentals=0),
    )


def place():
    return lax.axis_index("sec") % GROUP


def partners():
    here = place()
    across = (here + CORES) % GROUP
    return here, here ^ 1, across, across ^ 1


def dot(a, b):
    return jnp.dot(a, b, preferred_element_type=F32)


def dot_wide(a, b):
    return jnp.dot(a, b, precision=HIGH, preferred_element_type=F32)


def two_parts(x):
    high = x.astype(BF16)
    return high, (x - high.astype(F32)).astype(BF16)


def left_lanes(x):
    return lax.broadcasted_iota(jnp.int32, x.shape, 1) < x.shape[1] // 2


def swap_lanes(x):
    return pltpu.roll(x, x.shape[1] // 2, 1)


def pack(tall):
    half = tall.shape[0] // 2
    top, low = tall[:half], tall[half:]
    return jnp.where(left_lanes(top), top, swap_lanes(low))


def unpack(packed):
    return jnp.concatenate([packed, swap_lanes(packed)], axis=0)


def mask_tiles(pattern, coupling):
    high, wide = coupling.shape[0] // pattern.shape[1], coupling.shape[1] // pattern.shape[0]
    for i in range(pattern.shape[1]):
        for j in range(pattern.shape[0]):
            at = (slice(i * high, (i + 1) * high), slice(j * wide, (j + 1) * wide))
            tile = coupling[at]
            coupling[at] = jnp.where(pattern[j, i] == 1, tile, jnp.zeros_like(tile))


def pairs_kernel(owner_in, blocks_in, green, inject_in, out, owner, blocks, inject, held, product, slot_of, counts, sem, side):
    energies, orbitals, _ = green.shape
    sections = out.shape[0]
    count = owner.shape[0]
    named = held.shape[1] < orbitals
    small = [
        pltpu.make_async_copy(src, dst, side.at[k])
        for k, (src, dst) in enumerate(((owner_in, owner), (blocks_in, blocks), (inject_in, inject)))
    ]
    for move in small:
        move.start()

    def copy_of(e, q):
        first = pl.multiple_of(blocks[0, q] * BLK, BLK)
        to = pl.multiple_of(q * BLK, BLK)
        return pltpu.make_async_copy(green.at[e, pl.ds(first, BLK)], held.at[e, pl.ds(to, BLK)], sem.at[e])

    def whole(e):
        return pltpu.make_async_copy(green.at[e], held.at[e], sem.at[e])

    if not named:
        for e in range(energies):
            whole(e).start()
    for move in small[:2]:
        move.wait()
    if named:
        for e in range(energies):
            lax.fori_loop(0, count, lambda q, _, e=e: copy_of(e, q).start(), None, unroll=4)
    rows = CAP * energies * BLK
    lane = lax.broadcasted_iota(jnp.int32, (HEAD, out.shape[2]), 1)
    none = jnp.where(lane < CAP, -1.0, 0.0).astype(BF16)

    def blank(d, _):
        counts[d] = 0
        out[d, :rows, :] = jnp.zeros((rows, out.shape[2]), BF16)
        out[d, rows : rows + HEAD, :] = none
        return 0

    lax.fori_loop(0, sections, blank, 0)

    def rank(q, _):
        d = owner[q]
        r = counts[d]
        counts[d] = r + 1
        slot_of[q] = r
        head = out[d, rows : rows + HEAD, :].astype(F32)
        head = jnp.where(lane == r, blocks[1, q].astype(F32), head)
        out[d, rows : rows + HEAD, :] = head.astype(BF16)
        return 0

    lax.fori_loop(0, count, rank, 0)
    small[2].wait()
    for e in range(energies):
        whole_held = pltpu.make_async_copy(green.at[e, pl.ds(0, held.shape[1])], held.at[e], sem.at[e])
        whole_held.wait()
        product[...] = dot(held[e], inject[e]).astype(BF16)

        def fill(q, _):
            first = pl.multiple_of((q if named else blocks[0, q]) * BLK, BLK)
            to = pl.multiple_of((slot_of[q] * energies + e) * BLK, BLK)
            out[owner[q], pl.ds(to, BLK), :] = product[pl.ds(first, BLK), :]
            return 0

        lax.fori_loop(0, count, fill, 0, unroll=4)


def outgoing_pairs(owner, blocks, green, inject, sections):
    energies, orbitals, _ = green.shape
    columns = inject.shape[2]
    rows = min(orbitals, owner.shape[0] * BLK)
    return call(
        pairs_kernel,
        "pairs",
        [IN_HBM] * 4,
        shape(sections, CAP * energies * BLK + HEAD, columns),
        [
            pltpu.SMEM(owner.shape, jnp.int32),
            pltpu.SMEM(blocks.shape, jnp.int32),
            pltpu.VMEM(inject.shape, BF16),
            pltpu.VMEM((energies, rows, orbitals), BF16),
            pltpu.VMEM((rows, columns), BF16),
            pltpu.SMEM(owner.shape, jnp.int32),
            pltpu.SMEM((sections,), jnp.int32),
            pltpu.SemaphoreType.DMA((energies,)),
            pltpu.SemaphoreType.DMA((3,)),
        ],
        4.0,
        VMEM_WHOLE,
    )(owner, blocks, green, inject)


def maps_kernel(pattern, green, coupling, own, other, face_rows, couple, maps):
    energies, orbitals, _ = green.shape
    face = coupling.shape[1]
    couple[...] = coupling[...]
    mask_tiles(pattern, couple)
    for e in range(energies):
        rows = green[e, orbitals - face :, :]
        face_rows[e] = rows
        maps[e] = dot(rows, couple[...])
    mine = place() // CORES
    own[...] = maps[mine]
    other[...] = maps[1 - mine]


def face_maps(pattern, green, coupling):
    orbitals, face = coupling.shape
    square = shape(face, face, dtype=F32)
    return call(
        maps_kernel,
        "face_maps",
        [IN_SMEM, IN_VMEM, IN_VMEM],
        [square, square, shape(green.shape[0], face, orbitals)],
        [pltpu.VMEM(coupling.shape, BF16), pltpu.VMEM((green.shape[0], face, face), F32)],
        1.2,
    )(pattern, green, coupling)


def prop_kernel(pattern, green, coupling, _tie, out, couple):
    couple[...] = coupling[...]
    mask_tiles(pattern, couple)
    for e in range(green.shape[0]):
        out[e] = dot(green[e], couple[...]).astype(BF16)


def propagator(pattern, green, coupling, tie):
    energies, orbitals, _ = green.shape
    return call(
        prop_kernel,
        "prop",
        [IN_SMEM, IN_VMEM, IN_VMEM, IN_PLACE],
        shape(energies, orbitals, coupling.shape[1]),
        [pltpu.VMEM(coupling.shape, BF16)],
        1.5,
    )(pattern, green, coupling, tie)


def times(a, b):
    return dot(a[0], b[0]) + (dot(a[0], b[1]) + dot(a[1], b[0]))


def chain_kernel(own, near, across, far, total_out, sent_out, parts, maps):
    collect((own, near, across, far), maps)
    split = [two_parts(maps[j]) for j in range(GROUP)]
    lower, upper = two_parts(times(split[1], split[0])), two_parts(times(split[3], split[2]))
    total = times(upper, lower)
    total_out[...] = total
    sent_out[...] = total.astype(BF16)
    for j, (high, low) in enumerate(split):
        parts[0, j] = high
        parts[1, j] = low


def chain(maps):
    face = maps[0].shape[0]
    return call(
        chain_kernel,
        "chain_maps",
        [IN_VMEM] * GROUP,
        [shape(face, face, dtype=F32), shape(face, face), shape(2, GROUP, face, face)],
        [pltpu.VMEM((GROUP, face, face), F32)],
        0.9,
    )(*maps)


def source_kernel(received, inject, face_rows, _map, source, own, near, across, far, _same_map, quarters, total, heads, targets, sem):
    energies, orbitals, columns = inject.shape
    sections = received.shape[0]
    half = quarters.shape[1]
    rows = CAP * energies * BLK

    def read(s, _):
        block = received[s, rows : rows + HEAD, :].astype(F32)
        heads[pl.ds(s, 1), :] = block[:1].astype(jnp.int32)
        return 0

    lax.fori_loop(0, sections, read, 0, unroll=min(sections, 8))
    fetch = pltpu.make_async_copy(heads, targets, sem)
    fetch.start()
    total[...] = inject[...].astype(F32)
    fetch.wait()

    def add(s, _):
        for r in range(CAP):
            first = pl.multiple_of(jnp.maximum(targets[s, r], 0) * BLK, BLK)
            for e in range(energies):
                item = received[s, (r * energies + e) * BLK : (r * energies + e + 1) * BLK, :]
                total[e, pl.ds(first, BLK), :] += item.astype(F32)
        return 0

    lax.fori_loop(0, sections, add, 0, unroll=2)
    split = GROUP // energies
    for e in range(energies):
        source[e] = total[e].astype(BF16)
        tall = dot(face_rows[e], source[e])
        quarters[e * split] = pack(tall)
        second = jnp.where(left_lanes(tall[:half]), swap_lanes(tall[:half]), tall[half:])
        quarters[e * split + 1] = second
    for out, at in zip((own, near, across, far), partners()):
        out[...] = quarters[at].astype(BF16)


def placed_source(received, inject, face_rows, passed):
    face = face_rows.shape[1]
    energies, orbitals, columns = inject.shape
    sections = received.shape[0]
    return call(
        source_kernel,
        "source_and_face",
        [IN_VMEM, IN_VMEM, IN_VMEM, IN_PLACE],
        [shape(*inject.shape)] + [shape(face // 2, columns)] * GROUP + [shape(*passed.shape, dtype=F32)],
        [
            pltpu.VMEM((GROUP, face // 2, columns), F32),
            pltpu.VMEM(inject.shape, F32),
            pltpu.VMEM((sections, columns), jnp.int32),
            pltpu.SMEM((sections, columns), jnp.int32),
            pltpu.SemaphoreType.DMA,
        ],
        1.4,
        aliases={3: 1 + GROUP},
    )(received, inject, face_rows, passed)


def collect(refs, held):
    for ref, at in zip(refs, partners()):
        held[at] = ref[...]


def step(parts, j, shift, state):
    return unpack(shift.astype(F32)) + times((parts[0, j], parts[1, j]), two_parts(state))


def total_kernel(own, near, across, far, parts, _image, out, local, shifts):
    collect((own, near, across, far), shifts)
    state = unpack(shifts[0].astype(F32))
    for j in range(1, GROUP):
        local[j - 1] = state
        state = step(parts, j, shifts[j], state)
    out[...] = pack(state).astype(BF16)


def plane_total(shifts, parts, tie):
    half, columns = shifts[0].shape
    return call(
        total_kernel,
        "plane_total",
        [IN_VMEM] * (GROUP + 1) + [IN_PLACE],
        [shape(half, columns), shape(GROUP - 1, 2 * half, columns, dtype=F32)],
        [pltpu.VMEM((GROUP, half, columns), BF16)],
        3.0,
    )(*shifts, parts, tie)


def work_kernel(early, *refs):
    green, source, parts = refs[:3]
    held, (image, upto) = refs[3:-2], refs[-2:]
    low_plane = lax.axis_index("sec") // GROUP == 0

    @pl.when(low_plane if early else jnp.logical_not(low_plane))
    def _():
        for e in range(green.shape[0]):
            image[e] = dot(green[e], source[e])
        maps = (parts[0, 0], parts[1, 0])
        for j in range(1, GROUP - 1):
            maps = two_parts(times((parts[0, j], parts[1, j]), maps))
            upto[0, j - 1], upto[1, j - 1] = maps

    if held:

        @pl.when(low_plane)
        def _():
            image[...] = held[0][...]
            upto[...] = held[1][...]


def image_and_maps(green, source, parts, held=()):
    _, _, face, _ = parts.shape
    return call(
        functools.partial(work_kernel, not held),
        "image_and_maps",
        [IN_VMEM] * (3 + len(held)),
        [shape(*source.shape, dtype=F32), shape(2, GROUP - 2, face, face)],
        [],
        2.0,
    )(green, source, parts, *held)


def sweep_plane(state, parts, upto, local, out):
    two = two_parts(state)
    held = [pack(state)]
    for j in range(1, GROUP):
        maps = (parts[0, 0], parts[1, 0]) if j == 1 else (upto[0, j - 2], upto[1, j - 2])
        held.append(pack(local[j - 1] + times(maps, two)))
    work = out[GROUP]
    for j, item in enumerate(held):
        work[j] = item
    for ref, at in zip(out, partners()):
        ref[...] = work[at].astype(BF16)


def entering_kernel(third, near_one, second, far_one, got, other, parts, upto, local, *out):
    first_core = place() % CORES == 0
    first = near_one[...].astype(F32) + far_one[...].astype(F32)
    state = unpack(third[...].astype(F32))
    for below, (one, two) in ((second[...].astype(F32), (other, got)), (first, (got, other))):
        factor = jnp.where(first_core, one[...], two[...])
        high, low = two_parts(state)
        state = unpack(below) + dot(factor, high) + dot(factor, low)
    sweep_plane(state, parts, upto, local, out)


def entering_from_kernel(base, parts, upto, local, *out):
    sweep_plane(unpack(base[...]), parts, upto, local, out)


def entering(body, args):
    half, columns = args[0].shape
    return call(
        body,
        "entering",
        [IN_VMEM] * len(args),
        [shape(half, columns)] * GROUP,
        [pltpu.VMEM((GROUP, half, columns), F32)],
        1.4,
    )(*args)


def waves_kernel(own, near, across, far, prop, image, out, arrived):
    collect((own, near, across, far), arrived)
    split = GROUP // prop.shape[0]
    for e in range(prop.shape[0]):
        near, far = arrived[e * split].astype(F32), arrived[e * split + 1].astype(F32)
        left = left_lanes(near)
        top = jnp.where(left, near, swap_lanes(far))
        low = jnp.where(left, swap_lanes(near), far)
        incoming = jnp.concatenate([top, low], axis=0).astype(BF16)
        out[e] = (dot(prop[e], incoming) + image[e]).astype(BF16)


def final_waves(arrived, prop, image):
    half, columns = arrived[0].shape
    return call(
        waves_kernel,
        "waves",
        [IN_VMEM] * (GROUP + 2),
        shape(*image.shape),
        [pltpu.VMEM((GROUP, half, columns), BF16)],
        1.3,
    )(*arrived, prop, image)


def to_near(item, sections):
    return lax.ppermute(item, "sec", [(s, s ^ 1) for s in range(sections)])


def to_across(item, sections):
    return lax.ppermute(item, "sec", [(s, s // GROUP * GROUP + (s % GROUP + CORES) % GROUP) for s in range(sections)])


def to_far(item, sections):
    return lax.ppermute(item, "sec", [(s, s // GROUP * GROUP + (s % GROUP + CORES) % GROUP ^ 1) for s in range(sections)])


def exchange(own, near, across, far, sections):
    across, far = to_across(across, sections), to_far(far, sections)
    return [own, to_near(near, sections), across, far]


def up_shift(sections, k):
    return [(s, s + GROUP * k) for s in range(sections - GROUP * k)]


def spread(packed):
    half = packed.shape[1] // 2
    return jnp.concatenate([packed[:, :half], packed[:, half:]], axis=0)


def maps_up(total_map, sections):
    pairs = []
    for i in range(GROUP):
        if i % CORES == 0:
            pairs += [(GROUP + i, 2 * GROUP + i), (2 * GROUP + i, 3 * GROUP + i)]
        else:
            pairs += [(GROUP + i, 3 * GROUP + i)]
    got = lax.ppermute(total_map, "sec", pairs)
    return got, to_near(got, sections)


def between(item, *planes):
    pairs = [(p * GROUP + i, q * GROUP + i) for p, q in planes for i in range(GROUP)]
    return lax.ppermute(item, "sec", pairs)


def scan_below(total_map, total, sections):
    shift = lax.ppermute(spread(total).astype(F32), "sec", up_shift(sections, 1))
    joined = lax.ppermute(total_map, "sec", up_shift(sections, 1))
    stride = 1
    while stride < sections // GROUP:
        other = lax.ppermute(shift, "sec", up_shift(sections, stride))
        other_map = lax.ppermute(joined, "sec", up_shift(sections, stride))
        shift = shift + dot_wide(joined, other)
        joined = dot_wide(joined, other_map)
        stride *= 2
    half = shift.shape[0] // 2
    return jnp.concatenate([shift[:half], shift[half:]], axis=1)


def per_device(green, injected, coupling, pattern, owner, pair_blocks):
    sections = lax.axis_size("sec")
    green, inject = green[0], injected[0]

    coupling, tiles = coupling[0], pattern[0].T
    outgoing = outgoing_pairs(owner[:, 0], pair_blocks.T, green, inject, sections)
    received = lax.all_to_all(outgoing, "sec", split_axis=0, concat_axis=0, tiled=True)

    own_map, other_map, face_rows = face_maps(tiles, green, coupling)
    across = to_across(other_map, sections)
    near = to_near(own_map, sections)

    source, *quarters, across = placed_source(received, inject, face_rows, across)
    shifts = exchange(*quarters, sections)
    far = to_near(across, sections)
    four = sections // GROUP == 4
    whole, sent, parts = chain([own_map, near, across, far])
    early = image_and_maps(green, source, parts)
    maps = maps_up(sent, sections) if four else []
    total, local = plane_total(shifts, parts, early[0])
    if four:
        fourth = between(total, (1, 2), (2, 3))
        third = between(total, (0, 2), (1, 3))
        second = between(total, (0, 1))
        first = between(total, (0, 3))
        image, upto = image_and_maps(green, source, parts, early)
        entered = entering(entering_kernel, (first, second, third, fourth, *maps, parts, upto, local))
    else:
        base = scan_below(whole, total, sections)
        image, upto = image_and_maps(green, source, parts, early)
        entered = entering(entering_from_kernel, (base, parts, upto, local))
    arrived = exchange(*entered, sections)
    prop = propagator(tiles, green, coupling, entered[0])
    return final_waves(arrived, prop, image)[None]


def solution(mesh):
    in_specs = (
        P("sec", "grp", None, None),
        P("sec", "grp", None, None),
        P("sec", None, None),
        P("sec", None, None),
        P("sec", None),
        P("sec", None),
    )
    out_specs = P("sec", "grp", None, None)
    return jax.shard_map(
        per_device, mesh=mesh, in_specs=in_specs, out_specs=out_specs, check_vma=False
    )
```

```python
import functools

import jax
import jax.numpy as jnp
from jax import lax
from jax.experimental import pallas as pl
from jax.experimental.pallas import tpu as pltpu
from jax.sharding import PartitionSpec as P

BLK = 32
CAP = 2
GROUP = 4
HEAD = 8
CORES = 2

HIGH = lax.Precision.HIGHEST
F32 = jnp.float32
BF16 = jnp.bfloat16
VMEM_SMALL = 16 * 1024 * 1024
VMEM_WHOLE = 63400000
PEAK = 1.15e9

IN_VMEM = pl.BlockSpec(memory_space=pltpu.VMEM)
IN_SMEM = pl.BlockSpec(memory_space=pltpu.SMEM)
IN_HBM = pl.BlockSpec(memory_space=pltpu.HBM)
IN_PLACE = pl.BlockSpec(memory_space=pl.ANY)


def shape(*dims, dtype=BF16):
    return jax.ShapeDtypeStruct(dims, dtype)


def call(body, name, ins, outs, scratch, micros, vmem=VMEM_SMALL, aliases=None):
    places = list(range(len(outs))) if isinstance(outs, list) else 0
    return pl.pallas_call(
        body,
        name=name,
        in_specs=ins,
        out_shape=outs,
        out_specs=jax.tree.map(lambda k: IN_PLACE if k in (aliases or {}).values() else IN_VMEM, places),
        input_output_aliases=aliases or {},
        scratch_shapes=scratch,
        compiler_params=pltpu.CompilerParams(vmem_limit_bytes=vmem),
        cost_estimate=pl.CostEstimate(flops=int(micros * PEAK), bytes_accessed=0, transcendentals=0),
    )


def place():
    return lax.axis_index("sec") % GROUP


def partners():
    here = place()
    across = (here + CORES) % GROUP
    return here, across ^ 1, across, here ^ 1


def dot(a, b):
    return jnp.dot(a, b, preferred_element_type=F32)


def dot_wide(a, b):
    return jnp.dot(a, b, precision=HIGH, preferred_element_type=F32)


def two_parts(x):
    high = x.astype(BF16)
    return high, (x - high.astype(F32)).astype(BF16)


def left_lanes(x):
    return lax.broadcasted_iota(jnp.int32, x.shape, 1) < x.shape[1] // 2


def swap_lanes(x):
    return pltpu.roll(x, x.shape[1] // 2, 1)


def pack(tall):
    half = tall.shape[0] // 2
    top, low = tall[:half], tall[half:]
    return jnp.where(left_lanes(top), top, swap_lanes(low))


def unpack(packed):
    return jnp.concatenate([packed, swap_lanes(packed)], axis=0)


def mask_tiles(pattern, coupling):
    high, wide = coupling.shape[0] // pattern.shape[1], coupling.shape[1] // pattern.shape[0]
    for i in range(pattern.shape[1]):
        for j in range(pattern.shape[0]):
            at = (slice(i * high, (i + 1) * high), slice(j * wide, (j + 1) * wide))
            tile = coupling[at]
            coupling[at] = jnp.where(pattern[j, i] == 1, tile, jnp.zeros_like(tile))


def pairs_kernel(owner_in, blocks_in, green, inject_in, out, owner, blocks, inject, held, product, slot_of, counts, sem, side):
    energies, orbitals, _ = green.shape
    sections = out.shape[0]
    count = owner.shape[0]
    named = held.shape[1] < orbitals
    small = [
        pltpu.make_async_copy(src, dst, side.at[k])
        for k, (src, dst) in enumerate(((owner_in, owner), (blocks_in, blocks), (inject_in, inject)))
    ]
    for move in small:
        move.start()

    def copy_of(e, q):
        first = pl.multiple_of(blocks[0, q] * BLK, BLK)
        to = pl.multiple_of(q * BLK, BLK)
        return pltpu.make_async_copy(green.at[e, pl.ds(first, BLK)], held.at[e, pl.ds(to, BLK)], sem.at[e])

    def whole(e):
        return pltpu.make_async_copy(green.at[e], held.at[e], sem.at[e])

    if not named:
        for e in range(energies):
            whole(e).start()
    for move in small[:2]:
        move.wait()
    if named:
        for e in range(energies):
            lax.fori_loop(0, count, lambda q, _, e=e: copy_of(e, q).start(), None, unroll=4)
    rows = CAP * energies * BLK
    lane = lax.broadcasted_iota(jnp.int32, (HEAD, out.shape[2]), 1)
    none = jnp.where(lane < CAP, -1.0, 0.0).astype(BF16)

    def blank(d, _):
        counts[d] = 0
        out[d, :rows, :] = jnp.zeros((rows, out.shape[2]), BF16)
        out[d, rows : rows + HEAD, :] = none
        return 0

    lax.fori_loop(0, sections, blank, 0)

    def rank(q, _):
        d = owner[q]
        r = counts[d]
        counts[d] = r + 1
        slot_of[q] = r
        head = out[d, rows : rows + HEAD, :].astype(F32)
        head = jnp.where(lane == r, blocks[1, q].astype(F32), head)
        out[d, rows : rows + HEAD, :] = head.astype(BF16)
        return 0

    lax.fori_loop(0, count, rank, 0)
    small[2].wait()
    for e in range(energies):
        whole_held = pltpu.make_async_copy(green.at[e, pl.ds(0, held.shape[1])], held.at[e], sem.at[e])
        whole_held.wait()
        product[...] = dot(held[e], inject[e]).astype(BF16)

        def fill(q, _):
            first = pl.multiple_of((q if named else blocks[0, q]) * BLK, BLK)
            to = pl.multiple_of((slot_of[q] * energies + e) * BLK, BLK)
            out[owner[q], pl.ds(to, BLK), :] = product[pl.ds(first, BLK), :]
            return 0

        lax.fori_loop(0, count, fill, 0, unroll=4)


def outgoing_pairs(owner, blocks, green, inject, sections):
    energies, orbitals, _ = green.shape
    columns = inject.shape[2]
    rows = min(orbitals, owner.shape[0] * BLK)
    return call(
        pairs_kernel,
        "pairs",
        [IN_HBM] * 4,
        shape(sections, CAP * energies * BLK + HEAD, columns),
        [
            pltpu.SMEM(owner.shape, jnp.int32),
            pltpu.SMEM(blocks.shape, jnp.int32),
            pltpu.VMEM(inject.shape, BF16),
            pltpu.VMEM((energies, rows, orbitals), BF16),
            pltpu.VMEM((rows, columns), BF16),
            pltpu.SMEM(owner.shape, jnp.int32),
            pltpu.SMEM((sections,), jnp.int32),
            pltpu.SemaphoreType.DMA((energies,)),
            pltpu.SemaphoreType.DMA((3,)),
        ],
        4.0,
        VMEM_WHOLE,
    )(owner, blocks, green, inject)


def maps_kernel(pattern, green, coupling, own, other, face_rows, couple, maps):
    energies, orbitals, _ = green.shape
    face = coupling.shape[1]
    couple[...] = coupling[...]
    mask_tiles(pattern, couple)
    for e in range(energies):
        rows = green[e, orbitals - face :, :]
        face_rows[e] = rows
        maps[e] = dot(rows, couple[...])
    mine = place() // CORES
    own[...] = maps[mine]
    other[...] = maps[1 - mine]


def face_maps(pattern, green, coupling):
    orbitals, face = coupling.shape
    square = shape(face, face, dtype=F32)
    return call(
        maps_kernel,
        "face_maps",
        [IN_SMEM, IN_VMEM, IN_VMEM],
        [square, square, shape(green.shape[0], face, orbitals)],
        [pltpu.VMEM(coupling.shape, BF16), pltpu.VMEM((green.shape[0], face, face), F32)],
        1.2,
    )(pattern, green, coupling)


def prop_kernel(pattern, green, coupling, _tie, out, couple):
    couple[...] = coupling[...]
    mask_tiles(pattern, couple)
    for e in range(green.shape[0]):
        out[e] = dot(green[e], couple[...]).astype(BF16)


def propagator(pattern, green, coupling, tie):
    energies, orbitals, _ = green.shape
    return call(
        prop_kernel,
        "prop",
        [IN_SMEM, IN_VMEM, IN_VMEM, IN_PLACE],
        shape(energies, orbitals, coupling.shape[1]),
        [pltpu.VMEM(coupling.shape, BF16)],
        1.5,
    )(pattern, green, coupling, tie)


def times(a, b):
    return dot(a[0], b[0]) + (dot(a[0], b[1]) + dot(a[1], b[0]))


def chain_kernel(own, far, across, near, total_out, parts, maps):
    collect((own, far, across, near), maps)
    split = [two_parts(maps[j]) for j in range(GROUP)]
    lower, upper = two_parts(times(split[1], split[0])), two_parts(times(split[3], split[2]))
    total_out[...] = times(upper, lower).astype(total_out.dtype)
    for j, (high, low) in enumerate(split):
        parts[0, j] = high
        parts[1, j] = low


def chain(maps, dtype):
    face = maps[0].shape[0]
    return call(
        chain_kernel,
        "chain_maps",
        [IN_VMEM] * GROUP,
        [shape(face, face, dtype=dtype), shape(2, GROUP, face, face)],
        [pltpu.VMEM((GROUP, face, face), F32)],
        0.9,
    )(*maps)


def source_kernel(received, inject, face_rows, _map, source, own, far, across, near, _same_map, quarters, total, heads, targets, sem):
    energies, orbitals, columns = inject.shape
    sections = received.shape[0]
    half = quarters.shape[1]
    rows = CAP * energies * BLK

    def read(s, _):
        block = received[s, rows : rows + HEAD, :].astype(F32)
        heads[pl.ds(s, 1), :] = block[:1].astype(jnp.int32)
        return 0

    lax.fori_loop(0, sections, read, 0, unroll=min(sections, 8))
    fetch = pltpu.make_async_copy(heads, targets, sem)
    fetch.start()
    total[...] = inject[...].astype(F32)
    fetch.wait()

    def add(s, _):
        for r in range(CAP):
            first = pl.multiple_of(jnp.maximum(targets[s, r], 0) * BLK, BLK)
            for e in range(energies):
                item = received[s, (r * energies + e) * BLK : (r * energies + e + 1) * BLK, :]
                total[e, pl.ds(first, BLK), :] += item.astype(F32)
        return 0

    lax.fori_loop(0, sections, add, 0, unroll=2)
    split = GROUP // energies
    for e in range(energies):
        source[e] = total[e].astype(BF16)
        tall = dot(face_rows[e], source[e])
        quarters[e * split] = pack(tall)
        second = jnp.where(left_lanes(tall[:half]), swap_lanes(tall[:half]), tall[half:])
        quarters[e * split + 1] = second
    for out, at in zip((own, far, across, near), partners()):
        out[...] = quarters[at].astype(BF16)


def placed_source(received, inject, face_rows, passed):
    face = face_rows.shape[1]
    energies, orbitals, columns = inject.shape
    sections = received.shape[0]
    return call(
        source_kernel,
        "source_and_face",
        [IN_VMEM, IN_VMEM, IN_VMEM, IN_PLACE],
        [shape(*inject.shape)] + [shape(face // 2, columns)] * GROUP + [shape(*passed.shape, dtype=F32)],
        [
            pltpu.VMEM((GROUP, face // 2, columns), F32),
            pltpu.VMEM(inject.shape, F32),
            pltpu.VMEM((sections, columns), jnp.int32),
            pltpu.SMEM((sections, columns), jnp.int32),
            pltpu.SemaphoreType.DMA,
        ],
        1.4,
        aliases={3: 1 + GROUP},
    )(received, inject, face_rows, passed)


def collect(refs, held):
    for ref, at in zip(refs, partners()):
        held[at] = ref[...]


def step(parts, j, shift, state):
    return unpack(shift.astype(F32)) + times((parts[0, j], parts[1, j]), two_parts(state))


def total_kernel(own, far, across, near, parts, _image, out, local, shifts):
    collect((own, far, across, near), shifts)
    state = unpack(shifts[0].astype(F32))
    for j in range(1, GROUP):
        local[j - 1] = state
        state = step(parts, j, shifts[j], state)
    out[...] = pack(state).astype(BF16)


def plane_total(shifts, parts, tie):
    half, columns = shifts[0].shape
    return call(
        total_kernel,
        "plane_total",
        [IN_VMEM] * (GROUP + 1) + [IN_PLACE],
        [shape(half, columns), shape(GROUP - 1, 2 * half, columns, dtype=F32)],
        [pltpu.VMEM((GROUP, half, columns), BF16)],
        3.0,
    )(*shifts, parts, tie)


def work_kernel(early, *refs):
    green, source, parts = refs[:3]
    held, (image, upto) = refs[3:-2], refs[-2:]
    low_plane = lax.axis_index("sec") // GROUP == 0

    @pl.when(low_plane if early else jnp.logical_not(low_plane))
    def _():
        for e in range(green.shape[0]):
            image[e] = dot(green[e], source[e])
        maps = (parts[0, 0], parts[1, 0])
        for j in range(1, GROUP - 1):
            maps = two_parts(times((parts[0, j], parts[1, j]), maps))
            upto[0, j - 1], upto[1, j - 1] = maps

    if held:

        @pl.when(low_plane)
        def _():
            image[...] = held[0][...]
            upto[...] = held[1][...]


def image_and_maps(green, source, parts, held=()):
    _, _, face, _ = parts.shape
    return call(
        functools.partial(work_kernel, not held),
        "image_and_maps",
        [IN_VMEM] * (3 + len(held)),
        [shape(*source.shape, dtype=F32), shape(2, GROUP - 2, face, face)],
        [],
        2.0,
    )(green, source, parts, *held)


def sweep_plane(state, parts, upto, local, out):
    two = two_parts(state)
    held = [pack(state)]
    for j in range(1, GROUP):
        maps = (parts[0, 0], parts[1, 0]) if j == 1 else (upto[0, j - 2], upto[1, j - 2])
        held.append(pack(local[j - 1] + times(maps, two)))
    work = out[GROUP]
    for j, item in enumerate(held):
        work[j] = item
    for ref, at in zip(out, partners()):
        ref[...] = work[at].astype(BF16)


def entering_kernel(third, near_one, second, far_one, got, other, parts, upto, local, *out):
    first_core = place() % CORES == 0
    first = near_one[...].astype(F32) + far_one[...].astype(F32)
    state = unpack(third[...].astype(F32))
    for below, (one, two) in ((second[...].astype(F32), (other, got)), (first, (got, other))):
        factor = jnp.where(first_core, one[...], two[...])
        high, low = two_parts(state)
        state = unpack(below) + dot(factor, high) + dot(factor, low)
    sweep_plane(state, parts, upto, local, out)


def entering_from_kernel(base, parts, upto, local, *out):
    sweep_plane(unpack(base[...]), parts, upto, local, out)


def entering(body, args):
    half, columns = args[0].shape
    return call(
        body,
        "entering",
        [IN_VMEM] * len(args),
        [shape(half, columns)] * GROUP,
        [pltpu.VMEM((GROUP, half, columns), F32)],
        1.4,
    )(*args)


def waves_kernel(own, far, across, near, prop, image, out, arrived, wave, sem):
    collect((own, far, across, near), arrived)
    energies, orbitals, _ = prop.shape
    split = GROUP // energies
    pieces = sem.shape[1]
    size = orbitals // pieces
    moves = []
    for e in range(energies):
        first, second = arrived[e * split].astype(F32), arrived[e * split + 1].astype(F32)
        left = left_lanes(first)
        top = jnp.where(left, first, swap_lanes(second))
        low = jnp.where(left, swap_lanes(first), second)
        incoming = jnp.concatenate([top, low], axis=0).astype(BF16)
        for c in range(pieces):
            at = slice(c * size, (c + 1) * size)
            wave[e, at, :] = (dot(prop[e, at, :], incoming) + image[e, at, :]).astype(BF16)
            moves.append(pltpu.make_async_copy(wave.at[e, pl.ds(c * size, size)], out.at[e, pl.ds(c * size, size)], sem.at[e, c]))
            moves[-1].start()
    for move in moves:
        move.wait()


def final_waves(arrived, prop, image):
    half, columns = arrived[0].shape
    energies = prop.shape[0]
    return pl.pallas_call(
        waves_kernel,
        name="waves",
        in_specs=[IN_VMEM] * (GROUP + 2),
        out_shape=shape(*image.shape),
        out_specs=IN_HBM,
        scratch_shapes=[
            pltpu.VMEM((GROUP, half, columns), BF16),
            pltpu.VMEM(image.shape, BF16),
            pltpu.SemaphoreType.DMA((energies, 2)),
        ],
        compiler_params=pltpu.CompilerParams(vmem_limit_bytes=VMEM_SMALL),
        cost_estimate=pl.CostEstimate(flops=int(1.3 * PEAK), bytes_accessed=0, transcendentals=0),
    )(*arrived, prop, image)


def to_near(item, sections):
    return lax.ppermute(item, "sec", [(s, s ^ 1) for s in range(sections)])


def to_across(item, sections):
    return lax.ppermute(item, "sec", [(s, s // GROUP * GROUP + (s % GROUP + CORES) % GROUP) for s in range(sections)])


def to_far(item, sections):
    return lax.ppermute(item, "sec", [(s, s // GROUP * GROUP + (s % GROUP + CORES) % GROUP ^ 1) for s in range(sections)])


def exchange(own, far, across, near, sections):
    return [own, to_far(far, sections), to_across(across, sections), to_near(near, sections)]


def up_shift(sections, k):
    return [(s, s + GROUP * k) for s in range(sections - GROUP * k)]


def spread(packed):
    half = packed.shape[1] // 2
    return jnp.concatenate([packed[:, :half], packed[:, half:]], axis=0)


def maps_up(total_map, sections):
    pairs = []
    for i in range(GROUP):
        if i % CORES == 0:
            pairs += [(GROUP + i, 2 * GROUP + i), (2 * GROUP + i, 3 * GROUP + i)]
        else:
            pairs += [(GROUP + i, 3 * GROUP + i)]
    got = lax.ppermute(total_map, "sec", pairs)
    return got, to_near(got, sections)


def between(item, *planes):
    pairs = [(p * GROUP + i, q * GROUP + i) for p, q in planes for i in range(GROUP)]
    return lax.ppermute(item, "sec", pairs)


def scan_below(total_map, total, sections):
    shift = lax.ppermute(spread(total).astype(F32), "sec", up_shift(sections, 1))
    joined = lax.ppermute(total_map, "sec", up_shift(sections, 1))
    stride = 1
    while stride < sections // GROUP:
        other = lax.ppermute(shift, "sec", up_shift(sections, stride))
        other_map = lax.ppermute(joined, "sec", up_shift(sections, stride))
        shift = shift + dot_wide(joined, other)
        joined = dot_wide(joined, other_map)
        stride *= 2
    half = shift.shape[0] // 2
    return jnp.concatenate([shift[:half], shift[half:]], axis=1)


def per_device(green, injected, coupling, pattern, owner, pair_blocks):
    sections = lax.axis_size("sec")
    green, inject = green[0], injected[0]

    coupling, tiles = coupling[0], pattern[0].T
    outgoing = outgoing_pairs(owner[:, 0], pair_blocks.T, green, inject, sections)
    received = lax.all_to_all(outgoing, "sec", split_axis=0, concat_axis=0, tiled=True)

    own_map, other_map, face_rows = face_maps(tiles, green, coupling)
    across = to_across(other_map, sections)
    near = to_near(own_map, sections)

    source, *quarters, across = placed_source(received, inject, face_rows, across)
    shifts = exchange(*quarters, sections)
    far = to_near(across, sections)
    four = sections // GROUP == 4
    total_map, parts = chain([own_map, far, across, near], BF16 if four else F32)
    early = image_and_maps(green, source, parts)
    maps = maps_up(total_map, sections) if four else []
    total, local = plane_total(shifts, parts, early[0])
    if four:
        fourth = between(total, (1, 2), (2, 3))
        third = between(total, (0, 2), (1, 3))
        second = between(total, (0, 1))
        first = between(total, (0, 3))
        image, upto = image_and_maps(green, source, parts, early)
        entered = entering(entering_kernel, (first, second, third, fourth, *maps, parts, upto, local))
    else:
        base = scan_below(total_map, total, sections)
        image, upto = image_and_maps(green, source, parts, early)
        entered = entering(entering_from_kernel, (base, parts, upto, local))
    arrived = exchange(*entered, sections)
    prop = propagator(tiles, green, coupling, entered[0])
    return final_waves(arrived, prop, image)[None]


def solution(mesh):
    in_specs = (
        P("sec", "grp", None, None),
        P("sec", "grp", None, None),
        P("sec", None, None),
        P("sec", None, None),
        P("sec", None),
        P("sec", None),
    )
    out_specs = P("sec", "grp", None, None)
    return jax.shard_map(
        per_device, mesh=mesh, in_specs=in_specs, out_specs=out_specs, check_vma=False
    )
```

```python
import functools

import jax
import jax.numpy as jnp
from jax import lax
from jax.experimental import pallas as pl
from jax.experimental.pallas import tpu as pltpu
from jax.sharding import PartitionSpec as P

BLK = 32
CAP = 2
GROUP = 4
HEAD = 8
CORES = 2

HIGH = lax.Precision.HIGHEST
F32 = jnp.float32
BF16 = jnp.bfloat16
VMEM_SMALL = 16 * 1024 * 1024
VMEM_WHOLE = 63400000
PEAK = 1.15e9

IN_VMEM = pl.BlockSpec(memory_space=pltpu.VMEM)
IN_SMEM = pl.BlockSpec(memory_space=pltpu.SMEM)
IN_HBM = pl.BlockSpec(memory_space=pltpu.HBM)
IN_PLACE = pl.BlockSpec(memory_space=pl.ANY)


def shape(*dims, dtype=BF16):
    return jax.ShapeDtypeStruct(dims, dtype)


def call(body, name, ins, outs, scratch, micros, vmem=VMEM_SMALL, aliases=None):
    places = list(range(len(outs))) if isinstance(outs, list) else 0
    return pl.pallas_call(
        body,
        name=name,
        in_specs=ins,
        out_shape=outs,
        out_specs=jax.tree.map(lambda k: IN_PLACE if k in (aliases or {}).values() else IN_VMEM, places),
        input_output_aliases=aliases or {},
        scratch_shapes=scratch,
        compiler_params=pltpu.CompilerParams(vmem_limit_bytes=vmem),
        cost_estimate=pl.CostEstimate(flops=int(micros * PEAK), bytes_accessed=0, transcendentals=0),
    )


def place():
    return lax.axis_index("sec") % GROUP


def partners():
    here = place()
    across = (here + CORES) % GROUP
    return here, across ^ 1, across, here ^ 1


def dot(a, b):
    return jnp.dot(a, b, preferred_element_type=F32)


def dot_wide(a, b):
    return jnp.dot(a, b, precision=HIGH, preferred_element_type=F32)


def two_parts(x):
    high = x.astype(BF16)
    return high, (x - high.astype(F32)).astype(BF16)


def left_lanes(x):
    return lax.broadcasted_iota(jnp.int32, x.shape, 1) < x.shape[1] // 2


def swap_lanes(x):
    return pltpu.roll(x, x.shape[1] // 2, 1)


def pack(tall):
    half = tall.shape[0] // 2
    top, low = tall[:half], tall[half:]
    return jnp.where(left_lanes(top), top, swap_lanes(low))


def unpack(packed):
    return jnp.concatenate([packed, swap_lanes(packed)], axis=0)


def mask_tiles(pattern, coupling):
    high, wide = coupling.shape[0] // pattern.shape[1], coupling.shape[1] // pattern.shape[0]
    for i in range(pattern.shape[1]):
        for j in range(pattern.shape[0]):
            at = (slice(i * high, (i + 1) * high), slice(j * wide, (j + 1) * wide))
            tile = coupling[at]
            coupling[at] = jnp.where(pattern[j, i] == 1, tile, jnp.zeros_like(tile))


def pairs_kernel(owner_in, blocks_in, green, inject_in, out, owner, blocks, inject, held, product, slot_of, counts, sem, side):
    energies, orbitals, _ = green.shape
    sections = out.shape[0]
    count = owner.shape[0]
    named = held.shape[1] < orbitals
    small = [
        pltpu.make_async_copy(src, dst, side.at[k])
        for k, (src, dst) in enumerate(((owner_in, owner), (blocks_in, blocks), (inject_in, inject)))
    ]
    for move in small:
        move.start()

    def copy_of(e, q):
        first = pl.multiple_of(blocks[0, q] * BLK, BLK)
        to = pl.multiple_of(q * BLK, BLK)
        return pltpu.make_async_copy(green.at[e, pl.ds(first, BLK)], held.at[e, pl.ds(to, BLK)], sem.at[e])

    def whole(e):
        return pltpu.make_async_copy(green.at[e], held.at[e], sem.at[e])

    if not named:
        for e in range(energies):
            whole(e).start()
    for move in small[:2]:
        move.wait()
    if named:
        for e in range(energies):
            lax.fori_loop(0, count, lambda q, _, e=e: copy_of(e, q).start(), None, unroll=4)
    rows = CAP * energies * BLK
    lane = lax.broadcasted_iota(jnp.int32, (HEAD, out.shape[2]), 1)
    none = jnp.where(lane < CAP, -1.0, 0.0).astype(BF16)

    def blank(d, _):
        counts[d] = 0
        out[d, :rows, :] = jnp.zeros((rows, out.shape[2]), BF16)
        out[d, rows : rows + HEAD, :] = none
        return 0

    lax.fori_loop(0, sections, blank, 0)

    def rank(q, _):
        d = owner[q]
        r = counts[d]
        counts[d] = r + 1
        slot_of[q] = r
        head = out[d, rows : rows + HEAD, :].astype(F32)
        head = jnp.where(lane == r, blocks[1, q].astype(F32), head)
        out[d, rows : rows + HEAD, :] = head.astype(BF16)
        return 0

    lax.fori_loop(0, count, rank, 0)
    small[2].wait()
    for e in range(energies):
        whole_held = pltpu.make_async_copy(green.at[e, pl.ds(0, held.shape[1])], held.at[e], sem.at[e])
        whole_held.wait()
        product[...] = dot(held[e], inject[e]).astype(BF16)

        def fill(q, _):
            first = pl.multiple_of((q if named else blocks[0, q]) * BLK, BLK)
            to = pl.multiple_of((slot_of[q] * energies + e) * BLK, BLK)
            out[owner[q], pl.ds(to, BLK), :] = product[pl.ds(first, BLK), :]
            return 0

        lax.fori_loop(0, count, fill, 0, unroll=4)


def outgoing_pairs(owner, blocks, green, inject, sections):
    energies, orbitals, _ = green.shape
    columns = inject.shape[2]
    rows = min(orbitals, owner.shape[0] * BLK)
    return call(
        pairs_kernel,
        "pairs",
        [IN_HBM] * 4,
        shape(sections, CAP * energies * BLK + HEAD, columns),
        [
            pltpu.SMEM(owner.shape, jnp.int32),
            pltpu.SMEM(blocks.shape, jnp.int32),
            pltpu.VMEM(inject.shape, BF16),
            pltpu.VMEM((energies, rows, orbitals), BF16),
            pltpu.VMEM((rows, columns), BF16),
            pltpu.SMEM(owner.shape, jnp.int32),
            pltpu.SMEM((sections,), jnp.int32),
            pltpu.SemaphoreType.DMA((energies,)),
            pltpu.SemaphoreType.DMA((3,)),
        ],
        4.0,
        VMEM_WHOLE,
    )(owner, blocks, green, inject)


def maps_kernel(pattern, green, coupling, own, other, face_rows, couple, maps):
    energies, orbitals, _ = green.shape
    face = coupling.shape[1]
    couple[...] = coupling[...]
    mask_tiles(pattern, couple)
    for e in range(energies):
        rows = green[e, orbitals - face :, :]
        face_rows[e] = rows
        maps[e] = dot(rows, couple[...])
    mine = place() // CORES
    own[...] = maps[mine]
    other[...] = maps[1 - mine]


def face_maps(pattern, green, coupling):
    orbitals, face = coupling.shape
    square = shape(face, face, dtype=F32)
    return call(
        maps_kernel,
        "face_maps",
        [IN_SMEM, IN_VMEM, IN_VMEM],
        [square, square, shape(green.shape[0], face, orbitals)],
        [pltpu.VMEM(coupling.shape, BF16), pltpu.VMEM((green.shape[0], face, face), F32)],
        1.2,
    )(pattern, green, coupling)


def prop_kernel(pattern, green, coupling, _tie, out, couple):
    couple[...] = coupling[...]
    mask_tiles(pattern, couple)
    for e in range(green.shape[0]):
        out[e] = dot(green[e], couple[...]).astype(BF16)


def propagator(pattern, green, coupling, tie):
    energies, orbitals, _ = green.shape
    return call(
        prop_kernel,
        "prop",
        [IN_SMEM, IN_VMEM, IN_VMEM, IN_PLACE],
        shape(energies, orbitals, coupling.shape[1]),
        [pltpu.VMEM(coupling.shape, BF16)],
        1.5,
    )(pattern, green, coupling, tie)


def times(a, b):
    return dot(a[0], b[0]) + (dot(a[0], b[1]) + dot(a[1], b[0]))


def chain_kernel(own, far, across, near, total_out, parts, maps):
    collect((own, far, across, near), maps)
    split = [two_parts(maps[j]) for j in range(GROUP)]
    lower, upper = two_parts(times(split[1], split[0])), two_parts(times(split[3], split[2]))
    total_out[...] = times(upper, lower).astype(total_out.dtype)
    for j, (high, low) in enumerate(split):
        parts[0, j] = high
        parts[1, j] = low


def chain(maps, dtype):
    face = maps[0].shape[0]
    return call(
        chain_kernel,
        "chain_maps",
        [IN_VMEM] * GROUP,
        [shape(face, face, dtype=dtype), shape(2, GROUP, face, face)],
        [pltpu.VMEM((GROUP, face, face), F32)],
        0.9,
    )(*maps)


def source_kernel(received, inject, face_rows, source, own, far, across, near, quarters, total, heads, targets, sem):
    energies, orbitals, columns = inject.shape
    sections = received.shape[0]
    half = quarters.shape[1]
    rows = CAP * energies * BLK

    def read(s, _):
        block = received[s, rows : rows + HEAD, :].astype(F32)
        heads[pl.ds(s, 1), :] = block[:1].astype(jnp.int32)
        return 0

    lax.fori_loop(0, sections, read, 0, unroll=min(sections, 8))
    fetch = pltpu.make_async_copy(heads, targets, sem)
    fetch.start()
    total[...] = inject[...].astype(F32)
    fetch.wait()

    def add(s, _):
        for r in range(CAP):
            first = pl.multiple_of(jnp.maximum(targets[s, r], 0) * BLK, BLK)
            for e in range(energies):
                item = received[s, (r * energies + e) * BLK : (r * energies + e + 1) * BLK, :]
                total[e, pl.ds(first, BLK), :] += item.astype(F32)
        return 0

    lax.fori_loop(0, sections, add, 0, unroll=2)
    split = GROUP // energies
    for e in range(energies):
        source[e] = total[e].astype(BF16)
        tall = dot(face_rows[e], source[e])
        quarters[e * split] = pack(tall)
        second = jnp.where(left_lanes(tall[:half]), swap_lanes(tall[:half]), tall[half:])
        quarters[e * split + 1] = second
    for out, at in zip((own, far, across, near), partners()):
        out[...] = quarters[at].astype(BF16)


def after_kernel(_packets, _map, _same_map):
    pass


def handed_on(item, packets):
    return call(
        after_kernel,
        "after_exchange",
        [IN_PLACE] * 2,
        [shape(*item.shape, dtype=item.dtype)],
        [],
        0.1,
        aliases={1: 0},
    )(packets, item)[0]


def placed_source(received, inject, face_rows):
    face = face_rows.shape[1]
    energies, orbitals, columns = inject.shape
    sections = received.shape[0]
    return call(
        source_kernel,
        "source_and_face",
        [IN_VMEM, IN_VMEM, IN_VMEM],
        [shape(*inject.shape)] + [shape(face // 2, columns)] * GROUP,
        [
            pltpu.VMEM((GROUP, face // 2, columns), F32),
            pltpu.VMEM(inject.shape, F32),
            pltpu.VMEM((sections, columns), jnp.int32),
            pltpu.SMEM((sections, columns), jnp.int32),
            pltpu.SemaphoreType.DMA,
        ],
        1.4,
    )(received, inject, face_rows)


def collect(refs, held):
    for ref, at in zip(refs, partners()):
        held[at] = ref[...]


def step(parts, j, shift, state):
    return unpack(shift.astype(F32)) + times((parts[0, j], parts[1, j]), two_parts(state))


def total_kernel(own, far, across, near, parts, _image, out, local, shifts):
    collect((own, far, across, near), shifts)
    state = unpack(shifts[0].astype(F32))
    for j in range(1, GROUP):
        local[j - 1] = state
        state = step(parts, j, shifts[j], state)
    out[...] = pack(state).astype(BF16)


def plane_total(shifts, parts, tie):
    half, columns = shifts[0].shape
    return call(
        total_kernel,
        "plane_total",
        [IN_VMEM] * (GROUP + 1) + [IN_PLACE],
        [shape(half, columns), shape(GROUP - 1, 2 * half, columns, dtype=F32)],
        [pltpu.VMEM((GROUP, half, columns), BF16)],
        3.0,
    )(*shifts, parts, tie)


def work_kernel(early, *refs):
    green, source, parts = refs[:3]
    held, (image, upto) = refs[3:-2], refs[-2:]
    low_plane = lax.axis_index("sec") // GROUP == 0

    @pl.when(low_plane if early else jnp.logical_not(low_plane))
    def _():
        for e in range(green.shape[0]):
            image[e] = dot(green[e], source[e])
        maps = (parts[0, 0], parts[1, 0])
        for j in range(1, GROUP - 1):
            maps = two_parts(times((parts[0, j], parts[1, j]), maps))
            upto[0, j - 1], upto[1, j - 1] = maps

    if held:

        @pl.when(low_plane)
        def _():
            image[...] = held[0][...]
            upto[...] = held[1][...]


def image_and_maps(green, source, parts, held=()):
    _, _, face, _ = parts.shape
    return call(
        functools.partial(work_kernel, not held),
        "image_and_maps",
        [IN_VMEM] * (3 + len(held)),
        [shape(*source.shape, dtype=F32), shape(2, GROUP - 2, face, face)],
        [],
        2.0,
    )(green, source, parts, *held)


def sweep_plane(state, parts, upto, local, out):
    two = two_parts(state)
    held = [pack(state)]
    for j in range(1, GROUP):
        maps = (parts[0, 0], parts[1, 0]) if j == 1 else (upto[0, j - 2], upto[1, j - 2])
        held.append(pack(local[j - 1] + times(maps, two)))
    work = out[GROUP]
    for j, item in enumerate(held):
        work[j] = item
    for ref, at in zip(out, partners()):
        ref[...] = work[at].astype(BF16)


def entering_kernel(third, near_one, second, far_one, got, other, parts, upto, local, *out):
    first_core = place() % CORES == 0
    first = near_one[...].astype(F32) + far_one[...].astype(F32)
    state = unpack(third[...].astype(F32))
    for below, (one, two) in ((second[...].astype(F32), (other, got)), (first, (got, other))):
        factor = jnp.where(first_core, one[...], two[...])
        high, low = two_parts(state)
        state = unpack(below) + dot(factor, high) + dot(factor, low)
    sweep_plane(state, parts, upto, local, out)


def entering_from_kernel(base, parts, upto, local, *out):
    sweep_plane(unpack(base[...]), parts, upto, local, out)


def entering(body, args):
    half, columns = args[0].shape
    return call(
        body,
        "entering",
        [IN_VMEM] * len(args),
        [shape(half, columns)] * GROUP,
        [pltpu.VMEM((GROUP, half, columns), F32)],
        1.4,
    )(*args)


def waves_kernel(own, far, across, near, prop, image, out, arrived, wave, sem):
    collect((own, far, across, near), arrived)
    energies, orbitals, _ = prop.shape
    split = GROUP // energies
    pieces = sem.shape[1]
    size = orbitals // pieces
    moves = []
    for e in range(energies):
        first, second = arrived[e * split].astype(F32), arrived[e * split + 1].astype(F32)
        left = left_lanes(first)
        top = jnp.where(left, first, swap_lanes(second))
        low = jnp.where(left, swap_lanes(first), second)
        incoming = jnp.concatenate([top, low], axis=0).astype(BF16)
        for c in range(pieces):
            at = slice(c * size, (c + 1) * size)
            wave[e, at, :] = (dot(prop[e, at, :], incoming) + image[e, at, :]).astype(BF16)
            moves.append(pltpu.make_async_copy(wave.at[e, pl.ds(c * size, size)], out.at[e, pl.ds(c * size, size)], sem.at[e, c]))
            moves[-1].start()
    for move in moves:
        move.wait()


def final_waves(arrived, prop, image):
    half, columns = arrived[0].shape
    energies = prop.shape[0]
    return pl.pallas_call(
        waves_kernel,
        name="waves",
        in_specs=[IN_VMEM] * (GROUP + 2),
        out_shape=shape(*image.shape),
        out_specs=IN_HBM,
        scratch_shapes=[
            pltpu.VMEM((GROUP, half, columns), BF16),
            pltpu.VMEM(image.shape, BF16),
            pltpu.SemaphoreType.DMA((energies, 2)),
        ],
        compiler_params=pltpu.CompilerParams(vmem_limit_bytes=VMEM_SMALL),
        cost_estimate=pl.CostEstimate(flops=int(1.3 * PEAK), bytes_accessed=0, transcendentals=0),
    )(*arrived, prop, image)


def to_near(item, sections):
    return lax.ppermute(item, "sec", [(s, s ^ 1) for s in range(sections)])


def to_across(item, sections):
    return lax.ppermute(item, "sec", [(s, s // GROUP * GROUP + (s % GROUP + CORES) % GROUP) for s in range(sections)])


def to_far(item, sections):
    return lax.ppermute(item, "sec", [(s, s // GROUP * GROUP + (s % GROUP + CORES) % GROUP ^ 1) for s in range(sections)])


def exchange(own, far, across, near, sections):
    return [own, to_far(far, sections), to_across(across, sections), to_near(near, sections)]


def up_shift(sections, k):
    return [(s, s + GROUP * k) for s in range(sections - GROUP * k)]


def spread(packed):
    half = packed.shape[1] // 2
    return jnp.concatenate([packed[:, :half], packed[:, half:]], axis=0)


def maps_up(total_map, sections):
    pairs = []
    for i in range(GROUP):
        if i % CORES == 0:
            pairs += [(GROUP + i, 2 * GROUP + i), (2 * GROUP + i, 3 * GROUP + i)]
        else:
            pairs += [(GROUP + i, 3 * GROUP + i)]
    got = lax.ppermute(total_map, "sec", pairs)
    return got, lax.ppermute(got, "sec", [(s, s ^ 1) for s in range(2 * GROUP, sections)])


def between(item, *planes):
    pairs = [(p * GROUP + i, q * GROUP + i) for p, q in planes for i in range(GROUP)]
    return lax.ppermute(item, "sec", pairs)


def scan_below(total_map, total, sections):
    shift = lax.ppermute(spread(total).astype(F32), "sec", up_shift(sections, 1))
    joined = lax.ppermute(total_map, "sec", up_shift(sections, 1))
    stride = 1
    while stride < sections // GROUP:
        other = lax.ppermute(shift, "sec", up_shift(sections, stride))
        other_map = lax.ppermute(joined, "sec", up_shift(sections, stride))
        shift = shift + dot_wide(joined, other)
        joined = dot_wide(joined, other_map)
        stride *= 2
    half = shift.shape[0] // 2
    return jnp.concatenate([shift[:half], shift[half:]], axis=1)


def per_device(green, injected, coupling, pattern, owner, pair_blocks):
    sections = lax.axis_size("sec")
    green, inject = green[0], injected[0]

    coupling, tiles = coupling[0], pattern[0].T
    outgoing = outgoing_pairs(owner[:, 0], pair_blocks.T, green, inject, sections)
    received = lax.all_to_all(outgoing, "sec", split_axis=0, concat_axis=0, tiled=True)

    own_map, other_map, face_rows = face_maps(tiles, green, coupling)
    across = to_across(other_map, sections)
    near = to_near(own_map, sections)

    across = handed_on(across, received)
    far = to_near(across, sections)
    source, *quarters = placed_source(received, inject, face_rows)
    shifts = exchange(*quarters, sections)
    four = sections // GROUP == 4
    total_map, parts = chain([own_map, far, across, near], BF16 if four else F32)
    early = image_and_maps(green, source, parts)
    maps = maps_up(total_map, sections) if four else []
    total, local = plane_total(shifts, parts, early[0])
    if four:
        fourth = between(total, (1, 2), (2, 3))
        third = between(total, (0, 2), (1, 3))
        second = between(total, (0, 1))
        first = between(total, (0, 3))
        image, upto = image_and_maps(green, source, parts, early)
        entered = entering(entering_kernel, (first, second, third, fourth, *maps, parts, upto, local))
    else:
        base = scan_below(total_map, total, sections)
        image, upto = image_and_maps(green, source, parts, early)
        entered = entering(entering_from_kernel, (base, parts, upto, local))
    arrived = exchange(*entered, sections)
    prop = propagator(tiles, green, coupling, entered[0])
    return final_waves(arrived, prop, image)[None]


def solution(mesh):
    in_specs = (
        P("sec", "grp", None, None),
        P("sec", "grp", None, None),
        P("sec", None, None),
        P("sec", None, None),
        P("sec", None),
        P("sec", None),
    )
    out_specs = P("sec", "grp", None, None)
    return jax.shard_map(
        per_device, mesh=mesh, in_specs=in_specs, out_specs=out_specs, check_vma=False
    )
```

```python
import functools

import jax
import jax.numpy as jnp
from jax import lax
from jax.experimental import pallas as pl
from jax.experimental.pallas import tpu as pltpu
from jax.sharding import PartitionSpec as P

BLK = 32
CAP = 2
GROUP = 4
HEAD = 8
CORES = 2

HIGH = lax.Precision.HIGHEST
F32 = jnp.float32
BF16 = jnp.bfloat16
VMEM_SMALL = 16 * 1024 * 1024
VMEM_WHOLE = 63400000
PEAK = 1.15e9

IN_VMEM = pl.BlockSpec(memory_space=pltpu.VMEM)
IN_SMEM = pl.BlockSpec(memory_space=pltpu.SMEM)
IN_HBM = pl.BlockSpec(memory_space=pltpu.HBM)
IN_PLACE = pl.BlockSpec(memory_space=pl.ANY)


def shape(*dims, dtype=BF16):
    return jax.ShapeDtypeStruct(dims, dtype)


def call(body, name, ins, outs, scratch, micros, vmem=VMEM_SMALL, aliases=None):
    places = list(range(len(outs))) if isinstance(outs, list) else 0
    return pl.pallas_call(
        body,
        name=name,
        in_specs=ins,
        out_shape=outs,
        out_specs=jax.tree.map(lambda k: IN_PLACE if k in (aliases or {}).values() else IN_VMEM, places),
        input_output_aliases=aliases or {},
        scratch_shapes=scratch,
        compiler_params=pltpu.CompilerParams(vmem_limit_bytes=vmem),
        cost_estimate=pl.CostEstimate(flops=int(micros * PEAK), bytes_accessed=0, transcendentals=0),
    )


def place():
    return lax.axis_index("sec") % GROUP


def partners():
    here = place()
    across = (here + CORES) % GROUP
    return here, across ^ 1, across, here ^ 1


def dot(a, b):
    return jnp.dot(a, b, preferred_element_type=F32)


def dot_wide(a, b):
    return jnp.dot(a, b, precision=HIGH, preferred_element_type=F32)


def two_parts(x):
    high = x.astype(BF16)
    return high, (x - high.astype(F32)).astype(BF16)


def left_lanes(x):
    return lax.broadcasted_iota(jnp.int32, x.shape, 1) < x.shape[1] // 2


def swap_lanes(x):
    return pltpu.roll(x, x.shape[1] // 2, 1)


def pack(tall):
    half = tall.shape[0] // 2
    top, low = tall[:half], tall[half:]
    return jnp.where(left_lanes(top), top, swap_lanes(low))


def unpack(packed):
    return jnp.concatenate([packed, swap_lanes(packed)], axis=0)


def mask_tiles(pattern, coupling):
    high, wide = coupling.shape[0] // pattern.shape[1], coupling.shape[1] // pattern.shape[0]
    for i in range(pattern.shape[1]):
        for j in range(pattern.shape[0]):
            at = (slice(i * high, (i + 1) * high), slice(j * wide, (j + 1) * wide))
            tile = coupling[at]
            coupling[at] = jnp.where(pattern[j, i] == 1, tile, jnp.zeros_like(tile))


def pairs_kernel(owner_in, blocks_in, green, inject_in, out, owner, blocks, inject, held, product, slot_of, counts, sem, side):
    energies, orbitals, _ = green.shape
    sections = out.shape[0]
    count = owner.shape[0]
    named = held.shape[1] < orbitals
    small = [
        pltpu.make_async_copy(src, dst, side.at[k])
        for k, (src, dst) in enumerate(((owner_in, owner), (blocks_in, blocks), (inject_in, inject)))
    ]
    for move in small:
        move.start()

    def copy_of(e, q):
        first = pl.multiple_of(blocks[0, q] * BLK, BLK)
        to = pl.multiple_of(q * BLK, BLK)
        return pltpu.make_async_copy(green.at[e, pl.ds(first, BLK)], held.at[e, pl.ds(to, BLK)], sem.at[e])

    def whole(e):
        return pltpu.make_async_copy(green.at[e], held.at[e], sem.at[e])

    if not named:
        for e in range(energies):
            whole(e).start()
    for move in small[:2]:
        move.wait()
    if named:
        for e in range(energies):
            lax.fori_loop(0, count, lambda q, _, e=e: copy_of(e, q).start(), None, unroll=4)
    rows = CAP * energies * BLK
    lane = lax.broadcasted_iota(jnp.int32, (HEAD, out.shape[2]), 1)
    none = jnp.where(lane < CAP, -1.0, 0.0).astype(BF16)

    def blank(d, _):
        counts[d] = 0
        out[d, :rows, :] = jnp.zeros((rows, out.shape[2]), BF16)
        out[d, rows : rows + HEAD, :] = none
        return 0

    lax.fori_loop(0, sections, blank, 0)

    def rank(q, _):
        d = owner[q]
        r = counts[d]
        counts[d] = r + 1
        slot_of[q] = r
        head = out[d, rows : rows + HEAD, :].astype(F32)
        head = jnp.where(lane == r, blocks[1, q].astype(F32), head)
        out[d, rows : rows + HEAD, :] = head.astype(BF16)
        return 0

    lax.fori_loop(0, count, rank, 0)
    small[2].wait()
    for e in range(energies):
        whole_held = pltpu.make_async_copy(green.at[e, pl.ds(0, held.shape[1])], held.at[e], sem.at[e])
        whole_held.wait()
        product[...] = dot(held[e], inject[e]).astype(BF16)

        def fill(q, _):
            first = pl.multiple_of((q if named else blocks[0, q]) * BLK, BLK)
            to = pl.multiple_of((slot_of[q] * energies + e) * BLK, BLK)
            out[owner[q], pl.ds(to, BLK), :] = product[pl.ds(first, BLK), :]
            return 0

        lax.fori_loop(0, count, fill, 0, unroll=4)


def outgoing_pairs(owner, blocks, green, inject, sections):
    energies, orbitals, _ = green.shape
    columns = inject.shape[2]
    rows = min(orbitals, owner.shape[0] * BLK)
    return call(
        pairs_kernel,
        "pairs",
        [IN_HBM] * 4,
        shape(sections, CAP * energies * BLK + HEAD, columns),
        [
            pltpu.SMEM(owner.shape, jnp.int32),
            pltpu.SMEM(blocks.shape, jnp.int32),
            pltpu.VMEM(inject.shape, BF16),
            pltpu.VMEM((energies, rows, orbitals), BF16),
            pltpu.VMEM((rows, columns), BF16),
            pltpu.SMEM(owner.shape, jnp.int32),
            pltpu.SMEM((sections,), jnp.int32),
            pltpu.SemaphoreType.DMA((energies,)),
            pltpu.SemaphoreType.DMA((3,)),
        ],
        4.0,
        VMEM_WHOLE,
    )(owner, blocks, green, inject)


def maps_kernel(pattern, green, coupling, own, other, face_rows, couple, maps):
    energies, orbitals, _ = green.shape
    face = coupling.shape[1]
    couple[...] = coupling[...]
    mask_tiles(pattern, couple)
    for e in range(energies):
        rows = green[e, orbitals - face :, :]
        face_rows[e] = rows
        maps[e] = dot(rows, couple[...])
    mine = place() // CORES
    own[...] = maps[mine]
    other[...] = maps[1 - mine]


def face_maps(pattern, green, coupling):
    orbitals, face = coupling.shape
    square = shape(face, face, dtype=F32)
    return call(
        maps_kernel,
        "face_maps",
        [IN_SMEM, IN_VMEM, IN_VMEM],
        [square, square, shape(green.shape[0], face, orbitals)],
        [pltpu.VMEM(coupling.shape, BF16), pltpu.VMEM((green.shape[0], face, face), F32)],
        1.2,
    )(pattern, green, coupling)


def prop_kernel(pattern, green, coupling, _tie, out, couple):
    couple[...] = coupling[...]
    mask_tiles(pattern, couple)
    for e in range(green.shape[0]):
        out[e] = dot(green[e], couple[...]).astype(BF16)


def propagator(pattern, green, coupling, tie):
    energies, orbitals, _ = green.shape
    return call(
        prop_kernel,
        "prop",
        [IN_SMEM, IN_VMEM, IN_VMEM, IN_PLACE],
        shape(energies, orbitals, coupling.shape[1]),
        [pltpu.VMEM(coupling.shape, BF16)],
        1.5,
    )(pattern, green, coupling, tie)


def times_maps(stack, high, low):
    face = high.shape[0]
    y = dot(stack, jnp.concatenate([high, low], axis=1))
    return y[:face, :face] + (y[:face, face:] + y[face:, :face])


def with_low(x):
    high = x.astype(BF16).astype(F32)
    return jnp.where(left_lanes(x), high, swap_lanes(x - high)).astype(BF16)


def from_stack(y):
    face = y.shape[0] // 2
    return y[:face] + (swap_lanes(y[:face]) + y[face:])


def stacked(high, low):
    return jnp.concatenate([high, low], axis=0)


def chain_kernel(own, far, across, near, total_out, parts, maps):
    collect((own, far, across, near), maps)
    split = [two_parts(maps[j]) for j in range(GROUP)]
    for j, two in enumerate(split):
        parts[j] = stacked(*two)
    lower, upper = two_parts(times_maps(parts[1], *split[0])), two_parts(times_maps(parts[3], *split[2]))
    total_out[...] = times_maps(stacked(*upper), *lower).astype(total_out.dtype)


def chain(maps, dtype):
    face = maps[0].shape[0]
    return call(
        chain_kernel,
        "chain_maps",
        [IN_VMEM] * GROUP,
        [shape(face, face, dtype=dtype), shape(GROUP, 2 * face, face)],
        [pltpu.VMEM((GROUP, face, face), F32)],
        0.9,
    )(*maps)


def source_kernel(received, inject, face_rows, source, own, far, across, near, quarters, heads, targets, sem, *totals):
    energies, orbitals, columns = inject.shape
    sections = received.shape[0]
    half = quarters.shape[1]
    rows = CAP * energies * BLK

    def read(s, _):
        block = received[s, rows : rows + HEAD, :].astype(F32)
        heads[pl.ds(s, 1), :] = block[:1].astype(jnp.int32)
        return 0

    lax.fori_loop(0, sections, read, 0, unroll=min(sections, 8))
    fetch = pltpu.make_async_copy(heads, targets, sem)
    fetch.start()
    for e, total in enumerate(totals):
        total[...] = inject[e].astype(F32)
    fetch.wait()

    def add(s, _):
        for r in range(CAP):
            first = pl.multiple_of(jnp.maximum(targets[s, r], 0) * BLK, BLK)
            for e, total in enumerate(totals):
                item = received[s, (r * energies + e) * BLK : (r * energies + e + 1) * BLK, :]
                total[pl.ds(first, BLK), :] += item.astype(F32)
        return 0

    lax.fori_loop(0, sections, add, 0, unroll=2)
    split = GROUP // energies
    for e in range(energies):
        source[e] = totals[e][...].astype(BF16)
        tall = dot(face_rows[e], source[e])
        quarters[e * split] = pack(tall)
        second = jnp.where(left_lanes(tall[:half]), swap_lanes(tall[:half]), tall[half:])
        quarters[e * split + 1] = second
    for out, at in zip((own, far, across, near), partners()):
        out[...] = quarters[at].astype(BF16)


def after_kernel(_packets, _map, _same_map):
    pass


def handed_on(item, packets):
    return call(
        after_kernel,
        "after_exchange",
        [IN_PLACE] * 2,
        [shape(*item.shape, dtype=item.dtype)],
        [],
        0.1,
        aliases={1: 0},
    )(packets, item)[0]


def placed_source(received, inject, face_rows):
    face = face_rows.shape[1]
    energies, orbitals, columns = inject.shape
    sections = received.shape[0]
    return call(
        source_kernel,
        "source_and_face",
        [IN_VMEM, IN_VMEM, IN_VMEM],
        [shape(*inject.shape)] + [shape(face // 2, columns)] * GROUP,
        [
            pltpu.VMEM((GROUP, face // 2, columns), F32),
            pltpu.VMEM((sections, columns), jnp.int32),
            pltpu.SMEM((sections, columns), jnp.int32),
            pltpu.SemaphoreType.DMA,
        ]
        + [pltpu.VMEM((orbitals, columns), F32)] * energies,
        1.4,
    )(received, inject, face_rows)


def collect(refs, held):
    for ref, at in zip(refs, partners()):
        held[at] = ref[...]


def step(parts, j, shift, state):
    return unpack(shift.astype(F32)) + from_stack(dot(parts[j], with_low(state)))


def total_kernel(own, far, across, near, parts, _image, out, local, shifts):
    collect((own, far, across, near), shifts)
    state = unpack(shifts[0].astype(F32))
    for j in range(1, GROUP):
        local[j - 1] = state
        state = step(parts, j, shifts[j], state)
    out[...] = pack(state).astype(BF16)


def plane_total(shifts, parts, tie):
    half, columns = shifts[0].shape
    return call(
        total_kernel,
        "plane_total",
        [IN_VMEM] * (GROUP + 1) + [IN_PLACE],
        [shape(half, columns), shape(GROUP - 1, 2 * half, columns, dtype=F32)],
        [pltpu.VMEM((GROUP, half, columns), BF16)],
        3.0,
    )(*shifts, parts, tie)


def work_kernel(early, *refs):
    green, source, parts = refs[:3]
    held, (image, upto) = refs[3:-2], refs[-2:]
    low_plane = lax.axis_index("sec") // GROUP == 0

    @pl.when(low_plane if early else jnp.logical_not(low_plane))
    def _():
        for e in range(green.shape[0]):
            image[e] = dot(green[e], source[e])
        face = parts.shape[2]
        high, low = parts[0, :face, :], parts[0, face:, :]
        upto[: 2 * face, :] = parts[0]
        for j in range(1, GROUP - 1):
            high, low = two_parts(times_maps(parts[j], high, low))
            upto[2 * j * face : 2 * (j + 1) * face, :] = stacked(high, low)

    if held:

        @pl.when(low_plane)
        def _():
            image[...] = held[0][...]
            upto[...] = held[1][...]


def image_and_maps(green, source, parts, held=()):
    _, _, face = parts.shape
    return call(
        functools.partial(work_kernel, not held),
        "image_and_maps",
        [IN_VMEM] * (3 + len(held)),
        [shape(*source.shape, dtype=F32), shape((GROUP - 1) * 2 * face, face)],
        [],
        2.0,
    )(green, source, parts, *held)


def sweep_plane(state, upto, local, out):
    y = dot(upto[...], with_low(state))
    size = 2 * state.shape[0]
    held = [pack(state)]
    for j in range(GROUP - 1):
        held.append(pack(local[j] + from_stack(y[j * size : (j + 1) * size])))
    work = out[GROUP]
    for j, item in enumerate(held):
        work[j] = item
    for ref, at in zip(out, partners()):
        ref[...] = work[at].astype(BF16)


def entering_kernel(third, near_one, second, far_one, got, other, upto, local, *out):
    first_core = place() % CORES == 0
    first = near_one[...].astype(F32) + far_one[...].astype(F32)
    state = unpack(third[...].astype(F32))
    for below, (one, two) in ((second[...].astype(F32), (other, got)), (first, (got, other))):
        factor = jnp.where(first_core, one[...], two[...])
        y = dot(factor, with_low(state))
        state = unpack(below) + (y + swap_lanes(y))
    sweep_plane(state, upto, local, out)


def entering_from_kernel(base, upto, local, *out):
    sweep_plane(unpack(base[...]), upto, local, out)


def entering(body, args):
    half, columns = args[0].shape
    return call(
        body,
        "entering",
        [IN_VMEM] * len(args),
        [shape(half, columns)] * GROUP,
        [pltpu.VMEM((GROUP, half, columns), F32)],
        1.4,
    )(*args)


def waves_kernel(own, far, across, near, prop, image, out, arrived, wave, sem):
    collect((own, far, across, near), arrived)
    energies, orbitals, _ = prop.shape
    split = GROUP // energies
    pieces = sem.shape[1]
    size = orbitals // pieces
    moves = []
    for e in range(energies):
        first, second = arrived[e * split].astype(F32), arrived[e * split + 1].astype(F32)
        left = left_lanes(first)
        top = jnp.where(left, first, swap_lanes(second))
        low = jnp.where(left, swap_lanes(first), second)
        incoming = jnp.concatenate([top, low], axis=0).astype(BF16)
        for c in range(pieces):
            at = slice(c * size, (c + 1) * size)
            wave[e, at, :] = (dot(prop[e, at, :], incoming) + image[e, at, :]).astype(BF16)
            moves.append(pltpu.make_async_copy(wave.at[e, pl.ds(c * size, size)], out.at[e, pl.ds(c * size, size)], sem.at[e, c]))
            moves[-1].start()
    for move in moves:
        move.wait()


def final_waves(arrived, prop, image):
    half, columns = arrived[0].shape
    energies = prop.shape[0]
    return pl.pallas_call(
        waves_kernel,
        name="waves",
        in_specs=[IN_VMEM] * (GROUP + 2),
        out_shape=shape(*image.shape),
        out_specs=IN_HBM,
        scratch_shapes=[
            pltpu.VMEM((GROUP, half, columns), BF16),
            pltpu.VMEM(image.shape, BF16),
            pltpu.SemaphoreType.DMA((energies, 2)),
        ],
        compiler_params=pltpu.CompilerParams(vmem_limit_bytes=VMEM_SMALL),
        cost_estimate=pl.CostEstimate(flops=int(1.3 * PEAK), bytes_accessed=0, transcendentals=0),
    )(*arrived, prop, image)


def to_near(item, sections):
    return lax.ppermute(item, "sec", [(s, s ^ 1) for s in range(sections)])


def to_across(item, sections):
    return lax.ppermute(item, "sec", [(s, s // GROUP * GROUP + (s % GROUP + CORES) % GROUP) for s in range(sections)])


def to_far(item, sections):
    return lax.ppermute(item, "sec", [(s, s // GROUP * GROUP + (s % GROUP + CORES) % GROUP ^ 1) for s in range(sections)])


def exchange(own, far, across, near, sections):
    return [own, to_far(far, sections), to_across(across, sections), to_near(near, sections)]


def up_shift(sections, k):
    return [(s, s + GROUP * k) for s in range(sections - GROUP * k)]


def spread(packed):
    half = packed.shape[1] // 2
    return jnp.concatenate([packed[:, :half], packed[:, half:]], axis=0)


def maps_up(total_map, sections):
    pairs = []
    for i in range(GROUP):
        if i % CORES == 0:
            pairs += [(GROUP + i, 2 * GROUP + i), (2 * GROUP + i, 3 * GROUP + i)]
        else:
            pairs += [(GROUP + i, 3 * GROUP + i)]
    got = lax.ppermute(total_map, "sec", pairs)
    return got, lax.ppermute(got, "sec", [(s, s ^ 1) for s in range(2 * GROUP, sections)])


def between(item, *planes):
    pairs = [(p * GROUP + i, q * GROUP + i) for p, q in planes for i in range(GROUP)]
    return lax.ppermute(item, "sec", pairs)


def scan_below(total_map, total, sections):
    shift = lax.ppermute(spread(total).astype(F32), "sec", up_shift(sections, 1))
    joined = lax.ppermute(total_map, "sec", up_shift(sections, 1))
    stride = 1
    while stride < sections // GROUP:
        other = lax.ppermute(shift, "sec", up_shift(sections, stride))
        other_map = lax.ppermute(joined, "sec", up_shift(sections, stride))
        shift = shift + dot_wide(joined, other)
        joined = dot_wide(joined, other_map)
        stride *= 2
    half = shift.shape[0] // 2
    return jnp.concatenate([shift[:half], shift[half:]], axis=1)


def per_device(green, injected, coupling, pattern, owner, pair_blocks):
    sections = lax.axis_size("sec")
    green, inject = green[0], injected[0]

    coupling, tiles = coupling[0], pattern[0].T
    outgoing = outgoing_pairs(owner[:, 0], pair_blocks.T, green, inject, sections)
    received = lax.all_to_all(outgoing, "sec", split_axis=0, concat_axis=0, tiled=True)

    own_map, other_map, face_rows = face_maps(tiles, green, coupling)
    across = to_across(other_map, sections)
    near = to_near(own_map, sections)

    across = handed_on(across, received)
    far = to_near(across, sections)
    source, *quarters = placed_source(received, inject, face_rows)
    shifts = exchange(*quarters, sections)
    four = sections // GROUP == 4
    total_map, parts = chain([own_map, far, across, near], BF16 if four else F32)
    early = image_and_maps(green, source, parts)
    maps = maps_up(total_map, sections) if four else []
    total, local = plane_total(shifts, parts, early[0])
    if four:
        fourth = between(total, (1, 2), (2, 3))
        third = between(total, (0, 2), (1, 3))
        second = between(total, (0, 1))
        first = between(total, (0, 3))
        image, upto = image_and_maps(green, source, parts, early)
        entered = entering(entering_kernel, (first, second, third, fourth, *maps, upto, local))
    else:
        base = scan_below(total_map, total, sections)
        image, upto = image_and_maps(green, source, parts, early)
        entered = entering(entering_from_kernel, (base, upto, local))
    arrived = exchange(*entered, sections)
    prop = propagator(tiles, green, coupling, entered[0])
    return final_waves(arrived, prop, image)[None]


def solution(mesh):
    in_specs = (
        P("sec", "grp", None, None),
        P("sec", "grp", None, None),
        P("sec", None, None),
        P("sec", None, None),
        P("sec", None),
        P("sec", None),
    )
    out_specs = P("sec", "grp", None, None)
    return jax.shard_map(
        per_device, mesh=mesh, in_specs=in_specs, out_specs=out_specs, check_vma=False
    )
```

```python
import functools

import jax
import jax.numpy as jnp
from jax import lax
from jax.experimental import pallas as pl
from jax.experimental.pallas import tpu as pltpu
from jax.sharding import PartitionSpec as P

BLK = 32
CAP = 2
GROUP = 4
HEAD = 8
CORES = 2

HIGH = lax.Precision.HIGHEST
F32 = jnp.float32
BF16 = jnp.bfloat16
VMEM_SMALL = 16 * 1024 * 1024
VMEM_WHOLE = 63400000
PEAK = 1.15e9

IN_VMEM = pl.BlockSpec(memory_space=pltpu.VMEM)
IN_SMEM = pl.BlockSpec(memory_space=pltpu.SMEM)
IN_HBM = pl.BlockSpec(memory_space=pltpu.HBM)
IN_PLACE = pl.BlockSpec(memory_space=pl.ANY)


def shape(*dims, dtype=BF16):
    return jax.ShapeDtypeStruct(dims, dtype)


def call(body, name, ins, outs, scratch, micros, vmem=VMEM_SMALL, aliases=None):
    places = list(range(len(outs))) if isinstance(outs, list) else 0
    return pl.pallas_call(
        body,
        name=name,
        in_specs=ins,
        out_shape=outs,
        out_specs=jax.tree.map(lambda k: IN_PLACE if k in (aliases or {}).values() else IN_VMEM, places),
        input_output_aliases=aliases or {},
        scratch_shapes=scratch,
        compiler_params=pltpu.CompilerParams(vmem_limit_bytes=vmem),
        cost_estimate=pl.CostEstimate(flops=int(micros * PEAK), bytes_accessed=0, transcendentals=0),
    )


def place():
    return lax.axis_index("sec") % GROUP


def partners():
    here = place()
    across = (here + CORES) % GROUP
    return here, across ^ 1, across, here ^ 1


def dot(a, b):
    return jnp.dot(a, b, preferred_element_type=F32)


def dot_wide(a, b):
    return jnp.dot(a, b, precision=HIGH, preferred_element_type=F32)


def two_parts(x):
    high = x.astype(BF16)
    return high, (x - high.astype(F32)).astype(BF16)


def dot_rows(a, b):
    return lax.dot_general(a, b, (((1,), (1,)), ((), ())), preferred_element_type=F32)


def step_by(state, maps):
    high, low = two_parts(state)
    rows = state.shape[0]
    y = dot_rows(jnp.concatenate([high, low], axis=0), maps[0])
    return y[:rows] + (y[rows:] + dot_rows(high, maps[1]))


def mask_tiles(pattern, coupling):
    high, wide = coupling.shape[0] // pattern.shape[1], coupling.shape[1] // pattern.shape[0]
    for i in range(pattern.shape[1]):
        for j in range(pattern.shape[0]):
            at = (slice(i * high, (i + 1) * high), slice(j * wide, (j + 1) * wide))
            tile = coupling[at]
            coupling[at] = jnp.where(pattern[j, i] == 1, tile, jnp.zeros_like(tile))


def pairs_kernel(owner_in, blocks_in, green, inject_in, out, owner, blocks, inject, held, product, slot_of, counts, sem, side):
    energies, orbitals, _ = green.shape
    sections = out.shape[0]
    count = owner.shape[0]
    named = held.shape[1] < orbitals
    small = [
        pltpu.make_async_copy(src, dst, side.at[k])
        for k, (src, dst) in enumerate(((owner_in, owner), (blocks_in, blocks), (inject_in, inject)))
    ]
    for move in small:
        move.start()

    def copy_of(e, q):
        first = pl.multiple_of(blocks[0, q] * BLK, BLK)
        to = pl.multiple_of(q * BLK, BLK)
        return pltpu.make_async_copy(green.at[e, pl.ds(first, BLK)], held.at[e, pl.ds(to, BLK)], sem.at[e])

    def whole(e):
        return pltpu.make_async_copy(green.at[e], held.at[e], sem.at[e])

    if not named:
        for e in range(energies):
            whole(e).start()
    for move in small[:2]:
        move.wait()
    if named:
        for e in range(energies):
            lax.fori_loop(0, count, lambda q, _, e=e: copy_of(e, q).start(), None, unroll=4)
    rows = CAP * energies * BLK
    lane = lax.broadcasted_iota(jnp.int32, (HEAD, out.shape[2]), 1)
    none = jnp.where(lane < CAP, -1.0, 0.0).astype(BF16)

    def blank(d, _):
        counts[d] = 0
        out[d, :rows, :] = jnp.zeros((rows, out.shape[2]), BF16)
        out[d, rows : rows + HEAD, :] = none
        return 0

    lax.fori_loop(0, sections, blank, 0)

    def rank(q, _):
        d = owner[q]
        r = counts[d]
        counts[d] = r + 1
        slot_of[q] = r
        head = out[d, rows : rows + HEAD, :].astype(F32)
        head = jnp.where(lane == r, blocks[1, q].astype(F32), head)
        out[d, rows : rows + HEAD, :] = head.astype(BF16)
        return 0

    lax.fori_loop(0, count, rank, 0)
    small[2].wait()
    for e in range(energies):
        whole_held = pltpu.make_async_copy(green.at[e, pl.ds(0, held.shape[1])], held.at[e], sem.at[e])
        whole_held.wait()
        product[...] = dot(held[e], inject[e]).astype(BF16)

        def fill(q, _):
            first = pl.multiple_of((q if named else blocks[0, q]) * BLK, BLK)
            to = pl.multiple_of((slot_of[q] * energies + e) * BLK, BLK)
            out[owner[q], pl.ds(to, BLK), :] = product[pl.ds(first, BLK), :]
            return 0

        lax.fori_loop(0, count, fill, 0, unroll=4)


def outgoing_pairs(owner, blocks, green, inject, sections):
    energies, orbitals, _ = green.shape
    columns = inject.shape[2]
    rows = min(orbitals, owner.shape[0] * BLK)
    return call(
        pairs_kernel,
        "pairs",
        [IN_HBM] * 4,
        shape(sections, CAP * energies * BLK + HEAD, columns),
        [
            pltpu.SMEM(owner.shape, jnp.int32),
            pltpu.SMEM(blocks.shape, jnp.int32),
            pltpu.VMEM(inject.shape, BF16),
            pltpu.VMEM((energies, rows, orbitals), BF16),
            pltpu.VMEM((rows, columns), BF16),
            pltpu.SMEM(owner.shape, jnp.int32),
            pltpu.SMEM((sections,), jnp.int32),
            pltpu.SemaphoreType.DMA((energies,)),
            pltpu.SemaphoreType.DMA((3,)),
        ],
        4.0,
        VMEM_WHOLE,
    )(owner, blocks, green, inject)


def maps_kernel(pattern, green, coupling, own, other, face_rows, couple, maps):
    energies, orbitals, _ = green.shape
    face = coupling.shape[1]
    couple[...] = coupling[...]
    mask_tiles(pattern, couple)
    for e in range(energies):
        rows = green[e, orbitals - face :, :]
        face_rows[e] = rows
        maps[e] = dot(rows, couple[...])
    mine = place() // CORES
    own[...] = maps[mine]
    other[...] = maps[1 - mine]


def face_maps(pattern, green, coupling):
    orbitals, face = coupling.shape
    square = shape(face, face, dtype=F32)
    return call(
        maps_kernel,
        "face_maps",
        [IN_SMEM, IN_VMEM, IN_VMEM],
        [square, square, shape(green.shape[0], face, orbitals)],
        [pltpu.VMEM(coupling.shape, BF16), pltpu.VMEM((green.shape[0], face, face), F32)],
        1.2,
    )(pattern, green, coupling)


def prop_kernel(pattern, green, coupling, _tie, out, couple):
    couple[...] = coupling[...]
    mask_tiles(pattern, couple)
    for e in range(green.shape[0]):
        out[e] = dot(green[e], couple[...]).astype(BF16)


def propagator(pattern, green, coupling, tie):
    energies, orbitals, _ = green.shape
    return call(
        prop_kernel,
        "prop",
        [IN_SMEM, IN_VMEM, IN_VMEM, IN_PLACE],
        shape(energies, orbitals, coupling.shape[1]),
        [pltpu.VMEM(coupling.shape, BF16)],
        1.5,
    )(pattern, green, coupling, tie)


def times(a, b):
    return dot(a[0], b[0]) + (dot(a[0], b[1]) + dot(a[1], b[0]))


def chain_kernel(own, far, across, near, total_out, parts, maps):
    collect((own, far, across, near), maps)
    split = [two_parts(maps[j]) for j in range(GROUP)]
    lower, upper = two_parts(times(split[1], split[0])), two_parts(times(split[3], split[2]))
    total_out[...] = times(upper, lower).astype(total_out.dtype)
    for j, (high, low) in enumerate(split):
        parts[0, j] = high
        parts[1, j] = low


def chain(maps, dtype):
    face = maps[0].shape[0]
    return call(
        chain_kernel,
        "chain_maps",
        [IN_VMEM] * GROUP,
        [shape(face, face, dtype=dtype), shape(2, GROUP, face, face)],
        [pltpu.VMEM((GROUP, face, face), F32)],
        0.9,
    )(*maps)


def source_kernel(received, inject, face_rows, source, own, far, across, near, quarters, total, heads, targets, sem):
    energies, orbitals, columns = inject.shape
    sections = received.shape[0]
    wide_rows = quarters.shape[1]
    rows = CAP * energies * BLK

    def read(s, _):
        block = received[s, rows : rows + HEAD, :].astype(F32)
        heads[pl.ds(s, 1), :] = block[:1].astype(jnp.int32)
        return 0

    lax.fori_loop(0, sections, read, 0, unroll=min(sections, 8))
    fetch = pltpu.make_async_copy(heads, targets, sem)
    fetch.start()
    total[...] = inject[...].astype(F32)
    fetch.wait()

    def add(s, _):
        for r in range(CAP):
            first = pl.multiple_of(jnp.maximum(targets[s, r], 0) * BLK, BLK)
            for e in range(energies):
                item = received[s, (r * energies + e) * BLK : (r * energies + e + 1) * BLK, :]
                total[e, pl.ds(first, BLK), :] += item.astype(F32)
        return 0

    lax.fori_loop(0, sections, add, 0, unroll=2)
    split = GROUP // energies
    for e in range(energies):
        source[e] = total[e].astype(BF16)
        tall = dot(face_rows[e], source[e])
        wide = tall.T
        for h in range(split):
            quarters[e * split + h] = wide[h * wide_rows : (h + 1) * wide_rows]
    for out, at in zip((own, far, across, near), partners()):
        out[...] = quarters[at].astype(BF16)


def after_kernel(_packets, _map, _same_map):
    pass


def handed_on(item, packets):
    return call(
        after_kernel,
        "after_exchange",
        [IN_PLACE] * 2,
        [shape(*item.shape, dtype=item.dtype)],
        [],
        0.1,
        aliases={1: 0},
    )(packets, item)[0]


def placed_source(received, inject, face_rows):
    face = face_rows.shape[1]
    energies, orbitals, columns = inject.shape
    sections = received.shape[0]
    return call(
        source_kernel,
        "source_and_face",
        [IN_VMEM, IN_VMEM, IN_VMEM],
        [shape(*inject.shape)] + [shape(columns * energies // GROUP, face)] * GROUP,
        [
            pltpu.VMEM((GROUP, columns * energies // GROUP, face), F32),
            pltpu.VMEM(inject.shape, F32),
            pltpu.VMEM((sections, columns), jnp.int32),
            pltpu.SMEM((sections, columns), jnp.int32),
            pltpu.SemaphoreType.DMA,
        ],
        1.4,
    )(received, inject, face_rows)


def collect(refs, held):
    for ref, at in zip(refs, partners()):
        held[at] = ref[...]


def total_kernel(own, far, across, near, parts, _image, out, local, shifts):
    collect((own, far, across, near), shifts)
    state = shifts[0].astype(F32)
    for j in range(1, GROUP):
        local[j - 1] = state
        state = shifts[j].astype(F32) + step_by(state, (parts[0, j], parts[1, j]))
    out[...] = state.astype(BF16)


def plane_total(shifts, parts, tie):
    rows, face = shifts[0].shape
    return call(
        total_kernel,
        "plane_total",
        [IN_VMEM] * (GROUP + 1) + [IN_PLACE],
        [shape(rows, face), shape(GROUP - 1, rows, face, dtype=F32)],
        [pltpu.VMEM((GROUP, rows, face), BF16)],
        3.0,
    )(*shifts, parts, tie)


def work_kernel(early, *refs):
    green, source, parts = refs[:3]
    held, (image, upto) = refs[3:-2], refs[-2:]
    low_plane = lax.axis_index("sec") // GROUP == 0

    @pl.when(low_plane if early else jnp.logical_not(low_plane))
    def _():
        for e in range(green.shape[0]):
            image[e] = dot(green[e], source[e])
        maps = (parts[0, 0], parts[1, 0])
        for j in range(1, GROUP - 1):
            maps = two_parts(times((parts[0, j], parts[1, j]), maps))
            upto[0, j - 1], upto[1, j - 1] = maps

    if held:

        @pl.when(low_plane)
        def _():
            image[...] = held[0][...]
            upto[...] = held[1][...]


def image_and_maps(green, source, parts, held=()):
    _, _, face, _ = parts.shape
    return call(
        functools.partial(work_kernel, not held),
        "image_and_maps",
        [IN_VMEM] * (3 + len(held)),
        [shape(*source.shape, dtype=F32), shape(2, GROUP - 2, face, face)],
        [],
        2.0,
    )(green, source, parts, *held)


def sweep_plane(state, parts, upto, local, out):
    held = [state]
    for j in range(1, GROUP):
        maps = (parts[0, 0], parts[1, 0]) if j == 1 else (upto[0, j - 2], upto[1, j - 2])
        held.append(local[j - 1] + step_by(state, maps))
    work = out[GROUP]
    for j, item in enumerate(held):
        work[j] = item
    for ref, at in zip(out, partners()):
        ref[...] = work[at].astype(BF16)


def entering_kernel(third, near_one, second, far_one, got, other, parts, upto, local, *out):
    first_core = place() % CORES == 0
    first = near_one[...].astype(F32) + far_one[...].astype(F32)
    state = third[...].astype(F32)
    rows = state.shape[0]
    for below, (one, two) in ((second[...].astype(F32), (other, got)), (first, (got, other))):
        factor = jnp.where(first_core, one[...], two[...])
        y = dot_rows(jnp.concatenate(two_parts(state), axis=0), factor)
        state = below + (y[:rows] + y[rows:])
    sweep_plane(state, parts, upto, local, out)


def entering_from_kernel(base, parts, upto, local, *out):
    sweep_plane(base[...], parts, upto, local, out)


def entering(body, args):
    half, columns = args[0].shape
    return call(
        body,
        "entering",
        [IN_VMEM] * len(args),
        [shape(half, columns)] * GROUP,
        [pltpu.VMEM((GROUP, half, columns), F32)],
        1.4,
    )(*args)


def waves_kernel(own, far, across, near, prop, image, out, arrived, wave, sem):
    collect((own, far, across, near), arrived)
    energies, orbitals, _ = prop.shape
    split = GROUP // energies
    pieces = sem.shape[1]
    size = orbitals // pieces
    moves = []
    for e in range(energies):
        incoming = jnp.concatenate([arrived[e * split + h] for h in range(split)], axis=0)
        for c in range(pieces):
            at = slice(c * size, (c + 1) * size)
            wave[e, at, :] = (dot_rows(prop[e, at, :], incoming) + image[e, at, :]).astype(BF16)
            moves.append(pltpu.make_async_copy(wave.at[e, pl.ds(c * size, size)], out.at[e, pl.ds(c * size, size)], sem.at[e, c]))
            moves[-1].start()
    for move in moves:
        move.wait()


def final_waves(arrived, prop, image):
    half, columns = arrived[0].shape
    energies = prop.shape[0]
    return pl.pallas_call(
        waves_kernel,
        name="waves",
        in_specs=[IN_VMEM] * (GROUP + 2),
        out_shape=shape(*image.shape),
        out_specs=IN_HBM,
        scratch_shapes=[
            pltpu.VMEM((GROUP, half, columns), BF16),
            pltpu.VMEM(image.shape, BF16),
            pltpu.SemaphoreType.DMA((energies, 2)),
        ],
        compiler_params=pltpu.CompilerParams(vmem_limit_bytes=VMEM_SMALL),
        cost_estimate=pl.CostEstimate(flops=int(1.3 * PEAK), bytes_accessed=0, transcendentals=0),
    )(*arrived, prop, image)


def to_near(item, sections):
    return lax.ppermute(item, "sec", [(s, s ^ 1) for s in range(sections)])


def to_across(item, sections):
    return lax.ppermute(item, "sec", [(s, s // GROUP * GROUP + (s % GROUP + CORES) % GROUP) for s in range(sections)])


def to_far(item, sections):
    return lax.ppermute(item, "sec", [(s, s // GROUP * GROUP + (s % GROUP + CORES) % GROUP ^ 1) for s in range(sections)])


def exchange(own, far, across, near, sections):
    return [own, to_far(far, sections), to_across(across, sections), to_near(near, sections)]


def up_shift(sections, k):
    return [(s, s + GROUP * k) for s in range(sections - GROUP * k)]


def maps_up(total_map, sections):
    pairs = []
    for i in range(GROUP):
        if i % CORES == 0:
            pairs += [(GROUP + i, 2 * GROUP + i), (2 * GROUP + i, 3 * GROUP + i)]
        else:
            pairs += [(GROUP + i, 3 * GROUP + i)]
    got = lax.ppermute(total_map, "sec", pairs)
    return got, lax.ppermute(got, "sec", [(s, s ^ 1) for s in range(2 * GROUP, sections)])


def between(item, *planes):
    pairs = [(p * GROUP + i, q * GROUP + i) for p, q in planes for i in range(GROUP)]
    return lax.ppermute(item, "sec", pairs)


def scan_below(total_map, total, sections):
    shift = lax.ppermute(total.astype(F32), "sec", up_shift(sections, 1))
    joined = lax.ppermute(total_map, "sec", up_shift(sections, 1))
    stride = 1
    while stride < sections // GROUP:
        other = lax.ppermute(shift, "sec", up_shift(sections, stride))
        other_map = lax.ppermute(joined, "sec", up_shift(sections, stride))
        shift = shift + dot_wide(other, joined.T)
        joined = dot_wide(joined, other_map)
        stride *= 2
    return shift


def per_device(green, injected, coupling, pattern, owner, pair_blocks):
    sections = lax.axis_size("sec")
    green, inject = green[0], injected[0]

    coupling, tiles = coupling[0], pattern[0].T
    outgoing = outgoing_pairs(owner[:, 0], pair_blocks.T, green, inject, sections)
    received = lax.all_to_all(outgoing, "sec", split_axis=0, concat_axis=0, tiled=True)

    own_map, other_map, face_rows = face_maps(tiles, green, coupling)
    across = to_across(other_map, sections)
    near = to_near(own_map, sections)

    across = handed_on(across, received)
    far = to_near(across, sections)
    source, *quarters = placed_source(received, inject, face_rows)
    shifts = exchange(*quarters, sections)
    four = sections // GROUP == 4
    total_map, parts = chain([own_map, far, across, near], BF16 if four else F32)
    early = image_and_maps(green, source, parts)
    maps = maps_up(total_map, sections) if four else []
    total, local = plane_total(shifts, parts, early[0])
    if four:
        fourth = between(total, (1, 2), (2, 3))
        third = between(total, (0, 2), (1, 3))
        second = between(total, (0, 1))
        first = between(total, (0, 3))
        image, upto = image_and_maps(green, source, parts, early)
        entered = entering(entering_kernel, (first, second, third, fourth, *maps, parts, upto, local))
    else:
        base = scan_below(total_map, total, sections)
        image, upto = image_and_maps(green, source, parts, early)
        entered = entering(entering_from_kernel, (base, parts, upto, local))
    arrived = exchange(*entered, sections)
    prop = propagator(tiles, green, coupling, entered[0])
    return final_waves(arrived, prop, image)[None]


def solution(mesh):
    in_specs = (
        P("sec", "grp", None, None),
        P("sec", "grp", None, None),
        P("sec", None, None),
        P("sec", None, None),
        P("sec", None),
        P("sec", None),
    )
    out_specs = P("sec", "grp", None, None)
    return jax.shard_map(
        per_device, mesh=mesh, in_specs=in_specs, out_specs=out_specs, check_vma=False
    )
```

```python
import functools

import jax
import jax.numpy as jnp
from jax import lax
from jax.experimental import pallas as pl
from jax.experimental.pallas import tpu as pltpu
from jax.sharding import PartitionSpec as P

BLK = 32
CAP = 2
GROUP = 4
HEAD = 8
CORES = 2

HIGH = lax.Precision.HIGHEST
F32 = jnp.float32
BF16 = jnp.bfloat16
VMEM_SMALL = 16 * 1024 * 1024
VMEM_WHOLE = 63400000
PEAK = 1.15e9

IN_VMEM = pl.BlockSpec(memory_space=pltpu.VMEM)
IN_SMEM = pl.BlockSpec(memory_space=pltpu.SMEM)
IN_HBM = pl.BlockSpec(memory_space=pltpu.HBM)
IN_PLACE = pl.BlockSpec(memory_space=pl.ANY)


def shape(*dims, dtype=BF16):
    return jax.ShapeDtypeStruct(dims, dtype)


def call(body, name, ins, outs, scratch, micros, vmem=VMEM_SMALL, aliases=None):
    places = list(range(len(outs))) if isinstance(outs, list) else 0
    return pl.pallas_call(
        body,
        name=name,
        in_specs=ins,
        out_shape=outs,
        out_specs=jax.tree.map(lambda k: IN_PLACE if k in (aliases or {}).values() else IN_VMEM, places),
        input_output_aliases=aliases or {},
        scratch_shapes=scratch,
        compiler_params=pltpu.CompilerParams(vmem_limit_bytes=vmem),
        cost_estimate=pl.CostEstimate(flops=int(micros * PEAK), bytes_accessed=0, transcendentals=0),
    )


def place():
    return lax.axis_index("sec") % GROUP


def partners():
    here = place()
    across = (here + CORES) % GROUP
    return here, across ^ 1, across, here ^ 1


def dot(a, b):
    return jnp.dot(a, b, preferred_element_type=F32)


def dot_wide(a, b):
    return jnp.dot(a, b, precision=HIGH, preferred_element_type=F32)


def two_parts(x):
    high = x.astype(BF16)
    return high, (x - high.astype(F32)).astype(BF16)


def dot_rows(a, b):
    return lax.dot_general(a, b, (((1,), (1,)), ((), ())), preferred_element_type=F32)


def step_by(state, maps):
    high, low = two_parts(state)
    rows = state.shape[0]
    y = dot_rows(jnp.concatenate([high, low], axis=0), maps[0])
    return y[:rows] + (y[rows:] + dot_rows(high, maps[1]))


def mask_tiles(pattern, coupling):
    high, wide = coupling.shape[0] // pattern.shape[1], coupling.shape[1] // pattern.shape[0]
    for i in range(pattern.shape[1]):
        for j in range(pattern.shape[0]):
            at = (slice(i * high, (i + 1) * high), slice(j * wide, (j + 1) * wide))
            tile = coupling[at]
            coupling[at] = jnp.where(pattern[j, i] == 1, tile, jnp.zeros_like(tile))


def pairs_kernel(owner_in, blocks_in, green, inject_in, out, owner, blocks, inject, held, product, slot_of, counts, sem, side):
    energies, orbitals, _ = green.shape
    sections = out.shape[0]
    count = owner.shape[0]
    named = held.shape[1] < orbitals
    small = [
        pltpu.make_async_copy(src, dst, side.at[k])
        for k, (src, dst) in enumerate(((owner_in, owner), (blocks_in, blocks), (inject_in, inject)))
    ]
    for move in small:
        move.start()

    def copy_of(e, q):
        first = pl.multiple_of(blocks[0, q] * BLK, BLK)
        to = pl.multiple_of(q * BLK, BLK)
        return pltpu.make_async_copy(green.at[e, pl.ds(first, BLK)], held.at[e, pl.ds(to, BLK)], sem.at[e])

    def whole(e):
        return pltpu.make_async_copy(green.at[e], held.at[e], sem.at[e])

    if not named:
        for e in range(energies):
            whole(e).start()
    for move in small[:2]:
        move.wait()
    if named:
        for e in range(energies):
            lax.fori_loop(0, count, lambda q, _, e=e: copy_of(e, q).start(), None, unroll=4)
    rows = CAP * energies * BLK
    lane = lax.broadcasted_iota(jnp.int32, (HEAD, out.shape[2]), 1)
    none = jnp.where(lane < CAP, -1.0, 0.0).astype(BF16)

    def blank(d, _):
        counts[d] = 0
        out[d, :rows, :] = jnp.zeros((rows, out.shape[2]), BF16)
        out[d, rows : rows + HEAD, :] = none
        return 0

    lax.fori_loop(0, sections, blank, 0)

    def rank(q, _):
        d = owner[q]
        r = counts[d]
        counts[d] = r + 1
        slot_of[q] = r
        head = out[d, rows : rows + HEAD, :].astype(F32)
        head = jnp.where(lane == r, blocks[1, q].astype(F32), head)
        out[d, rows : rows + HEAD, :] = head.astype(BF16)
        return 0

    lax.fori_loop(0, count, rank, 0)
    small[2].wait()
    for e in range(energies):
        whole_held = pltpu.make_async_copy(green.at[e, pl.ds(0, held.shape[1])], held.at[e], sem.at[e])
        whole_held.wait()
        product[...] = dot(held[e], inject[e]).astype(BF16)

        def fill(q, _):
            first = pl.multiple_of((q if named else blocks[0, q]) * BLK, BLK)
            to = pl.multiple_of((slot_of[q] * energies + e) * BLK, BLK)
            out[owner[q], pl.ds(to, BLK), :] = product[pl.ds(first, BLK), :]
            return 0

        lax.fori_loop(0, count, fill, 0, unroll=4)


def outgoing_pairs(owner, blocks, green, inject, sections):
    energies, orbitals, _ = green.shape
    columns = inject.shape[2]
    rows = min(orbitals, owner.shape[0] * BLK)
    return call(
        pairs_kernel,
        "pairs",
        [IN_HBM] * 4,
        shape(sections, CAP * energies * BLK + HEAD, columns),
        [
            pltpu.SMEM(owner.shape, jnp.int32),
            pltpu.SMEM(blocks.shape, jnp.int32),
            pltpu.VMEM(inject.shape, BF16),
            pltpu.VMEM((energies, rows, orbitals), BF16),
            pltpu.VMEM((rows, columns), BF16),
            pltpu.SMEM(owner.shape, jnp.int32),
            pltpu.SMEM((sections,), jnp.int32),
            pltpu.SemaphoreType.DMA((energies,)),
            pltpu.SemaphoreType.DMA((3,)),
        ],
        4.0,
        VMEM_WHOLE,
    )(owner, blocks, green, inject)


def maps_kernel(pattern_in, green, coupling_in, own, other, pattern, coupling, rows, maps, sem, side):
    energies, orbitals, _ = green.shape
    face = coupling.shape[1]
    tiles = pltpu.make_async_copy(pattern_in, pattern, side.at[0])
    whole = pltpu.make_async_copy(coupling_in, coupling, side.at[1])
    tiles.start()
    whole.start()
    moves = [
        pltpu.make_async_copy(green.at[e, pl.ds(orbitals - face, face)], rows.at[e], sem.at[e]) for e in range(energies)
    ]
    for move in moves:
        move.start()
    tiles.wait()
    whole.wait()
    mask_tiles(pattern, coupling)
    for e, move in enumerate(moves):
        move.wait()
        maps[e] = dot(rows[e], coupling[...])
    mine = place() // CORES
    own[...] = maps[mine]
    other[...] = maps[1 - mine]


def face_maps(pattern, green, coupling):
    energies, orbitals, _ = green.shape
    face = coupling.shape[1]
    square = shape(face, face, dtype=F32)
    return call(
        maps_kernel,
        "face_maps",
        [IN_HBM] * 3,
        [square, square],
        [
            pltpu.SMEM(pattern.shape, jnp.int32),
            pltpu.VMEM(coupling.shape, BF16),
            pltpu.VMEM((energies, face, orbitals), BF16),
            pltpu.VMEM((energies, face, face), F32),
            pltpu.SemaphoreType.DMA((energies,)),
            pltpu.SemaphoreType.DMA((2,)),
        ],
        2.0,
        VMEM_WHOLE,
    )(pattern, green, coupling)


def rows_kernel(green, _map, out):
    for e in range(green.shape[0]):
        out[e] = green[e, green.shape[1] - out.shape[1] :, :]


def face_rows_of(green, own_map):
    energies, _, orbitals = green.shape
    return call(
        rows_kernel, "face_rows", [IN_VMEM, IN_PLACE], shape(energies, own_map.shape[0], orbitals), [], 0.4
    )(green, own_map)


def prop_kernel(pattern, green, coupling, _tie, out, couple):
    couple[...] = coupling[...]
    mask_tiles(pattern, couple)
    for e in range(green.shape[0]):
        out[e] = dot(green[e], couple[...]).astype(BF16)


def propagator(pattern, green, coupling, tie):
    energies, orbitals, _ = green.shape
    return call(
        prop_kernel,
        "prop",
        [IN_SMEM, IN_VMEM, IN_VMEM, IN_PLACE],
        shape(energies, orbitals, coupling.shape[1]),
        [pltpu.VMEM(coupling.shape, BF16)],
        1.5,
    )(pattern, green, coupling, tie)


def times(a, b):
    return dot(a[0], b[0]) + (dot(a[0], b[1]) + dot(a[1], b[0]))


def chain_kernel(own, far, across, near, total_out, parts, maps):
    collect((own, far, across, near), maps)
    split = [two_parts(maps[j]) for j in range(GROUP)]
    lower, upper = two_parts(times(split[1], split[0])), two_parts(times(split[3], split[2]))
    total_out[...] = times(upper, lower).astype(total_out.dtype)
    for j, (high, low) in enumerate(split):
        parts[0, j] = high
        parts[1, j] = low


def chain(maps, dtype):
    face = maps[0].shape[0]
    return call(
        chain_kernel,
        "chain_maps",
        [IN_VMEM] * GROUP,
        [shape(face, face, dtype=dtype), shape(2, GROUP, face, face)],
        [pltpu.VMEM((GROUP, face, face), F32)],
        0.9,
    )(*maps)


def source_kernel(received, inject, face_rows, source, own, far, across, near, quarters, total, heads, targets, sem):
    energies, orbitals, columns = inject.shape
    sections = received.shape[0]
    wide_rows = quarters.shape[1]
    rows = CAP * energies * BLK

    def read(s, _):
        block = received[s, rows : rows + HEAD, :].astype(F32)
        heads[pl.ds(s, 1), :] = block[:1].astype(jnp.int32)
        return 0

    lax.fori_loop(0, sections, read, 0, unroll=min(sections, 8))
    fetch = pltpu.make_async_copy(heads, targets, sem)
    fetch.start()
    total[...] = inject[...].astype(F32)
    fetch.wait()

    def add(s, _):
        for r in range(CAP):
            first = pl.multiple_of(jnp.maximum(targets[s, r], 0) * BLK, BLK)
            for e in range(energies):
                item = received[s, (r * energies + e) * BLK : (r * energies + e + 1) * BLK, :]
                total[e, pl.ds(first, BLK), :] += item.astype(F32)
        return 0

    lax.fori_loop(0, sections, add, 0, unroll=2)
    split = GROUP // energies
    for e in range(energies):
        source[e] = total[e].astype(BF16)
        tall = dot(face_rows[e], source[e])
        wide = tall.T
        for h in range(split):
            quarters[e * split + h] = wide[h * wide_rows : (h + 1) * wide_rows]
    for out, at in zip((own, far, across, near), partners()):
        out[...] = quarters[at].astype(BF16)


def after_kernel(_packets, _map, _same_map):
    pass


def handed_on(item, packets):
    return call(
        after_kernel,
        "after_exchange",
        [IN_PLACE] * 2,
        [shape(*item.shape, dtype=item.dtype)],
        [],
        0.1,
        aliases={1: 0},
    )(packets, item)[0]


def placed_source(received, inject, face_rows):
    face = face_rows.shape[1]
    energies, orbitals, columns = inject.shape
    sections = received.shape[0]
    return call(
        source_kernel,
        "source_and_face",
        [IN_VMEM, IN_VMEM, IN_VMEM],
        [shape(*inject.shape)] + [shape(columns * energies // GROUP, face)] * GROUP,
        [
            pltpu.VMEM((GROUP, columns * energies // GROUP, face), F32),
            pltpu.VMEM(inject.shape, F32),
            pltpu.VMEM((sections, columns), jnp.int32),
            pltpu.SMEM((sections, columns), jnp.int32),
            pltpu.SemaphoreType.DMA,
        ],
        1.4,
    )(received, inject, face_rows)


def collect(refs, held):
    for ref, at in zip(refs, partners()):
        held[at] = ref[...]


def total_kernel(own, far, across, near, parts, _image, out, local, shifts):
    collect((own, far, across, near), shifts)
    state = shifts[0].astype(F32)
    for j in range(1, GROUP):
        local[j - 1] = state
        state = shifts[j].astype(F32) + step_by(state, (parts[0, j], parts[1, j]))
    out[...] = state.astype(BF16)


def plane_total(shifts, parts, tie):
    rows, face = shifts[0].shape
    return call(
        total_kernel,
        "plane_total",
        [IN_VMEM] * (GROUP + 1) + [IN_PLACE],
        [shape(rows, face), shape(GROUP - 1, rows, face, dtype=F32)],
        [pltpu.VMEM((GROUP, rows, face), BF16)],
        3.0,
    )(*shifts, parts, tie)


def work_kernel(early, *refs):
    green, source, parts = refs[:3]
    held, (image, upto) = refs[3:-2], refs[-2:]
    low_plane = lax.axis_index("sec") // GROUP == 0

    @pl.when(low_plane if early else jnp.logical_not(low_plane))
    def _():
        for e in range(green.shape[0]):
            image[e] = dot(green[e], source[e])
        maps = (parts[0, 0], parts[1, 0])
        for j in range(1, GROUP - 1):
            maps = two_parts(times((parts[0, j], parts[1, j]), maps))
            upto[0, j - 1], upto[1, j - 1] = maps

    if held:

        @pl.when(low_plane)
        def _():
            image[...] = held[0][...]
            upto[...] = held[1][...]


def image_and_maps(green, source, parts, held=()):
    _, _, face, _ = parts.shape
    return call(
        functools.partial(work_kernel, not held),
        "image_and_maps",
        [IN_VMEM] * (3 + len(held)),
        [shape(*source.shape, dtype=F32), shape(2, GROUP - 2, face, face)],
        [],
        2.0,
    )(green, source, parts, *held)


def sweep_plane(state, parts, upto, local, out):
    held = [state]
    for j in range(1, GROUP):
        maps = (parts[0, 0], parts[1, 0]) if j == 1 else (upto[0, j - 2], upto[1, j - 2])
        held.append(local[j - 1] + step_by(state, maps))
    work = out[GROUP]
    for j, item in enumerate(held):
        work[j] = item
    for ref, at in zip(out, partners()):
        ref[...] = work[at].astype(BF16)


def entering_kernel(third, near_one, second, far_one, got, other, parts, upto, local, *out):
    first_core = place() % CORES == 0
    first = near_one[...].astype(F32) + far_one[...].astype(F32)
    state = third[...].astype(F32)
    rows = state.shape[0]
    for below, (one, two) in ((second[...].astype(F32), (other, got)), (first, (got, other))):
        factor = jnp.where(first_core, one[...], two[...])
        y = dot_rows(jnp.concatenate(two_parts(state), axis=0), factor)
        state = below + (y[:rows] + y[rows:])
    sweep_plane(state, parts, upto, local, out)


def entering_from_kernel(base, parts, upto, local, *out):
    sweep_plane(base[...], parts, upto, local, out)


def entering(body, args):
    half, columns = args[0].shape
    return call(
        body,
        "entering",
        [IN_VMEM] * len(args),
        [shape(half, columns)] * GROUP,
        [pltpu.VMEM((GROUP, half, columns), F32)],
        1.4,
    )(*args)


def waves_kernel(own, far, across, near, prop, image, out, arrived, wave, sem):
    collect((own, far, across, near), arrived)
    energies, orbitals, _ = prop.shape
    split = GROUP // energies
    pieces = sem.shape[1]
    size = orbitals // pieces
    moves = []
    for e in range(energies):
        incoming = jnp.concatenate([arrived[e * split + h] for h in range(split)], axis=0)
        for c in range(pieces):
            at = slice(c * size, (c + 1) * size)
            wave[e, at, :] = (dot_rows(prop[e, at, :], incoming) + image[e, at, :]).astype(BF16)
            moves.append(pltpu.make_async_copy(wave.at[e, pl.ds(c * size, size)], out.at[e, pl.ds(c * size, size)], sem.at[e, c]))
            moves[-1].start()
    for move in moves:
        move.wait()


def final_waves(arrived, prop, image):
    half, columns = arrived[0].shape
    energies = prop.shape[0]
    return pl.pallas_call(
        waves_kernel,
        name="waves",
        in_specs=[IN_VMEM] * (GROUP + 2),
        out_shape=shape(*image.shape),
        out_specs=IN_HBM,
        scratch_shapes=[
            pltpu.VMEM((GROUP, half, columns), BF16),
            pltpu.VMEM(image.shape, BF16),
            pltpu.SemaphoreType.DMA((energies, 2)),
        ],
        compiler_params=pltpu.CompilerParams(vmem_limit_bytes=VMEM_SMALL),
        cost_estimate=pl.CostEstimate(flops=int(1.3 * PEAK), bytes_accessed=0, transcendentals=0),
    )(*arrived, prop, image)


def to_near(item, sections):
    return lax.ppermute(item, "sec", [(s, s ^ 1) for s in range(sections)])


def to_across(item, sections):
    return lax.ppermute(item, "sec", [(s, s // GROUP * GROUP + (s % GROUP + CORES) % GROUP) for s in range(sections)])


def to_far(item, sections):
    return lax.ppermute(item, "sec", [(s, s // GROUP * GROUP + (s % GROUP + CORES) % GROUP ^ 1) for s in range(sections)])


def exchange(own, far, across, near, sections):
    return [own, to_far(far, sections), to_across(across, sections), to_near(near, sections)]


def up_shift(sections, k):
    return [(s, s + GROUP * k) for s in range(sections - GROUP * k)]


def maps_up(total_map, sections):
    pairs = []
    for i in range(GROUP):
        if i % CORES == 0:
            pairs += [(GROUP + i, 2 * GROUP + i), (2 * GROUP + i, 3 * GROUP + i)]
        else:
            pairs += [(GROUP + i, 3 * GROUP + i)]
    got = lax.ppermute(total_map, "sec", pairs)
    return got, lax.ppermute(got, "sec", [(s, s ^ 1) for s in range(2 * GROUP, sections)])


def between(item, *planes):
    pairs = [(p * GROUP + i, q * GROUP + i) for p, q in planes for i in range(GROUP)]
    return lax.ppermute(item, "sec", pairs)


def scan_below(total_map, total, sections):
    shift = lax.ppermute(total.astype(F32), "sec", up_shift(sections, 1))
    joined = lax.ppermute(total_map, "sec", up_shift(sections, 1))
    stride = 1
    while stride < sections // GROUP:
        other = lax.ppermute(shift, "sec", up_shift(sections, stride))
        other_map = lax.ppermute(joined, "sec", up_shift(sections, stride))
        shift = shift + dot_wide(other, joined.T)
        joined = dot_wide(joined, other_map)
        stride *= 2
    return shift


def per_device(green, injected, coupling, pattern, owner, pair_blocks):
    sections = lax.axis_size("sec")
    green, inject = green[0], injected[0]

    coupling, tiles = coupling[0], pattern[0].T
    outgoing = outgoing_pairs(owner[:, 0], pair_blocks.T, green, inject, sections)
    received = lax.all_to_all(outgoing, "sec", split_axis=0, concat_axis=0, tiled=True)

    own_map, other_map = face_maps(tiles, green, coupling)
    face_rows = face_rows_of(green, own_map)
    across = to_across(other_map, sections)
    near = to_near(own_map, sections)

    across = handed_on(across, received)
    far = to_near(across, sections)
    source, *quarters = placed_source(received, inject, face_rows)
    shifts = exchange(*quarters, sections)
    four = sections // GROUP == 4
    total_map, parts = chain([own_map, far, across, near], BF16 if four else F32)
    early = image_and_maps(green, source, parts)
    maps = maps_up(total_map, sections) if four else []
    total, local = plane_total(shifts, parts, early[0])
    if four:
        fourth = between(total, (1, 2), (2, 3))
        third = between(total, (0, 2), (1, 3))
        second = between(total, (0, 1))
        first = between(total, (0, 3))
        image, upto = image_and_maps(green, source, parts, early)
        entered = entering(entering_kernel, (first, second, third, fourth, *maps, parts, upto, local))
    else:
        base = scan_below(total_map, total, sections)
        image, upto = image_and_maps(green, source, parts, early)
        entered = entering(entering_from_kernel, (base, parts, upto, local))
    arrived = exchange(*entered, sections)
    prop = propagator(tiles, green, coupling, entered[0])
    return final_waves(arrived, prop, image)[None]


def solution(mesh):
    in_specs = (
        P("sec", "grp", None, None),
        P("sec", "grp", None, None),
        P("sec", None, None),
        P("sec", None, None),
        P("sec", None),
        P("sec", None),
    )
    out_specs = P("sec", "grp", None, None)
    return jax.shard_map(
        per_device, mesh=mesh, in_specs=in_specs, out_specs=out_specs, check_vma=False
    )
```

```python
import functools

import jax
import jax.numpy as jnp
from jax import lax
from jax.experimental import pallas as pl
from jax.experimental.pallas import tpu as pltpu
from jax.sharding import PartitionSpec as P

BLK = 32
CAP = 2
GROUP = 4
HEAD = 8
CORES = 2

HIGH = lax.Precision.HIGHEST
F32 = jnp.float32
BF16 = jnp.bfloat16
VMEM_SMALL = 16 * 1024 * 1024
VMEM_WHOLE = 63400000
PEAK = 1.15e9

IN_VMEM = pl.BlockSpec(memory_space=pltpu.VMEM)
IN_SMEM = pl.BlockSpec(memory_space=pltpu.SMEM)
IN_HBM = pl.BlockSpec(memory_space=pltpu.HBM)
IN_PLACE = pl.BlockSpec(memory_space=pl.ANY)


def shape(*dims, dtype=BF16):
    return jax.ShapeDtypeStruct(dims, dtype)


def call(body, name, ins, outs, scratch, micros, vmem=VMEM_SMALL, aliases=None):
    places = list(range(len(outs))) if isinstance(outs, list) else 0
    return pl.pallas_call(
        body,
        name=name,
        in_specs=ins,
        out_shape=outs,
        out_specs=jax.tree.map(lambda k: IN_PLACE if k in (aliases or {}).values() else IN_VMEM, places),
        input_output_aliases=aliases or {},
        scratch_shapes=scratch,
        compiler_params=pltpu.CompilerParams(vmem_limit_bytes=vmem),
        cost_estimate=pl.CostEstimate(flops=int(micros * PEAK), bytes_accessed=0, transcendentals=0),
    )


def place():
    return lax.axis_index("sec") % GROUP


def partners():
    here = place()
    across = (here + CORES) % GROUP
    return here, across ^ 1, across, here ^ 1


def dot(a, b):
    return jnp.dot(a, b, preferred_element_type=F32)


def dot_wide(a, b):
    return jnp.dot(a, b, precision=HIGH, preferred_element_type=F32)


def two_parts(x):
    high = x.astype(BF16)
    return high, (x - high.astype(F32)).astype(BF16)


def dot_rows(a, b):
    return lax.dot_general(a, b, (((1,), (1,)), ((), ())), preferred_element_type=F32)


def step_by(state, maps):
    high, low = two_parts(state)
    rows = state.shape[0]
    y = dot_rows(jnp.concatenate([high, low], axis=0), maps[0])
    return y[:rows] + (y[rows:] + dot_rows(high, maps[1]))


def mask_tiles(pattern, coupling):
    high, wide = coupling.shape[0] // pattern.shape[1], coupling.shape[1] // pattern.shape[0]
    for i in range(pattern.shape[1]):
        for j in range(pattern.shape[0]):
            at = (slice(i * high, (i + 1) * high), slice(j * wide, (j + 1) * wide))
            tile = coupling[at]
            coupling[at] = jnp.where(pattern[j, i] == 1, tile, jnp.zeros_like(tile))


def pairs_kernel(owner_in, blocks_in, green, inject_in, out, owner, blocks, inject, held, product, slot_of, counts, sem, side):
    energies, orbitals, _ = green.shape
    sections = out.shape[0]
    count = owner.shape[0]
    named = held.shape[1] < orbitals
    small = [
        pltpu.make_async_copy(src, dst, side.at[k])
        for k, (src, dst) in enumerate(((owner_in, owner), (blocks_in, blocks), (inject_in, inject)))
    ]
    for move in small:
        move.start()

    def copy_of(e, q):
        first = pl.multiple_of(blocks[0, q] * BLK, BLK)
        to = pl.multiple_of(q * BLK, BLK)
        return pltpu.make_async_copy(green.at[e, pl.ds(first, BLK)], held.at[e, pl.ds(to, BLK)], sem.at[e])

    def whole(e):
        return pltpu.make_async_copy(green.at[e], held.at[e], sem.at[e])

    if not named:
        for e in range(energies):
            whole(e).start()
    for move in small[:2]:
        move.wait()
    if named:
        for e in range(energies):
            lax.fori_loop(0, count, lambda q, _, e=e: copy_of(e, q).start(), None, unroll=4)
    rows = CAP * energies * BLK
    lane = lax.broadcasted_iota(jnp.int32, (HEAD, out.shape[2]), 1)
    none = jnp.where(lane < CAP, -1.0, 0.0).astype(BF16)

    def blank(d, _):
        counts[d] = 0
        out[d, :rows, :] = jnp.zeros((rows, out.shape[2]), BF16)
        out[d, rows : rows + HEAD, :] = none
        return 0

    lax.fori_loop(0, sections, blank, 0)

    def rank(q, _):
        d = owner[q]
        r = counts[d]
        counts[d] = r + 1
        slot_of[q] = r
        head = out[d, rows : rows + HEAD, :].astype(F32)
        head = jnp.where(lane == r, blocks[1, q].astype(F32), head)
        out[d, rows : rows + HEAD, :] = head.astype(BF16)
        return 0

    lax.fori_loop(0, count, rank, 0)
    small[2].wait()
    for e in range(energies):
        whole_held = pltpu.make_async_copy(green.at[e, pl.ds(0, held.shape[1])], held.at[e], sem.at[e])
        whole_held.wait()
        product[...] = dot(held[e], inject[e]).astype(BF16)

        def fill(q, _):
            first = pl.multiple_of((q if named else blocks[0, q]) * BLK, BLK)
            to = pl.multiple_of((slot_of[q] * energies + e) * BLK, BLK)
            out[owner[q], pl.ds(to, BLK), :] = product[pl.ds(first, BLK), :]
            return 0

        lax.fori_loop(0, count, fill, 0, unroll=4)


def outgoing_pairs(owner, blocks, green, inject, sections):
    energies, orbitals, _ = green.shape
    columns = inject.shape[2]
    rows = min(orbitals, owner.shape[0] * BLK)
    return call(
        pairs_kernel,
        "pairs",
        [IN_HBM] * 4,
        shape(sections, CAP * energies * BLK + HEAD, columns),
        [
            pltpu.SMEM(owner.shape, jnp.int32),
            pltpu.SMEM(blocks.shape, jnp.int32),
            pltpu.VMEM(inject.shape, BF16),
            pltpu.VMEM((energies, rows, orbitals), BF16),
            pltpu.VMEM((rows, columns), BF16),
            pltpu.SMEM(owner.shape, jnp.int32),
            pltpu.SMEM((sections,), jnp.int32),
            pltpu.SemaphoreType.DMA((energies,)),
            pltpu.SemaphoreType.DMA((3,)),
        ],
        4.0,
        VMEM_WHOLE,
    )(owner, blocks, green, inject)


def maps_kernel(pattern, green, coupling, own, other, face_rows, couple, maps):
    energies, orbitals, _ = green.shape
    face = coupling.shape[1]
    couple[...] = coupling[...]
    mask_tiles(pattern, couple)
    for e in range(energies):
        rows = green[e, orbitals - face :, :]
        face_rows[e] = rows
        maps[e] = dot(rows, couple[...])
    mine = place() // CORES
    own[...] = maps[mine]
    other[...] = maps[1 - mine]


def face_maps(pattern, green, coupling):
    orbitals, face = coupling.shape
    square = shape(face, face, dtype=F32)
    return call(
        maps_kernel,
        "face_maps",
        [IN_SMEM, IN_VMEM, IN_VMEM],
        [square, square, shape(green.shape[0], face, orbitals)],
        [pltpu.VMEM(coupling.shape, BF16), pltpu.VMEM((green.shape[0], face, face), F32)],
        1.2,
    )(pattern, green, coupling)


def prop_kernel(pattern, green, coupling, _tie, out, couple):
    couple[...] = coupling[...]
    mask_tiles(pattern, couple)
    for e in range(green.shape[0]):
        out[e] = dot(green[e], couple[...]).astype(BF16)


def propagator(pattern, green, coupling, tie):
    energies, orbitals, _ = green.shape
    return call(
        prop_kernel,
        "prop",
        [IN_SMEM, IN_VMEM, IN_VMEM, IN_PLACE],
        shape(energies, orbitals, coupling.shape[1]),
        [pltpu.VMEM(coupling.shape, BF16)],
        1.5,
    )(pattern, green, coupling, tie)


def times(a, b):
    return dot(a[0], b[0]) + (dot(a[0], b[1]) + dot(a[1], b[0]))


def chain_kernel(own, far, across, near, total_out, parts, maps):
    collect((own, far, across, near), maps)
    split = [two_parts(maps[j]) for j in range(GROUP)]
    lower, upper = two_parts(times(split[1], split[0])), two_parts(times(split[3], split[2]))
    total_out[...] = times(upper, lower).astype(total_out.dtype)
    for j, (high, low) in enumerate(split):
        parts[0, j] = high
        parts[1, j] = low


def chain(maps, dtype):
    face = maps[0].shape[0]
    return call(
        chain_kernel,
        "chain_maps",
        [IN_VMEM] * GROUP,
        [shape(face, face, dtype=dtype), shape(2, GROUP, face, face)],
        [pltpu.VMEM((GROUP, face, face), F32)],
        0.9,
    )(*maps)


def source_kernel(received, inject, face_rows, source, own, far, across, near, quarters, total, heads, targets, sem):
    energies, orbitals, columns = inject.shape
    sections = received.shape[0]
    wide_rows = quarters.shape[1]
    rows = CAP * energies * BLK

    def read(s, _):
        block = received[s, rows : rows + HEAD, :].astype(F32)
        heads[pl.ds(s, 1), :] = block[:1].astype(jnp.int32)
        return 0

    lax.fori_loop(0, sections, read, 0, unroll=min(sections, 8))
    fetch = pltpu.make_async_copy(heads, targets, sem)
    fetch.start()
    total[...] = inject[...].astype(F32)
    fetch.wait()

    def add(s, _):
        for r in range(CAP):
            first = pl.multiple_of(jnp.maximum(targets[s, r], 0) * BLK, BLK)
            for e in range(energies):
                item = received[s, (r * energies + e) * BLK : (r * energies + e + 1) * BLK, :]
                total[e, pl.ds(first, BLK), :] += item.astype(F32)
        return 0

    lax.fori_loop(0, sections, add, 0, unroll=2)
    split = GROUP // energies
    for e in range(energies):
        source[e] = total[e].astype(BF16)
        tall = dot(face_rows[e], source[e])
        wide = tall.T
        for h in range(split):
            quarters[e * split + h] = wide[h * wide_rows : (h + 1) * wide_rows]
    for out, at in zip((own, far, across, near), partners()):
        out[...] = quarters[at].astype(BF16)


def after_kernel(_packets, _map, _same_map):
    pass


def handed_on(item, packets):
    return call(
        after_kernel,
        "after_exchange",
        [IN_PLACE] * 2,
        [shape(*item.shape, dtype=item.dtype)],
        [],
        0.1,
        aliases={1: 0},
    )(packets, item)[0]


def placed_source(received, inject, face_rows):
    face = face_rows.shape[1]
    energies, orbitals, columns = inject.shape
    sections = received.shape[0]
    return call(
        source_kernel,
        "source_and_face",
        [IN_VMEM, IN_VMEM, IN_VMEM],
        [shape(*inject.shape)] + [shape(columns * energies // GROUP, face)] * GROUP,
        [
            pltpu.VMEM((GROUP, columns * energies // GROUP, face), F32),
            pltpu.VMEM(inject.shape, F32),
            pltpu.VMEM((sections, columns), jnp.int32),
            pltpu.SMEM((sections, columns), jnp.int32),
            pltpu.SemaphoreType.DMA,
        ],
        1.4,
    )(received, inject, face_rows)


def collect(refs, held):
    for ref, at in zip(refs, partners()):
        held[at] = ref[...]


def total_kernel(own, far, across, near, parts, _image, out, local, shifts):
    collect((own, far, across, near), shifts)
    state = shifts[0].astype(F32)
    for j in range(1, GROUP):
        local[j - 1] = state
        state = shifts[j].astype(F32) + step_by(state, (parts[0, j], parts[1, j]))
    out[...] = state.astype(BF16)


def plane_total(shifts, parts, tie):
    rows, face = shifts[0].shape
    return call(
        total_kernel,
        "plane_total",
        [IN_VMEM] * (GROUP + 1) + [IN_PLACE],
        [shape(rows, face), shape(GROUP - 1, rows, face, dtype=F32)],
        [pltpu.VMEM((GROUP, rows, face), BF16)],
        3.0,
    )(*shifts, parts, tie)


def work_kernel(early, *refs):
    green, source, parts = refs[:3]
    held, (image, upto) = refs[3:-2], refs[-2:]
    low_plane = lax.axis_index("sec") // GROUP == 0

    @pl.when(low_plane if early else jnp.logical_not(low_plane))
    def _():
        for e in range(green.shape[0]):
            image[e] = dot(green[e], source[e])
        maps = (parts[0, 0], parts[1, 0])
        for j in range(1, GROUP - 1):
            maps = two_parts(times((parts[0, j], parts[1, j]), maps))
            upto[0, j - 1], upto[1, j - 1] = maps

    if held:

        @pl.when(low_plane)
        def _():
            image[...] = held[0][...]
            upto[...] = held[1][...]


def image_and_maps(green, source, parts, held=()):
    _, _, face, _ = parts.shape
    return call(
        functools.partial(work_kernel, not held),
        "image_and_maps",
        [IN_VMEM] * (3 + len(held)),
        [shape(*source.shape, dtype=F32), shape(2, GROUP - 2, face, face)],
        [],
        2.0,
    )(green, source, parts, *held)


def sweep_plane(state, parts, upto, local, out):
    held = [state]
    for j in range(1, GROUP):
        maps = (parts[0, 0], parts[1, 0]) if j == 1 else (upto[0, j - 2], upto[1, j - 2])
        held.append(local[j - 1] + step_by(state, maps))
    work = out[GROUP]
    for j, item in enumerate(held):
        work[j] = item
    for ref, at in zip(out, partners()):
        ref[...] = work[at].astype(BF16)


def entering_kernel(third, near_one, second, far_one, got, other, parts, upto, local, *out):
    first_core = place() % CORES == 0
    first = near_one[...].astype(F32) + far_one[...].astype(F32)
    state = third[...].astype(F32)
    rows = state.shape[0]
    for below, (one, two) in ((second[...].astype(F32), (other, got)), (first, (got, other))):
        factor = jnp.where(first_core, one[...], two[...])
        y = dot_rows(jnp.concatenate(two_parts(state), axis=0), factor)
        state = below + (y[:rows] + y[rows:])
    sweep_plane(state, parts, upto, local, out)


def entering_from_kernel(base, parts, upto, local, *out):
    sweep_plane(base[...], parts, upto, local, out)


def entering(body, args):
    half, columns = args[0].shape
    return call(
        body,
        "entering",
        [IN_VMEM] * len(args),
        [shape(half, columns)] * GROUP,
        [pltpu.VMEM((GROUP, half, columns), F32)],
        1.4,
    )(*args)


def waves_kernel(own, far, across, near, prop, image, out, arrived, wave, sem):
    collect((own, far, across, near), arrived)
    energies, orbitals, _ = prop.shape
    split = GROUP // energies
    pieces = sem.shape[1]
    size = orbitals // pieces
    moves = []
    for e in range(energies):
        incoming = jnp.concatenate([arrived[e * split + h] for h in range(split)], axis=0)
        for c in range(pieces):
            at = slice(c * size, (c + 1) * size)
            wave[e, at, :] = (dot_rows(prop[e, at, :], incoming) + image[e, at, :]).astype(BF16)
            moves.append(pltpu.make_async_copy(wave.at[e, pl.ds(c * size, size)], out.at[e, pl.ds(c * size, size)], sem.at[e, c]))
            moves[-1].start()
    for move in moves:
        move.wait()


def final_waves(arrived, prop, image):
    half, columns = arrived[0].shape
    energies = prop.shape[0]
    return pl.pallas_call(
        waves_kernel,
        name="waves",
        in_specs=[IN_VMEM] * (GROUP + 2),
        out_shape=shape(*image.shape),
        out_specs=IN_HBM,
        scratch_shapes=[
            pltpu.VMEM((GROUP, half, columns), BF16),
            pltpu.VMEM(image.shape, BF16),
            pltpu.SemaphoreType.DMA((energies, 2)),
        ],
        compiler_params=pltpu.CompilerParams(vmem_limit_bytes=VMEM_SMALL),
        cost_estimate=pl.CostEstimate(flops=int(1.3 * PEAK), bytes_accessed=0, transcendentals=0),
    )(*arrived, prop, image)


def to_near(item, sections):
    return lax.ppermute(item, "sec", [(s, s ^ 1) for s in range(sections)])


def to_across(item, sections):
    return lax.ppermute(item, "sec", [(s, s // GROUP * GROUP + (s % GROUP + CORES) % GROUP) for s in range(sections)])


def to_far(item, sections):
    return lax.ppermute(item, "sec", [(s, s // GROUP * GROUP + (s % GROUP + CORES) % GROUP ^ 1) for s in range(sections)])


def exchange(own, far, across, near, sections):
    return [own, to_far(far, sections), to_across(across, sections), to_near(near, sections)]


def up_shift(sections, k):
    return [(s, s + GROUP * k) for s in range(sections - GROUP * k)]


def maps_up(total_map, sections):
    pairs = []
    for i in range(GROUP):
        if i % CORES == 0:
            pairs += [(GROUP + i, 2 * GROUP + i), (2 * GROUP + i, 3 * GROUP + i)]
        else:
            pairs += [(GROUP + i, 3 * GROUP + i)]
    got = lax.ppermute(total_map, "sec", pairs)
    return got, lax.ppermute(got, "sec", [(s, s ^ 1) for s in range(2 * GROUP, sections)])


def between(item, *planes):
    pairs = [(p * GROUP + i, q * GROUP + i) for p, q in planes for i in range(GROUP)]
    return lax.ppermute(item, "sec", pairs)


def scan_below(total_map, total, sections):
    shift = lax.ppermute(total.astype(F32), "sec", up_shift(sections, 1))
    joined = lax.ppermute(total_map, "sec", up_shift(sections, 1))
    stride = 1
    while stride < sections // GROUP:
        other = lax.ppermute(shift, "sec", up_shift(sections, stride))
        other_map = lax.ppermute(joined, "sec", up_shift(sections, stride))
        shift = shift + dot_wide(other, joined.T)
        joined = dot_wide(joined, other_map)
        stride *= 2
    return shift


def per_device(green, injected, coupling, pattern, owner, pair_blocks):
    sections = lax.axis_size("sec")
    green, inject = green[0], injected[0]

    coupling, tiles = coupling[0], pattern[0].T
    outgoing = outgoing_pairs(owner[:, 0], pair_blocks.T, green, inject, sections)
    received = lax.all_to_all(outgoing, "sec", split_axis=0, concat_axis=0, tiled=True)

    own_map, other_map, face_rows = face_maps(tiles, green, coupling)
    across = to_across(other_map, sections)
    near = to_near(own_map, sections)

    source, *quarters = placed_source(received, inject, face_rows)
    shifts = exchange(*quarters, sections)
    across = handed_on(across, quarters[0])
    far = to_near(across, sections)
    four = sections // GROUP == 4
    total_map, parts = chain([own_map, far, across, near], BF16 if four else F32)
    early = image_and_maps(green, source, parts)
    maps = maps_up(total_map, sections) if four else []
    total, local = plane_total(shifts, parts, early[0])
    if four:
        fourth = between(total, (1, 2), (2, 3))
        third = between(total, (0, 2), (1, 3))
        second = between(total, (0, 1))
        first = between(total, (0, 3))
        image, upto = image_and_maps(green, source, parts, early)
        entered = entering(entering_kernel, (first, second, third, fourth, *maps, parts, upto, local))
    else:
        base = scan_below(total_map, total, sections)
        image, upto = image_and_maps(green, source, parts, early)
        entered = entering(entering_from_kernel, (base, parts, upto, local))
    arrived = exchange(*entered, sections)
    prop = propagator(tiles, green, coupling, entered[0])
    return final_waves(arrived, prop, image)[None]


def solution(mesh):
    in_specs = (
        P("sec", "grp", None, None),
        P("sec", "grp", None, None),
        P("sec", None, None),
        P("sec", None, None),
        P("sec", None),
        P("sec", None),
    )
    out_specs = P("sec", "grp", None, None)
    return jax.shard_map(
        per_device, mesh=mesh, in_specs=in_specs, out_specs=out_specs, check_vma=False
    )
```

```python
import functools

import jax
import jax.numpy as jnp
from jax import lax
from jax.experimental import pallas as pl
from jax.experimental.pallas import tpu as pltpu
from jax.sharding import PartitionSpec as P

BLK = 32
CAP = 2
GROUP = 4
HEAD = 8
CORES = 2

HIGH = lax.Precision.HIGHEST
F32 = jnp.float32
BF16 = jnp.bfloat16
VMEM_SMALL = 16 * 1024 * 1024
VMEM_WHOLE = 63400000
PEAK = 1.15e9

IN_VMEM = pl.BlockSpec(memory_space=pltpu.VMEM)
IN_SMEM = pl.BlockSpec(memory_space=pltpu.SMEM)
IN_HBM = pl.BlockSpec(memory_space=pltpu.HBM)
IN_PLACE = pl.BlockSpec(memory_space=pl.ANY)


def shape(*dims, dtype=BF16):
    return jax.ShapeDtypeStruct(dims, dtype)


def call(body, name, ins, outs, scratch, micros, vmem=VMEM_SMALL, aliases=None):
    places = list(range(len(outs))) if isinstance(outs, list) else 0
    return pl.pallas_call(
        body,
        name=name,
        in_specs=ins,
        out_shape=outs,
        out_specs=jax.tree.map(lambda k: IN_PLACE if k in (aliases or {}).values() else IN_VMEM, places),
        input_output_aliases=aliases or {},
        scratch_shapes=scratch,
        compiler_params=pltpu.CompilerParams(vmem_limit_bytes=vmem),
        cost_estimate=pl.CostEstimate(flops=int(micros * PEAK), bytes_accessed=0, transcendentals=0),
    )


def place():
    return lax.axis_index("sec") % GROUP


def partners():
    here = place()
    across = (here + CORES) % GROUP
    return here, across ^ 1, across, here ^ 1


def dot(a, b):
    return jnp.dot(a, b, preferred_element_type=F32)


def dot_wide(a, b):
    return jnp.dot(a, b, precision=HIGH, preferred_element_type=F32)


def two_parts(x):
    high = x.astype(BF16)
    return high, (x - high.astype(F32)).astype(BF16)


def dot_rows(a, b):
    return lax.dot_general(a, b, (((1,), (1,)), ((), ())), preferred_element_type=F32)


def step_by(state, maps):
    high, low = two_parts(state)
    rows = state.shape[0]
    y = dot_rows(jnp.concatenate([high, low], axis=0), maps[0])
    return y[:rows] + (y[rows:] + dot_rows(high, maps[1]))


def mask_tiles(pattern, coupling):
    high, wide = coupling.shape[0] // pattern.shape[1], coupling.shape[1] // pattern.shape[0]
    for i in range(pattern.shape[1]):
        for j in range(pattern.shape[0]):
            at = (slice(i * high, (i + 1) * high), slice(j * wide, (j + 1) * wide))
            tile = coupling[at]
            coupling[at] = jnp.where(pattern[j, i] == 1, tile, jnp.zeros_like(tile))


def pairs_kernel(owner_in, blocks_in, green, inject_in, out, owner, blocks, inject, held, product, slot_of, counts, sem, side):
    energies, orbitals, _ = green.shape
    sections = out.shape[0]
    count = owner.shape[0]
    named = held.shape[1] < orbitals
    small = [
        pltpu.make_async_copy(src, dst, side.at[k])
        for k, (src, dst) in enumerate(((owner_in, owner), (blocks_in, blocks), (inject_in, inject)))
    ]
    for move in small:
        move.start()

    def copy_of(e, q):
        first = pl.multiple_of(blocks[0, q] * BLK, BLK)
        to = pl.multiple_of(q * BLK, BLK)
        return pltpu.make_async_copy(green.at[e, pl.ds(first, BLK)], held.at[e, pl.ds(to, BLK)], sem.at[e])

    def whole(e):
        return pltpu.make_async_copy(green.at[e], held.at[e], sem.at[e])

    if not named:
        for e in range(energies):
            whole(e).start()
    for move in small[:2]:
        move.wait()
    if named:
        for e in range(energies):
            lax.fori_loop(0, count, lambda q, _, e=e: copy_of(e, q).start(), None, unroll=4)
    rows = CAP * energies * BLK
    lane = lax.broadcasted_iota(jnp.int32, (HEAD, out.shape[2]), 1)
    none = jnp.where(lane < CAP, -1.0, 0.0).astype(BF16)

    def blank(d, _):
        counts[d] = 0
        out[d, :rows, :] = jnp.zeros((rows, out.shape[2]), BF16)
        out[d, rows : rows + HEAD, :] = none
        return 0

    lax.fori_loop(0, sections, blank, 0)

    def rank(q, _):
        d = owner[q]
        r = counts[d]
        counts[d] = r + 1
        slot_of[q] = r
        head = out[d, rows : rows + HEAD, :].astype(F32)
        head = jnp.where(lane == r, blocks[1, q].astype(F32), head)
        out[d, rows : rows + HEAD, :] = head.astype(BF16)
        return 0

    lax.fori_loop(0, count, rank, 0)
    small[2].wait()
    for e in range(energies):
        whole_held = pltpu.make_async_copy(green.at[e, pl.ds(0, held.shape[1])], held.at[e], sem.at[e])
        whole_held.wait()
        product[...] = dot(held[e], inject[e]).astype(BF16)

        def fill(q, _):
            first = pl.multiple_of((q if named else blocks[0, q]) * BLK, BLK)
            to = pl.multiple_of((slot_of[q] * energies + e) * BLK, BLK)
            out[owner[q], pl.ds(to, BLK), :] = product[pl.ds(first, BLK), :]
            return 0

        lax.fori_loop(0, count, fill, 0, unroll=4)


def outgoing_pairs(owner, blocks, green, inject, sections):
    energies, orbitals, _ = green.shape
    columns = inject.shape[2]
    rows = min(orbitals, owner.shape[0] * BLK)
    return call(
        pairs_kernel,
        "pairs",
        [IN_HBM] * 4,
        shape(sections, CAP * energies * BLK + HEAD, columns),
        [
            pltpu.SMEM(owner.shape, jnp.int32),
            pltpu.SMEM(blocks.shape, jnp.int32),
            pltpu.VMEM(inject.shape, BF16),
            pltpu.VMEM((energies, rows, orbitals), BF16),
            pltpu.VMEM((rows, columns), BF16),
            pltpu.SMEM(owner.shape, jnp.int32),
            pltpu.SMEM((sections,), jnp.int32),
            pltpu.SemaphoreType.DMA((energies,)),
            pltpu.SemaphoreType.DMA((3,)),
        ],
        4.0,
        VMEM_WHOLE,
    )(owner, blocks, green, inject)


def maps_kernel(pattern, green, coupling, own, other, face_rows, couple, maps):
    energies, orbitals, _ = green.shape
    face = coupling.shape[1]
    couple[...] = coupling[...]
    mask_tiles(pattern, couple)
    for e in range(energies):
        rows = green[e, orbitals - face :, :]
        face_rows[e] = rows
        maps[e] = dot(rows, couple[...])
    mine = place() // CORES
    own[...] = maps[mine]
    other[...] = maps[1 - mine]


def face_maps(pattern, green, coupling):
    orbitals, face = coupling.shape
    square = shape(face, face, dtype=F32)
    return call(
        maps_kernel,
        "face_maps",
        [IN_SMEM, IN_VMEM, IN_VMEM],
        [square, square, shape(green.shape[0], face, orbitals)],
        [pltpu.VMEM(coupling.shape, BF16), pltpu.VMEM((green.shape[0], face, face), F32)],
        1.2,
    )(pattern, green, coupling)


def prop_kernel(pattern, green, coupling, _tie, out, couple):
    couple[...] = coupling[...]
    mask_tiles(pattern, couple)
    for e in range(green.shape[0]):
        out[e] = dot(green[e], couple[...]).astype(BF16)


def propagator(pattern, green, coupling, tie):
    energies, orbitals, _ = green.shape
    return call(
        prop_kernel,
        "prop",
        [IN_SMEM, IN_VMEM, IN_VMEM, IN_PLACE],
        shape(energies, orbitals, coupling.shape[1]),
        [pltpu.VMEM(coupling.shape, BF16)],
        1.5,
    )(pattern, green, coupling, tie)


def times(a, b):
    return dot(a[0], b[0]) + (dot(a[0], b[1]) + dot(a[1], b[0]))


def chain_kernel(own, far, across, near, total_out, parts, maps):
    collect((own, far, across, near), maps)
    split = [two_parts(maps[j]) for j in range(GROUP)]
    lower, upper = two_parts(times(split[1], split[0])), two_parts(times(split[3], split[2]))
    total_out[...] = times(upper, lower).astype(total_out.dtype)
    for j, (high, low) in enumerate(split):
        parts[0, j] = high
        parts[1, j] = low


def chain(maps, dtype):
    face = maps[0].shape[0]
    return call(
        chain_kernel,
        "chain_maps",
        [IN_VMEM] * GROUP,
        [shape(face, face, dtype=dtype), shape(2, GROUP, face, face)],
        [pltpu.VMEM((GROUP, face, face), F32)],
        0.9,
    )(*maps)


def source_kernel(received, inject, face_rows, source, own, far, across, near, quarters, total, heads, targets, sem):
    energies, orbitals, columns = inject.shape
    sections = received.shape[0]
    wide_rows = quarters.shape[1]
    rows = CAP * energies * BLK

    def read(s, _):
        block = received[s, rows : rows + HEAD, :].astype(F32)
        heads[pl.ds(s, 1), :] = block[:1].astype(jnp.int32)
        return 0

    lax.fori_loop(0, sections, read, 0, unroll=min(sections, 8))
    fetch = pltpu.make_async_copy(heads, targets, sem)
    fetch.start()
    total[...] = inject[...].astype(F32)
    fetch.wait()

    def add(s, _):
        for r in range(CAP):
            first = pl.multiple_of(jnp.maximum(targets[s, r], 0) * BLK, BLK)
            for e in range(energies):
                item = received[s, (r * energies + e) * BLK : (r * energies + e + 1) * BLK, :]
                total[e, pl.ds(first, BLK), :] += item.astype(F32)
        return 0

    lax.fori_loop(0, sections, add, 0, unroll=2)
    split = GROUP // energies
    for e in range(energies):
        source[e] = total[e].astype(BF16)
        tall = dot(face_rows[e], source[e])
        wide = tall.T
        for h in range(split):
            quarters[e * split + h] = wide[h * wide_rows : (h + 1) * wide_rows]
    for out, at in zip((own, far, across, near), partners()):
        out[...] = quarters[at].astype(BF16)


def after_kernel(_packets, _map, _same_map):
    pass


def handed_on(item, packets):
    return call(
        after_kernel,
        "after_exchange",
        [IN_PLACE] * 2,
        [shape(*item.shape, dtype=item.dtype)],
        [],
        0.1,
        aliases={1: 0},
    )(packets, item)[0]


def placed_source(received, inject, face_rows):
    face = face_rows.shape[1]
    energies, orbitals, columns = inject.shape
    sections = received.shape[0]
    return call(
        source_kernel,
        "source_and_face",
        [IN_VMEM, IN_VMEM, IN_VMEM],
        [shape(*inject.shape)] + [shape(columns * energies // GROUP, face)] * GROUP,
        [
            pltpu.VMEM((GROUP, columns * energies // GROUP, face), F32),
            pltpu.VMEM(inject.shape, F32),
            pltpu.VMEM((sections, columns), jnp.int32),
            pltpu.SMEM((sections, columns), jnp.int32),
            pltpu.SemaphoreType.DMA,
        ],
        1.4,
    )(received, inject, face_rows)


def collect(refs, held):
    for ref, at in zip(refs, partners()):
        held[at] = ref[...]


def total_kernel(own, far, across, near, parts, _image, out, local, shifts):
    collect((own, far, across, near), shifts)
    state = shifts[0].astype(F32)
    for j in range(1, GROUP):
        local[j - 1] = state
        state = shifts[j].astype(F32) + step_by(state, (parts[0, j], parts[1, j]))
    out[...] = state.astype(BF16)


def plane_total(shifts, parts, tie):
    rows, face = shifts[0].shape
    return call(
        total_kernel,
        "plane_total",
        [IN_VMEM] * (GROUP + 1) + [IN_PLACE],
        [shape(rows, face), shape(GROUP - 1, rows, face, dtype=F32)],
        [pltpu.VMEM((GROUP, rows, face), BF16)],
        3.0,
    )(*shifts, parts, tie)


def work_kernel(early, *refs):
    green, source, parts = refs[:3]
    held, (image, upto) = refs[3:-2], refs[-2:]
    low_plane = lax.axis_index("sec") // GROUP == 0

    @pl.when(low_plane if early else jnp.logical_not(low_plane))
    def _():
        for e in range(green.shape[0]):
            image[e] = dot(green[e], source[e])
        maps = (parts[0, 0], parts[1, 0])
        for j in range(1, GROUP - 1):
            maps = two_parts(times((parts[0, j], parts[1, j]), maps))
            upto[0, j - 1], upto[1, j - 1] = maps

    if held:

        @pl.when(low_plane)
        def _():
            image[...] = held[0][...]
            upto[...] = held[1][...]


def image_and_maps(green, source, parts, held=()):
    _, _, face, _ = parts.shape
    return call(
        functools.partial(work_kernel, not held),
        "image_and_maps",
        [IN_VMEM] * (3 + len(held)),
        [shape(*source.shape, dtype=F32), shape(2, GROUP - 2, face, face)],
        [],
        2.0,
    )(green, source, parts, *held)


def sweep_plane(state, parts, upto, local, out):
    held = [state]
    for j in range(1, GROUP):
        maps = (parts[0, 0], parts[1, 0]) if j == 1 else (upto[0, j - 2], upto[1, j - 2])
        held.append(local[j - 1] + step_by(state, maps))
    work = out[GROUP]
    for j, item in enumerate(held):
        work[j] = item
    for ref, at in zip(out, partners()):
        ref[...] = work[at].astype(BF16)


def entering_kernel(third, near_one, second, far_one, got, other, parts, upto, local, *out):
    first_core = place() % CORES == 0
    first = near_one[...].astype(F32) + far_one[...].astype(F32)
    state = third[...].astype(F32)
    rows = state.shape[0]
    for below, (one, two) in ((second[...].astype(F32), (other, got)), (first, (got, other))):
        factor = jnp.where(first_core, one[...], two[...])
        y = dot_rows(jnp.concatenate(two_parts(state), axis=0), factor)
        state = below + (y[:rows] + y[rows:])
    sweep_plane(state, parts, upto, local, out)


def entering_from_kernel(base, parts, upto, local, *out):
    sweep_plane(base[...], parts, upto, local, out)


def entering(body, args):
    half, columns = args[0].shape
    return call(
        body,
        "entering",
        [IN_VMEM] * len(args),
        [shape(half, columns)] * GROUP,
        [pltpu.VMEM((GROUP, half, columns), F32)],
        1.4,
    )(*args)


def waves_kernel(own, far, across, near, prop, image, out, arrived, wave, sem):
    collect((own, far, across, near), arrived)
    energies, orbitals, _ = prop.shape
    split = GROUP // energies
    pieces = sem.shape[1]
    size = orbitals // pieces
    moves = []
    for e in range(energies):
        incoming = jnp.concatenate([arrived[e * split + h] for h in range(split)], axis=0)
        for c in range(pieces):
            at = slice(c * size, (c + 1) * size)
            wave[e, at, :] = (dot_rows(prop[e, at, :], incoming) + image[e, at, :]).astype(BF16)
            moves.append(pltpu.make_async_copy(wave.at[e, pl.ds(c * size, size)], out.at[e, pl.ds(c * size, size)], sem.at[e, c]))
            moves[-1].start()
    for move in moves:
        move.wait()


def final_waves(arrived, prop, image):
    half, columns = arrived[0].shape
    energies = prop.shape[0]
    return pl.pallas_call(
        waves_kernel,
        name="waves",
        in_specs=[IN_VMEM] * (GROUP + 2),
        out_shape=shape(*image.shape),
        out_specs=IN_HBM,
        scratch_shapes=[
            pltpu.VMEM((GROUP, half, columns), BF16),
            pltpu.VMEM(image.shape, BF16),
            pltpu.SemaphoreType.DMA((energies, 2)),
        ],
        compiler_params=pltpu.CompilerParams(vmem_limit_bytes=VMEM_SMALL),
        cost_estimate=pl.CostEstimate(flops=int(1.3 * PEAK), bytes_accessed=0, transcendentals=0),
    )(*arrived, prop, image)


def to_near(item, sections):
    return lax.ppermute(item, "sec", [(s, s ^ 1) for s in range(sections)])


def to_across(item, sections):
    return lax.ppermute(item, "sec", [(s, s // GROUP * GROUP + (s % GROUP + CORES) % GROUP) for s in range(sections)])


def to_far(item, sections):
    return lax.ppermute(item, "sec", [(s, s // GROUP * GROUP + (s % GROUP + CORES) % GROUP ^ 1) for s in range(sections)])


def exchange(own, far, across, near, sections):
    return [own, to_far(far, sections), to_across(across, sections), to_near(near, sections)]


def up_shift(sections, k):
    return [(s, s + GROUP * k) for s in range(sections - GROUP * k)]


def maps_up(total_map, sections):
    pairs = []
    for i in range(GROUP):
        if i % CORES == 0:
            pairs += [(GROUP + i, 2 * GROUP + i), (2 * GROUP + i, 3 * GROUP + i)]
        else:
            pairs += [(GROUP + i, 3 * GROUP + i)]
    got = lax.ppermute(total_map, "sec", pairs)
    return got, lax.ppermute(got, "sec", [(s, s ^ 1) for s in range(2 * GROUP, sections)])


def between(item, *planes):
    pairs = [(p * GROUP + i, q * GROUP + i) for p, q in planes for i in range(GROUP)]
    return lax.ppermute(item, "sec", pairs)


def scan_below(total_map, total, sections):
    shift = lax.ppermute(total.astype(F32), "sec", up_shift(sections, 1))
    joined = lax.ppermute(total_map, "sec", up_shift(sections, 1))
    stride = 1
    while stride < sections // GROUP:
        other = lax.ppermute(shift, "sec", up_shift(sections, stride))
        other_map = lax.ppermute(joined, "sec", up_shift(sections, stride))
        shift = shift + dot_wide(other, joined.T)
        joined = dot_wide(joined, other_map)
        stride *= 2
    return shift


def per_device(green, injected, coupling, pattern, owner, pair_blocks):
    sections = lax.axis_size("sec")
    green, inject = green[0], injected[0]

    coupling, tiles = coupling[0], pattern[0].T
    outgoing = outgoing_pairs(owner[:, 0], pair_blocks.T, green, inject, sections)
    received = lax.all_to_all(outgoing, "sec", split_axis=0, concat_axis=0, tiled=True)

    own_map, other_map, face_rows = face_maps(tiles, green, coupling)
    across = to_across(other_map, sections)

    source, *quarters = placed_source(received, inject, face_rows)
    shifts = exchange(*quarters, sections)
    across = handed_on(across, quarters[0])
    near, far = to_near(handed_on(own_map, quarters[0]), sections), to_near(across, sections)
    four = sections // GROUP == 4
    total_map, parts = chain([own_map, far, across, near], BF16 if four else F32)
    early = image_and_maps(green, source, parts)
    maps = maps_up(total_map, sections) if four else []
    total, local = plane_total(shifts, parts, early[0])
    if four:
        fourth = between(total, (1, 2), (2, 3))
        third = between(total, (0, 2), (1, 3))
        second = between(total, (0, 1))
        first = between(total, (0, 3))
        image, upto = image_and_maps(green, source, parts, early)
        entered = entering(entering_kernel, (first, second, third, fourth, *maps, parts, upto, local))
    else:
        base = scan_below(total_map, total, sections)
        image, upto = image_and_maps(green, source, parts, early)
        entered = entering(entering_from_kernel, (base, parts, upto, local))
    arrived = exchange(*entered, sections)
    prop = propagator(tiles, green, coupling, entered[0])
    return final_waves(arrived, prop, image)[None]


def solution(mesh):
    in_specs = (
        P("sec", "grp", None, None),
        P("sec", "grp", None, None),
        P("sec", None, None),
        P("sec", None, None),
        P("sec", None),
        P("sec", None),
    )
    out_specs = P("sec", "grp", None, None)
    return jax.shard_map(
        per_device, mesh=mesh, in_specs=in_specs, out_specs=out_specs, check_vma=False
    )
```

```python
import functools

import jax
import jax.numpy as jnp
from jax import lax
from jax.experimental import pallas as pl
from jax.experimental.pallas import tpu as pltpu
from jax.sharding import PartitionSpec as P

BLK = 32
CAP = 2
GROUP = 4
HEAD = 8
CORES = 2

HIGH = lax.Precision.HIGHEST
F32 = jnp.float32
BF16 = jnp.bfloat16
VMEM_SMALL = 16 * 1024 * 1024
VMEM_WHOLE = 63400000
PEAK = 1.15e9

IN_VMEM = pl.BlockSpec(memory_space=pltpu.VMEM)
IN_SMEM = pl.BlockSpec(memory_space=pltpu.SMEM)
IN_HBM = pl.BlockSpec(memory_space=pltpu.HBM)
IN_PLACE = pl.BlockSpec(memory_space=pl.ANY)


def shape(*dims, dtype=BF16):
    return jax.ShapeDtypeStruct(dims, dtype)


def call(body, name, ins, outs, scratch, micros, vmem=VMEM_SMALL, aliases=None):
    places = list(range(len(outs))) if isinstance(outs, list) else 0
    return pl.pallas_call(
        body,
        name=name,
        in_specs=ins,
        out_shape=outs,
        out_specs=jax.tree.map(lambda k: IN_PLACE if k in (aliases or {}).values() else IN_VMEM, places),
        input_output_aliases=aliases or {},
        scratch_shapes=scratch,
        compiler_params=pltpu.CompilerParams(vmem_limit_bytes=vmem),
        cost_estimate=pl.CostEstimate(flops=int(micros * PEAK), bytes_accessed=0, transcendentals=0),
    )


def place():
    return lax.axis_index("sec") % GROUP


def partners():
    here = place()
    across = (here + CORES) % GROUP
    return here, across ^ 1, across, here ^ 1


def dot(a, b):
    return jnp.dot(a, b, preferred_element_type=F32)


def dot_wide(a, b):
    return jnp.dot(a, b, precision=HIGH, preferred_element_type=F32)


def two_parts(x):
    high = x.astype(BF16)
    return high, (x - high.astype(F32)).astype(BF16)


def dot_rows(a, b):
    return lax.dot_general(a, b, (((1,), (1,)), ((), ())), preferred_element_type=F32)


def step_by(state, maps):
    high, low = two_parts(state)
    rows = state.shape[0]
    y = dot_rows(jnp.concatenate([high, low], axis=0), maps[0])
    return y[:rows] + (y[rows:] + dot_rows(high, maps[1]))


def mask_tiles(pattern, coupling):
    high, wide = coupling.shape[0] // pattern.shape[1], coupling.shape[1] // pattern.shape[0]
    for i in range(pattern.shape[1]):
        for j in range(pattern.shape[0]):
            at = (slice(i * high, (i + 1) * high), slice(j * wide, (j + 1) * wide))
            tile = coupling[at]
            coupling[at] = jnp.where(pattern[j, i] == 1, tile, jnp.zeros_like(tile))


def pairs_kernel(owner_in, blocks_in, green, inject_in, out, owner, blocks, inject, held, product, slot_of, counts, sem, side):
    energies, orbitals, _ = green.shape
    sections = out.shape[0]
    count = owner.shape[0]
    named = held.shape[1] < orbitals
    small = [
        pltpu.make_async_copy(src, dst, side.at[k])
        for k, (src, dst) in enumerate(((owner_in, owner), (blocks_in, blocks), (inject_in, inject)))
    ]
    for move in small:
        move.start()

    def copy_of(e, q):
        first = pl.multiple_of(blocks[0, q] * BLK, BLK)
        to = pl.multiple_of(q * BLK, BLK)
        return pltpu.make_async_copy(green.at[e, pl.ds(first, BLK)], held.at[e, pl.ds(to, BLK)], sem.at[e])

    def whole(e):
        return pltpu.make_async_copy(green.at[e], held.at[e], sem.at[e])

    if not named:
        for e in range(energies):
            whole(e).start()
    for move in small[:2]:
        move.wait()
    if named:
        for e in range(energies):
            lax.fori_loop(0, count, lambda q, _, e=e: copy_of(e, q).start(), None, unroll=4)
    rows = CAP * energies * BLK
    lane = lax.broadcasted_iota(jnp.int32, (HEAD, out.shape[2]), 1)
    none = jnp.where(lane < CAP, -1.0, 0.0).astype(BF16)

    def blank(d, _):
        counts[d] = 0
        out[d, :rows, :] = jnp.zeros((rows, out.shape[2]), BF16)
        out[d, rows : rows + HEAD, :] = none
        return 0

    lax.fori_loop(0, sections, blank, 0)

    def rank(q, _):
        d = owner[q]
        r = counts[d]
        counts[d] = r + 1
        slot_of[q] = r
        head = out[d, rows : rows + HEAD, :].astype(F32)
        head = jnp.where(lane == r, blocks[1, q].astype(F32), head)
        out[d, rows : rows + HEAD, :] = head.astype(BF16)
        return 0

    lax.fori_loop(0, count, rank, 0)
    small[2].wait()
    for e in range(energies):
        whole_held = pltpu.make_async_copy(green.at[e, pl.ds(0, held.shape[1])], held.at[e], sem.at[e])
        whole_held.wait()
        product[...] = dot(held[e], inject[e]).astype(BF16)

        def fill(q, _):
            first = pl.multiple_of((q if named else blocks[0, q]) * BLK, BLK)
            to = pl.multiple_of((slot_of[q] * energies + e) * BLK, BLK)
            out[owner[q], pl.ds(to, BLK), :] = product[pl.ds(first, BLK), :]
            return 0

        lax.fori_loop(0, count, fill, 0, unroll=4)


def outgoing_pairs(owner, blocks, green, inject, sections):
    energies, orbitals, _ = green.shape
    columns = inject.shape[2]
    rows = min(orbitals, owner.shape[0] * BLK)
    return call(
        pairs_kernel,
        "pairs",
        [IN_HBM] * 4,
        shape(sections, CAP * energies * BLK + HEAD, columns),
        [
            pltpu.SMEM(owner.shape, jnp.int32),
            pltpu.SMEM(blocks.shape, jnp.int32),
            pltpu.VMEM(inject.shape, BF16),
            pltpu.VMEM((energies, rows, orbitals), BF16),
            pltpu.VMEM((rows, columns), BF16),
            pltpu.SMEM(owner.shape, jnp.int32),
            pltpu.SMEM((sections,), jnp.int32),
            pltpu.SemaphoreType.DMA((energies,)),
            pltpu.SemaphoreType.DMA((3,)),
        ],
        4.0,
        VMEM_WHOLE,
    )(owner, blocks, green, inject)


def maps_kernel(pattern, green, coupling, own, other, *refs):
    face_rows, (couple, maps) = refs[:-2], refs[-2:]
    energies, orbitals, _ = green.shape
    face = coupling.shape[1]
    couple[...] = coupling[...]
    mask_tiles(pattern, couple)
    for e in range(energies):
        rows = green[e, orbitals - face :, :]
        face_rows[e][...] = rows
        maps[e] = dot(rows, couple[...])
    mine = place() // CORES
    own[...] = maps[mine]
    other[...] = maps[1 - mine]


def face_maps(pattern, green, coupling):
    orbitals, face = coupling.shape
    square = shape(face, face, dtype=F32)
    return call(
        maps_kernel,
        "face_maps",
        [IN_SMEM, IN_VMEM, IN_VMEM],
        [square, square] + [shape(face, orbitals)] * green.shape[0],
        [pltpu.VMEM(coupling.shape, BF16), pltpu.VMEM((green.shape[0], face, face), F32)],
        1.2,
    )(pattern, green, coupling)


def prop_kernel(pattern, green, coupling, _tie, out, couple):
    couple[...] = coupling[...]
    mask_tiles(pattern, couple)
    for e in range(green.shape[0]):
        out[e] = dot(green[e], couple[...]).astype(BF16)


def propagator(pattern, green, coupling, tie):
    energies, orbitals, _ = green.shape
    return call(
        prop_kernel,
        "prop",
        [IN_SMEM, IN_VMEM, IN_VMEM, IN_PLACE],
        shape(energies, orbitals, coupling.shape[1]),
        [pltpu.VMEM(coupling.shape, BF16)],
        1.5,
    )(pattern, green, coupling, tie)


def times(a, b):
    return dot(a[0], b[0]) + (dot(a[0], b[1]) + dot(a[1], b[0]))


def chain_kernel(own, far, across, near, total_out, parts, maps):
    collect((own, far, across, near), maps)
    split = [two_parts(maps[j]) for j in range(GROUP)]
    lower, upper = two_parts(times(split[1], split[0])), two_parts(times(split[3], split[2]))
    total_out[...] = times(upper, lower).astype(total_out.dtype)
    for j, (high, low) in enumerate(split):
        parts[0, j] = high
        parts[1, j] = low


def chain(maps, dtype):
    face = maps[0].shape[0]
    return call(
        chain_kernel,
        "chain_maps",
        [IN_VMEM] * GROUP,
        [shape(face, face, dtype=dtype), shape(2, GROUP, face, face)],
        [pltpu.VMEM((GROUP, face, face), F32)],
        0.9,
    )(*maps)


def source_kernel(received, inject, *refs):
    energies, orbitals, columns = inject.shape
    face_rows = refs[:energies]
    source, own, far, across, near, quarters, total, heads, targets, sem = refs[energies:]
    sections = received.shape[0]
    wide_rows = quarters.shape[1]
    rows = CAP * energies * BLK

    def read(s, _):
        block = received[s, rows : rows + HEAD, :].astype(F32)
        heads[pl.ds(s, 1), :] = block[:1].astype(jnp.int32)
        return 0

    lax.fori_loop(0, sections, read, 0, unroll=min(sections, 8))
    fetch = pltpu.make_async_copy(heads, targets, sem)
    fetch.start()
    total[...] = inject[...].astype(F32)
    fetch.wait()

    def add(s, _):
        for r in range(CAP):
            first = pl.multiple_of(jnp.maximum(targets[s, r], 0) * BLK, BLK)
            for e in range(energies):
                item = received[s, (r * energies + e) * BLK : (r * energies + e + 1) * BLK, :]
                total[e, pl.ds(first, BLK), :] += item.astype(F32)
        return 0

    lax.fori_loop(0, sections, add, 0, unroll=2)
    split = GROUP // energies
    for e in range(energies):
        source[e] = total[e].astype(BF16)
        tall = dot(face_rows[e][...], source[e])
        wide = tall.T
        for h in range(split):
            quarters[e * split + h] = wide[h * wide_rows : (h + 1) * wide_rows]
    for out, at in zip((own, far, across, near), partners()):
        out[...] = quarters[at].astype(BF16)


def after_kernel(_packets, _map, _same_map):
    pass


def handed_on(item, packets):
    return call(
        after_kernel,
        "after_exchange",
        [IN_PLACE] * 2,
        [shape(*item.shape, dtype=item.dtype)],
        [],
        0.1,
        aliases={1: 0},
    )(packets, item)[0]


def placed_source(received, inject, face_rows):
    face = face_rows[0].shape[0]
    energies, orbitals, columns = inject.shape
    sections = received.shape[0]
    return call(
        source_kernel,
        "source_and_face",
        [IN_VMEM] * (2 + energies),
        [shape(*inject.shape)] + [shape(columns * energies // GROUP, face)] * GROUP,
        [
            pltpu.VMEM((GROUP, columns * energies // GROUP, face), F32),
            pltpu.VMEM(inject.shape, F32),
            pltpu.VMEM((sections, columns), jnp.int32),
            pltpu.SMEM((sections, columns), jnp.int32),
            pltpu.SemaphoreType.DMA,
        ],
        1.4,
    )(received, inject, *face_rows)


def collect(refs, held):
    for ref, at in zip(refs, partners()):
        held[at] = ref[...]


def total_kernel(own, far, across, near, parts, _image, out, local, shifts):
    collect((own, far, across, near), shifts)
    state = shifts[0].astype(F32)
    for j in range(1, GROUP):
        local[j - 1] = state
        state = shifts[j].astype(F32) + step_by(state, (parts[0, j], parts[1, j]))
    out[...] = state.astype(BF16)


def plane_total(shifts, parts, tie):
    rows, face = shifts[0].shape
    return call(
        total_kernel,
        "plane_total",
        [IN_VMEM] * (GROUP + 1) + [IN_PLACE],
        [shape(rows, face), shape(GROUP - 1, rows, face, dtype=F32)],
        [pltpu.VMEM((GROUP, rows, face), BF16)],
        3.0,
    )(*shifts, parts, tie)


def work_kernel(early, *refs):
    green, source, parts = refs[:3]
    held, (image, upto) = refs[3:-2], refs[-2:]
    low_plane = lax.axis_index("sec") // GROUP == 0

    @pl.when(low_plane if early else jnp.logical_not(low_plane))
    def _():
        for e in range(green.shape[0]):
            image[e] = dot(green[e], source[e])
        maps = (parts[0, 0], parts[1, 0])
        for j in range(1, GROUP - 1):
            maps = two_parts(times((parts[0, j], parts[1, j]), maps))
            upto[0, j - 1], upto[1, j - 1] = maps

    if held:

        @pl.when(low_plane)
        def _():
            image[...] = held[0][...]
            upto[...] = held[1][...]


def image_and_maps(green, source, parts, held=()):
    _, _, face, _ = parts.shape
    return call(
        functools.partial(work_kernel, not held),
        "image_and_maps",
        [IN_VMEM] * (3 + len(held)),
        [shape(*source.shape, dtype=F32), shape(2, GROUP - 2, face, face)],
        [],
        2.0,
    )(green, source, parts, *held)


def sweep_plane(state, parts, upto, local, out):
    held = [state]
    for j in range(1, GROUP):
        maps = (parts[0, 0], parts[1, 0]) if j == 1 else (upto[0, j - 2], upto[1, j - 2])
        held.append(local[j - 1] + step_by(state, maps))
    work = out[GROUP]
    for j, item in enumerate(held):
        work[j] = item
    for ref, at in zip(out, partners()):
        ref[...] = work[at].astype(BF16)


def entering_kernel(third, near_one, second, far_one, got, other, parts, upto, local, *out):
    first_core = place() % CORES == 0
    first = near_one[...].astype(F32) + far_one[...].astype(F32)
    state = third[...].astype(F32)
    rows = state.shape[0]
    for below, (one, two) in ((second[...].astype(F32), (other, got)), (first, (got, other))):
        factor = jnp.where(first_core, one[...], two[...])
        y = dot_rows(jnp.concatenate(two_parts(state), axis=0), factor)
        state = below + (y[:rows] + y[rows:])
    sweep_plane(state, parts, upto, local, out)


def entering_from_kernel(base, parts, upto, local, *out):
    sweep_plane(base[...], parts, upto, local, out)


def entering(body, args):
    half, columns = args[0].shape
    return call(
        body,
        "entering",
        [IN_VMEM] * len(args),
        [shape(half, columns)] * GROUP,
        [pltpu.VMEM((GROUP, half, columns), F32)],
        1.4,
    )(*args)


def waves_kernel(own, far, across, near, prop, image, out, arrived, wave, sem):
    collect((own, far, across, near), arrived)
    energies, orbitals, _ = prop.shape
    split = GROUP // energies
    pieces = sem.shape[1]
    size = orbitals // pieces
    moves = []
    for e in range(energies):
        incoming = jnp.concatenate([arrived[e * split + h] for h in range(split)], axis=0)
        for c in range(pieces):
            at = slice(c * size, (c + 1) * size)
            wave[e, at, :] = (dot_rows(prop[e, at, :], incoming) + image[e, at, :]).astype(BF16)
            moves.append(pltpu.make_async_copy(wave.at[e, pl.ds(c * size, size)], out.at[e, pl.ds(c * size, size)], sem.at[e, c]))
            moves[-1].start()
    for move in moves:
        move.wait()


def final_waves(arrived, prop, image):
    half, columns = arrived[0].shape
    energies = prop.shape[0]
    return pl.pallas_call(
        waves_kernel,
        name="waves",
        in_specs=[IN_VMEM] * (GROUP + 2),
        out_shape=shape(*image.shape),
        out_specs=IN_HBM,
        scratch_shapes=[
            pltpu.VMEM((GROUP, half, columns), BF16),
            pltpu.VMEM(image.shape, BF16),
            pltpu.SemaphoreType.DMA((energies, 2)),
        ],
        compiler_params=pltpu.CompilerParams(vmem_limit_bytes=VMEM_SMALL),
        cost_estimate=pl.CostEstimate(flops=int(1.3 * PEAK), bytes_accessed=0, transcendentals=0),
    )(*arrived, prop, image)


def to_near(item, sections):
    return lax.ppermute(item, "sec", [(s, s ^ 1) for s in range(sections)])


def to_across(item, sections):
    return lax.ppermute(item, "sec", [(s, s // GROUP * GROUP + (s % GROUP + CORES) % GROUP) for s in range(sections)])


def to_far(item, sections):
    return lax.ppermute(item, "sec", [(s, s // GROUP * GROUP + (s % GROUP + CORES) % GROUP ^ 1) for s in range(sections)])


def exchange(own, far, across, near, sections):
    return [own, to_far(far, sections), to_across(across, sections), to_near(near, sections)]


def up_shift(sections, k):
    return [(s, s + GROUP * k) for s in range(sections - GROUP * k)]


def maps_up(total_map, sections):
    pairs = []
    for i in range(GROUP):
        if i % CORES == 0:
            pairs += [(GROUP + i, 2 * GROUP + i), (2 * GROUP + i, 3 * GROUP + i)]
        else:
            pairs += [(GROUP + i, 3 * GROUP + i)]
    got = lax.ppermute(total_map, "sec", pairs)
    return got, lax.ppermute(got, "sec", [(s, s ^ 1) for s in range(2 * GROUP, sections)])


def between(item, *planes):
    pairs = [(p * GROUP + i, q * GROUP + i) for p, q in planes for i in range(GROUP)]
    return lax.ppermute(item, "sec", pairs)


def scan_below(total_map, total, sections):
    shift = lax.ppermute(total.astype(F32), "sec", up_shift(sections, 1))
    joined = lax.ppermute(total_map, "sec", up_shift(sections, 1))
    stride = 1
    while stride < sections // GROUP:
        other = lax.ppermute(shift, "sec", up_shift(sections, stride))
        other_map = lax.ppermute(joined, "sec", up_shift(sections, stride))
        shift = shift + dot_wide(other, joined.T)
        joined = dot_wide(joined, other_map)
        stride *= 2
    return shift


def per_device(green, injected, coupling, pattern, owner, pair_blocks):
    sections = lax.axis_size("sec")
    green, inject = green[0], injected[0]

    coupling, tiles = coupling[0], pattern[0].T
    outgoing = outgoing_pairs(owner[:, 0], pair_blocks.T, green, inject, sections)
    received = lax.all_to_all(outgoing, "sec", split_axis=0, concat_axis=0, tiled=True)

    own_map, other_map, *face_rows = face_maps(tiles, green, coupling)
    across = to_across(other_map, sections)
    near = to_near(own_map, sections)

    source, *quarters = placed_source(received, inject, face_rows)
    shifts = exchange(*quarters, sections)
    across = handed_on(across, quarters[0])
    far = to_near(across, sections)
    four = sections // GROUP == 4
    total_map, parts = chain([own_map, far, across, near], BF16 if four else F32)
    early = image_and_maps(green, source, parts)
    maps = maps_up(total_map, sections) if four else []
    total, local = plane_total(shifts, parts, early[0])
    if four:
        fourth = between(total, (1, 2), (2, 3))
        third = between(total, (0, 2), (1, 3))
        second = between(total, (0, 1))
        first = between(total, (0, 3))
        image, upto = image_and_maps(green, source, parts, early)
        entered = entering(entering_kernel, (first, second, third, fourth, *maps, parts, upto, local))
    else:
        base = scan_below(total_map, total, sections)
        image, upto = image_and_maps(green, source, parts, early)
        entered = entering(entering_from_kernel, (base, parts, upto, local))
    arrived = exchange(*entered, sections)
    prop = propagator(tiles, green, coupling, entered[0])
    return final_waves(arrived, prop, image)[None]


def solution(mesh):
    in_specs = (
        P("sec", "grp", None, None),
        P("sec", "grp", None, None),
        P("sec", None, None),
        P("sec", None, None),
        P("sec", None),
        P("sec", None),
    )
    out_specs = P("sec", "grp", None, None)
    return jax.shard_map(
        per_device, mesh=mesh, in_specs=in_specs, out_specs=out_specs, check_vma=False
    )
```

```python
import functools

import jax
import jax.numpy as jnp
from jax import lax
from jax.experimental import pallas as pl
from jax.experimental.pallas import tpu as pltpu
from jax.sharding import PartitionSpec as P

BLK = 32
CAP = 2
GROUP = 4
HEAD = 8
CORES = 2

HIGH = lax.Precision.HIGHEST
F32 = jnp.float32
BF16 = jnp.bfloat16
VMEM_SMALL = 16 * 1024 * 1024
VMEM_WHOLE = 63400000
PEAK = 1.15e9

IN_VMEM = pl.BlockSpec(memory_space=pltpu.VMEM)
IN_SMEM = pl.BlockSpec(memory_space=pltpu.SMEM)
IN_HBM = pl.BlockSpec(memory_space=pltpu.HBM)
IN_PLACE = pl.BlockSpec(memory_space=pl.ANY)


def shape(*dims, dtype=BF16):
    return jax.ShapeDtypeStruct(dims, dtype)


def call(body, name, ins, outs, scratch, micros, vmem=VMEM_SMALL, aliases=None):
    places = list(range(len(outs))) if isinstance(outs, list) else 0
    return pl.pallas_call(
        body,
        name=name,
        in_specs=ins,
        out_shape=outs,
        out_specs=jax.tree.map(lambda k: IN_PLACE if k in (aliases or {}).values() else IN_VMEM, places),
        input_output_aliases=aliases or {},
        scratch_shapes=scratch,
        compiler_params=pltpu.CompilerParams(vmem_limit_bytes=vmem),
        cost_estimate=pl.CostEstimate(flops=int(micros * PEAK), bytes_accessed=0, transcendentals=0),
    )


def place():
    return lax.axis_index("sec") % GROUP


def partners():
    here = place()
    across = (here + CORES) % GROUP
    return here, across ^ 1, across, here ^ 1


def dot(a, b):
    return jnp.dot(a, b, preferred_element_type=F32)


def dot_wide(a, b):
    return jnp.dot(a, b, precision=HIGH, preferred_element_type=F32)


def two_parts(x):
    high = x.astype(BF16)
    return high, (x - high.astype(F32)).astype(BF16)


def dot_rows(a, b):
    return lax.dot_general(a, b, (((1,), (1,)), ((), ())), preferred_element_type=F32)


def step_by(state, maps):
    high, low = two_parts(state)
    rows = state.shape[0]
    y = dot_rows(jnp.concatenate([high, low], axis=0), maps[0])
    return y[:rows] + (y[rows:] + dot_rows(high, maps[1]))


def mask_tiles(pattern, coupling):
    high, wide = coupling.shape[0] // pattern.shape[1], coupling.shape[1] // pattern.shape[0]
    for i in range(pattern.shape[1]):
        for j in range(pattern.shape[0]):
            at = (slice(i * high, (i + 1) * high), slice(j * wide, (j + 1) * wide))
            tile = coupling[at]
            coupling[at] = jnp.where(pattern[j, i] == 1, tile, jnp.zeros_like(tile))


def pairs_kernel(owner_in, blocks_in, green, inject_in, out, owner, blocks, inject, held, product, slot_of, counts, sem, side):
    energies, orbitals, _ = green.shape
    sections = out.shape[0]
    count = owner.shape[0]
    named = held.shape[1] < orbitals
    small = [
        pltpu.make_async_copy(src, dst, side.at[k])
        for k, (src, dst) in enumerate(((owner_in, owner), (blocks_in, blocks), (inject_in, inject)))
    ]
    for move in small:
        move.start()

    def copy_of(e, q):
        first = pl.multiple_of(blocks[0, q] * BLK, BLK)
        to = pl.multiple_of(q * BLK, BLK)
        return pltpu.make_async_copy(green.at[e, pl.ds(first, BLK)], held.at[e, pl.ds(to, BLK)], sem.at[e])

    def whole(e):
        return pltpu.make_async_copy(green.at[e], held.at[e], sem.at[e])

    if not named:
        for e in range(energies):
            whole(e).start()
    for move in small[:2]:
        move.wait()
    if named:
        for e in range(energies):
            lax.fori_loop(0, count, lambda q, _, e=e: copy_of(e, q).start(), None, unroll=4)
    rows = CAP * energies * BLK
    lane = lax.broadcasted_iota(jnp.int32, (HEAD, out.shape[2]), 1)
    none = jnp.where(lane < CAP, -1.0, 0.0).astype(BF16)

    def blank(d, _):
        counts[d] = 0
        out[d, :rows, :] = jnp.zeros((rows, out.shape[2]), BF16)
        out[d, rows : rows + HEAD, :] = none
        return 0

    lax.fori_loop(0, sections, blank, 0)

    def rank(q, _):
        d = owner[q]
        r = counts[d]
        counts[d] = r + 1
        slot_of[q] = r
        head = out[d, rows : rows + HEAD, :].astype(F32)
        head = jnp.where(lane == r, blocks[1, q].astype(F32), head)
        out[d, rows : rows + HEAD, :] = head.astype(BF16)
        return 0

    lax.fori_loop(0, count, rank, 0)
    small[2].wait()
    for e in range(energies):
        whole_held = pltpu.make_async_copy(green.at[e, pl.ds(0, held.shape[1])], held.at[e], sem.at[e])
        whole_held.wait()
        product[...] = dot(held[e], inject[e]).astype(BF16)

        def fill(q, _):
            first = pl.multiple_of((q if named else blocks[0, q]) * BLK, BLK)
            to = pl.multiple_of((slot_of[q] * energies + e) * BLK, BLK)
            out[owner[q], pl.ds(to, BLK), :] = product[pl.ds(first, BLK), :]
            return 0

        lax.fori_loop(0, count, fill, 0, unroll=4)


def outgoing_pairs(owner, blocks, green, inject, sections):
    energies, orbitals, _ = green.shape
    columns = inject.shape[2]
    rows = min(orbitals, owner.shape[0] * BLK)
    return call(
        pairs_kernel,
        "pairs",
        [IN_HBM] * 4,
        shape(sections, CAP * energies * BLK + HEAD, columns),
        [
            pltpu.SMEM(owner.shape, jnp.int32),
            pltpu.SMEM(blocks.shape, jnp.int32),
            pltpu.VMEM(inject.shape, BF16),
            pltpu.VMEM((energies, rows, orbitals), BF16),
            pltpu.VMEM((rows, columns), BF16),
            pltpu.SMEM(owner.shape, jnp.int32),
            pltpu.SMEM((sections,), jnp.int32),
            pltpu.SemaphoreType.DMA((energies,)),
            pltpu.SemaphoreType.DMA((3,)),
        ],
        4.0,
        VMEM_WHOLE,
    )(owner, blocks, green, inject)


def maps_kernel(pattern, green, coupling, own, other, *refs):
    face_rows, (couple, maps) = refs[:-2], refs[-2:]
    energies, orbitals, _ = green.shape
    face = coupling.shape[1]
    couple[...] = coupling[...]
    mask_tiles(pattern, couple)
    for e in range(energies):
        rows = green[e, orbitals - face :, :]
        face_rows[e][...] = rows
        maps[e] = dot(rows, couple[...])
    mine = place() // CORES
    own[...] = maps[mine]
    other[...] = maps[1 - mine]


def face_maps(pattern, green, coupling):
    orbitals, face = coupling.shape
    square = shape(face, face, dtype=F32)
    return call(
        maps_kernel,
        "face_maps",
        [IN_SMEM, IN_VMEM, IN_VMEM],
        [square, square] + [shape(face, orbitals)] * green.shape[0],
        [pltpu.VMEM(coupling.shape, BF16), pltpu.VMEM((green.shape[0], face, face), F32)],
        1.2,
    )(pattern, green, coupling)


def prop_kernel(pattern, green, coupling, _tie, out, couple):
    couple[...] = coupling[...]
    mask_tiles(pattern, couple)
    for e in range(green.shape[0]):
        out[e] = dot(green[e], couple[...]).astype(BF16)


def propagator(pattern, green, coupling, tie):
    energies, orbitals, _ = green.shape
    return call(
        prop_kernel,
        "prop",
        [IN_SMEM, IN_VMEM, IN_VMEM, IN_PLACE],
        shape(energies, orbitals, coupling.shape[1]),
        [pltpu.VMEM(coupling.shape, BF16)],
        1.5,
    )(pattern, green, coupling, tie)


def times(a, b):
    return dot(a[0], b[0]) + (dot(a[0], b[1]) + dot(a[1], b[0]))


def chain_kernel(own, far, across, near, total_out, parts, maps):
    collect((own, far, across, near), maps)
    split = [two_parts(maps[j]) for j in range(GROUP)]
    lower, upper = two_parts(times(split[1], split[0])), two_parts(times(split[3], split[2]))
    total_out[...] = times(upper, lower).astype(total_out.dtype)
    for j, (high, low) in enumerate(split):
        parts[0, j] = high
        parts[1, j] = low


def chain(maps, dtype):
    face = maps[0].shape[0]
    return call(
        chain_kernel,
        "chain_maps",
        [IN_VMEM] * GROUP,
        [shape(face, face, dtype=dtype), shape(2, GROUP, face, face)],
        [pltpu.VMEM((GROUP, face, face), F32)],
        0.9,
    )(*maps)


def source_kernel(received, inject, *refs):
    energies, orbitals, columns = inject.shape
    face_rows = refs[:energies]
    source, own, far, across, near, quarters, total, heads, targets, sem = refs[energies:]
    sections = received.shape[0]
    wide_rows = quarters.shape[1]
    rows = CAP * energies * BLK

    def read(s, _):
        block = received[s, rows : rows + HEAD, :].astype(F32)
        heads[pl.ds(s, 1), :] = block[:1].astype(jnp.int32)
        return 0

    lax.fori_loop(0, sections, read, 0, unroll=min(sections, 8))
    fetch = pltpu.make_async_copy(heads, targets, sem)
    fetch.start()
    total[...] = inject[...].astype(F32)
    fetch.wait()

    def add(s, _):
        for r in range(CAP):
            first = pl.multiple_of(jnp.maximum(targets[s, r], 0) * BLK, BLK)
            for e in range(energies):
                item = received[s, (r * energies + e) * BLK : (r * energies + e + 1) * BLK, :]
                total[e, pl.ds(first, BLK), :] += item.astype(F32)
        return 0

    lax.fori_loop(0, sections, add, 0, unroll=2)
    split = GROUP // energies
    for e in range(energies):
        source[e] = total[e].astype(BF16)
        tall = dot(face_rows[e][...], source[e])
        wide = tall.T
        for h in range(split):
            quarters[e * split + h] = wide[h * wide_rows : (h + 1) * wide_rows]
    for out, at in zip((own, far, across, near), partners()):
        out[...] = quarters[at].astype(BF16)


def after_kernel(_packets, _map, _same_map):
    pass


def handed_on(item, packets):
    return call(
        after_kernel,
        "after_exchange",
        [IN_PLACE] * 2,
        [shape(*item.shape, dtype=item.dtype)],
        [],
        0.1,
        aliases={1: 0},
    )(packets, item)[0]


def placed_source(received, inject, face_rows):
    face = face_rows[0].shape[0]
    energies, orbitals, columns = inject.shape
    sections = received.shape[0]
    return call(
        source_kernel,
        "source_and_face",
        [IN_VMEM] * (2 + energies),
        [shape(*inject.shape)] + [shape(columns * energies // GROUP, face)] * GROUP,
        [
            pltpu.VMEM((GROUP, columns * energies // GROUP, face), F32),
            pltpu.VMEM(inject.shape, F32),
            pltpu.VMEM((sections, columns), jnp.int32),
            pltpu.SMEM((sections, columns), jnp.int32),
            pltpu.SemaphoreType.DMA,
        ],
        1.4,
    )(received, inject, *face_rows)


def collect(refs, held):
    for ref, at in zip(refs, partners()):
        held[at] = ref[...]


def total_kernel(own, far, across, near, parts, _image, out, local, shifts):
    collect((own, far, across, near), shifts)
    state = shifts[0].astype(F32)
    for j in range(1, GROUP):
        local[j - 1] = state
        state = shifts[j].astype(F32) + step_by(state, (parts[0, j], parts[1, j]))
    out[...] = state.astype(BF16)


def plane_total(shifts, parts, tie):
    rows, face = shifts[0].shape
    return call(
        total_kernel,
        "plane_total",
        [IN_VMEM] * (GROUP + 1) + [IN_PLACE],
        [shape(rows, face), shape(GROUP - 1, rows, face, dtype=F32)],
        [pltpu.VMEM((GROUP, rows, face), BF16)],
        3.0,
    )(*shifts, parts, tie)


def work_kernel(early, *refs):
    green, source, parts = refs[:3]
    held, (image, upto) = refs[3:-2], refs[-2:]
    low_plane = lax.axis_index("sec") // GROUP == 0

    @pl.when(low_plane if early else jnp.logical_not(low_plane))
    def _():
        for e in range(green.shape[0]):
            image[e] = dot(green[e], source[e])
        maps = (parts[0, 0], parts[1, 0])
        for j in range(1, GROUP - 1):
            maps = two_parts(times((parts[0, j], parts[1, j]), maps))
            upto[0, j - 1], upto[1, j - 1] = maps

    if held:

        @pl.when(low_plane)
        def _():
            image[...] = held[0][...]
            upto[...] = held[1][...]


def image_and_maps(green, source, parts, held=()):
    _, _, face, _ = parts.shape
    return call(
        functools.partial(work_kernel, not held),
        "image_and_maps",
        [IN_VMEM] * (3 + len(held)),
        [shape(*source.shape, dtype=F32), shape(2, GROUP - 2, face, face)],
        [],
        2.0,
    )(green, source, parts, *held)


def sweep_plane(state, parts, upto, local, out):
    held = [state]
    for j in range(1, GROUP):
        maps = (parts[0, 0], parts[1, 0]) if j == 1 else (upto[0, j - 2], upto[1, j - 2])
        held.append(local[j - 1] + step_by(state, maps))
    work = out[GROUP]
    for j, item in enumerate(held):
        work[j] = item
    for ref, at in zip(out, partners()):
        ref[...] = work[at].astype(BF16)


def entering_kernel(third, near_one, second, far_one, got, other, parts, upto, local, *out):
    first_core = place() % CORES == 0
    first = near_one[...].astype(F32) + far_one[...].astype(F32)
    state = third[...].astype(F32)
    rows = state.shape[0]
    for below, (one, two) in ((second[...].astype(F32), (other, got)), (first, (got, other))):
        factor = jnp.where(first_core, one[...], two[...])
        y = dot_rows(jnp.concatenate(two_parts(state), axis=0), factor)
        state = below + (y[:rows] + y[rows:])
    sweep_plane(state, parts, upto, local, out)


def entering_from_kernel(base, parts, upto, local, *out):
    sweep_plane(base[...], parts, upto, local, out)


def entering(body, args):
    half, columns = args[0].shape
    return call(
        body,
        "entering",
        [IN_VMEM] * len(args),
        [shape(half, columns)] * GROUP,
        [pltpu.VMEM((GROUP, half, columns), F32)],
        1.4,
    )(*args)


def waves_kernel(own, far, across, near, prop, image, out, arrived, wave, sem):
    collect((own, far, across, near), arrived)
    energies, orbitals, _ = prop.shape
    split = GROUP // energies
    pieces = sem.shape[1]
    size = orbitals // pieces
    moves = []
    for e in range(energies):
        incoming = jnp.concatenate([arrived[e * split + h] for h in range(split)], axis=0)
        for c in range(pieces):
            at = slice(c * size, (c + 1) * size)
            wave[e, at, :] = (dot_rows(prop[e, at, :], incoming) + image[e, at, :]).astype(BF16)
            moves.append(pltpu.make_async_copy(wave.at[e, pl.ds(c * size, size)], out.at[e, pl.ds(c * size, size)], sem.at[e, c]))
            moves[-1].start()
    for move in moves:
        move.wait()


def final_waves(arrived, prop, image):
    half, columns = arrived[0].shape
    energies = prop.shape[0]
    return pl.pallas_call(
        waves_kernel,
        name="waves",
        in_specs=[IN_VMEM] * (GROUP + 2),
        out_shape=shape(*image.shape),
        out_specs=IN_HBM,
        scratch_shapes=[
            pltpu.VMEM((GROUP, half, columns), BF16),
            pltpu.VMEM(image.shape, BF16),
            pltpu.SemaphoreType.DMA((energies, 2)),
        ],
        compiler_params=pltpu.CompilerParams(vmem_limit_bytes=VMEM_SMALL),
        cost_estimate=pl.CostEstimate(flops=int(1.3 * PEAK), bytes_accessed=0, transcendentals=0),
    )(*arrived, prop, image)


def to_near(item, sections):
    return lax.ppermute(item, "sec", [(s, s ^ 1) for s in range(sections)])


def to_across(item, sections):
    return lax.ppermute(item, "sec", [(s, s // GROUP * GROUP + (s % GROUP + CORES) % GROUP) for s in range(sections)])


def to_far(item, sections):
    return lax.ppermute(item, "sec", [(s, s // GROUP * GROUP + (s % GROUP + CORES) % GROUP ^ 1) for s in range(sections)])


def exchange(own, far, across, near, sections):
    return [own, to_far(far, sections), to_across(across, sections), to_near(near, sections)]


def up_shift(sections, k):
    return [(s, s + GROUP * k) for s in range(sections - GROUP * k)]


def maps_up(total_map, sections):
    pairs = []
    for i in range(GROUP):
        if i % CORES == 0:
            pairs += [(GROUP + i, 2 * GROUP + i), (2 * GROUP + i, 3 * GROUP + i)]
        else:
            pairs += [(GROUP + i, 3 * GROUP + i)]
    got = lax.ppermute(total_map, "sec", pairs)
    return got, lax.ppermute(got, "sec", [(s, s ^ 1) for s in range(2 * GROUP, sections)])


def between(item, *planes):
    pairs = [(p * GROUP + i, q * GROUP + i) for p, q in planes for i in range(GROUP)]
    return lax.ppermute(item, "sec", pairs)


def scan_below(total_map, total, sections):
    shift = lax.ppermute(total.astype(F32), "sec", up_shift(sections, 1))
    joined = lax.ppermute(total_map, "sec", up_shift(sections, 1))
    stride = 1
    while stride < sections // GROUP:
        other = lax.ppermute(shift, "sec", up_shift(sections, stride))
        other_map = lax.ppermute(joined, "sec", up_shift(sections, stride))
        shift = shift + dot_wide(other, joined.T)
        joined = dot_wide(joined, other_map)
        stride *= 2
    return shift


def per_device(green, injected, coupling, pattern, owner, pair_blocks):
    sections = lax.axis_size("sec")
    green, inject = green[0], injected[0]

    coupling, tiles = coupling[0], pattern[0].T
    outgoing = outgoing_pairs(owner[:, 0], pair_blocks.T, green, inject, sections)
    received = lax.all_to_all(outgoing, "sec", split_axis=0, concat_axis=0, tiled=True)

    own_map, other_map, *face_rows = face_maps(tiles, green, coupling)
    across = to_across(other_map, sections)

    source, *quarters = placed_source(received, inject, face_rows)
    shifts = exchange(*quarters, sections)
    across = handed_on(across, quarters[0])
    near, far = to_near(handed_on(own_map, quarters[0]), sections), to_near(across, sections)
    four = sections // GROUP == 4
    total_map, parts = chain([own_map, far, across, near], BF16 if four else F32)
    early = image_and_maps(green, source, parts)
    maps = maps_up(total_map, sections) if four else []
    total, local = plane_total(shifts, parts, early[0])
    if four:
        fourth = between(total, (1, 2), (2, 3))
        third = between(total, (0, 2), (1, 3))
        second = between(total, (0, 1))
        first = between(total, (0, 3))
        image, upto = image_and_maps(green, source, parts, early)
        entered = entering(entering_kernel, (first, second, third, fourth, *maps, parts, upto, local))
    else:
        base = scan_below(total_map, total, sections)
        image, upto = image_and_maps(green, source, parts, early)
        entered = entering(entering_from_kernel, (base, parts, upto, local))
    arrived = exchange(*entered, sections)
    prop = propagator(tiles, green, coupling, entered[0])
    return final_waves(arrived, prop, image)[None]


def solution(mesh):
    in_specs = (
        P("sec", "grp", None, None),
        P("sec", "grp", None, None),
        P("sec", None, None),
        P("sec", None, None),
        P("sec", None),
        P("sec", None),
    )
    out_specs = P("sec", "grp", None, None)
    return jax.shard_map(
        per_device, mesh=mesh, in_specs=in_specs, out_specs=out_specs, check_vma=False
    )
```

```python
import functools

import jax
import jax.numpy as jnp
from jax import lax
from jax.experimental import pallas as pl
from jax.experimental.pallas import tpu as pltpu
from jax.sharding import PartitionSpec as P

BLK = 32
CAP = 2
GROUP = 4
HEAD = 8
CORES = 2

HIGH = lax.Precision.HIGHEST
F32 = jnp.float32
BF16 = jnp.bfloat16
VMEM_SMALL = 16 * 1024 * 1024
VMEM_WHOLE = 63400000
PEAK = 1.15e9

IN_VMEM = pl.BlockSpec(memory_space=pltpu.VMEM)
IN_SMEM = pl.BlockSpec(memory_space=pltpu.SMEM)
IN_HBM = pl.BlockSpec(memory_space=pltpu.HBM)
IN_PLACE = pl.BlockSpec(memory_space=pl.ANY)


def shape(*dims, dtype=BF16):
    return jax.ShapeDtypeStruct(dims, dtype)


def call(body, name, ins, outs, scratch, micros, vmem=VMEM_SMALL, aliases=None):
    places = list(range(len(outs))) if isinstance(outs, list) else 0
    return pl.pallas_call(
        body,
        name=name,
        in_specs=ins,
        out_shape=outs,
        out_specs=jax.tree.map(lambda k: IN_PLACE if k in (aliases or {}).values() else IN_VMEM, places),
        input_output_aliases=aliases or {},
        scratch_shapes=scratch,
        compiler_params=pltpu.CompilerParams(vmem_limit_bytes=vmem),
        cost_estimate=pl.CostEstimate(flops=int(micros * PEAK), bytes_accessed=0, transcendentals=0),
    )


def place():
    return lax.axis_index("sec") % GROUP


def partners():
    here = place()
    across = (here + CORES) % GROUP
    return here, across ^ 1, across, here ^ 1


def dot(a, b):
    return jnp.dot(a, b, preferred_element_type=F32)


def dot_wide(a, b):
    return jnp.dot(a, b, precision=HIGH, preferred_element_type=F32)


def two_parts(x):
    high = x.astype(BF16)
    return high, (x - high.astype(F32)).astype(BF16)


def dot_rows(a, b):
    return lax.dot_general(a, b, (((1,), (1,)), ((), ())), preferred_element_type=F32)


def step_by(state, maps):
    high, low = two_parts(state)
    rows = state.shape[0]
    y = dot_rows(jnp.concatenate([high, low], axis=0), maps[0])
    return y[:rows] + (y[rows:] + dot_rows(high, maps[1]))


def mask_tiles(pattern, coupling):
    high, wide = coupling.shape[0] // pattern.shape[1], coupling.shape[1] // pattern.shape[0]
    for i in range(pattern.shape[1]):
        for j in range(pattern.shape[0]):
            at = (slice(i * high, (i + 1) * high), slice(j * wide, (j + 1) * wide))
            tile = coupling[at]
            coupling[at] = jnp.where(pattern[j, i] == 1, tile, jnp.zeros_like(tile))


def pairs_kernel(owner_in, blocks_in, green, inject_in, out, owner, blocks, inject, held, product, slot_of, counts, sem, side):
    energies, orbitals, _ = green.shape
    sections = out.shape[0]
    count = owner.shape[0]
    named = held.shape[1] < orbitals
    small = [
        pltpu.make_async_copy(src, dst, side.at[k])
        for k, (src, dst) in enumerate(((owner_in, owner), (blocks_in, blocks), (inject_in, inject)))
    ]
    for move in small:
        move.start()

    def copy_of(e, q):
        first = pl.multiple_of(blocks[0, q] * BLK, BLK)
        to = pl.multiple_of(q * BLK, BLK)
        return pltpu.make_async_copy(green.at[e, pl.ds(first, BLK)], held.at[e, pl.ds(to, BLK)], sem.at[e])

    def whole(e):
        return pltpu.make_async_copy(green.at[e], held.at[e], sem.at[e])

    if not named:
        for e in range(energies):
            whole(e).start()
    for move in small[:2]:
        move.wait()
    if named:
        for e in range(energies):
            lax.fori_loop(0, count, lambda q, _, e=e: copy_of(e, q).start(), None, unroll=4)
    rows = CAP * energies * BLK
    lane = lax.broadcasted_iota(jnp.int32, (HEAD, out.shape[2]), 1)
    none = jnp.where(lane < CAP, -1.0, 0.0).astype(BF16)

    def blank(d, _):
        counts[d] = 0
        out[d, :rows, :] = jnp.zeros((rows, out.shape[2]), BF16)
        out[d, rows : rows + HEAD, :] = none
        return 0

    lax.fori_loop(0, sections, blank, 0)

    def rank(q, _):
        d = owner[q]
        r = counts[d]
        counts[d] = r + 1
        slot_of[q] = r
        head = out[d, rows : rows + HEAD, :].astype(F32)
        head = jnp.where(lane == r, blocks[1, q].astype(F32), head)
        out[d, rows : rows + HEAD, :] = head.astype(BF16)
        return 0

    lax.fori_loop(0, count, rank, 0)
    small[2].wait()
    for e in range(energies):
        whole_held = pltpu.make_async_copy(green.at[e, pl.ds(0, held.shape[1])], held.at[e], sem.at[e])
        whole_held.wait()
        product[...] = dot(held[e], inject[e]).astype(BF16)

        def fill(q, _):
            first = pl.multiple_of((q if named else blocks[0, q]) * BLK, BLK)
            to = pl.multiple_of((slot_of[q] * energies + e) * BLK, BLK)
            out[owner[q], pl.ds(to, BLK), :] = product[pl.ds(first, BLK), :]
            return 0

        lax.fori_loop(0, count, fill, 0, unroll=4)


def outgoing_pairs(owner, blocks, green, inject, sections):
    energies, orbitals, _ = green.shape
    columns = inject.shape[2]
    rows = min(orbitals, owner.shape[0] * BLK)
    return call(
        pairs_kernel,
        "pairs",
        [IN_HBM] * 4,
        shape(sections, CAP * energies * BLK + HEAD, columns),
        [
            pltpu.SMEM(owner.shape, jnp.int32),
            pltpu.SMEM(blocks.shape, jnp.int32),
            pltpu.VMEM(inject.shape, BF16),
            pltpu.VMEM((energies, rows, orbitals), BF16),
            pltpu.VMEM((rows, columns), BF16),
            pltpu.SMEM(owner.shape, jnp.int32),
            pltpu.SMEM((sections,), jnp.int32),
            pltpu.SemaphoreType.DMA((energies,)),
            pltpu.SemaphoreType.DMA((3,)),
        ],
        4.0,
        VMEM_WHOLE,
    )(owner, blocks, green, inject)


def maps_kernel(pattern, green, coupling, own, other, *refs):
    face_rows, (couple, maps) = refs[:-2], refs[-2:]
    energies, orbitals, _ = green.shape
    face = coupling.shape[1]
    couple[...] = coupling[...]
    mask_tiles(pattern, couple)
    for e in range(energies):
        rows = green[e, orbitals - face :, :]
        face_rows[e][...] = rows
        maps[e] = dot(rows, couple[...])
    mine = place() // CORES
    own[...] = maps[mine]
    other[...] = maps[1 - mine]


def face_maps(pattern, green, coupling):
    orbitals, face = coupling.shape
    square = shape(face, face, dtype=F32)
    return call(
        maps_kernel,
        "face_maps",
        [IN_SMEM, IN_VMEM, IN_VMEM],
        [square, square] + [shape(face, orbitals)] * green.shape[0],
        [pltpu.VMEM(coupling.shape, BF16), pltpu.VMEM((green.shape[0], face, face), F32)],
        1.2,
    )(pattern, green, coupling)


def prop_kernel(pattern, green, coupling, _tie, out, couple):
    couple[...] = coupling[...]
    mask_tiles(pattern, couple)
    for e in range(green.shape[0]):
        out[e] = dot(green[e], couple[...]).astype(BF16)


def propagator(pattern, green, coupling, tie):
    energies, orbitals, _ = green.shape
    return call(
        prop_kernel,
        "prop",
        [IN_SMEM, IN_VMEM, IN_VMEM, IN_PLACE],
        shape(energies, orbitals, coupling.shape[1]),
        [pltpu.VMEM(coupling.shape, BF16)],
        1.5,
    )(pattern, green, coupling, tie)


def times(a, b):
    return dot(a[0], b[0]) + (dot(a[0], b[1]) + dot(a[1], b[0]))


def chain_kernel(own, far, across, near, total_out, parts, maps):
    collect((own, far, across, near), maps)
    split = [two_parts(maps[j]) for j in range(GROUP)]
    lower, upper = two_parts(times(split[1], split[0])), two_parts(times(split[3], split[2]))
    total_out[...] = times(upper, lower).astype(total_out.dtype)
    for j, (high, low) in enumerate(split):
        parts[0, j] = high
        parts[1, j] = low


def chain(maps, dtype):
    face = maps[0].shape[0]
    return call(
        chain_kernel,
        "chain_maps",
        [IN_VMEM] * GROUP,
        [shape(face, face, dtype=dtype), shape(2, GROUP, face, face)],
        [pltpu.VMEM((GROUP, face, face), F32)],
        0.9,
    )(*maps)


def source_kernel(received, inject, source, heads, targets, total, sem):
    energies, orbitals, columns = inject.shape
    sections = received.shape[0]
    rows = CAP * energies * BLK

    def read(s, _):
        block = received[s, rows : rows + HEAD, :].astype(F32)
        heads[pl.ds(s, 1), :] = block[:1].astype(jnp.int32)
        return 0

    lax.fori_loop(0, sections, read, 0, unroll=min(sections, 8))
    fetch = pltpu.make_async_copy(heads, targets, sem)
    fetch.start()
    total[...] = inject[...].astype(F32)
    fetch.wait()

    def add(s, _):
        for r in range(CAP):
            first = pl.multiple_of(jnp.maximum(targets[s, r], 0) * BLK, BLK)
            for e in range(energies):
                item = received[s, (r * energies + e) * BLK : (r * energies + e + 1) * BLK, :]
                total[e, pl.ds(first, BLK), :] += item.astype(F32)
        return 0

    lax.fori_loop(0, sections, add, 0, unroll=2)
    source[...] = total[...].astype(BF16)


def placed_source(received, inject):
    energies, orbitals, columns = inject.shape
    sections = received.shape[0]
    return call(
        source_kernel,
        "source",
        [IN_VMEM] * 2,
        shape(*inject.shape),
        [
            pltpu.VMEM((sections, columns), jnp.int32),
            pltpu.SMEM((sections, columns), jnp.int32),
            pltpu.VMEM(inject.shape, F32),
            pltpu.SemaphoreType.DMA,
        ],
        1.0,
    )(received, inject)


def quarters_kernel(source, *refs):
    energies = source.shape[0]
    face_rows = refs[:energies]
    own, far, across, near, quarters = refs[energies:]
    split = GROUP // energies
    size = quarters.shape[1]
    for e in range(energies):
        wide = dot(face_rows[e][...], source[e]).T
        for h in range(split):
            quarters[e * split + h] = wide[h * size : (h + 1) * size]
    for out, at in zip((own, far, across, near), partners()):
        out[...] = quarters[at].astype(BF16)


def face_quarters(source, face_rows):
    energies, _, columns = source.shape
    face = face_rows[0].shape[0]
    rows = columns * energies // GROUP
    return call(
        quarters_kernel,
        "face_quarters",
        [IN_VMEM] * (1 + energies),
        [shape(rows, face)] * GROUP,
        [pltpu.VMEM((GROUP, rows, face), F32)],
        0.6,
    )(source, *face_rows)


def after_kernel(_packets, _map, _same_map):
    pass


def handed_on(item, packets):
    return call(
        after_kernel,
        "after_exchange",
        [IN_PLACE] * 2,
        [shape(*item.shape, dtype=item.dtype)],
        [],
        0.1,
        aliases={1: 0},
    )(packets, item)[0]


def collect(refs, held):
    for ref, at in zip(refs, partners()):
        held[at] = ref[...]


def total_kernel(own, far, across, near, parts, _image, out, local, shifts):
    collect((own, far, across, near), shifts)
    state = shifts[0].astype(F32)
    for j in range(1, GROUP):
        local[j - 1] = state
        state = shifts[j].astype(F32) + step_by(state, (parts[0, j], parts[1, j]))
    out[...] = state.astype(BF16)


def plane_total(shifts, parts, tie):
    rows, face = shifts[0].shape
    return call(
        total_kernel,
        "plane_total",
        [IN_VMEM] * (GROUP + 1) + [IN_PLACE],
        [shape(rows, face), shape(GROUP - 1, rows, face, dtype=F32)],
        [pltpu.VMEM((GROUP, rows, face), BF16)],
        3.0,
    )(*shifts, parts, tie)


def work_kernel(early, *refs):
    green, source, parts = refs[:3]
    held, (image, upto) = refs[3:-2], refs[-2:]
    low_plane = lax.axis_index("sec") // GROUP == 0

    @pl.when(low_plane if early else jnp.logical_not(low_plane))
    def _():
        for e in range(green.shape[0]):
            image[e] = dot(green[e], source[e])
        maps = (parts[0, 0], parts[1, 0])
        for j in range(1, GROUP - 1):
            maps = two_parts(times((parts[0, j], parts[1, j]), maps))
            upto[0, j - 1], upto[1, j - 1] = maps

    if held:

        @pl.when(low_plane)
        def _():
            image[...] = held[0][...]
            upto[...] = held[1][...]


def image_and_maps(green, source, parts, held=()):
    _, _, face, _ = parts.shape
    return call(
        functools.partial(work_kernel, not held),
        "image_and_maps",
        [IN_VMEM] * (3 + len(held)),
        [shape(*source.shape, dtype=F32), shape(2, GROUP - 2, face, face)],
        [],
        2.0,
    )(green, source, parts, *held)


def sweep_plane(state, parts, upto, local, out):
    held = [state]
    for j in range(1, GROUP):
        maps = (parts[0, 0], parts[1, 0]) if j == 1 else (upto[0, j - 2], upto[1, j - 2])
        held.append(local[j - 1] + step_by(state, maps))
    work = out[GROUP]
    for j, item in enumerate(held):
        work[j] = item
    for ref, at in zip(out, partners()):
        ref[...] = work[at].astype(BF16)


def entering_kernel(third, near_one, second, far_one, got, other, parts, upto, local, *out):
    first_core = place() % CORES == 0
    first = near_one[...].astype(F32) + far_one[...].astype(F32)
    state = third[...].astype(F32)
    rows = state.shape[0]
    for below, (one, two) in ((second[...].astype(F32), (other, got)), (first, (got, other))):
        factor = jnp.where(first_core, one[...], two[...])
        y = dot_rows(jnp.concatenate(two_parts(state), axis=0), factor)
        state = below + (y[:rows] + y[rows:])
    sweep_plane(state, parts, upto, local, out)


def entering_from_kernel(base, parts, upto, local, *out):
    sweep_plane(base[...], parts, upto, local, out)


def entering(body, args):
    half, columns = args[0].shape
    return call(
        body,
        "entering",
        [IN_VMEM] * len(args),
        [shape(half, columns)] * GROUP,
        [pltpu.VMEM((GROUP, half, columns), F32)],
        1.4,
    )(*args)


def waves_kernel(own, far, across, near, prop, image, out, arrived, wave, sem):
    collect((own, far, across, near), arrived)
    energies, orbitals, _ = prop.shape
    split = GROUP // energies
    pieces = sem.shape[1]
    size = orbitals // pieces
    moves = []
    for e in range(energies):
        incoming = jnp.concatenate([arrived[e * split + h] for h in range(split)], axis=0)
        for c in range(pieces):
            at = slice(c * size, (c + 1) * size)
            wave[e, at, :] = (dot_rows(prop[e, at, :], incoming) + image[e, at, :]).astype(BF16)
            moves.append(pltpu.make_async_copy(wave.at[e, pl.ds(c * size, size)], out.at[e, pl.ds(c * size, size)], sem.at[e, c]))
            moves[-1].start()
    for move in moves:
        move.wait()


def final_waves(arrived, prop, image):
    half, columns = arrived[0].shape
    energies = prop.shape[0]
    return pl.pallas_call(
        waves_kernel,
        name="waves",
        in_specs=[IN_VMEM] * (GROUP + 2),
        out_shape=shape(*image.shape),
        out_specs=IN_HBM,
        scratch_shapes=[
            pltpu.VMEM((GROUP, half, columns), BF16),
            pltpu.VMEM(image.shape, BF16),
            pltpu.SemaphoreType.DMA((energies, 2)),
        ],
        compiler_params=pltpu.CompilerParams(vmem_limit_bytes=VMEM_SMALL),
        cost_estimate=pl.CostEstimate(flops=int(1.3 * PEAK), bytes_accessed=0, transcendentals=0),
    )(*arrived, prop, image)


def to_near(item, sections):
    return lax.ppermute(item, "sec", [(s, s ^ 1) for s in range(sections)])


def to_across(item, sections):
    return lax.ppermute(item, "sec", [(s, s // GROUP * GROUP + (s % GROUP + CORES) % GROUP) for s in range(sections)])


def to_far(item, sections):
    return lax.ppermute(item, "sec", [(s, s // GROUP * GROUP + (s % GROUP + CORES) % GROUP ^ 1) for s in range(sections)])


def exchange(own, far, across, near, sections):
    return [own, to_far(far, sections), to_across(across, sections), to_near(near, sections)]


def up_shift(sections, k):
    return [(s, s + GROUP * k) for s in range(sections - GROUP * k)]


def maps_up(total_map, sections):
    pairs = []
    for i in range(GROUP):
        if i % CORES == 0:
            pairs += [(GROUP + i, 2 * GROUP + i), (2 * GROUP + i, 3 * GROUP + i)]
        else:
            pairs += [(GROUP + i, 3 * GROUP + i)]
    got = lax.ppermute(total_map, "sec", pairs)
    return got, lax.ppermute(got, "sec", [(s, s ^ 1) for s in range(2 * GROUP, sections)])


def between(item, *planes):
    pairs = [(p * GROUP + i, q * GROUP + i) for p, q in planes for i in range(GROUP)]
    return lax.ppermute(item, "sec", pairs)


def scan_below(total_map, total, sections):
    shift = lax.ppermute(total.astype(F32), "sec", up_shift(sections, 1))
    joined = lax.ppermute(total_map, "sec", up_shift(sections, 1))
    stride = 1
    while stride < sections // GROUP:
        other = lax.ppermute(shift, "sec", up_shift(sections, stride))
        other_map = lax.ppermute(joined, "sec", up_shift(sections, stride))
        shift = shift + dot_wide(other, joined.T)
        joined = dot_wide(joined, other_map)
        stride *= 2
    return shift


def per_device(green, injected, coupling, pattern, owner, pair_blocks):
    sections = lax.axis_size("sec")
    green, inject = green[0], injected[0]

    coupling, tiles = coupling[0], pattern[0].T
    outgoing = outgoing_pairs(owner[:, 0], pair_blocks.T, green, inject, sections)
    received = lax.all_to_all(outgoing, "sec", split_axis=0, concat_axis=0, tiled=True)

    own_map, other_map, *face_rows = face_maps(tiles, green, coupling)
    across = to_across(other_map, sections)
    near = to_near(own_map, sections)

    source = placed_source(received, inject)
    quarters = face_quarters(source, face_rows)
    shifts = exchange(*quarters, sections)
    across = handed_on(across, quarters[0])
    far = to_near(across, sections)
    four = sections // GROUP == 4
    total_map, parts = chain([own_map, far, across, near], BF16 if four else F32)
    early = image_and_maps(green, source, parts)
    maps = maps_up(total_map, sections) if four else []
    total, local = plane_total(shifts, parts, early[0])
    if four:
        fourth = between(total, (1, 2), (2, 3))
        third = between(total, (0, 2), (1, 3))
        second = between(total, (0, 1))
        first = between(total, (0, 3))
        image, upto = image_and_maps(green, source, parts, early)
        entered = entering(entering_kernel, (first, second, third, fourth, *maps, parts, upto, local))
    else:
        base = scan_below(total_map, total, sections)
        image, upto = image_and_maps(green, source, parts, early)
        entered = entering(entering_from_kernel, (base, parts, upto, local))
    arrived = exchange(*entered, sections)
    prop = propagator(tiles, green, coupling, entered[0])
    return final_waves(arrived, prop, image)[None]


def solution(mesh):
    in_specs = (
        P("sec", "grp", None, None),
        P("sec", "grp", None, None),
        P("sec", None, None),
        P("sec", None, None),
        P("sec", None),
        P("sec", None),
    )
    out_specs = P("sec", "grp", None, None)
    return jax.shard_map(
        per_device, mesh=mesh, in_specs=in_specs, out_specs=out_specs, check_vma=False
    )
```

```python
import functools

import jax
import jax.numpy as jnp
from jax import lax
from jax.experimental import pallas as pl
from jax.experimental.pallas import tpu as pltpu
from jax.sharding import PartitionSpec as P

BLK = 32
CAP = 2
GROUP = 4
HEAD = 8
CORES = 2

HIGH = lax.Precision.HIGHEST
F32 = jnp.float32
BF16 = jnp.bfloat16
VMEM_SMALL = 16 * 1024 * 1024
VMEM_WHOLE = 63400000
PEAK = 1.15e9

IN_VMEM = pl.BlockSpec(memory_space=pltpu.VMEM)
IN_SMEM = pl.BlockSpec(memory_space=pltpu.SMEM)
IN_HBM = pl.BlockSpec(memory_space=pltpu.HBM)
IN_PLACE = pl.BlockSpec(memory_space=pl.ANY)


def shape(*dims, dtype=BF16):
    return jax.ShapeDtypeStruct(dims, dtype)


def call(body, name, ins, outs, scratch, micros, vmem=VMEM_SMALL, aliases=None):
    places = list(range(len(outs))) if isinstance(outs, list) else 0
    return pl.pallas_call(
        body,
        name=name,
        in_specs=ins,
        out_shape=outs,
        out_specs=jax.tree.map(lambda k: IN_PLACE if k in (aliases or {}).values() else IN_VMEM, places),
        input_output_aliases=aliases or {},
        scratch_shapes=scratch,
        compiler_params=pltpu.CompilerParams(vmem_limit_bytes=vmem),
        cost_estimate=pl.CostEstimate(flops=int(micros * PEAK), bytes_accessed=0, transcendentals=0),
    )


def place():
    return lax.axis_index("sec") % GROUP


def partners():
    here = place()
    across = (here + CORES) % GROUP
    return here, across ^ 1, across, here ^ 1


def dot(a, b):
    return jnp.dot(a, b, preferred_element_type=F32)


def dot_wide(a, b):
    return jnp.dot(a, b, precision=HIGH, preferred_element_type=F32)


def two_parts(x):
    high = x.astype(BF16)
    return high, (x - high.astype(F32)).astype(BF16)


def dot_rows(a, b):
    return lax.dot_general(a, b, (((1,), (1,)), ((), ())), preferred_element_type=F32)


def step_by(state, maps):
    high, low = two_parts(state)
    rows = state.shape[0]
    y = dot_rows(jnp.concatenate([high, low], axis=0), maps[0])
    return y[:rows] + (y[rows:] + dot_rows(high, maps[1]))


def mask_tiles(pattern, coupling):
    high, wide = coupling.shape[0] // pattern.shape[1], coupling.shape[1] // pattern.shape[0]
    for i in range(pattern.shape[1]):
        for j in range(pattern.shape[0]):
            at = (slice(i * high, (i + 1) * high), slice(j * wide, (j + 1) * wide))
            tile = coupling[at]
            coupling[at] = jnp.where(pattern[j, i] == 1, tile, jnp.zeros_like(tile))


def pairs_kernel(owner_in, blocks_in, green, inject_in, out, owner, blocks, inject, held, product, slot_of, counts, sem, side):
    energies, orbitals, _ = green.shape
    sections = out.shape[0]
    count = owner.shape[0]
    named = held.shape[1] < orbitals
    small = [
        pltpu.make_async_copy(src, dst, side.at[k])
        for k, (src, dst) in enumerate(((owner_in, owner), (blocks_in, blocks), (inject_in, inject)))
    ]
    for move in small:
        move.start()

    def copy_of(e, q):
        first = pl.multiple_of(blocks[0, q] * BLK, BLK)
        to = pl.multiple_of(q * BLK, BLK)
        return pltpu.make_async_copy(green.at[e, pl.ds(first, BLK)], held.at[e, pl.ds(to, BLK)], sem.at[e])

    def whole(e):
        return pltpu.make_async_copy(green.at[e], held.at[e], sem.at[e])

    if not named:
        for e in range(energies):
            whole(e).start()
    for move in small[:2]:
        move.wait()
    if named:
        for e in range(energies):
            lax.fori_loop(0, count, lambda q, _, e=e: copy_of(e, q).start(), None, unroll=4)
    rows = CAP * energies * BLK
    lane = lax.broadcasted_iota(jnp.int32, (HEAD, out.shape[2]), 1)
    none = jnp.where(lane < CAP, -1.0, 0.0).astype(BF16)

    def blank(d, _):
        counts[d] = 0
        out[d, :rows, :] = jnp.zeros((rows, out.shape[2]), BF16)
        out[d, rows : rows + HEAD, :] = none
        return 0

    lax.fori_loop(0, sections, blank, 0)

    def rank(q, _):
        d = owner[q]
        r = counts[d]
        counts[d] = r + 1
        slot_of[q] = r
        head = out[d, rows : rows + HEAD, :].astype(F32)
        head = jnp.where(lane == r, blocks[1, q].astype(F32), head)
        out[d, rows : rows + HEAD, :] = head.astype(BF16)
        return 0

    lax.fori_loop(0, count, rank, 0)
    small[2].wait()
    for e in range(energies):
        whole_held = pltpu.make_async_copy(green.at[e, pl.ds(0, held.shape[1])], held.at[e], sem.at[e])
        whole_held.wait()
        product[...] = dot(held[e], inject[e]).astype(BF16)

        def fill(q, _):
            first = pl.multiple_of((q if named else blocks[0, q]) * BLK, BLK)
            to = pl.multiple_of((slot_of[q] * energies + e) * BLK, BLK)
            out[owner[q], pl.ds(to, BLK), :] = product[pl.ds(first, BLK), :]
            return 0

        lax.fori_loop(0, count, fill, 0, unroll=4)


def outgoing_pairs(owner, blocks, green, inject, sections):
    energies, orbitals, _ = green.shape
    columns = inject.shape[2]
    rows = min(orbitals, owner.shape[0] * BLK)
    return call(
        pairs_kernel,
        "pairs",
        [IN_HBM] * 4,
        shape(sections, CAP * energies * BLK + HEAD, columns),
        [
            pltpu.SMEM(owner.shape, jnp.int32),
            pltpu.SMEM(blocks.shape, jnp.int32),
            pltpu.VMEM(inject.shape, BF16),
            pltpu.VMEM((energies, rows, orbitals), BF16),
            pltpu.VMEM((rows, columns), BF16),
            pltpu.SMEM(owner.shape, jnp.int32),
            pltpu.SMEM((sections,), jnp.int32),
            pltpu.SemaphoreType.DMA((energies,)),
            pltpu.SemaphoreType.DMA((3,)),
        ],
        4.0,
        VMEM_WHOLE,
    )(owner, blocks, green, inject)


def maps_kernel(pattern, green, coupling, own, other, *refs):
    face_rows, (couple, maps) = refs[:-2], refs[-2:]
    energies, orbitals, _ = green.shape
    face = coupling.shape[1]
    couple[...] = coupling[...]
    mask_tiles(pattern, couple)
    for e in range(energies):
        rows = green[e, orbitals - face :, :]
        face_rows[e][...] = rows
        maps[e] = dot(rows, couple[...])
    mine = place() // CORES
    own[...] = maps[mine]
    other[...] = maps[1 - mine]


def face_maps(pattern, green, coupling):
    orbitals, face = coupling.shape
    square = shape(face, face, dtype=F32)
    return call(
        maps_kernel,
        "face_maps",
        [IN_SMEM, IN_VMEM, IN_VMEM],
        [square, square] + [shape(face, orbitals)] * green.shape[0],
        [pltpu.VMEM(coupling.shape, BF16), pltpu.VMEM((green.shape[0], face, face), F32)],
        1.2,
    )(pattern, green, coupling)


def prop_kernel(pattern, green, coupling, _tie, out, couple):
    couple[...] = coupling[...]
    mask_tiles(pattern, couple)
    for e in range(green.shape[0]):
        out[e] = dot(green[e], couple[...]).astype(BF16)


def propagator(pattern, green, coupling, tie):
    energies, orbitals, _ = green.shape
    return call(
        prop_kernel,
        "prop",
        [IN_SMEM, IN_VMEM, IN_VMEM, IN_PLACE],
        shape(energies, orbitals, coupling.shape[1]),
        [pltpu.VMEM(coupling.shape, BF16)],
        1.5,
    )(pattern, green, coupling, tie)


def times(a, b):
    return dot(a[0], b[0]) + (dot(a[0], b[1]) + dot(a[1], b[0]))


def chain_kernel(own, far, across, near, total_out, parts, maps):
    collect((own, far, across, near), maps)
    split = [two_parts(maps[j]) for j in range(GROUP)]
    lower, upper = two_parts(times(split[1], split[0])), two_parts(times(split[3], split[2]))
    total_out[...] = times(upper, lower).astype(total_out.dtype)
    for j, (high, low) in enumerate(split):
        parts[0, j] = high
        parts[1, j] = low


def chain(maps, dtype):
    face = maps[0].shape[0]
    return call(
        chain_kernel,
        "chain_maps",
        [IN_VMEM] * GROUP,
        [shape(face, face, dtype=dtype), shape(2, GROUP, face, face)],
        [pltpu.VMEM((GROUP, face, face), F32)],
        0.9,
    )(*maps)


def source_kernel(received, inject, source, heads, targets, total, sem):
    energies, orbitals, columns = inject.shape
    sections = received.shape[0]
    rows = CAP * energies * BLK

    def read(s, _):
        block = received[s, rows : rows + HEAD, :].astype(F32)
        heads[pl.ds(s, 1), :] = block[:1].astype(jnp.int32)
        return 0

    lax.fori_loop(0, sections, read, 0, unroll=min(sections, 8))
    fetch = pltpu.make_async_copy(heads, targets, sem)
    fetch.start()
    total[...] = inject[...].astype(F32)
    fetch.wait()

    def add(s, _):
        for r in range(CAP):
            first = pl.multiple_of(jnp.maximum(targets[s, r], 0) * BLK, BLK)
            for e in range(energies):
                item = received[s, (r * energies + e) * BLK : (r * energies + e + 1) * BLK, :]
                total[e, pl.ds(first, BLK), :] += item.astype(F32)
        return 0

    lax.fori_loop(0, sections, add, 0, unroll=2)
    source[...] = total[...].astype(BF16)


def placed_source(received, inject):
    energies, orbitals, columns = inject.shape
    sections = received.shape[0]
    return call(
        source_kernel,
        "source",
        [IN_VMEM] * 2,
        shape(*inject.shape),
        [
            pltpu.VMEM((sections, columns), jnp.int32),
            pltpu.SMEM((sections, columns), jnp.int32),
            pltpu.VMEM(inject.shape, F32),
            pltpu.SemaphoreType.DMA,
        ],
        1.0,
    )(received, inject)


def quarters_kernel(source, *refs):
    energies = source.shape[0]
    face_rows = refs[:energies]
    own, far, across, near, quarters = refs[energies:]
    split = GROUP // energies
    size = quarters.shape[1]
    for e in range(energies):
        wide = dot(face_rows[e][...], source[e]).T
        for h in range(split):
            quarters[e * split + h] = wide[h * size : (h + 1) * size]
    for out, at in zip((own, far, across, near), partners()):
        out[...] = quarters[at].astype(BF16)


def face_quarters(source, face_rows):
    energies, _, columns = source.shape
    face = face_rows[0].shape[0]
    rows = columns * energies // GROUP
    return call(
        quarters_kernel,
        "face_quarters",
        [IN_VMEM] * (1 + energies),
        [shape(rows, face)] * GROUP,
        [pltpu.VMEM((GROUP, rows, face), F32)],
        0.6,
    )(source, *face_rows)


def after_kernel(_packets, _map, _same_map):
    pass


def handed_on(item, packets):
    return call(
        after_kernel,
        "after_exchange",
        [IN_PLACE] * 2,
        [shape(*item.shape, dtype=item.dtype)],
        [],
        0.1,
        aliases={1: 0},
    )(packets, item)[0]


def collect(refs, held):
    for ref, at in zip(refs, partners()):
        held[at] = ref[...]


def total_kernel(own, far, across, near, parts, _image, out, local, shifts):
    collect((own, far, across, near), shifts)
    state = shifts[0].astype(F32)
    for j in range(1, GROUP):
        local[j - 1] = state
        state = shifts[j].astype(F32) + step_by(state, (parts[0, j], parts[1, j]))
    out[...] = state.astype(BF16)


def plane_total(shifts, parts, tie):
    rows, face = shifts[0].shape
    return call(
        total_kernel,
        "plane_total",
        [IN_VMEM] * (GROUP + 1) + [IN_PLACE],
        [shape(rows, face), shape(GROUP - 1, rows, face, dtype=F32)],
        [pltpu.VMEM((GROUP, rows, face), BF16)],
        3.0,
    )(*shifts, parts, tie)


def work_kernel(early, *refs):
    green, source, parts = refs[:3]
    held, (image, upto) = refs[3:-2], refs[-2:]
    low_plane = lax.axis_index("sec") // GROUP == 0

    @pl.when(low_plane if early else jnp.logical_not(low_plane))
    def _():
        for e in range(green.shape[0]):
            image[e] = dot(green[e], source[e])
        maps = (parts[0, 0], parts[1, 0])
        for j in range(1, GROUP - 1):
            maps = two_parts(times((parts[0, j], parts[1, j]), maps))
            upto[0, j - 1], upto[1, j - 1] = maps

    if held:

        @pl.when(low_plane)
        def _():
            image[...] = held[0][...]
            upto[...] = held[1][...]


def image_and_maps(green, source, parts, held=()):
    _, _, face, _ = parts.shape
    return call(
        functools.partial(work_kernel, not held),
        "image_and_maps",
        [IN_VMEM] * (3 + len(held)),
        [shape(*source.shape, dtype=F32), shape(2, GROUP - 2, face, face)],
        [],
        2.0,
    )(green, source, parts, *held)


def sweep_plane(state, parts, upto, local, out):
    held = [state]
    for j in range(1, GROUP):
        maps = (parts[0, 0], parts[1, 0]) if j == 1 else (upto[0, j - 2], upto[1, j - 2])
        held.append(local[j - 1] + step_by(state, maps))
    work = out[GROUP]
    for j, item in enumerate(held):
        work[j] = item
    for ref, at in zip(out, partners()):
        ref[...] = work[at].astype(BF16)


def entering_kernel(third, near_one, second, far_one, got, other, parts, upto, local, *out):
    first_core = place() % CORES == 0
    first = near_one[...].astype(F32) + far_one[...].astype(F32)
    state = third[...].astype(F32)
    rows = state.shape[0]
    for below, (one, two) in ((second[...].astype(F32), (other, got)), (first, (got, other))):
        factor = jnp.where(first_core, one[...], two[...])
        y = dot_rows(jnp.concatenate(two_parts(state), axis=0), factor)
        state = below + (y[:rows] + y[rows:])
    sweep_plane(state, parts, upto, local, out)


def entering_from_kernel(base, parts, upto, local, *out):
    sweep_plane(base[...], parts, upto, local, out)


def entering(body, args):
    half, columns = args[0].shape
    return call(
        body,
        "entering",
        [IN_VMEM] * len(args),
        [shape(half, columns)] * GROUP,
        [pltpu.VMEM((GROUP, half, columns), F32)],
        1.4,
    )(*args)


def waves_kernel(own, far, across, near, prop, image, out, arrived, wave, sem):
    collect((own, far, across, near), arrived)
    energies, orbitals, _ = prop.shape
    split = GROUP // energies
    pieces = sem.shape[1]
    size = orbitals // pieces
    moves = []
    for e in range(energies):
        incoming = jnp.concatenate([arrived[e * split + h] for h in range(split)], axis=0)
        for c in range(pieces):
            at = slice(c * size, (c + 1) * size)
            wave[e, at, :] = (dot_rows(prop[e, at, :], incoming) + image[e, at, :]).astype(BF16)
            moves.append(pltpu.make_async_copy(wave.at[e, pl.ds(c * size, size)], out.at[e, pl.ds(c * size, size)], sem.at[e, c]))
            moves[-1].start()
    for move in moves:
        move.wait()


def final_waves(arrived, prop, image):
    half, columns = arrived[0].shape
    energies = prop.shape[0]
    return pl.pallas_call(
        waves_kernel,
        name="waves",
        in_specs=[IN_VMEM] * (GROUP + 2),
        out_shape=shape(*image.shape),
        out_specs=IN_HBM,
        scratch_shapes=[
            pltpu.VMEM((GROUP, half, columns), BF16),
            pltpu.VMEM(image.shape, BF16),
            pltpu.SemaphoreType.DMA((energies, 2)),
        ],
        compiler_params=pltpu.CompilerParams(vmem_limit_bytes=VMEM_SMALL),
        cost_estimate=pl.CostEstimate(flops=int(1.3 * PEAK), bytes_accessed=0, transcendentals=0),
    )(*arrived, prop, image)


def to_near(item, sections):
    return lax.ppermute(item, "sec", [(s, s ^ 1) for s in range(sections)])


def to_across(item, sections):
    return lax.ppermute(item, "sec", [(s, s // GROUP * GROUP + (s % GROUP + CORES) % GROUP) for s in range(sections)])


def to_far(item, sections):
    return lax.ppermute(item, "sec", [(s, s // GROUP * GROUP + (s % GROUP + CORES) % GROUP ^ 1) for s in range(sections)])


def exchange(own, far, across, near, sections):
    return [own, to_far(far, sections), to_across(across, sections), to_near(near, sections)]


def up_shift(sections, k):
    return [(s, s + GROUP * k) for s in range(sections - GROUP * k)]


def maps_up(total_map, sections):
    pairs = []
    for i in range(GROUP):
        if i % CORES == 0:
            pairs += [(GROUP + i, 2 * GROUP + i), (2 * GROUP + i, 3 * GROUP + i)]
        else:
            pairs += [(GROUP + i, 3 * GROUP + i)]
    got = lax.ppermute(total_map, "sec", pairs)
    return got, to_near(got, sections)


def between(item, *planes):
    pairs = [(p * GROUP + i, q * GROUP + i) for p, q in planes for i in range(GROUP)]
    return lax.ppermute(item, "sec", pairs)


def scan_below(total_map, total, sections):
    shift = lax.ppermute(total.astype(F32), "sec", up_shift(sections, 1))
    joined = lax.ppermute(total_map, "sec", up_shift(sections, 1))
    stride = 1
    while stride < sections // GROUP:
        other = lax.ppermute(shift, "sec", up_shift(sections, stride))
        other_map = lax.ppermute(joined, "sec", up_shift(sections, stride))
        shift = shift + dot_wide(other, joined.T)
        joined = dot_wide(joined, other_map)
        stride *= 2
    return shift


def per_device(green, injected, coupling, pattern, owner, pair_blocks):
    sections = lax.axis_size("sec")
    green, inject = green[0], injected[0]

    coupling, tiles = coupling[0], pattern[0].T
    outgoing = outgoing_pairs(owner[:, 0], pair_blocks.T, green, inject, sections)
    received = lax.all_to_all(outgoing, "sec", split_axis=0, concat_axis=0, tiled=True)

    own_map, other_map, *face_rows = face_maps(tiles, green, coupling)
    across = to_across(other_map, sections)
    near = to_near(own_map, sections)

    source = placed_source(received, inject)
    quarters = face_quarters(source, face_rows)
    shifts = exchange(*quarters, sections)
    across = handed_on(across, quarters[0])
    far = to_near(across, sections)
    four = sections // GROUP == 4
    total_map, parts = chain([own_map, far, across, near], BF16 if four else F32)
    early = image_and_maps(green, source, parts)
    maps = maps_up(total_map, sections) if four else []
    total, local = plane_total(shifts, parts, early[0])
    if four:
        fourth = between(total, (1, 2), (2, 3))
        third = between(total, (0, 2), (1, 3))
        second = between(total, (0, 1))
        first = between(total, (0, 3))
        image, upto = image_and_maps(green, source, parts, early)
        entered = entering(entering_kernel, (first, second, third, fourth, *maps, parts, upto, local))
    else:
        base = scan_below(total_map, total, sections)
        image, upto = image_and_maps(green, source, parts, early)
        entered = entering(entering_from_kernel, (base, parts, upto, local))
    arrived = exchange(*entered, sections)
    prop = propagator(tiles, green, coupling, entered[0])
    return final_waves(arrived, prop, image)[None]


def solution(mesh):
    in_specs = (
        P("sec", "grp", None, None),
        P("sec", "grp", None, None),
        P("sec", None, None),
        P("sec", None, None),
        P("sec", None),
        P("sec", None),
    )
    out_specs = P("sec", "grp", None, None)
    return jax.shard_map(
        per_device, mesh=mesh, in_specs=in_specs, out_specs=out_specs, check_vma=False
    )
```

```python
import functools

import jax
import jax.numpy as jnp
from jax import lax
from jax.experimental import pallas as pl
from jax.experimental.pallas import tpu as pltpu
from jax.sharding import PartitionSpec as P

BLK = 32
CAP = 2
GROUP = 4
HEAD = 8
CORES = 2

HIGH = lax.Precision.HIGHEST
F32 = jnp.float32
BF16 = jnp.bfloat16
VMEM_SMALL = 16 * 1024 * 1024
VMEM_WHOLE = 63400000
PEAK = 1.15e9

IN_VMEM = pl.BlockSpec(memory_space=pltpu.VMEM)
IN_SMEM = pl.BlockSpec(memory_space=pltpu.SMEM)
IN_HBM = pl.BlockSpec(memory_space=pltpu.HBM)
IN_PLACE = pl.BlockSpec(memory_space=pl.ANY)


def shape(*dims, dtype=BF16):
    return jax.ShapeDtypeStruct(dims, dtype)


def call(body, name, ins, outs, scratch, micros, vmem=VMEM_SMALL, aliases=None):
    places = list(range(len(outs))) if isinstance(outs, list) else 0
    return pl.pallas_call(
        body,
        name=name,
        in_specs=ins,
        out_shape=outs,
        out_specs=jax.tree.map(lambda k: IN_PLACE if k in (aliases or {}).values() else IN_VMEM, places),
        input_output_aliases=aliases or {},
        scratch_shapes=scratch,
        compiler_params=pltpu.CompilerParams(vmem_limit_bytes=vmem),
        cost_estimate=pl.CostEstimate(flops=int(micros * PEAK), bytes_accessed=0, transcendentals=0),
    )


def place():
    return lax.axis_index("sec") % GROUP


def partners():
    here = place()
    across = (here + CORES) % GROUP
    return here, across ^ 1, across, here ^ 1


def dot(a, b):
    return jnp.dot(a, b, preferred_element_type=F32)


def dot_wide(a, b):
    return jnp.dot(a, b, precision=HIGH, preferred_element_type=F32)


def two_parts(x):
    high = x.astype(BF16)
    return high, (x - high.astype(F32)).astype(BF16)


def dot_rows(a, b):
    return lax.dot_general(a, b, (((1,), (1,)), ((), ())), preferred_element_type=F32)


def step_by(state, maps):
    high, low = two_parts(state)
    rows = state.shape[0]
    y = dot_rows(jnp.concatenate([high, low], axis=0), maps[0])
    return y[:rows] + (y[rows:] + dot_rows(high, maps[1]))


def mask_tiles(pattern, coupling):
    high, wide = coupling.shape[0] // pattern.shape[1], coupling.shape[1] // pattern.shape[0]
    for i in range(pattern.shape[1]):
        for j in range(pattern.shape[0]):
            at = (slice(i * high, (i + 1) * high), slice(j * wide, (j + 1) * wide))
            tile = coupling[at]
            coupling[at] = jnp.where(pattern[j, i] == 1, tile, jnp.zeros_like(tile))


def pairs_kernel(owner_in, blocks_in, green, inject_in, out, owner, blocks, inject, held, product, slot_of, counts, sem, side, done, *packets):
    energies, orbitals, _ = green.shape
    sections = out.shape[0]
    count = owner.shape[0]
    named = held.shape[1] < orbitals
    parts = sem.shape[1]
    size = held.shape[1] // parts
    small = [
        pltpu.make_async_copy(src, dst, side.at[k])
        for k, (src, dst) in enumerate(((owner_in, owner), (blocks_in, blocks), (inject_in, inject)))
    ]
    for move in small:
        move.start()

    def copy_of(e, c, q):
        first = pl.multiple_of(blocks[0, q] * BLK, BLK)
        to = pl.multiple_of(q * BLK, BLK)
        return pltpu.make_async_copy(green.at[e, pl.ds(first, BLK)], held.at[e, pl.ds(to, BLK)], sem.at[e, c])

    def part_of(e, c):
        at = pl.ds(c * size, size)
        return pltpu.make_async_copy(green.at[e, at], held.at[e, at], sem.at[e, c])

    if not named:
        for e in range(energies):
            for c in range(parts):
                part_of(e, c).start()
    for move in small[:2]:
        move.wait()
    if named:
        for e in range(energies):
            for c in range(parts):
                lax.fori_loop(
                    c * (count // parts),
                    (c + 1) * (count // parts),
                    lambda q, _, e=e, c=c: copy_of(e, c, q).start(),
                    None,
                    unroll=4,
                )
    rows = CAP * BLK
    head = packets[-1]
    columns = out.shape[2]
    lane = lax.broadcasted_iota(jnp.int32, (HEAD, columns), 1)
    none = jnp.where(lane < CAP, -1.0, 0.0).astype(BF16)

    def blank(d, _):
        counts[d] = 0
        for packet in packets:
            packet[d, :rows, :] = jnp.zeros((rows, columns), BF16)
        head[d, rows : rows + HEAD, :] = none
        return 0

    lax.fori_loop(0, sections, blank, 0)

    def rank(q, _):
        d = owner[q]
        r = counts[d]
        counts[d] = r + 1
        slot_of[q] = r
        line = head[d, rows : rows + HEAD, :].astype(F32)
        line = jnp.where(lane == r, blocks[1, q].astype(F32), line)
        head[d, rows : rows + HEAD, :] = line.astype(BF16)
        return 0

    lax.fori_loop(0, count, rank, 0)
    small[2].wait()
    moves = []
    for e, packet in enumerate(packets):
        for c in range(parts):
            part_of(e, c).wait()
            at = slice(c * size, (c + 1) * size)
            product[e, at, :] = dot(held[e, at, :], inject[e]).astype(BF16)

        def fill(q, _):
            first = pl.multiple_of((q if named else blocks[0, q]) * BLK, BLK)
            to = pl.multiple_of(slot_of[q] * BLK, BLK)
            packet[owner[q], pl.ds(to, BLK), :] = product[e, pl.ds(first, BLK), :]
            return 0

        lax.fori_loop(0, count, fill, 0, unroll=4)
        moves.append(pltpu.make_async_copy(packet, out.at[:, pl.ds(e * rows, packet.shape[1])], done.at[e]))
        moves[-1].start()
    for move in moves:
        move.wait()


def outgoing_pairs(owner, blocks, green, inject, sections):
    energies, orbitals, _ = green.shape
    columns = inject.shape[2]
    rows = min(orbitals, owner.shape[0] * BLK)
    part = CAP * BLK
    parts = 2
    return pl.pallas_call(
        pairs_kernel,
        name="pairs",
        in_specs=[IN_HBM] * 4,
        out_shape=shape(sections, part * energies + HEAD, columns),
        out_specs=IN_HBM,
        scratch_shapes=[
            pltpu.SMEM(owner.shape, jnp.int32),
            pltpu.SMEM(blocks.shape, jnp.int32),
            pltpu.VMEM(inject.shape, BF16),
            pltpu.VMEM((energies, rows, orbitals), BF16),
            pltpu.VMEM((energies, rows, columns), BF16),
            pltpu.SMEM(owner.shape, jnp.int32),
            pltpu.SMEM((sections,), jnp.int32),
            pltpu.SemaphoreType.DMA((energies, parts)),
            pltpu.SemaphoreType.DMA((3,)),
            pltpu.SemaphoreType.DMA((energies,)),
        ]
        + [pltpu.VMEM((sections, part + (HEAD if e == energies - 1 else 0), columns), BF16) for e in range(energies)],
        compiler_params=pltpu.CompilerParams(vmem_limit_bytes=VMEM_WHOLE),
        cost_estimate=pl.CostEstimate(flops=int(4.0 * PEAK), bytes_accessed=0, transcendentals=0),
    )(owner, blocks, green, inject)


def maps_kernel(pattern, green, coupling, own, other, *refs):
    face_rows, (couple, maps) = refs[:-2], refs[-2:]
    energies, orbitals, _ = green.shape
    face = coupling.shape[1]
    couple[...] = coupling[...]
    mask_tiles(pattern, couple)
    for e in range(energies):
        rows = green[e, orbitals - face :, :]
        face_rows[e][...] = rows
        maps[e] = dot(rows, couple[...])
    mine = place() // CORES
    own[...] = maps[mine]
    other[...] = maps[1 - mine]


def face_maps(pattern, green, coupling):
    orbitals, face = coupling.shape
    square = shape(face, face, dtype=F32)
    return call(
        maps_kernel,
        "face_maps",
        [IN_SMEM, IN_VMEM, IN_VMEM],
        [square, square] + [shape(face, orbitals)] * green.shape[0],
        [pltpu.VMEM(coupling.shape, BF16), pltpu.VMEM((green.shape[0], face, face), F32)],
        1.2,
    )(pattern, green, coupling)


def prop_kernel(pattern, green, coupling, _tie, out, couple):
    couple[...] = coupling[...]
    mask_tiles(pattern, couple)
    for e in range(green.shape[0]):
        out[e] = dot(green[e], couple[...]).astype(BF16)


def propagator(pattern, green, coupling, tie):
    energies, orbitals, _ = green.shape
    return call(
        prop_kernel,
        "prop",
        [IN_SMEM, IN_VMEM, IN_VMEM, IN_PLACE],
        shape(energies, orbitals, coupling.shape[1]),
        [pltpu.VMEM(coupling.shape, BF16)],
        1.5,
    )(pattern, green, coupling, tie)


def times(a, b):
    return dot(a[0], b[0]) + (dot(a[0], b[1]) + dot(a[1], b[0]))


def chain_kernel(own, far, across, near, total_out, parts, maps):
    collect((own, far, across, near), maps)
    split = [two_parts(maps[j]) for j in range(GROUP)]
    lower, upper = two_parts(times(split[1], split[0])), two_parts(times(split[3], split[2]))
    total_out[...] = times(upper, lower).astype(total_out.dtype)
    for j, (high, low) in enumerate(split):
        parts[0, j] = high
        parts[1, j] = low


def chain(maps, dtype):
    face = maps[0].shape[0]
    return call(
        chain_kernel,
        "chain_maps",
        [IN_VMEM] * GROUP,
        [shape(face, face, dtype=dtype), shape(2, GROUP, face, face)],
        [pltpu.VMEM((GROUP, face, face), F32)],
        0.9,
    )(*maps)


def source_kernel(received, inject, source, heads, targets, total, sem):
    energies, orbitals, columns = inject.shape
    sections = received.shape[0]
    rows = CAP * energies * BLK

    def read(s, _):
        block = received[s, rows : rows + HEAD, :].astype(F32)
        heads[pl.ds(s, 1), :] = block[:1].astype(jnp.int32)
        return 0

    lax.fori_loop(0, sections, read, 0, unroll=min(sections, 8))
    fetch = pltpu.make_async_copy(heads, targets, sem)
    fetch.start()
    total[...] = inject[...].astype(F32)
    fetch.wait()

    def add(s, _):
        for r in range(CAP):
            first = pl.multiple_of(jnp.maximum(targets[s, r], 0) * BLK, BLK)
            for e in range(energies):
                item = received[s, (e * CAP + r) * BLK : (e * CAP + r + 1) * BLK, :]
                total[e, pl.ds(first, BLK), :] += item.astype(F32)
        return 0

    lax.fori_loop(0, sections, add, 0, unroll=2)
    source[...] = total[...].astype(BF16)


def placed_source(received, inject):
    energies, orbitals, columns = inject.shape
    sections = received.shape[0]
    return call(
        source_kernel,
        "source",
        [IN_VMEM] * 2,
        shape(*inject.shape),
        [
            pltpu.VMEM((sections, columns), jnp.int32),
            pltpu.SMEM((sections, columns), jnp.int32),
            pltpu.VMEM(inject.shape, F32),
            pltpu.SemaphoreType.DMA,
        ],
        1.0,
    )(received, inject)


def quarters_kernel(source, *refs):
    energies = source.shape[0]
    face_rows = refs[:energies]
    own, far, across, near, quarters = refs[energies:]
    split = GROUP // energies
    size = quarters.shape[1]
    for e in range(energies):
        wide = dot(face_rows[e][...], source[e]).T
        for h in range(split):
            quarters[e * split + h] = wide[h * size : (h + 1) * size]
    for out, at in zip((own, far, across, near), partners()):
        out[...] = quarters[at].astype(BF16)


def face_quarters(source, face_rows):
    energies, _, columns = source.shape
    face = face_rows[0].shape[0]
    rows = columns * energies // GROUP
    return call(
        quarters_kernel,
        "face_quarters",
        [IN_VMEM] * (1 + energies),
        [shape(rows, face)] * GROUP,
        [pltpu.VMEM((GROUP, rows, face), F32)],
        0.6,
    )(source, *face_rows)


def after_kernel(_packets, _map, _same_map):
    pass


def handed_on(item, packets):
    return call(
        after_kernel,
        "after_exchange",
        [IN_PLACE] * 2,
        [shape(*item.shape, dtype=item.dtype)],
        [],
        0.1,
        aliases={1: 0},
    )(packets, item)[0]


def collect(refs, held):
    for ref, at in zip(refs, partners()):
        held[at] = ref[...]


def total_kernel(own, far, across, near, parts, _image, out, local, shifts):
    collect((own, far, across, near), shifts)
    state = shifts[0].astype(F32)
    for j in range(1, GROUP):
        local[j - 1] = state
        state = shifts[j].astype(F32) + step_by(state, (parts[0, j], parts[1, j]))
    out[...] = state.astype(BF16)


def plane_total(shifts, parts, tie):
    rows, face = shifts[0].shape
    return call(
        total_kernel,
        "plane_total",
        [IN_VMEM] * (GROUP + 1) + [IN_PLACE],
        [shape(rows, face), shape(GROUP - 1, rows, face, dtype=F32)],
        [pltpu.VMEM((GROUP, rows, face), BF16)],
        3.0,
    )(*shifts, parts, tie)


def work_kernel(early, *refs):
    green, source, parts = refs[:3]
    held, (image, upto) = refs[3:-2], refs[-2:]
    low_plane = lax.axis_index("sec") // GROUP == 0

    @pl.when(low_plane if early else jnp.logical_not(low_plane))
    def _():
        for e in range(green.shape[0]):
            image[e] = dot(green[e], source[e])
        maps = (parts[0, 0], parts[1, 0])
        for j in range(1, GROUP - 1):
            maps = two_parts(times((parts[0, j], parts[1, j]), maps))
            upto[0, j - 1], upto[1, j - 1] = maps

    if held:

        @pl.when(low_plane)
        def _():
            image[...] = held[0][...]
            upto[...] = held[1][...]


def image_and_maps(green, source, parts, held=()):
    _, _, face, _ = parts.shape
    return call(
        functools.partial(work_kernel, not held),
        "image_and_maps",
        [IN_VMEM] * (3 + len(held)),
        [shape(*source.shape, dtype=F32), shape(2, GROUP - 2, face, face)],
        [],
        2.0,
    )(green, source, parts, *held)


def sweep_plane(state, parts, upto, local, out):
    held = [state]
    for j in range(1, GROUP):
        maps = (parts[0, 0], parts[1, 0]) if j == 1 else (upto[0, j - 2], upto[1, j - 2])
        held.append(local[j - 1] + step_by(state, maps))
    work = out[GROUP]
    for j, item in enumerate(held):
        work[j] = item
    for ref, at in zip(out, partners()):
        ref[...] = work[at].astype(BF16)


def entering_kernel(third, near_one, second, far_one, got, other, parts, upto, local, *out):
    first_core = place() % CORES == 0
    first = near_one[...].astype(F32) + far_one[...].astype(F32)
    state = third[...].astype(F32)
    rows = state.shape[0]
    for below, (one, two) in ((second[...].astype(F32), (other, got)), (first, (got, other))):
        factor = jnp.where(first_core, one[...], two[...])
        y = dot_rows(jnp.concatenate(two_parts(state), axis=0), factor)
        state = below + (y[:rows] + y[rows:])
    sweep_plane(state, parts, upto, local, out)


def entering_from_kernel(base, parts, upto, local, *out):
    sweep_plane(base[...], parts, upto, local, out)


def entering(body, args):
    half, columns = args[0].shape
    return call(
        body,
        "entering",
        [IN_VMEM] * len(args),
        [shape(half, columns)] * GROUP,
        [pltpu.VMEM((GROUP, half, columns), F32)],
        1.4,
    )(*args)


def waves_kernel(own, far, across, near, prop, image, out, arrived, wave, sem):
    collect((own, far, across, near), arrived)
    energies, orbitals, _ = prop.shape
    split = GROUP // energies
    pieces = sem.shape[1]
    size = orbitals // pieces
    moves = []
    for e in range(energies):
        incoming = jnp.concatenate([arrived[e * split + h] for h in range(split)], axis=0)
        for c in range(pieces):
            at = slice(c * size, (c + 1) * size)
            wave[e, at, :] = (dot_rows(prop[e, at, :], incoming) + image[e, at, :]).astype(BF16)
            moves.append(pltpu.make_async_copy(wave.at[e, pl.ds(c * size, size)], out.at[e, pl.ds(c * size, size)], sem.at[e, c]))
            moves[-1].start()
    for move in moves:
        move.wait()


def final_waves(arrived, prop, image):
    half, columns = arrived[0].shape
    energies = prop.shape[0]
    return pl.pallas_call(
        waves_kernel,
        name="waves",
        in_specs=[IN_VMEM] * (GROUP + 2),
        out_shape=shape(*image.shape),
        out_specs=IN_HBM,
        scratch_shapes=[
            pltpu.VMEM((GROUP, half, columns), BF16),
            pltpu.VMEM(image.shape, BF16),
            pltpu.SemaphoreType.DMA((energies, 2)),
        ],
        compiler_params=pltpu.CompilerParams(vmem_limit_bytes=VMEM_SMALL),
        cost_estimate=pl.CostEstimate(flops=int(1.3 * PEAK), bytes_accessed=0, transcendentals=0),
    )(*arrived, prop, image)


def to_near(item, sections):
    return lax.ppermute(item, "sec", [(s, s ^ 1) for s in range(sections)])


def to_across(item, sections):
    return lax.ppermute(item, "sec", [(s, s // GROUP * GROUP + (s % GROUP + CORES) % GROUP) for s in range(sections)])


def to_far(item, sections):
    return lax.ppermute(item, "sec", [(s, s // GROUP * GROUP + (s % GROUP + CORES) % GROUP ^ 1) for s in range(sections)])


def exchange(own, far, across, near, sections):
    return [own, to_far(far, sections), to_across(across, sections), to_near(near, sections)]


def up_shift(sections, k):
    return [(s, s + GROUP * k) for s in range(sections - GROUP * k)]


def maps_up(total_map, sections):
    pairs = []
    for i in range(GROUP):
        if i % CORES == 0:
            pairs += [(GROUP + i, 2 * GROUP + i), (2 * GROUP + i, 3 * GROUP + i)]
        else:
            pairs += [(GROUP + i, 3 * GROUP + i)]
    got = lax.ppermute(total_map, "sec", pairs)
    return got, lax.ppermute(got, "sec", [(s, s ^ 1) for s in range(2 * GROUP, sections)])


def between(item, *planes):
    pairs = [(p * GROUP + i, q * GROUP + i) for p, q in planes for i in range(GROUP)]
    return lax.ppermute(item, "sec", pairs)


def scan_below(total_map, total, sections):
    shift = lax.ppermute(total.astype(F32), "sec", up_shift(sections, 1))
    joined = lax.ppermute(total_map, "sec", up_shift(sections, 1))
    stride = 1
    while stride < sections // GROUP:
        other = lax.ppermute(shift, "sec", up_shift(sections, stride))
        other_map = lax.ppermute(joined, "sec", up_shift(sections, stride))
        shift = shift + dot_wide(other, joined.T)
        joined = dot_wide(joined, other_map)
        stride *= 2
    return shift


def per_device(green, injected, coupling, pattern, owner, pair_blocks):
    sections = lax.axis_size("sec")
    green, inject = green[0], injected[0]

    coupling, tiles = coupling[0], pattern[0].T
    outgoing = outgoing_pairs(owner[:, 0], pair_blocks.T, green, inject, sections)
    received = lax.all_to_all(outgoing, "sec", split_axis=0, concat_axis=0, tiled=True)

    own_map, other_map, *face_rows = face_maps(tiles, green, coupling)
    across = to_across(other_map, sections)
    near = to_near(own_map, sections)

    source = placed_source(received, inject)
    quarters = face_quarters(source, face_rows)
    shifts = exchange(*quarters, sections)
    across = handed_on(across, quarters[0])
    far = to_near(across, sections)
    four = sections // GROUP == 4
    total_map, parts = chain([own_map, far, across, near], BF16 if four else F32)
    early = image_and_maps(green, source, parts)
    maps = maps_up(total_map, sections) if four else []
    total, local = plane_total(shifts, parts, early[0])
    if four:
        fourth = between(total, (1, 2), (2, 3))
        third = between(total, (0, 2), (1, 3))
        second = between(total, (0, 1))
        first = between(total, (0, 3))
        image, upto = image_and_maps(green, source, parts, early)
        entered = entering(entering_kernel, (first, second, third, fourth, *maps, parts, upto, local))
    else:
        base = scan_below(total_map, total, sections)
        image, upto = image_and_maps(green, source, parts, early)
        entered = entering(entering_from_kernel, (base, parts, upto, local))
    arrived = exchange(*entered, sections)
    prop = propagator(tiles, green, coupling, entered[0])
    return final_waves(arrived, prop, image)[None]


def solution(mesh):
    in_specs = (
        P("sec", "grp", None, None),
        P("sec", "grp", None, None),
        P("sec", None, None),
        P("sec", None, None),
        P("sec", None),
        P("sec", None),
    )
    out_specs = P("sec", "grp", None, None)
    return jax.shard_map(
        per_device, mesh=mesh, in_specs=in_specs, out_specs=out_specs, check_vma=False
    )
```

```python
import functools

import jax
import jax.numpy as jnp
from jax import lax
from jax.experimental import pallas as pl
from jax.experimental.pallas import tpu as pltpu
from jax.sharding import PartitionSpec as P

BLK = 32
CAP = 2
GROUP = 4
HEAD = 8
CORES = 2

HIGH = lax.Precision.HIGHEST
F32 = jnp.float32
BF16 = jnp.bfloat16
VMEM_SMALL = 16 * 1024 * 1024
VMEM_WHOLE = 63400000
PEAK = 1.15e9

IN_VMEM = pl.BlockSpec(memory_space=pltpu.VMEM)
IN_SMEM = pl.BlockSpec(memory_space=pltpu.SMEM)
IN_HBM = pl.BlockSpec(memory_space=pltpu.HBM)
IN_PLACE = pl.BlockSpec(memory_space=pl.ANY)


def shape(*dims, dtype=BF16):
    return jax.ShapeDtypeStruct(dims, dtype)


def call(body, name, ins, outs, scratch, micros, vmem=VMEM_SMALL, aliases=None):
    places = list(range(len(outs))) if isinstance(outs, list) else 0
    return pl.pallas_call(
        body,
        name=name,
        in_specs=ins,
        out_shape=outs,
        out_specs=jax.tree.map(lambda k: IN_PLACE if k in (aliases or {}).values() else IN_VMEM, places),
        input_output_aliases=aliases or {},
        scratch_shapes=scratch,
        compiler_params=pltpu.CompilerParams(vmem_limit_bytes=vmem),
        cost_estimate=pl.CostEstimate(flops=int(micros * PEAK), bytes_accessed=0, transcendentals=0),
    )


def place():
    return lax.axis_index("sec") % GROUP


def partners():
    here = place()
    across = (here + CORES) % GROUP
    return here, across ^ 1, across, here ^ 1


def dot(a, b):
    return jnp.dot(a, b, preferred_element_type=F32)


def dot_wide(a, b):
    return jnp.dot(a, b, precision=HIGH, preferred_element_type=F32)


def two_parts(x):
    high = x.astype(BF16)
    return high, (x - high.astype(F32)).astype(BF16)


def dot_rows(a, b):
    return lax.dot_general(a, b, (((1,), (1,)), ((), ())), preferred_element_type=F32)


def step_by(state, maps):
    high, low = two_parts(state)
    rows = state.shape[0]
    y = dot_rows(jnp.concatenate([high, low], axis=0), maps[0])
    return y[:rows] + (y[rows:] + dot_rows(high, maps[1]))


def mask_tiles(pattern, coupling):
    high, wide = coupling.shape[0] // pattern.shape[1], coupling.shape[1] // pattern.shape[0]
    for i in range(pattern.shape[1]):
        for j in range(pattern.shape[0]):
            at = (slice(i * high, (i + 1) * high), slice(j * wide, (j + 1) * wide))
            tile = coupling[at]
            coupling[at] = jnp.where(pattern[j, i] == 1, tile, jnp.zeros_like(tile))


def pairs_kernel(owner_in, blocks_in, green, inject_in, out, owner, blocks, inject, held, product, slot_of, counts, sem, side, done, *packets):
    energies, orbitals, _ = green.shape
    sections = out.shape[0]
    count = owner.shape[0]
    named = held.shape[1] < orbitals
    parts = sem.shape[1]
    size = held.shape[1] // parts
    small = [
        pltpu.make_async_copy(src, dst, side.at[k])
        for k, (src, dst) in enumerate(((owner_in, owner), (blocks_in, blocks), (inject_in, inject)))
    ]
    for move in small:
        move.start()

    def copy_of(e, c, q):
        first = pl.multiple_of(blocks[0, q] * BLK, BLK)
        to = pl.multiple_of(q * BLK, BLK)
        return pltpu.make_async_copy(green.at[e, pl.ds(first, BLK)], held.at[e, pl.ds(to, BLK)], sem.at[e, c])

    def part_of(e, c):
        at = pl.ds(c * size, size)
        return pltpu.make_async_copy(green.at[e, at], held.at[e, at], sem.at[e, c])

    if not named:
        for e in range(energies):
            for c in range(parts):
                part_of(e, c).start()
    for move in small[:2]:
        move.wait()
    if named:
        for e in range(energies):
            for c in range(parts):
                lax.fori_loop(
                    c * (count // parts),
                    (c + 1) * (count // parts),
                    lambda q, _, e=e, c=c: copy_of(e, c, q).start(),
                    None,
                    unroll=4,
                )
    rows = CAP * BLK
    head = packets[-1]
    columns = out.shape[2]
    lane = lax.broadcasted_iota(jnp.int32, (HEAD, columns), 1)
    none = jnp.where(lane < CAP, -1.0, 0.0).astype(BF16)

    def blank(d, _):
        counts[d] = 0
        for packet in packets:
            packet[d, :rows, :] = jnp.zeros((rows, columns), BF16)
        head[d, rows : rows + HEAD, :] = none
        return 0

    lax.fori_loop(0, sections, blank, 0)

    def rank(q, _):
        d = owner[q]
        r = counts[d]
        counts[d] = r + 1
        slot_of[q] = r
        line = head[d, rows : rows + HEAD, :].astype(F32)
        line = jnp.where(lane == r, blocks[1, q].astype(F32), line)
        head[d, rows : rows + HEAD, :] = line.astype(BF16)
        return 0

    lax.fori_loop(0, count, rank, 0)
    small[2].wait()
    moves = []
    for e, packet in enumerate(packets):

        def fill(q, _, e=e, packet=packet):
            first = pl.multiple_of((q if named else blocks[0, q]) * BLK, BLK)
            to = pl.multiple_of(slot_of[q] * BLK, BLK)
            packet[owner[q], pl.ds(to, BLK), :] = product[e, pl.ds(first, BLK), :]
            return 0

        for c in range(parts):
            part_of(e, c).wait()
            at = slice(c * size, (c + 1) * size)
            product[e, at, :] = dot(held[e, at, :], inject[e]).astype(BF16)
            if named:
                lax.fori_loop(c * (count // parts), (c + 1) * (count // parts), fill, 0, unroll=4)
        if not named:
            lax.fori_loop(0, count, fill, 0, unroll=4)
        moves.append(pltpu.make_async_copy(packet, out.at[:, pl.ds(e * rows, packet.shape[1])], done.at[e]))
        moves[-1].start()
    for move in moves:
        move.wait()


def outgoing_pairs(owner, blocks, green, inject, sections):
    energies, orbitals, _ = green.shape
    columns = inject.shape[2]
    rows = min(orbitals, owner.shape[0] * BLK)
    part = CAP * BLK
    parts = 4
    return pl.pallas_call(
        pairs_kernel,
        name="pairs",
        in_specs=[IN_HBM] * 4,
        out_shape=shape(sections, part * energies + HEAD, columns),
        out_specs=IN_HBM,
        scratch_shapes=[
            pltpu.SMEM(owner.shape, jnp.int32),
            pltpu.SMEM(blocks.shape, jnp.int32),
            pltpu.VMEM(inject.shape, BF16),
            pltpu.VMEM((energies, rows, orbitals), BF16),
            pltpu.VMEM((energies, rows, columns), BF16),
            pltpu.SMEM(owner.shape, jnp.int32),
            pltpu.SMEM((sections,), jnp.int32),
            pltpu.SemaphoreType.DMA((energies, parts)),
            pltpu.SemaphoreType.DMA((3,)),
            pltpu.SemaphoreType.DMA((energies,)),
        ]
        + [pltpu.VMEM((sections, part + (HEAD if e == energies - 1 else 0), columns), BF16) for e in range(energies)],
        compiler_params=pltpu.CompilerParams(vmem_limit_bytes=VMEM_WHOLE),
        cost_estimate=pl.CostEstimate(flops=int(4.0 * PEAK), bytes_accessed=0, transcendentals=0),
    )(owner, blocks, green, inject)


def maps_kernel(pattern, green, coupling, own, other, *refs):
    face_rows, (couple, maps) = refs[:-2], refs[-2:]
    energies, orbitals, _ = green.shape
    face = coupling.shape[1]
    couple[...] = coupling[...]
    mask_tiles(pattern, couple)
    for e in range(energies):
        rows = green[e, orbitals - face :, :]
        face_rows[e][...] = rows
        maps[e] = dot(rows, couple[...])
    mine = place() // CORES
    own[...] = maps[mine]
    other[...] = maps[1 - mine]


def face_maps(pattern, green, coupling):
    orbitals, face = coupling.shape
    square = shape(face, face, dtype=F32)
    return call(
        maps_kernel,
        "face_maps",
        [IN_SMEM, IN_VMEM, IN_VMEM],
        [square, square] + [shape(face, orbitals)] * green.shape[0],
        [pltpu.VMEM(coupling.shape, BF16), pltpu.VMEM((green.shape[0], face, face), F32)],
        1.2,
    )(pattern, green, coupling)


def prop_kernel(pattern, green, coupling, _tie, out, couple):
    couple[...] = coupling[...]
    mask_tiles(pattern, couple)
    for e in range(green.shape[0]):
        out[e] = dot(green[e], couple[...]).astype(BF16)


def propagator(pattern, green, coupling, tie):
    energies, orbitals, _ = green.shape
    return call(
        prop_kernel,
        "prop",
        [IN_SMEM, IN_VMEM, IN_VMEM, IN_PLACE],
        shape(energies, orbitals, coupling.shape[1]),
        [pltpu.VMEM(coupling.shape, BF16)],
        1.5,
    )(pattern, green, coupling, tie)


def times(a, b):
    return dot(a[0], b[0]) + (dot(a[0], b[1]) + dot(a[1], b[0]))


def chain_kernel(own, far, across, near, total_out, parts, maps):
    collect((own, far, across, near), maps)
    split = [two_parts(maps[j]) for j in range(GROUP)]
    lower, upper = two_parts(times(split[1], split[0])), two_parts(times(split[3], split[2]))
    total_out[...] = times(upper, lower).astype(total_out.dtype)
    for j, (high, low) in enumerate(split):
        parts[0, j] = high
        parts[1, j] = low


def chain(maps, dtype):
    face = maps[0].shape[0]
    return call(
        chain_kernel,
        "chain_maps",
        [IN_VMEM] * GROUP,
        [shape(face, face, dtype=dtype), shape(2, GROUP, face, face)],
        [pltpu.VMEM((GROUP, face, face), F32)],
        0.9,
    )(*maps)


def source_kernel(received, inject, source, heads, targets, total, sem):
    energies, orbitals, columns = inject.shape
    sections = received.shape[0]
    rows = CAP * energies * BLK

    def read(s, _):
        block = received[s, rows : rows + HEAD, :].astype(F32)
        heads[pl.ds(s, 1), :] = block[:1].astype(jnp.int32)
        return 0

    lax.fori_loop(0, sections, read, 0, unroll=min(sections, 8))
    fetch = pltpu.make_async_copy(heads, targets, sem)
    fetch.start()
    total[...] = inject[...].astype(F32)
    fetch.wait()

    def add(s, _):
        for r in range(CAP):
            first = pl.multiple_of(jnp.maximum(targets[s, r], 0) * BLK, BLK)
            for e in range(energies):
                item = received[s, (e * CAP + r) * BLK : (e * CAP + r + 1) * BLK, :]
                total[e, pl.ds(first, BLK), :] += item.astype(F32)
        return 0

    lax.fori_loop(0, sections, add, 0, unroll=2)
    source[...] = total[...].astype(BF16)


def placed_source(received, inject):
    energies, orbitals, columns = inject.shape
    sections = received.shape[0]
    return call(
        source_kernel,
        "source",
        [IN_VMEM] * 2,
        shape(*inject.shape),
        [
            pltpu.VMEM((sections, columns), jnp.int32),
            pltpu.SMEM((sections, columns), jnp.int32),
            pltpu.VMEM(inject.shape, F32),
            pltpu.SemaphoreType.DMA,
        ],
        1.0,
    )(received, inject)


def quarters_kernel(source, *refs):
    energies = source.shape[0]
    face_rows = refs[:energies]
    own, far, across, near, quarters = refs[energies:]
    split = GROUP // energies
    size = quarters.shape[1]
    for e in range(energies):
        wide = dot(face_rows[e][...], source[e]).T
        for h in range(split):
            quarters[e * split + h] = wide[h * size : (h + 1) * size]
    for out, at in zip((own, far, across, near), partners()):
        out[...] = quarters[at].astype(BF16)


def face_quarters(source, face_rows):
    energies, _, columns = source.shape
    face = face_rows[0].shape[0]
    rows = columns * energies // GROUP
    return call(
        quarters_kernel,
        "face_quarters",
        [IN_VMEM] * (1 + energies),
        [shape(rows, face)] * GROUP,
        [pltpu.VMEM((GROUP, rows, face), F32)],
        0.6,
    )(source, *face_rows)


def after_kernel(_packets, _map, _same_map):
    pass


def handed_on(item, packets):
    return call(
        after_kernel,
        "after_exchange",
        [IN_PLACE] * 2,
        [shape(*item.shape, dtype=item.dtype)],
        [],
        0.1,
        aliases={1: 0},
    )(packets, item)[0]


def collect(refs, held):
    for ref, at in zip(refs, partners()):
        held[at] = ref[...]


def total_kernel(own, far, across, near, parts, _image, out, local, shifts):
    collect((own, far, across, near), shifts)
    state = shifts[0].astype(F32)
    for j in range(1, GROUP):
        local[j - 1] = state
        state = shifts[j].astype(F32) + step_by(state, (parts[0, j], parts[1, j]))
    out[...] = state.astype(BF16)


def plane_total(shifts, parts, tie):
    rows, face = shifts[0].shape
    return call(
        total_kernel,
        "plane_total",
        [IN_VMEM] * (GROUP + 1) + [IN_PLACE],
        [shape(rows, face), shape(GROUP - 1, rows, face, dtype=F32)],
        [pltpu.VMEM((GROUP, rows, face), BF16)],
        3.0,
    )(*shifts, parts, tie)


def work_kernel(early, *refs):
    green, source, parts = refs[:3]
    held, (image, upto) = refs[3:-2], refs[-2:]
    plane = lax.axis_index("sec") // GROUP
    first, second = plane == 0, plane == 1

    @pl.when(first if early else jnp.logical_not(first))
    def _():
        for e in range(green.shape[0]):
            image[e] = dot(green[e], source[e])

    @pl.when(jnp.logical_not(second) if early else second)
    def _():
        maps = (parts[0, 0], parts[1, 0])
        for j in range(1, GROUP - 1):
            maps = two_parts(times((parts[0, j], parts[1, j]), maps))
            upto[0, j - 1], upto[1, j - 1] = maps

    if held:

        @pl.when(first)
        def _():
            image[...] = held[0][...]

        @pl.when(jnp.logical_not(second))
        def _():
            upto[...] = held[1][...]


def image_and_maps(green, source, parts, held=()):
    _, _, face, _ = parts.shape
    return call(
        functools.partial(work_kernel, not held),
        "image_and_maps",
        [IN_VMEM] * (3 + len(held)),
        [shape(*source.shape, dtype=F32), shape(2, GROUP - 2, face, face)],
        [],
        2.0,
    )(green, source, parts, *held)


def sweep_plane(state, parts, upto, local, out):
    held = [state]
    for j in range(1, GROUP):
        maps = (parts[0, 0], parts[1, 0]) if j == 1 else (upto[0, j - 2], upto[1, j - 2])
        held.append(local[j - 1] + step_by(state, maps))
    work = out[GROUP]
    for j, item in enumerate(held):
        work[j] = item
    for ref, at in zip(out, partners()):
        ref[...] = work[at].astype(BF16)


def entering_kernel(third, near_one, second, far_one, got, other, parts, upto, local, *out):
    first_core = place() % CORES == 0
    first = near_one[...].astype(F32) + far_one[...].astype(F32)
    state = third[...].astype(F32)
    rows = state.shape[0]
    for below, (one, two) in ((second[...].astype(F32), (other, got)), (first, (got, other))):
        factor = jnp.where(first_core, one[...], two[...])
        y = dot_rows(jnp.concatenate(two_parts(state), axis=0), factor)
        state = below + (y[:rows] + y[rows:])
    sweep_plane(state, parts, upto, local, out)


def entering_from_kernel(base, parts, upto, local, *out):
    sweep_plane(base[...], parts, upto, local, out)


def entering(body, args):
    half, columns = args[0].shape
    return call(
        body,
        "entering",
        [IN_VMEM] * len(args),
        [shape(half, columns)] * GROUP,
        [pltpu.VMEM((GROUP, half, columns), F32)],
        1.4,
    )(*args)


def waves_kernel(own, far, across, near, prop, image, out, arrived, wave, sem):
    collect((own, far, across, near), arrived)
    energies, orbitals, _ = prop.shape
    split = GROUP // energies
    pieces = sem.shape[1]
    size = orbitals // pieces
    moves = []
    for e in range(energies):
        incoming = jnp.concatenate([arrived[e * split + h] for h in range(split)], axis=0)
        for c in range(pieces):
            at = slice(c * size, (c + 1) * size)
            wave[e, at, :] = (dot_rows(prop[e, at, :], incoming) + image[e, at, :]).astype(BF16)
            moves.append(pltpu.make_async_copy(wave.at[e, pl.ds(c * size, size)], out.at[e, pl.ds(c * size, size)], sem.at[e, c]))
            moves[-1].start()
    for move in moves:
        move.wait()


def final_waves(arrived, prop, image):
    half, columns = arrived[0].shape
    energies = prop.shape[0]
    return pl.pallas_call(
        waves_kernel,
        name="waves",
        in_specs=[IN_VMEM] * (GROUP + 2),
        out_shape=shape(*image.shape),
        out_specs=IN_HBM,
        scratch_shapes=[
            pltpu.VMEM((GROUP, half, columns), BF16),
            pltpu.VMEM(image.shape, BF16),
            pltpu.SemaphoreType.DMA((energies, 4)),
        ],
        compiler_params=pltpu.CompilerParams(vmem_limit_bytes=VMEM_SMALL),
        cost_estimate=pl.CostEstimate(flops=int(1.3 * PEAK), bytes_accessed=0, transcendentals=0),
    )(*arrived, prop, image)


def to_near(item, sections):
    return lax.ppermute(item, "sec", [(s, s ^ 1) for s in range(sections)])


def to_across(item, sections):
    return lax.ppermute(item, "sec", [(s, s // GROUP * GROUP + (s % GROUP + CORES) % GROUP) for s in range(sections)])


def to_far(item, sections):
    return lax.ppermute(item, "sec", [(s, s // GROUP * GROUP + (s % GROUP + CORES) % GROUP ^ 1) for s in range(sections)])


def exchange(own, far, across, near, sections):
    return [own, to_far(far, sections), to_across(across, sections), to_near(near, sections)]


def up_shift(sections, k):
    return [(s, s + GROUP * k) for s in range(sections - GROUP * k)]


def maps_up(total_map, sections):
    pairs = []
    for i in range(GROUP):
        if i % CORES == 0:
            pairs += [(GROUP + i, 2 * GROUP + i), (2 * GROUP + i, 3 * GROUP + i)]
        else:
            pairs += [(GROUP + i, 3 * GROUP + i)]
    got = lax.ppermute(total_map, "sec", pairs)
    return got, lax.ppermute(got, "sec", [(s, s ^ 1) for s in range(2 * GROUP, sections)])


def between(item, *planes):
    pairs = [(p * GROUP + i, q * GROUP + i) for p, q in planes for i in range(GROUP)]
    return lax.ppermute(item, "sec", pairs)


def scan_below(total_map, total, sections):
    shift = lax.ppermute(total.astype(F32), "sec", up_shift(sections, 1))
    joined = lax.ppermute(total_map, "sec", up_shift(sections, 1))
    stride = 1
    while stride < sections // GROUP:
        other = lax.ppermute(shift, "sec", up_shift(sections, stride))
        other_map = lax.ppermute(joined, "sec", up_shift(sections, stride))
        shift = shift + dot_wide(other, joined.T)
        joined = dot_wide(joined, other_map)
        stride *= 2
    return shift


def per_device(green, injected, coupling, pattern, owner, pair_blocks):
    sections = lax.axis_size("sec")
    green, inject = green[0], injected[0]

    coupling, tiles = coupling[0], pattern[0].T
    outgoing = outgoing_pairs(owner[:, 0], pair_blocks.T, green, inject, sections)
    received = lax.all_to_all(outgoing, "sec", split_axis=0, concat_axis=0, tiled=True)

    own_map, other_map, *face_rows = face_maps(tiles, green, coupling)
    across = to_across(other_map, sections)
    near = to_near(own_map, sections)

    source = placed_source(received, inject)
    quarters = face_quarters(source, face_rows)
    shifts = exchange(*quarters, sections)
    across = handed_on(across, quarters[0])
    far = to_near(across, sections)
    four = sections // GROUP == 4
    total_map, parts = chain([own_map, far, across, near], BF16 if four else F32)
    early = image_and_maps(green, source, parts)
    maps = maps_up(total_map, sections) if four else []
    total, local = plane_total(shifts, parts, early[0])
    if four:
        fourth = between(total, (1, 2), (2, 3))
        third = between(total, (0, 2), (1, 3))
        second = between(total, (0, 1))
        first = between(total, (0, 3))
        image, upto = image_and_maps(green, source, parts, early)
        entered = entering(entering_kernel, (first, second, third, fourth, *maps, parts, upto, local))
    else:
        base = scan_below(total_map, total, sections)
        image, upto = image_and_maps(green, source, parts, early)
        entered = entering(entering_from_kernel, (base, parts, upto, local))
    arrived = exchange(*entered, sections)
    prop = propagator(tiles, green, coupling, entered[0])
    return final_waves(arrived, prop, image)[None]


def solution(mesh):
    in_specs = (
        P("sec", "grp", None, None),
        P("sec", "grp", None, None),
        P("sec", None, None),
        P("sec", None, None),
        P("sec", None),
        P("sec", None),
    )
    out_specs = P("sec", "grp", None, None)
    return jax.shard_map(
        per_device, mesh=mesh, in_specs=in_specs, out_specs=out_specs, check_vma=False
    )
```

```python
import functools

import jax
import jax.numpy as jnp
from jax import lax
from jax.experimental import pallas as pl
from jax.experimental.pallas import tpu as pltpu
from jax.sharding import PartitionSpec as P

BLK = 32
CAP = 2
GROUP = 4
HEAD = 8
CORES = 2

HIGH = lax.Precision.HIGHEST
F32 = jnp.float32
BF16 = jnp.bfloat16
VMEM_SMALL = 16 * 1024 * 1024
VMEM_WHOLE = 63400000
PEAK = 1.15e9

IN_VMEM = pl.BlockSpec(memory_space=pltpu.VMEM)
IN_SMEM = pl.BlockSpec(memory_space=pltpu.SMEM)
IN_HBM = pl.BlockSpec(memory_space=pltpu.HBM)
IN_PLACE = pl.BlockSpec(memory_space=pl.ANY)


def shape(*dims, dtype=BF16):
    return jax.ShapeDtypeStruct(dims, dtype)


def call(body, name, ins, outs, scratch, micros, vmem=VMEM_SMALL, aliases=None):
    places = list(range(len(outs))) if isinstance(outs, list) else 0
    return pl.pallas_call(
        body,
        name=name,
        in_specs=ins,
        out_shape=outs,
        out_specs=jax.tree.map(lambda k: IN_PLACE if k in (aliases or {}).values() else IN_VMEM, places),
        input_output_aliases=aliases or {},
        scratch_shapes=scratch,
        compiler_params=pltpu.CompilerParams(vmem_limit_bytes=vmem),
        cost_estimate=pl.CostEstimate(flops=int(micros * PEAK), bytes_accessed=0, transcendentals=0),
    )


def place():
    return lax.axis_index("sec") % GROUP


def partners():
    here = place()
    across = (here + CORES) % GROUP
    return here, across ^ 1, across, here ^ 1


def dot(a, b):
    return jnp.dot(a, b, preferred_element_type=F32)


def dot_wide(a, b):
    return jnp.dot(a, b, precision=HIGH, preferred_element_type=F32)


def two_parts(x):
    high = x.astype(BF16)
    return high, (x - high.astype(F32)).astype(BF16)


def dot_rows(a, b):
    return lax.dot_general(a, b, (((1,), (1,)), ((), ())), preferred_element_type=F32)


def step_by(state, maps):
    high, low = two_parts(state)
    rows = state.shape[0]
    y = dot_rows(jnp.concatenate([high, low], axis=0), maps[0])
    return y[:rows] + (y[rows:] + dot_rows(high, maps[1]))


def mask_tiles(pattern, coupling):
    high, wide = coupling.shape[0] // pattern.shape[1], coupling.shape[1] // pattern.shape[0]
    for i in range(pattern.shape[1]):
        for j in range(pattern.shape[0]):
            at = (slice(i * high, (i + 1) * high), slice(j * wide, (j + 1) * wide))
            tile = coupling[at]
            coupling[at] = jnp.where(pattern[j, i] == 1, tile, jnp.zeros_like(tile))


def pairs_kernel(owner_in, blocks_in, green, inject_in, out, owner, blocks, inject, held, product, slot_of, counts, sem, side, done, *packets):
    energies, orbitals, _ = green.shape
    sections = out.shape[0]
    count = owner.shape[0]
    named = held.shape[1] < orbitals
    parts = sem.shape[1]
    size = held.shape[1] // parts
    small = [
        pltpu.make_async_copy(src, dst, side.at[k])
        for k, (src, dst) in enumerate(((owner_in, owner), (blocks_in, blocks), (inject_in, inject)))
    ]
    for move in small:
        move.start()

    def copy_of(e, c, q):
        first = pl.multiple_of(blocks[0, q] * BLK, BLK)
        to = pl.multiple_of(q * BLK, BLK)
        return pltpu.make_async_copy(green.at[e, pl.ds(first, BLK)], held.at[e, pl.ds(to, BLK)], sem.at[e, c])

    def part_of(e, c):
        at = pl.ds(c * size, size)
        return pltpu.make_async_copy(green.at[e, at], held.at[e, at], sem.at[e, c])

    if not named:
        for e in range(energies):
            for c in range(parts):
                part_of(e, c).start()
    for move in small[:2]:
        move.wait()
    if named:
        for e in range(energies):
            for c in range(parts):
                lax.fori_loop(
                    c * (count // parts),
                    (c + 1) * (count // parts),
                    lambda q, _, e=e, c=c: copy_of(e, c, q).start(),
                    None,
                    unroll=4,
                )
    rows = CAP * BLK
    head = packets[-1]
    columns = out.shape[2]
    lane = lax.broadcasted_iota(jnp.int32, (HEAD, columns), 1)
    none = jnp.where(lane < CAP, -1.0, 0.0).astype(BF16)

    def blank(d, _):
        counts[d] = 0
        for packet in packets:
            packet[d, :rows, :] = jnp.zeros((rows, columns), BF16)
        head[d, rows : rows + HEAD, :] = none
        return 0

    lax.fori_loop(0, sections, blank, 0)

    def rank(q, _):
        d = owner[q]
        r = counts[d]
        counts[d] = r + 1
        slot_of[q] = r
        line = head[d, rows : rows + HEAD, :].astype(F32)
        line = jnp.where(lane == r, blocks[1, q].astype(F32), line)
        head[d, rows : rows + HEAD, :] = line.astype(BF16)
        return 0

    lax.fori_loop(0, count, rank, 0)
    small[2].wait()
    moves = []
    for e, packet in enumerate(packets):

        def fill(q, _, e=e, packet=packet):
            first = pl.multiple_of((q if named else blocks[0, q]) * BLK, BLK)
            to = pl.multiple_of(slot_of[q] * BLK, BLK)
            packet[owner[q], pl.ds(to, BLK), :] = product[e, pl.ds(first, BLK), :]
            return 0

        for c in range(parts):
            part_of(e, c).wait()
            at = slice(c * size, (c + 1) * size)
            product[e, at, :] = dot(held[e, at, :], inject[e]).astype(BF16)
            if named:
                lax.fori_loop(c * (count // parts), (c + 1) * (count // parts), fill, 0, unroll=4)
        if not named:
            lax.fori_loop(0, count, fill, 0, unroll=4)
        moves.append(pltpu.make_async_copy(packet, out.at[:, pl.ds(e * rows, packet.shape[1])], done.at[e]))
        moves[-1].start()
    for move in moves:
        move.wait()


def outgoing_pairs(owner, blocks, green, inject, sections):
    energies, orbitals, _ = green.shape
    columns = inject.shape[2]
    rows = min(orbitals, owner.shape[0] * BLK)
    part = CAP * BLK
    parts = 2
    return pl.pallas_call(
        pairs_kernel,
        name="pairs",
        in_specs=[IN_HBM] * 4,
        out_shape=shape(sections, part * energies + HEAD, columns),
        out_specs=IN_HBM,
        scratch_shapes=[
            pltpu.SMEM(owner.shape, jnp.int32),
            pltpu.SMEM(blocks.shape, jnp.int32),
            pltpu.VMEM(inject.shape, BF16),
            pltpu.VMEM((energies, rows, orbitals), BF16),
            pltpu.VMEM((energies, rows, columns), BF16),
            pltpu.SMEM(owner.shape, jnp.int32),
            pltpu.SMEM((sections,), jnp.int32),
            pltpu.SemaphoreType.DMA((energies, parts)),
            pltpu.SemaphoreType.DMA((3,)),
            pltpu.SemaphoreType.DMA((energies,)),
        ]
        + [pltpu.VMEM((sections, part + (HEAD if e == energies - 1 else 0), columns), BF16) for e in range(energies)],
        compiler_params=pltpu.CompilerParams(vmem_limit_bytes=VMEM_WHOLE),
        cost_estimate=pl.CostEstimate(flops=int(4.0 * PEAK), bytes_accessed=0, transcendentals=0),
    )(owner, blocks, green, inject)


def maps_kernel(pattern, green, coupling, own, other, *refs):
    face_rows, (couple, maps) = refs[:-2], refs[-2:]
    energies, orbitals, _ = green.shape
    face = coupling.shape[1]
    couple[...] = coupling[...]
    mask_tiles(pattern, couple)
    for e in range(energies):
        rows = green[e, orbitals - face :, :]
        face_rows[e][...] = rows
        maps[e] = dot(rows, couple[...])
    mine = place() // CORES
    own[...] = maps[mine]
    other[...] = maps[1 - mine]


def face_maps(pattern, green, coupling):
    orbitals, face = coupling.shape
    square = shape(face, face, dtype=F32)
    return call(
        maps_kernel,
        "face_maps",
        [IN_SMEM, IN_VMEM, IN_VMEM],
        [square, square] + [shape(face, orbitals)] * green.shape[0],
        [pltpu.VMEM(coupling.shape, BF16), pltpu.VMEM((green.shape[0], face, face), F32)],
        1.2,
    )(pattern, green, coupling)


def prop_kernel(pattern, green, coupling, _tie, out, couple):
    couple[...] = coupling[...]
    mask_tiles(pattern, couple)
    for e in range(green.shape[0]):
        out[e] = dot(green[e], couple[...]).astype(BF16)


def propagator(pattern, green, coupling, tie):
    energies, orbitals, _ = green.shape
    return call(
        prop_kernel,
        "prop",
        [IN_SMEM, IN_VMEM, IN_VMEM, IN_PLACE],
        shape(energies, orbitals, coupling.shape[1]),
        [pltpu.VMEM(coupling.shape, BF16)],
        1.5,
    )(pattern, green, coupling, tie)


def times(a, b):
    return dot(a[0], b[0]) + (dot(a[0], b[1]) + dot(a[1], b[0]))


def chain_kernel(own, far, across, near, total_out, parts, maps):
    collect((own, far, across, near), maps)
    split = [two_parts(maps[j]) for j in range(GROUP)]
    lower, upper = two_parts(times(split[1], split[0])), two_parts(times(split[3], split[2]))
    total_out[...] = times(upper, lower).astype(total_out.dtype)
    for j, (high, low) in enumerate(split):
        parts[0, j] = high
        parts[1, j] = low


def chain(maps, dtype):
    face = maps[0].shape[0]
    return call(
        chain_kernel,
        "chain_maps",
        [IN_VMEM] * GROUP,
        [shape(face, face, dtype=dtype), shape(2, GROUP, face, face)],
        [pltpu.VMEM((GROUP, face, face), F32)],
        0.9,
    )(*maps)


def source_kernel(received, inject, source, heads, targets, total, sem):
    energies, orbitals, columns = inject.shape
    sections = received.shape[0]
    rows = CAP * energies * BLK

    def read(s, _):
        block = received[s, rows : rows + HEAD, :].astype(F32)
        heads[pl.ds(s, 1), :] = block[:1].astype(jnp.int32)
        return 0

    lax.fori_loop(0, sections, read, 0, unroll=min(sections, 8))
    fetch = pltpu.make_async_copy(heads, targets, sem)
    fetch.start()
    total[...] = inject[...].astype(F32)
    fetch.wait()

    def add(s, _):
        for r in range(CAP):
            first = pl.multiple_of(jnp.maximum(targets[s, r], 0) * BLK, BLK)
            for e in range(energies):
                item = received[s, (e * CAP + r) * BLK : (e * CAP + r + 1) * BLK, :]
                total[e, pl.ds(first, BLK), :] += item.astype(F32)
        return 0

    lax.fori_loop(0, sections, add, 0, unroll=2)
    source[...] = total[...].astype(BF16)


def placed_source(received, inject):
    energies, orbitals, columns = inject.shape
    sections = received.shape[0]
    return call(
        source_kernel,
        "source",
        [IN_VMEM] * 2,
        shape(*inject.shape),
        [
            pltpu.VMEM((sections, columns), jnp.int32),
            pltpu.SMEM((sections, columns), jnp.int32),
            pltpu.VMEM(inject.shape, F32),
            pltpu.SemaphoreType.DMA,
        ],
        1.0,
    )(received, inject)


def quarters_kernel(source, *refs):
    energies = source.shape[0]
    face_rows = refs[:energies]
    own, far, across, near, quarters = refs[energies:]
    split = GROUP // energies
    size = quarters.shape[1]
    for e in range(energies):
        wide = dot(face_rows[e][...], source[e]).T
        for h in range(split):
            quarters[e * split + h] = wide[h * size : (h + 1) * size]
    for out, at in zip((own, far, across, near), partners()):
        out[...] = quarters[at].astype(BF16)


def face_quarters(source, face_rows):
    energies, _, columns = source.shape
    face = face_rows[0].shape[0]
    rows = columns * energies // GROUP
    return call(
        quarters_kernel,
        "face_quarters",
        [IN_VMEM] * (1 + energies),
        [shape(rows, face)] * GROUP,
        [pltpu.VMEM((GROUP, rows, face), F32)],
        0.6,
    )(source, *face_rows)


def after_kernel(_packets, _map, _same_map):
    pass


def handed_on(item, packets):
    return call(
        after_kernel,
        "after_exchange",
        [IN_PLACE] * 2,
        [shape(*item.shape, dtype=item.dtype)],
        [],
        0.1,
        aliases={1: 0},
    )(packets, item)[0]


def collect(refs, held):
    for ref, at in zip(refs, partners()):
        held[at] = ref[...]


def total_kernel(own, far, across, near, parts, _image, out, local, shifts):
    collect((own, far, across, near), shifts)
    state = shifts[0].astype(F32)
    for j in range(1, GROUP):
        local[j - 1] = state
        state = shifts[j].astype(F32) + step_by(state, (parts[0, j], parts[1, j]))
    out[...] = state.astype(BF16)


def plane_total(shifts, parts, tie):
    rows, face = shifts[0].shape
    return call(
        total_kernel,
        "plane_total",
        [IN_VMEM] * (GROUP + 1) + [IN_PLACE],
        [shape(rows, face), shape(GROUP - 1, rows, face, dtype=F32)],
        [pltpu.VMEM((GROUP, rows, face), BF16)],
        3.0,
    )(*shifts, parts, tie)


def work_kernel(early, *refs):
    green, source, parts = refs[:3]
    held, (image, upto) = refs[3:-2], refs[-2:]
    plane = lax.axis_index("sec") // GROUP
    first, second = plane == 0, plane == 1

    @pl.when(first if early else jnp.logical_not(first))
    def _():
        for e in range(green.shape[0]):
            image[e] = dot(green[e], source[e])

    @pl.when(jnp.logical_not(second) if early else second)
    def _():
        maps = (parts[0, 0], parts[1, 0])
        for j in range(1, GROUP - 1):
            maps = two_parts(times((parts[0, j], parts[1, j]), maps))
            upto[0, j - 1], upto[1, j - 1] = maps

    if held:

        @pl.when(first)
        def _():
            image[...] = held[0][...]

        @pl.when(jnp.logical_not(second))
        def _():
            upto[...] = held[1][...]


def image_and_maps(green, source, parts, held=()):
    _, _, face, _ = parts.shape
    return call(
        functools.partial(work_kernel, not held),
        "image_and_maps",
        [IN_VMEM] * (3 + len(held)),
        [shape(*source.shape, dtype=F32), shape(2, GROUP - 2, face, face)],
        [],
        2.0 if held else 0.5,
    )(green, source, parts, *held)


def sweep_plane(state, parts, upto, local, out):
    held = [state]
    for j in range(1, GROUP):
        maps = (parts[0, 0], parts[1, 0]) if j == 1 else (upto[0, j - 2], upto[1, j - 2])
        held.append(local[j - 1] + step_by(state, maps))
    work = out[GROUP]
    for j, item in enumerate(held):
        work[j] = item
    for ref, at in zip(out, partners()):
        ref[...] = work[at].astype(BF16)


def entering_kernel(third, near_one, second, far_one, got, other, parts, upto, local, *out):
    first_core = place() % CORES == 0
    first = near_one[...].astype(F32) + far_one[...].astype(F32)
    state = third[...].astype(F32)
    rows = state.shape[0]
    for below, (one, two) in ((second[...].astype(F32), (other, got)), (first, (got, other))):
        factor = jnp.where(first_core, one[...], two[...])
        y = dot_rows(jnp.concatenate(two_parts(state), axis=0), factor)
        state = below + (y[:rows] + y[rows:])
    sweep_plane(state, parts, upto, local, out)


def entering_from_kernel(base, parts, upto, local, *out):
    sweep_plane(base[...], parts, upto, local, out)


def entering(body, args):
    half, columns = args[0].shape
    return call(
        body,
        "entering",
        [IN_VMEM] * len(args),
        [shape(half, columns)] * GROUP,
        [pltpu.VMEM((GROUP, half, columns), F32)],
        1.4,
    )(*args)


def waves_kernel(own, far, across, near, prop, image, out, arrived, wave, sem):
    collect((own, far, across, near), arrived)
    energies, orbitals, _ = prop.shape
    split = GROUP // energies
    pieces = sem.shape[1]
    size = orbitals // pieces
    moves = []
    for e in range(energies):
        incoming = jnp.concatenate([arrived[e * split + h] for h in range(split)], axis=0)
        for c in range(pieces):
            at = slice(c * size, (c + 1) * size)
            wave[e, at, :] = (dot_rows(prop[e, at, :], incoming) + image[e, at, :]).astype(BF16)
            moves.append(pltpu.make_async_copy(wave.at[e, pl.ds(c * size, size)], out.at[e, pl.ds(c * size, size)], sem.at[e, c]))
            moves[-1].start()
    for move in moves:
        move.wait()


def final_waves(arrived, prop, image):
    half, columns = arrived[0].shape
    energies = prop.shape[0]
    return pl.pallas_call(
        waves_kernel,
        name="waves",
        in_specs=[IN_VMEM] * (GROUP + 2),
        out_shape=shape(*image.shape),
        out_specs=IN_HBM,
        scratch_shapes=[
            pltpu.VMEM((GROUP, half, columns), BF16),
            pltpu.VMEM(image.shape, BF16),
            pltpu.SemaphoreType.DMA((energies, 4)),
        ],
        compiler_params=pltpu.CompilerParams(vmem_limit_bytes=VMEM_SMALL),
        cost_estimate=pl.CostEstimate(flops=int(1.3 * PEAK), bytes_accessed=0, transcendentals=0),
    )(*arrived, prop, image)


def to_near(item, sections):
    return lax.ppermute(item, "sec", [(s, s ^ 1) for s in range(sections)])


def to_across(item, sections):
    return lax.ppermute(item, "sec", [(s, s // GROUP * GROUP + (s % GROUP + CORES) % GROUP) for s in range(sections)])


def to_far(item, sections):
    return lax.ppermute(item, "sec", [(s, s // GROUP * GROUP + (s % GROUP + CORES) % GROUP ^ 1) for s in range(sections)])


def exchange(own, far, across, near, sections):
    return [own, to_far(far, sections), to_across(across, sections), to_near(near, sections)]


def up_shift(sections, k):
    return [(s, s + GROUP * k) for s in range(sections - GROUP * k)]


def maps_up(total_map, sections):
    pairs = []
    for i in range(GROUP):
        if i % CORES == 0:
            pairs += [(GROUP + i, 2 * GROUP + i), (2 * GROUP + i, 3 * GROUP + i)]
        else:
            pairs += [(GROUP + i, 3 * GROUP + i)]
    got = lax.ppermute(total_map, "sec", pairs)
    return got, lax.ppermute(got, "sec", [(s, s ^ 1) for s in range(2 * GROUP, sections)])


def between(item, *planes):
    pairs = [(p * GROUP + i, q * GROUP + i) for p, q in planes for i in range(GROUP)]
    return lax.ppermute(item, "sec", pairs)


def scan_below(total_map, total, sections):
    shift = lax.ppermute(total.astype(F32), "sec", up_shift(sections, 1))
    joined = lax.ppermute(total_map, "sec", up_shift(sections, 1))
    stride = 1
    while stride < sections // GROUP:
        other = lax.ppermute(shift, "sec", up_shift(sections, stride))
        other_map = lax.ppermute(joined, "sec", up_shift(sections, stride))
        shift = shift + dot_wide(other, joined.T)
        joined = dot_wide(joined, other_map)
        stride *= 2
    return shift


def per_device(green, injected, coupling, pattern, owner, pair_blocks):
    sections = lax.axis_size("sec")
    green, inject = green[0], injected[0]

    coupling, tiles = coupling[0], pattern[0].T
    outgoing = outgoing_pairs(owner[:, 0], pair_blocks.T, green, inject, sections)
    received = lax.all_to_all(outgoing, "sec", split_axis=0, concat_axis=0, tiled=True)

    own_map, other_map, *face_rows = face_maps(tiles, green, coupling)
    across = to_across(other_map, sections)
    near = to_near(own_map, sections)

    source = placed_source(received, inject)
    quarters = face_quarters(source, face_rows)
    shifts = exchange(*quarters, sections)
    across = handed_on(across, quarters[0])
    far = to_near(across, sections)
    four = sections // GROUP == 4
    total_map, parts = chain([own_map, far, across, near], BF16 if four else F32)
    early = image_and_maps(green, source, parts)
    maps = maps_up(total_map, sections) if four else []
    total, local = plane_total(shifts, parts, early[0])
    if four:
        fourth = between(total, (1, 2), (2, 3))
        third = between(total, (0, 2), (1, 3))
        second = between(total, (0, 1))
        first = between(total, (0, 3))
        image, upto = image_and_maps(green, source, parts, early)
        entered = entering(entering_kernel, (first, second, third, fourth, *maps, parts, upto, local))
    else:
        base = scan_below(total_map, total, sections)
        image, upto = image_and_maps(green, source, parts, early)
        entered = entering(entering_from_kernel, (base, parts, upto, local))
    arrived = exchange(*entered, sections)
    prop = propagator(tiles, green, coupling, entered[0])
    return final_waves(arrived, prop, image)[None]


def solution(mesh):
    in_specs = (
        P("sec", "grp", None, None),
        P("sec", "grp", None, None),
        P("sec", None, None),
        P("sec", None, None),
        P("sec", None),
        P("sec", None),
    )
    out_specs = P("sec", "grp", None, None)
    return jax.shard_map(
        per_device, mesh=mesh, in_specs=in_specs, out_specs=out_specs, check_vma=False
    )
```

```python
import functools

import jax
import jax.numpy as jnp
from jax import lax
from jax.experimental import pallas as pl
from jax.experimental.pallas import tpu as pltpu
from jax.sharding import PartitionSpec as P

BLK = 32
CAP = 2
GROUP = 4
HEAD = 8
CORES = 2

HIGH = lax.Precision.HIGHEST
F32 = jnp.float32
BF16 = jnp.bfloat16
VMEM_SMALL = 16 * 1024 * 1024
VMEM_WHOLE = 63400000
PEAK = 1.15e9

IN_VMEM = pl.BlockSpec(memory_space=pltpu.VMEM)
IN_SMEM = pl.BlockSpec(memory_space=pltpu.SMEM)
IN_HBM = pl.BlockSpec(memory_space=pltpu.HBM)
IN_PLACE = pl.BlockSpec(memory_space=pl.ANY)


def shape(*dims, dtype=BF16):
    return jax.ShapeDtypeStruct(dims, dtype)


def call(body, name, ins, outs, scratch, micros, vmem=VMEM_SMALL, aliases=None):
    places = list(range(len(outs))) if isinstance(outs, list) else 0
    return pl.pallas_call(
        body,
        name=name,
        in_specs=ins,
        out_shape=outs,
        out_specs=jax.tree.map(lambda k: IN_PLACE if k in (aliases or {}).values() else IN_VMEM, places),
        input_output_aliases=aliases or {},
        scratch_shapes=scratch,
        compiler_params=pltpu.CompilerParams(vmem_limit_bytes=vmem),
        cost_estimate=pl.CostEstimate(flops=int(micros * PEAK), bytes_accessed=0, transcendentals=0),
    )


def place():
    return lax.axis_index("sec") % GROUP


def partners():
    here = place()
    across = (here + CORES) % GROUP
    return here, across ^ 1, across, here ^ 1


def dot(a, b):
    return jnp.dot(a, b, preferred_element_type=F32)


def dot_wide(a, b):
    return jnp.dot(a, b, precision=HIGH, preferred_element_type=F32)


def two_parts(x):
    high = x.astype(BF16)
    return high, (x - high.astype(F32)).astype(BF16)


def dot_rows(a, b):
    return lax.dot_general(a, b, (((1,), (1,)), ((), ())), preferred_element_type=F32)


def step_by(state, maps):
    high, low = two_parts(state)
    rows = state.shape[0]
    y = dot_rows(jnp.concatenate([high, low], axis=0), maps[0])
    return y[:rows] + (y[rows:] + dot_rows(high, maps[1]))


def mask_tiles(pattern, coupling):
    high, wide = coupling.shape[0] // pattern.shape[1], coupling.shape[1] // pattern.shape[0]
    for i in range(pattern.shape[1]):
        for j in range(pattern.shape[0]):
            at = (slice(i * high, (i + 1) * high), slice(j * wide, (j + 1) * wide))
            tile = coupling[at]
            coupling[at] = jnp.where(pattern[j, i] == 1, tile, jnp.zeros_like(tile))


def pairs_kernel(owner_in, blocks_in, green, inject_in, out, owner, blocks, inject, held, product, slot_of, counts, sem, side, done, *packets):
    energies, orbitals, _ = green.shape
    sections = out.shape[0]
    count = owner.shape[0]
    named = held.shape[1] < orbitals
    parts = sem.shape[1]
    size = held.shape[1] // parts
    small = [
        pltpu.make_async_copy(src, dst, side.at[k])
        for k, (src, dst) in enumerate(((owner_in, owner), (blocks_in, blocks), (inject_in, inject)))
    ]
    for move in small:
        move.start()

    def copy_of(e, c, q):
        first = pl.multiple_of(blocks[0, q] * BLK, BLK)
        to = pl.multiple_of(q * BLK, BLK)
        return pltpu.make_async_copy(green.at[e, pl.ds(first, BLK)], held.at[e, pl.ds(to, BLK)], sem.at[e, c])

    def part_of(e, c):
        at = pl.ds(c * size, size)
        return pltpu.make_async_copy(green.at[e, at], held.at[e, at], sem.at[e, c])

    if not named:
        for e in range(energies):
            for c in range(parts):
                part_of(e, c).start()
    for move in small[:2]:
        move.wait()
    if named:
        for e in range(energies):
            for c in range(parts):
                lax.fori_loop(
                    c * (count // parts),
                    (c + 1) * (count // parts),
                    lambda q, _, e=e, c=c: copy_of(e, c, q).start(),
                    None,
                    unroll=4,
                )
    rows = CAP * BLK
    head = packets[-1]
    columns = out.shape[2]
    lane = lax.broadcasted_iota(jnp.int32, (HEAD, columns), 1)
    none = jnp.where(lane < CAP, -1.0, 0.0).astype(BF16)

    def blank(d, _):
        counts[d] = 0
        for packet in packets:
            packet[d, :rows, :] = jnp.zeros((rows, columns), BF16)
        head[d, rows : rows + HEAD, :] = none
        return 0

    lax.fori_loop(0, sections, blank, 0)

    def rank(q, _):
        d = owner[q]
        r = counts[d]
        counts[d] = r + 1
        slot_of[q] = r
        line = head[d, rows : rows + HEAD, :].astype(F32)
        line = jnp.where(lane == r, blocks[1, q].astype(F32), line)
        head[d, rows : rows + HEAD, :] = line.astype(BF16)
        return 0

    lax.fori_loop(0, count, rank, 0)
    small[2].wait()
    moves = []
    for e, packet in enumerate(packets):
        for c in range(parts):
            part_of(e, c).wait()
            at = slice(c * size, (c + 1) * size)
            product[e, at, :] = dot(held[e, at, :], inject[e]).astype(BF16)

        def fill(q, _):
            first = pl.multiple_of((q if named else blocks[0, q]) * BLK, BLK)
            to = pl.multiple_of(slot_of[q] * BLK, BLK)
            packet[owner[q], pl.ds(to, BLK), :] = product[e, pl.ds(first, BLK), :]
            return 0

        lax.fori_loop(0, count, fill, 0, unroll=4)
        moves.append(pltpu.make_async_copy(packet, out.at[:, pl.ds(e * rows, packet.shape[1])], done.at[e]))
        moves[-1].start()
    for move in moves:
        move.wait()


def outgoing_pairs(owner, blocks, green, inject, sections):
    energies, orbitals, _ = green.shape
    columns = inject.shape[2]
    rows = min(orbitals, owner.shape[0] * BLK)
    part = CAP * BLK
    parts = 2
    return pl.pallas_call(
        pairs_kernel,
        name="pairs",
        in_specs=[IN_HBM] * 4,
        out_shape=shape(sections, part * energies + HEAD, columns),
        out_specs=IN_HBM,
        scratch_shapes=[
            pltpu.SMEM(owner.shape, jnp.int32),
            pltpu.SMEM(blocks.shape, jnp.int32),
            pltpu.VMEM(inject.shape, BF16),
            pltpu.VMEM((energies, rows, orbitals), BF16),
            pltpu.VMEM((energies, rows, columns), BF16),
            pltpu.SMEM(owner.shape, jnp.int32),
            pltpu.SMEM((sections,), jnp.int32),
            pltpu.SemaphoreType.DMA((energies, parts)),
            pltpu.SemaphoreType.DMA((3,)),
            pltpu.SemaphoreType.DMA((energies,)),
        ]
        + [pltpu.VMEM((sections, part + (HEAD if e == energies - 1 else 0), columns), BF16) for e in range(energies)],
        compiler_params=pltpu.CompilerParams(vmem_limit_bytes=VMEM_WHOLE),
        cost_estimate=pl.CostEstimate(flops=int(4.0 * PEAK), bytes_accessed=0, transcendentals=0),
    )(owner, blocks, green, inject)


def maps_kernel(pattern, green, coupling, own, other, *refs):
    face_rows, (couple, maps) = refs[:-2], refs[-2:]
    energies, orbitals, _ = green.shape
    face = coupling.shape[1]
    couple[...] = coupling[...]
    mask_tiles(pattern, couple)
    for e in range(energies):
        rows = green[e, orbitals - face :, :]
        face_rows[e][...] = rows
        maps[e] = dot(rows, couple[...])
    mine = place() // CORES
    own[...] = maps[mine]
    other[...] = maps[1 - mine]


def face_maps(pattern, green, coupling):
    orbitals, face = coupling.shape
    square = shape(face, face, dtype=F32)
    return call(
        maps_kernel,
        "face_maps",
        [IN_SMEM, IN_VMEM, IN_VMEM],
        [square, square] + [shape(face, orbitals)] * green.shape[0],
        [pltpu.VMEM(coupling.shape, BF16), pltpu.VMEM((green.shape[0], face, face), F32)],
        1.2,
    )(pattern, green, coupling)


def prop_kernel(pattern, green, coupling, _tie, out, couple):
    couple[...] = coupling[...]
    mask_tiles(pattern, couple)
    for e in range(green.shape[0]):
        out[e] = dot(green[e], couple[...]).astype(BF16)


def propagator(pattern, green, coupling, tie):
    energies, orbitals, _ = green.shape
    return call(
        prop_kernel,
        "prop",
        [IN_SMEM, IN_VMEM, IN_VMEM, IN_PLACE],
        shape(energies, orbitals, coupling.shape[1]),
        [pltpu.VMEM(coupling.shape, BF16)],
        1.5,
    )(pattern, green, coupling, tie)


def times(a, b):
    return dot(a[0], b[0]) + (dot(a[0], b[1]) + dot(a[1], b[0]))


def chain_kernel(own, far, across, near, total_out, parts, maps):
    collect((own, far, across, near), maps)
    split = [two_parts(maps[j]) for j in range(GROUP)]
    lower, upper = two_parts(times(split[1], split[0])), two_parts(times(split[3], split[2]))
    total_out[...] = times(upper, lower).astype(total_out.dtype)
    for j, (high, low) in enumerate(split):
        parts[0, j] = high
        parts[1, j] = low


def chain(maps, dtype):
    face = maps[0].shape[0]
    return call(
        chain_kernel,
        "chain_maps",
        [IN_VMEM] * GROUP,
        [shape(face, face, dtype=dtype), shape(2, GROUP, face, face)],
        [pltpu.VMEM((GROUP, face, face), F32)],
        0.9,
    )(*maps)


def source_kernel(received, inject, source, heads, targets, total, sem):
    energies, orbitals, columns = inject.shape
    sections = received.shape[0]
    rows = CAP * energies * BLK

    def read(s, _):
        block = received[s, rows : rows + HEAD, :].astype(F32)
        heads[pl.ds(s, 1), :] = block[:1].astype(jnp.int32)
        return 0

    lax.fori_loop(0, sections, read, 0, unroll=min(sections, 8))
    fetch = pltpu.make_async_copy(heads, targets, sem)
    fetch.start()
    total[...] = inject[...].astype(F32)
    fetch.wait()

    def add(s, _):
        for r in range(CAP):
            first = pl.multiple_of(jnp.maximum(targets[s, r], 0) * BLK, BLK)
            for e in range(energies):
                item = received[s, (e * CAP + r) * BLK : (e * CAP + r + 1) * BLK, :]
                total[e, pl.ds(first, BLK), :] += item.astype(F32)
        return 0

    lax.fori_loop(0, sections, add, 0, unroll=min(sections, 8))
    source[...] = total[...].astype(BF16)


def placed_source(received, inject):
    energies, orbitals, columns = inject.shape
    sections = received.shape[0]
    return call(
        source_kernel,
        "source",
        [IN_VMEM] * 2,
        shape(*inject.shape),
        [
            pltpu.VMEM((sections, columns), jnp.int32),
            pltpu.SMEM((sections, columns), jnp.int32),
            pltpu.VMEM(inject.shape, F32),
            pltpu.SemaphoreType.DMA,
        ],
        1.0,
    )(received, inject)


def quarters_kernel(source, *refs):
    energies = source.shape[0]
    face_rows = refs[:energies]
    own, far, across, near, quarters = refs[energies:]
    split = GROUP // energies
    size = quarters.shape[1]
    for e in range(energies):
        wide = dot(face_rows[e][...], source[e]).T
        for h in range(split):
            quarters[e * split + h] = wide[h * size : (h + 1) * size]
    for out, at in zip((own, far, across, near), partners()):
        out[...] = quarters[at].astype(BF16)


def face_quarters(source, face_rows):
    energies, _, columns = source.shape
    face = face_rows[0].shape[0]
    rows = columns * energies // GROUP
    return call(
        quarters_kernel,
        "face_quarters",
        [IN_VMEM] * (1 + energies),
        [shape(rows, face)] * GROUP,
        [pltpu.VMEM((GROUP, rows, face), F32)],
        0.6,
    )(source, *face_rows)


def after_kernel(_packets, _map, _same_map):
    pass


def handed_on(item, packets):
    return call(
        after_kernel,
        "after_exchange",
        [IN_PLACE] * 2,
        [shape(*item.shape, dtype=item.dtype)],
        [],
        0.1,
        aliases={1: 0},
    )(packets, item)[0]


def collect(refs, held):
    for ref, at in zip(refs, partners()):
        held[at] = ref[...]


def total_kernel(own, far, across, near, parts, _image, out, local, shifts):
    collect((own, far, across, near), shifts)
    state = shifts[0].astype(F32)
    for j in range(1, GROUP):
        local[j - 1] = state
        state = shifts[j].astype(F32) + step_by(state, (parts[0, j], parts[1, j]))
    out[...] = state.astype(BF16)


def plane_total(shifts, parts, tie):
    rows, face = shifts[0].shape
    return call(
        total_kernel,
        "plane_total",
        [IN_VMEM] * (GROUP + 1) + [IN_PLACE],
        [shape(rows, face), shape(GROUP - 1, rows, face, dtype=F32)],
        [pltpu.VMEM((GROUP, rows, face), BF16)],
        3.0,
    )(*shifts, parts, tie)


def work_kernel(early, *refs):
    green, source, parts = refs[:3]
    held, (image, upto) = refs[3:-2], refs[-2:]
    low_plane = lax.axis_index("sec") // GROUP == 0

    @pl.when(low_plane if early else jnp.logical_not(low_plane))
    def _():
        for e in range(green.shape[0]):
            image[e] = dot(green[e], source[e])
        maps = (parts[0, 0], parts[1, 0])
        for j in range(1, GROUP - 1):
            maps = two_parts(times((parts[0, j], parts[1, j]), maps))
            upto[0, j - 1], upto[1, j - 1] = maps

    if held:

        @pl.when(low_plane)
        def _():
            image[...] = held[0][...]
            upto[...] = held[1][...]


def image_and_maps(green, source, parts, held=()):
    _, _, face, _ = parts.shape
    return call(
        functools.partial(work_kernel, not held),
        "image_and_maps",
        [IN_VMEM] * (3 + len(held)),
        [shape(*source.shape, dtype=F32), shape(2, GROUP - 2, face, face)],
        [],
        2.0,
    )(green, source, parts, *held)


def sweep_plane(state, parts, upto, local, out):
    held = [state]
    for j in range(1, GROUP):
        maps = (parts[0, 0], parts[1, 0]) if j == 1 else (upto[0, j - 2], upto[1, j - 2])
        held.append(local[j - 1] + step_by(state, maps))
    work = out[GROUP]
    for j, item in enumerate(held):
        work[j] = item
    for ref, at in zip(out, partners()):
        ref[...] = work[at].astype(BF16)


def entering_kernel(third, near_one, second, far_one, got, other, parts, upto, local, *out):
    first_core = place() % CORES == 0
    first = near_one[...].astype(F32) + far_one[...].astype(F32)
    state = third[...].astype(F32)
    rows = state.shape[0]
    for below, (one, two) in ((second[...].astype(F32), (other, got)), (first, (got, other))):
        factor = jnp.where(first_core, one[...], two[...])
        y = dot_rows(jnp.concatenate(two_parts(state), axis=0), factor)
        state = below + (y[:rows] + y[rows:])
    sweep_plane(state, parts, upto, local, out)


def entering_from_kernel(base, parts, upto, local, *out):
    sweep_plane(base[...], parts, upto, local, out)


def entering(body, args):
    half, columns = args[0].shape
    return call(
        body,
        "entering",
        [IN_VMEM] * len(args),
        [shape(half, columns)] * GROUP,
        [pltpu.VMEM((GROUP, half, columns), F32)],
        1.4,
    )(*args)


def waves_kernel(own, far, across, near, prop, image, out, arrived, wave, sem):
    collect((own, far, across, near), arrived)
    energies, orbitals, _ = prop.shape
    split = GROUP // energies
    pieces = sem.shape[1]
    size = orbitals // pieces
    moves = []
    for e in range(energies):
        incoming = jnp.concatenate([arrived[e * split + h] for h in range(split)], axis=0)
        for c in range(pieces):
            at = slice(c * size, (c + 1) * size)
            wave[e, at, :] = (dot_rows(prop[e, at, :], incoming) + image[e, at, :]).astype(BF16)
            moves.append(pltpu.make_async_copy(wave.at[e, pl.ds(c * size, size)], out.at[e, pl.ds(c * size, size)], sem.at[e, c]))
            moves[-1].start()
    for move in moves:
        move.wait()


def final_waves(arrived, prop, image):
    half, columns = arrived[0].shape
    energies = prop.shape[0]
    return pl.pallas_call(
        waves_kernel,
        name="waves",
        in_specs=[IN_VMEM] * (GROUP + 2),
        out_shape=shape(*image.shape),
        out_specs=IN_HBM,
        scratch_shapes=[
            pltpu.VMEM((GROUP, half, columns), BF16),
            pltpu.VMEM(image.shape, BF16),
            pltpu.SemaphoreType.DMA((energies, 2)),
        ],
        compiler_params=pltpu.CompilerParams(vmem_limit_bytes=VMEM_SMALL),
        cost_estimate=pl.CostEstimate(flops=int(1.3 * PEAK), bytes_accessed=0, transcendentals=0),
    )(*arrived, prop, image)


def to_near(item, sections):
    return lax.ppermute(item, "sec", [(s, s ^ 1) for s in range(sections)])


def to_across(item, sections):
    return lax.ppermute(item, "sec", [(s, s // GROUP * GROUP + (s % GROUP + CORES) % GROUP) for s in range(sections)])


def to_far(item, sections):
    return lax.ppermute(item, "sec", [(s, s // GROUP * GROUP + (s % GROUP + CORES) % GROUP ^ 1) for s in range(sections)])


def exchange(own, far, across, near, sections):
    return [own, to_far(far, sections), to_across(across, sections), to_near(near, sections)]


def up_shift(sections, k):
    return [(s, s + GROUP * k) for s in range(sections - GROUP * k)]


def maps_up(total_map, sections):
    pairs = []
    for i in range(GROUP):
        if i % CORES == 0:
            pairs += [(GROUP + i, 2 * GROUP + i), (2 * GROUP + i, 3 * GROUP + i)]
        else:
            pairs += [(GROUP + i, 3 * GROUP + i)]
    got = lax.ppermute(total_map, "sec", pairs)
    return got, lax.ppermute(got, "sec", [(s, s ^ 1) for s in range(2 * GROUP, sections)])


def between(item, *planes):
    pairs = [(p * GROUP + i, q * GROUP + i) for p, q in planes for i in range(GROUP)]
    return lax.ppermute(item, "sec", pairs)


def scan_below(total_map, total, sections):
    shift = lax.ppermute(total.astype(F32), "sec", up_shift(sections, 1))
    joined = lax.ppermute(total_map, "sec", up_shift(sections, 1))
    stride = 1
    while stride < sections // GROUP:
        other = lax.ppermute(shift, "sec", up_shift(sections, stride))
        other_map = lax.ppermute(joined, "sec", up_shift(sections, stride))
        shift = shift + dot_wide(other, joined.T)
        joined = dot_wide(joined, other_map)
        stride *= 2
    return shift


def per_device(green, injected, coupling, pattern, owner, pair_blocks):
    sections = lax.axis_size("sec")
    green, inject = green[0], injected[0]

    coupling, tiles = coupling[0], pattern[0].T
    outgoing = outgoing_pairs(owner[:, 0], pair_blocks.T, green, inject, sections)
    received = lax.all_to_all(outgoing, "sec", split_axis=0, concat_axis=0, tiled=True)

    own_map, other_map, *face_rows = face_maps(tiles, green, coupling)
    across = to_across(other_map, sections)
    near = to_near(own_map, sections)

    source = placed_source(received, inject)
    quarters = face_quarters(source, face_rows)
    shifts = exchange(*quarters, sections)
    across = handed_on(across, quarters[0])
    far = to_near(across, sections)
    four = sections // GROUP == 4
    total_map, parts = chain([own_map, far, across, near], BF16 if four else F32)
    early = image_and_maps(green, source, parts)
    maps = maps_up(total_map, sections) if four else []
    total, local = plane_total(shifts, parts, early[0])
    if four:
        fourth = between(total, (1, 2), (2, 3))
        third = between(total, (0, 2), (1, 3))
        second = between(total, (0, 1))
        first = between(total, (0, 3))
        image, upto = image_and_maps(green, source, parts, early)
        entered = entering(entering_kernel, (first, second, third, fourth, *maps, parts, upto, local))
    else:
        base = scan_below(total_map, total, sections)
        image, upto = image_and_maps(green, source, parts, early)
        entered = entering(entering_from_kernel, (base, parts, upto, local))
    arrived = exchange(*entered, sections)
    prop = propagator(tiles, green, coupling, entered[0])
    return final_waves(arrived, prop, image)[None]


def solution(mesh):
    in_specs = (
        P("sec", "grp", None, None),
        P("sec", "grp", None, None),
        P("sec", None, None),
        P("sec", None, None),
        P("sec", None),
        P("sec", None),
    )
    out_specs = P("sec", "grp", None, None)
    return jax.shard_map(
        per_device, mesh=mesh, in_specs=in_specs, out_specs=out_specs, check_vma=False
    )
```

```python
import functools

import jax
import jax.numpy as jnp
from jax import lax
from jax.experimental import pallas as pl
from jax.experimental.pallas import tpu as pltpu
from jax.sharding import PartitionSpec as P

BLK = 32
CAP = 2
GROUP = 4
HEAD = 8
CORES = 2

HIGH = lax.Precision.HIGHEST
F32 = jnp.float32
BF16 = jnp.bfloat16
VMEM_SMALL = 16 * 1024 * 1024
VMEM_WHOLE = 63400000
PEAK = 1.15e9

IN_VMEM = pl.BlockSpec(memory_space=pltpu.VMEM)
IN_SMEM = pl.BlockSpec(memory_space=pltpu.SMEM)
IN_HBM = pl.BlockSpec(memory_space=pltpu.HBM)
IN_PLACE = pl.BlockSpec(memory_space=pl.ANY)


def shape(*dims, dtype=BF16):
    return jax.ShapeDtypeStruct(dims, dtype)


def call(body, name, ins, outs, scratch, micros, vmem=VMEM_SMALL, aliases=None):
    places = list(range(len(outs))) if isinstance(outs, list) else 0
    return pl.pallas_call(
        body,
        name=name,
        in_specs=ins,
        out_shape=outs,
        out_specs=jax.tree.map(lambda k: IN_PLACE if k in (aliases or {}).values() else IN_VMEM, places),
        input_output_aliases=aliases or {},
        scratch_shapes=scratch,
        compiler_params=pltpu.CompilerParams(vmem_limit_bytes=vmem),
        cost_estimate=pl.CostEstimate(flops=int(micros * PEAK), bytes_accessed=0, transcendentals=0),
    )


def place():
    return lax.axis_index("sec") % GROUP


def partners():
    here = place()
    across = (here + CORES) % GROUP
    return here, across ^ 1, across, here ^ 1


def dot(a, b):
    return jnp.dot(a, b, preferred_element_type=F32)


def dot_wide(a, b):
    return jnp.dot(a, b, precision=HIGH, preferred_element_type=F32)


def two_parts(x):
    high = x.astype(BF16)
    return high, (x - high.astype(F32)).astype(BF16)


def dot_rows(a, b):
    return lax.dot_general(a, b, (((1,), (1,)), ((), ())), preferred_element_type=F32)


def step_by(state, maps):
    high, low = two_parts(state)
    rows = state.shape[0]
    y = dot_rows(jnp.concatenate([high, low], axis=0), maps[0])
    return y[:rows] + (y[rows:] + dot_rows(high, maps[1]))


def mask_tiles(pattern, coupling):
    high, wide = coupling.shape[0] // pattern.shape[1], coupling.shape[1] // pattern.shape[0]
    for i in range(pattern.shape[1]):
        for j in range(pattern.shape[0]):
            at = (slice(i * high, (i + 1) * high), slice(j * wide, (j + 1) * wide))
            tile = coupling[at]
            coupling[at] = jnp.where(pattern[j, i] == 1, tile, jnp.zeros_like(tile))


def pairs_kernel(owner_in, blocks_in, green, inject_in, out, owner, blocks, inject, held, product, slot_of, counts, sem, side, done, *packets):
    energies, orbitals, _ = green.shape
    sections = out.shape[0]
    count = owner.shape[0]
    named = held.shape[1] < orbitals
    parts = sem.shape[1]
    size = held.shape[1] // parts
    small = [
        pltpu.make_async_copy(src, dst, side.at[k])
        for k, (src, dst) in enumerate(((owner_in, owner), (blocks_in, blocks), (inject_in, inject)))
    ]
    for move in small:
        move.start()

    def copy_of(e, c, q):
        first = pl.multiple_of(blocks[0, q] * BLK, BLK)
        to = pl.multiple_of(q * BLK, BLK)
        return pltpu.make_async_copy(green.at[e, pl.ds(first, BLK)], held.at[e, pl.ds(to, BLK)], sem.at[e, c])

    def part_of(e, c):
        at = pl.ds(c * size, size)
        return pltpu.make_async_copy(green.at[e, at], held.at[e, at], sem.at[e, c])

    if not named:
        for e in range(energies):
            for c in range(parts):
                part_of(e, c).start()
    for move in small[:2]:
        move.wait()
    if named:
        for e in range(energies):
            for c in range(parts):
                lax.fori_loop(
                    c * (count // parts),
                    (c + 1) * (count // parts),
                    lambda q, _, e=e, c=c: copy_of(e, c, q).start(),
                    None,
                    unroll=4,
                )
    rows = CAP * BLK
    head = packets[-1]
    columns = out.shape[2]
    lane = lax.broadcasted_iota(jnp.int32, (HEAD, columns), 1)
    none = jnp.where(lane < CAP, -1.0, 0.0).astype(BF16)

    def blank(d, _):
        counts[d] = 0
        for packet in packets:
            packet[d, :rows, :] = jnp.zeros((rows, columns), BF16)
        head[d, rows : rows + HEAD, :] = none
        return 0

    lax.fori_loop(0, sections, blank, 0)

    def rank(q, _):
        d = owner[q]
        r = counts[d]
        counts[d] = r + 1
        slot_of[q] = r
        line = head[d, rows : rows + HEAD, :].astype(F32)
        line = jnp.where(lane == r, blocks[1, q].astype(F32), line)
        head[d, rows : rows + HEAD, :] = line.astype(BF16)
        return 0

    lax.fori_loop(0, count, rank, 0)
    small[2].wait()
    moves = []
    for e, packet in enumerate(packets):
        for c in range(parts):
            part_of(e, c).wait()
            at = slice(c * size, (c + 1) * size)
            product[e, at, :] = dot(held[e, at, :], inject[e]).astype(BF16)

        def fill(q, _):
            first = pl.multiple_of((q if named else blocks[0, q]) * BLK, BLK)
            to = pl.multiple_of(slot_of[q] * BLK, BLK)
            packet[owner[q], pl.ds(to, BLK), :] = product[e, pl.ds(first, BLK), :]
            return 0

        lax.fori_loop(0, count, fill, 0, unroll=4)
        moves.append(pltpu.make_async_copy(packet, out.at[:, pl.ds(e * rows, packet.shape[1])], done.at[e]))
        moves[-1].start()
    for move in moves:
        move.wait()


def outgoing_pairs(owner, blocks, green, inject, sections):
    energies, orbitals, _ = green.shape
    columns = inject.shape[2]
    rows = min(orbitals, owner.shape[0] * BLK)
    part = CAP * BLK
    parts = 2
    return pl.pallas_call(
        pairs_kernel,
        name="pairs",
        in_specs=[IN_HBM] * 4,
        out_shape=shape(sections, part * energies + HEAD, columns),
        out_specs=IN_HBM,
        scratch_shapes=[
            pltpu.SMEM(owner.shape, jnp.int32),
            pltpu.SMEM(blocks.shape, jnp.int32),
            pltpu.VMEM(inject.shape, BF16),
            pltpu.VMEM((energies, rows, orbitals), BF16),
            pltpu.VMEM((energies, rows, columns), BF16),
            pltpu.SMEM(owner.shape, jnp.int32),
            pltpu.SMEM((sections,), jnp.int32),
            pltpu.SemaphoreType.DMA((energies, parts)),
            pltpu.SemaphoreType.DMA((3,)),
            pltpu.SemaphoreType.DMA((energies,)),
        ]
        + [pltpu.VMEM((sections, part + (HEAD if e == energies - 1 else 0), columns), BF16) for e in range(energies)],
        compiler_params=pltpu.CompilerParams(vmem_limit_bytes=VMEM_WHOLE),
        cost_estimate=pl.CostEstimate(flops=int(4.0 * PEAK), bytes_accessed=0, transcendentals=0),
    )(owner, blocks, green, inject)


def maps_kernel(pattern, green, coupling, own, other, *refs):
    face_rows, (couple, maps) = refs[:-2], refs[-2:]
    energies, orbitals, _ = green.shape
    face = coupling.shape[1]
    couple[...] = coupling[...]
    mask_tiles(pattern, couple)
    for e in range(energies):
        rows = green[e, orbitals - face :, :]
        face_rows[e][...] = rows
        maps[e] = dot(rows, couple[...])
    mine = place() // CORES
    own[...] = maps[mine]
    other[...] = maps[1 - mine]


def face_maps(pattern, green, coupling):
    orbitals, face = coupling.shape
    square = shape(face, face, dtype=F32)
    return call(
        maps_kernel,
        "face_maps",
        [IN_SMEM, IN_VMEM, IN_VMEM],
        [square, square] + [shape(face, orbitals)] * green.shape[0],
        [pltpu.VMEM(coupling.shape, BF16), pltpu.VMEM((green.shape[0], face, face), F32)],
        1.2,
    )(pattern, green, coupling)


def prop_kernel(pattern, green, coupling, _tie, out, couple):
    couple[...] = coupling[...]
    mask_tiles(pattern, couple)
    for e in range(green.shape[0]):
        out[e] = dot(green[e], couple[...]).astype(BF16)


def propagator(pattern, green, coupling, tie):
    energies, orbitals, _ = green.shape
    return call(
        prop_kernel,
        "prop",
        [IN_SMEM, IN_VMEM, IN_VMEM, IN_PLACE],
        shape(energies, orbitals, coupling.shape[1]),
        [pltpu.VMEM(coupling.shape, BF16)],
        1.5,
    )(pattern, green, coupling, tie)


def times(a, b):
    return dot(a[0], b[0]) + (dot(a[0], b[1]) + dot(a[1], b[0]))


def chain_kernel(own, far, across, near, total_out, parts, maps):
    collect((own, far, across, near), maps)
    split = [two_parts(maps[j]) for j in range(GROUP)]
    lower, upper = two_parts(times(split[1], split[0])), two_parts(times(split[3], split[2]))
    total_out[...] = times(upper, lower).astype(total_out.dtype)
    for j, (high, low) in enumerate(split):
        parts[0, j] = high
        parts[1, j] = low


def chain(maps, dtype):
    face = maps[0].shape[0]
    return call(
        chain_kernel,
        "chain_maps",
        [IN_VMEM] * GROUP,
        [shape(face, face, dtype=dtype), shape(2, GROUP, face, face)],
        [pltpu.VMEM((GROUP, face, face), F32)],
        0.9,
    )(*maps)


def source_kernel(received, inject, source, heads, targets, total, sem):
    energies, orbitals, columns = inject.shape
    sections = received.shape[0]
    rows = CAP * energies * BLK

    def read(s, _):
        block = received[s, rows : rows + HEAD, :].astype(F32)
        heads[pl.ds(s, 1), :] = block[:1].astype(jnp.int32)
        return 0

    lax.fori_loop(0, sections, read, 0, unroll=min(sections, 8))
    fetch = pltpu.make_async_copy(heads, targets, sem)
    fetch.start()
    total[...] = inject[...].astype(F32)
    fetch.wait()

    def add(s, _):
        for r in range(CAP):
            first = pl.multiple_of(jnp.maximum(targets[s, r], 0) * BLK, BLK)
            for e in range(energies):
                item = received[s, (e * CAP + r) * BLK : (e * CAP + r + 1) * BLK, :]
                total[e, pl.ds(first, BLK), :] += item.astype(F32)
        return 0

    lax.fori_loop(0, sections, add, 0, unroll=min(sections, 8))
    source[...] = total[...].astype(BF16)


def placed_source(received, inject):
    energies, orbitals, columns = inject.shape
    sections = received.shape[0]
    return call(
        source_kernel,
        "source",
        [IN_VMEM] * 2,
        shape(*inject.shape),
        [
            pltpu.VMEM((sections, columns), jnp.int32),
            pltpu.SMEM((sections, columns), jnp.int32),
            pltpu.VMEM(inject.shape, F32),
            pltpu.SemaphoreType.DMA,
        ],
        1.0,
    )(received, inject)


def quarters_kernel(source, *refs):
    energies = source.shape[0]
    face_rows = refs[:energies]
    own, far, across, near, quarters = refs[energies:]
    split = GROUP // energies
    size = quarters.shape[1]
    for e in range(energies):
        wide = dot(face_rows[e][...], source[e]).T
        for h in range(split):
            quarters[e * split + h] = wide[h * size : (h + 1) * size]
    for out, at in zip((own, far, across, near), partners()):
        out[...] = quarters[at].astype(BF16)


def face_quarters(source, face_rows):
    energies, _, columns = source.shape
    face = face_rows[0].shape[0]
    rows = columns * energies // GROUP
    return call(
        quarters_kernel,
        "face_quarters",
        [IN_VMEM] * (1 + energies),
        [shape(rows, face)] * GROUP,
        [pltpu.VMEM((GROUP, rows, face), F32)],
        0.6,
    )(source, *face_rows)


def after_kernel(_packets, _map, _same_map):
    pass


def handed_on(item, packets):
    return call(
        after_kernel,
        "after_exchange",
        [IN_PLACE] * 2,
        [shape(*item.shape, dtype=item.dtype)],
        [],
        0.1,
        aliases={1: 0},
    )(packets, item)[0]


def collect(refs, held):
    for ref, at in zip(refs, partners()):
        held[at] = ref[...]


def total_kernel(own, across, far, near, parts, _image, out, local, shifts):
    collect((own, far, across, near), shifts)
    state = shifts[0].astype(F32)
    for j in range(1, GROUP):
        local[j - 1] = state
        state = shifts[j].astype(F32) + step_by(state, (parts[0, j], parts[1, j]))
    out[...] = state.astype(BF16)


def plane_total(shifts, parts, tie):
    rows, face = shifts[0].shape
    return call(
        total_kernel,
        "plane_total",
        [IN_VMEM] * (GROUP + 1) + [IN_PLACE],
        [shape(rows, face), shape(GROUP - 1, rows, face, dtype=F32)],
        [pltpu.VMEM((GROUP, rows, face), BF16)],
        3.0,
    )(shifts[0], shifts[2], shifts[1], shifts[3], parts, tie)


def work_kernel(early, *refs):
    green, source, parts = refs[:3]
    held, (image, upto) = refs[3:-2], refs[-2:]
    low_plane = lax.axis_index("sec") // GROUP == 0

    @pl.when(low_plane if early else jnp.logical_not(low_plane))
    def _():
        for e in range(green.shape[0]):
            image[e] = dot(green[e], source[e])
        maps = (parts[0, 0], parts[1, 0])
        for j in range(1, GROUP - 1):
            maps = two_parts(times((parts[0, j], parts[1, j]), maps))
            upto[0, j - 1], upto[1, j - 1] = maps

    if held:

        @pl.when(low_plane)
        def _():
            image[...] = held[0][...]
            upto[...] = held[1][...]


def image_and_maps(green, source, parts, held=()):
    _, _, face, _ = parts.shape
    return call(
        functools.partial(work_kernel, not held),
        "image_and_maps",
        [IN_VMEM] * (3 + len(held)),
        [shape(*source.shape, dtype=F32), shape(2, GROUP - 2, face, face)],
        [],
        2.0,
    )(green, source, parts, *held)


def sweep_plane(state, parts, upto, local, out):
    held = [state]
    for j in range(1, GROUP):
        maps = (parts[0, 0], parts[1, 0]) if j == 1 else (upto[0, j - 2], upto[1, j - 2])
        held.append(local[j - 1] + step_by(state, maps))
    work = out[GROUP]
    for j, item in enumerate(held):
        work[j] = item
    for ref, at in zip(out, partners()):
        ref[...] = work[at].astype(BF16)


def entering_kernel(third, near_one, second, far_one, got, other, parts, upto, local, *out):
    first_core = place() % CORES == 0
    first = near_one[...].astype(F32) + far_one[...].astype(F32)
    state = third[...].astype(F32)
    rows = state.shape[0]
    for below, (one, two) in ((second[...].astype(F32), (other, got)), (first, (got, other))):
        factor = jnp.where(first_core, one[...], two[...])
        y = dot_rows(jnp.concatenate(two_parts(state), axis=0), factor)
        state = below + (y[:rows] + y[rows:])
    sweep_plane(state, parts, upto, local, out)


def entering_from_kernel(base, parts, upto, local, *out):
    sweep_plane(base[...], parts, upto, local, out)


def entering(body, args):
    half, columns = args[0].shape
    return call(
        body,
        "entering",
        [IN_VMEM] * len(args),
        [shape(half, columns)] * GROUP,
        [pltpu.VMEM((GROUP, half, columns), F32)],
        1.4,
    )(*args)


def waves_kernel(own, far, across, near, prop, image, out, arrived, wave, sem):
    collect((own, far, across, near), arrived)
    energies, orbitals, _ = prop.shape
    split = GROUP // energies
    pieces = sem.shape[1]
    size = orbitals // pieces
    moves = []
    for e in range(energies):
        incoming = jnp.concatenate([arrived[e * split + h] for h in range(split)], axis=0)
        for c in range(pieces):
            at = slice(c * size, (c + 1) * size)
            wave[e, at, :] = (dot_rows(prop[e, at, :], incoming) + image[e, at, :]).astype(BF16)
            moves.append(pltpu.make_async_copy(wave.at[e, pl.ds(c * size, size)], out.at[e, pl.ds(c * size, size)], sem.at[e, c]))
            moves[-1].start()
    for move in moves:
        move.wait()


def final_waves(arrived, prop, image):
    half, columns = arrived[0].shape
    energies = prop.shape[0]
    return pl.pallas_call(
        waves_kernel,
        name="waves",
        in_specs=[IN_VMEM] * (GROUP + 2),
        out_shape=shape(*image.shape),
        out_specs=IN_HBM,
        scratch_shapes=[
            pltpu.VMEM((GROUP, half, columns), BF16),
            pltpu.VMEM(image.shape, BF16),
            pltpu.SemaphoreType.DMA((energies, 2)),
        ],
        compiler_params=pltpu.CompilerParams(vmem_limit_bytes=VMEM_SMALL),
        cost_estimate=pl.CostEstimate(flops=int(1.3 * PEAK), bytes_accessed=0, transcendentals=0),
    )(*arrived, prop, image)


def to_near(item, sections):
    return lax.ppermute(item, "sec", [(s, s ^ 1) for s in range(sections)])


def to_across(item, sections):
    return lax.ppermute(item, "sec", [(s, s // GROUP * GROUP + (s % GROUP + CORES) % GROUP) for s in range(sections)])


def to_far(item, sections):
    return lax.ppermute(item, "sec", [(s, s // GROUP * GROUP + (s % GROUP + CORES) % GROUP ^ 1) for s in range(sections)])


def exchange(own, far, across, near, sections):
    return [own, to_far(far, sections), to_across(across, sections), to_near(near, sections)]


def up_shift(sections, k):
    return [(s, s + GROUP * k) for s in range(sections - GROUP * k)]


def maps_up(total_map, sections):
    pairs = []
    for i in range(GROUP):
        if i % CORES == 0:
            pairs += [(GROUP + i, 2 * GROUP + i), (2 * GROUP + i, 3 * GROUP + i)]
        else:
            pairs += [(GROUP + i, 3 * GROUP + i)]
    got = lax.ppermute(total_map, "sec", pairs)
    return got, lax.ppermute(got, "sec", [(s, s ^ 1) for s in range(2 * GROUP, sections)])


def between(item, *planes):
    pairs = [(p * GROUP + i, q * GROUP + i) for p, q in planes for i in range(GROUP)]
    return lax.ppermute(item, "sec", pairs)


def scan_below(total_map, total, sections):
    shift = lax.ppermute(total.astype(F32), "sec", up_shift(sections, 1))
    joined = lax.ppermute(total_map, "sec", up_shift(sections, 1))
    stride = 1
    while stride < sections // GROUP:
        other = lax.ppermute(shift, "sec", up_shift(sections, stride))
        other_map = lax.ppermute(joined, "sec", up_shift(sections, stride))
        shift = shift + dot_wide(other, joined.T)
        joined = dot_wide(joined, other_map)
        stride *= 2
    return shift


def per_device(green, injected, coupling, pattern, owner, pair_blocks):
    sections = lax.axis_size("sec")
    green, inject = green[0], injected[0]

    coupling, tiles = coupling[0], pattern[0].T
    outgoing = outgoing_pairs(owner[:, 0], pair_blocks.T, green, inject, sections)
    received = lax.all_to_all(outgoing, "sec", split_axis=0, concat_axis=0, tiled=True)

    own_map, other_map, *face_rows = face_maps(tiles, green, coupling)
    across = to_across(other_map, sections)
    near = to_near(own_map, sections)

    source = placed_source(received, inject)
    quarters = face_quarters(source, face_rows)
    shifts = exchange(*quarters, sections)
    across = handed_on(across, quarters[0])
    far = to_near(across, sections)
    four = sections // GROUP == 4
    total_map, parts = chain([own_map, far, across, near], BF16 if four else F32)
    early = image_and_maps(green, source, parts)
    maps = maps_up(total_map, sections) if four else []
    total, local = plane_total(shifts, parts, early[0])
    if four:
        fourth = between(total, (1, 2), (2, 3))
        third = between(total, (0, 2), (1, 3))
        second = between(total, (0, 1))
        first = between(total, (0, 3))
        image, upto = image_and_maps(green, source, parts, early)
        entered = entering(entering_kernel, (first, second, third, fourth, *maps, parts, upto, local))
    else:
        base = scan_below(total_map, total, sections)
        image, upto = image_and_maps(green, source, parts, early)
        entered = entering(entering_from_kernel, (base, parts, upto, local))
    arrived = exchange(*entered, sections)
    prop = propagator(tiles, green, coupling, entered[0])
    return final_waves(arrived, prop, image)[None]


def solution(mesh):
    in_specs = (
        P("sec", "grp", None, None),
        P("sec", "grp", None, None),
        P("sec", None, None),
        P("sec", None, None),
        P("sec", None),
        P("sec", None),
    )
    out_specs = P("sec", "grp", None, None)
    return jax.shard_map(
        per_device, mesh=mesh, in_specs=in_specs, out_specs=out_specs, check_vma=False
    )
```

```python
import functools

import jax
import jax.numpy as jnp
from jax import lax
from jax.experimental import pallas as pl
from jax.experimental.pallas import tpu as pltpu
from jax.sharding import PartitionSpec as P

BLK = 32
CAP = 2
GROUP = 4
HEAD = 8
CORES = 2

HIGH = lax.Precision.HIGHEST
F32 = jnp.float32
BF16 = jnp.bfloat16
VMEM_SMALL = 16 * 1024 * 1024
VMEM_WHOLE = 63400000
PEAK = 1.15e9

IN_VMEM = pl.BlockSpec(memory_space=pltpu.VMEM)
IN_SMEM = pl.BlockSpec(memory_space=pltpu.SMEM)
IN_HBM = pl.BlockSpec(memory_space=pltpu.HBM)
IN_PLACE = pl.BlockSpec(memory_space=pl.ANY)


def shape(*dims, dtype=BF16):
    return jax.ShapeDtypeStruct(dims, dtype)


def call(body, name, ins, outs, scratch, micros, vmem=VMEM_SMALL, aliases=None):
    places = list(range(len(outs))) if isinstance(outs, list) else 0
    return pl.pallas_call(
        body,
        name=name,
        in_specs=ins,
        out_shape=outs,
        out_specs=jax.tree.map(lambda k: IN_PLACE if k in (aliases or {}).values() else IN_VMEM, places),
        input_output_aliases=aliases or {},
        scratch_shapes=scratch,
        compiler_params=pltpu.CompilerParams(vmem_limit_bytes=vmem),
        cost_estimate=pl.CostEstimate(flops=int(micros * PEAK), bytes_accessed=0, transcendentals=0),
    )


def place():
    return lax.axis_index("sec") % GROUP


def partners():
    here = place()
    across = (here + CORES) % GROUP
    return here, across ^ 1, across, here ^ 1


def dot(a, b):
    return jnp.dot(a, b, preferred_element_type=F32)


def dot_wide(a, b):
    return jnp.dot(a, b, precision=HIGH, preferred_element_type=F32)


def two_parts(x):
    high = x.astype(BF16)
    return high, (x - high.astype(F32)).astype(BF16)


def dot_rows(a, b):
    return lax.dot_general(a, b, (((1,), (1,)), ((), ())), preferred_element_type=F32)


def step_by(state, maps):
    high, low = two_parts(state)
    rows = state.shape[0]
    y = dot_rows(jnp.concatenate([high, low], axis=0), maps[0])
    return y[:rows] + (y[rows:] + dot_rows(high, maps[1]))


def mask_tiles(pattern, coupling):
    high, wide = coupling.shape[0] // pattern.shape[1], coupling.shape[1] // pattern.shape[0]
    for i in range(pattern.shape[1]):
        for j in range(pattern.shape[0]):
            at = (slice(i * high, (i + 1) * high), slice(j * wide, (j + 1) * wide))
            tile = coupling[at]
            coupling[at] = jnp.where(pattern[j, i] == 1, tile, jnp.zeros_like(tile))


def pairs_kernel(owner_in, blocks_in, green, inject_in, out, owner, blocks, inject, held, product, slot_of, counts, sem, side, done, *packets):
    energies, orbitals, _ = green.shape
    sections = out.shape[0]
    count = owner.shape[0]
    named = held.shape[1] < orbitals
    parts = sem.shape[1]
    size = held.shape[1] // parts
    small = [
        pltpu.make_async_copy(src, dst, side.at[k])
        for k, (src, dst) in enumerate(((owner_in, owner), (blocks_in, blocks), (inject_in, inject)))
    ]
    for move in small:
        move.start()

    def copy_of(e, c, q):
        first = pl.multiple_of(blocks[0, q] * BLK, BLK)
        to = pl.multiple_of(q * BLK, BLK)
        return pltpu.make_async_copy(green.at[e, pl.ds(first, BLK)], held.at[e, pl.ds(to, BLK)], sem.at[e, c])

    def part_of(e, c):
        at = pl.ds(c * size, size)
        return pltpu.make_async_copy(green.at[e, at], held.at[e, at], sem.at[e, c])

    if not named:
        for e in range(energies):
            for c in range(parts):
                part_of(e, c).start()
    for move in small[:2]:
        move.wait()
    if named:
        for e in range(energies):
            for c in range(parts):
                lax.fori_loop(
                    c * (count // parts),
                    (c + 1) * (count // parts),
                    lambda q, _, e=e, c=c: copy_of(e, c, q).start(),
                    None,
                    unroll=4,
                )
    rows = CAP * BLK
    head = packets[-1]
    columns = out.shape[2]
    lane = lax.broadcasted_iota(jnp.int32, (HEAD, columns), 1)
    none = jnp.where(lane < CAP, -1.0, 0.0).astype(BF16)

    def blank(d, _):
        counts[d] = 0
        for packet in packets:
            packet[d, :rows, :] = jnp.zeros((rows, columns), BF16)
        head[d, rows : rows + HEAD, :] = none
        return 0

    lax.fori_loop(0, sections, blank, 0)

    def rank(q, _):
        d = owner[q]
        r = counts[d]
        counts[d] = r + 1
        slot_of[q] = r
        line = head[d, rows : rows + HEAD, :].astype(F32)
        line = jnp.where(lane == r, blocks[1, q].astype(F32), line)
        head[d, rows : rows + HEAD, :] = line.astype(BF16)
        return 0

    lax.fori_loop(0, count, rank, 0)
    small[2].wait()
    moves = []
    for e, packet in enumerate(packets):
        for c in range(parts):
            part_of(e, c).wait()
            at = slice(c * size, (c + 1) * size)
            product[e, at, :] = dot(held[e, at, :], inject[e]).astype(BF16)

        def fill(q, _):
            first = pl.multiple_of((q if named else blocks[0, q]) * BLK, BLK)
            to = pl.multiple_of(slot_of[q] * BLK, BLK)
            packet[owner[q], pl.ds(to, BLK), :] = product[e, pl.ds(first, BLK), :]
            return 0

        lax.fori_loop(0, count, fill, 0, unroll=4)
        moves.append(pltpu.make_async_copy(packet, out.at[:, pl.ds(e * rows, packet.shape[1])], done.at[e]))
        moves[-1].start()
    for move in moves:
        move.wait()


def outgoing_pairs(owner, blocks, green, inject, sections):
    energies, orbitals, _ = green.shape
    columns = inject.shape[2]
    rows = min(orbitals, owner.shape[0] * BLK)
    part = CAP * BLK
    parts = 2
    return pl.pallas_call(
        pairs_kernel,
        name="pairs",
        in_specs=[IN_HBM] * 4,
        out_shape=shape(sections, part * energies + HEAD, columns),
        out_specs=IN_HBM,
        scratch_shapes=[
            pltpu.SMEM(owner.shape, jnp.int32),
            pltpu.SMEM(blocks.shape, jnp.int32),
            pltpu.VMEM(inject.shape, BF16),
            pltpu.VMEM((energies, rows, orbitals), BF16),
            pltpu.VMEM((energies, rows, columns), BF16),
            pltpu.SMEM(owner.shape, jnp.int32),
            pltpu.SMEM((sections,), jnp.int32),
            pltpu.SemaphoreType.DMA((energies, parts)),
            pltpu.SemaphoreType.DMA((3,)),
            pltpu.SemaphoreType.DMA((energies,)),
        ]
        + [pltpu.VMEM((sections, part + (HEAD if e == energies - 1 else 0), columns), BF16) for e in range(energies)],
        compiler_params=pltpu.CompilerParams(vmem_limit_bytes=VMEM_WHOLE),
        cost_estimate=pl.CostEstimate(flops=int(4.0 * PEAK), bytes_accessed=0, transcendentals=0),
    )(owner, blocks, green, inject)


def maps_kernel(pattern, green, coupling, own, other, *refs):
    face_rows, (couple, maps) = refs[:-2], refs[-2:]
    energies, orbitals, _ = green.shape
    face = coupling.shape[1]
    couple[...] = coupling[...]
    mask_tiles(pattern, couple)
    for e in range(energies):
        rows = green[e, orbitals - face :, :]
        face_rows[e][...] = rows
        maps[e] = dot(rows, couple[...])
    mine = place() // CORES
    own[...] = maps[mine]
    other[...] = maps[1 - mine]


def face_maps(pattern, green, coupling):
    orbitals, face = coupling.shape
    square = shape(face, face, dtype=F32)
    return call(
        maps_kernel,
        "face_maps",
        [IN_SMEM, IN_VMEM, IN_VMEM],
        [square, square] + [shape(face, orbitals)] * green.shape[0],
        [pltpu.VMEM(coupling.shape, BF16), pltpu.VMEM((green.shape[0], face, face), F32)],
        1.2,
    )(pattern, green, coupling)


def prop_kernel(pattern, green, coupling, _tie, out, couple):
    couple[...] = coupling[...]
    mask_tiles(pattern, couple)
    for e in range(green.shape[0]):
        out[e] = dot(green[e], couple[...]).astype(BF16)


def propagator(pattern, green, coupling, tie):
    energies, orbitals, _ = green.shape
    return call(
        prop_kernel,
        "prop",
        [IN_SMEM, IN_VMEM, IN_VMEM, IN_PLACE],
        shape(energies, orbitals, coupling.shape[1]),
        [pltpu.VMEM(coupling.shape, BF16)],
        1.5,
    )(pattern, green, coupling, tie)


def times(a, b):
    return dot(a[0], b[0]) + (dot(a[0], b[1]) + dot(a[1], b[0]))


def chain_kernel(own, far, across, near, total_out, parts, maps):
    collect((own, far, across, near), maps)
    split = [two_parts(maps[j]) for j in range(GROUP)]
    lower, upper = two_parts(times(split[1], split[0])), two_parts(times(split[3], split[2]))
    total_out[...] = times(upper, lower).astype(total_out.dtype)
    for j, (high, low) in enumerate(split):
        parts[0, j] = high
        parts[1, j] = low


def chain(maps, dtype):
    face = maps[0].shape[0]
    return call(
        chain_kernel,
        "chain_maps",
        [IN_VMEM] * GROUP,
        [shape(face, face, dtype=dtype), shape(2, GROUP, face, face)],
        [pltpu.VMEM((GROUP, face, face), F32)],
        0.9,
    )(*maps)


def source_kernel(received, inject, source, heads, targets, total, sem):
    energies, orbitals, columns = inject.shape
    sections = received.shape[0]
    rows = CAP * energies * BLK

    def read(s, _):
        block = received[s, rows : rows + HEAD, :].astype(F32)
        heads[pl.ds(s, 1), :] = block[:1].astype(jnp.int32)
        return 0

    lax.fori_loop(0, sections, read, 0, unroll=min(sections, 8))
    fetch = pltpu.make_async_copy(heads, targets, sem)
    fetch.start()
    total[...] = inject[...].astype(F32)
    fetch.wait()

    def add(s, _):
        for r in range(CAP):
            first = pl.multiple_of(jnp.maximum(targets[s, r], 0) * BLK, BLK)
            for e in range(energies):
                item = received[s, (e * CAP + r) * BLK : (e * CAP + r + 1) * BLK, :]
                total[e, pl.ds(first, BLK), :] += item.astype(F32)
        return 0

    lax.fori_loop(0, sections, add, 0, unroll=min(sections, 8))
    source[...] = total[...].astype(BF16)


def placed_source(received, inject):
    energies, orbitals, columns = inject.shape
    sections = received.shape[0]
    return call(
        source_kernel,
        "source",
        [IN_VMEM] * 2,
        shape(*inject.shape),
        [
            pltpu.VMEM((sections, columns), jnp.int32),
            pltpu.SMEM((sections, columns), jnp.int32),
            pltpu.VMEM(inject.shape, F32),
            pltpu.SemaphoreType.DMA,
        ],
        1.0,
    )(received, inject)


def quarters_kernel(source, *refs):
    energies = source.shape[0]
    face_rows = refs[:energies]
    own, far, across, near, quarters = refs[energies:]
    split = GROUP // energies
    size = quarters.shape[1]
    for e in range(energies):
        wide = dot(face_rows[e][...], source[e]).astype(BF16).T
        for h in range(split):
            quarters[e * split + h] = wide[h * size : (h + 1) * size]
    for out, at in zip((own, far, across, near), partners()):
        out[...] = quarters[at]


def face_quarters(source, face_rows):
    energies, _, columns = source.shape
    face = face_rows[0].shape[0]
    rows = columns * energies // GROUP
    return call(
        quarters_kernel,
        "face_quarters",
        [IN_VMEM] * (1 + energies),
        [shape(rows, face)] * GROUP,
        [pltpu.VMEM((GROUP, rows, face), BF16)],
        0.6,
    )(source, *face_rows)


def after_kernel(_packets, _map, _same_map):
    pass


def handed_on(item, packets):
    return call(
        after_kernel,
        "after_exchange",
        [IN_PLACE] * 2,
        [shape(*item.shape, dtype=item.dtype)],
        [],
        0.1,
        aliases={1: 0},
    )(packets, item)[0]


def collect(refs, held):
    for ref, at in zip(refs, partners()):
        held[at] = ref[...]


def total_kernel(own, far, across, near, parts, _image, out, local, shifts):
    collect((own, far, across, near), shifts)
    state = shifts[0].astype(F32)
    for j in range(1, GROUP):
        local[j - 1] = state
        state = shifts[j].astype(F32) + step_by(state, (parts[0, j], parts[1, j]))
    out[...] = state.astype(BF16)


def plane_total(shifts, parts, tie):
    rows, face = shifts[0].shape
    return call(
        total_kernel,
        "plane_total",
        [IN_VMEM] * (GROUP + 1) + [IN_PLACE],
        [shape(rows, face), shape(GROUP - 1, rows, face, dtype=F32)],
        [pltpu.VMEM((GROUP, rows, face), BF16)],
        3.0,
    )(*shifts, parts, tie)


def work_kernel(early, *refs):
    green, source, parts = refs[:3]
    held, (image, upto) = refs[3:-2], refs[-2:]
    low_plane = lax.axis_index("sec") // GROUP == 0

    @pl.when(low_plane if early else jnp.logical_not(low_plane))
    def _():
        for e in range(green.shape[0]):
            image[e] = dot(green[e], source[e])
        maps = (parts[0, 0], parts[1, 0])
        for j in range(1, GROUP - 1):
            maps = two_parts(times((parts[0, j], parts[1, j]), maps))
            upto[0, j - 1], upto[1, j - 1] = maps

    if held:

        @pl.when(low_plane)
        def _():
            image[...] = held[0][...]
            upto[...] = held[1][...]


def image_and_maps(green, source, parts, held=()):
    _, _, face, _ = parts.shape
    return call(
        functools.partial(work_kernel, not held),
        "image_and_maps",
        [IN_VMEM] * (3 + len(held)),
        [shape(*source.shape, dtype=F32), shape(2, GROUP - 2, face, face)],
        [],
        2.0,
    )(green, source, parts, *held)


def sweep_plane(state, parts, upto, local, out):
    held = [state]
    for j in range(1, GROUP):
        maps = (parts[0, 0], parts[1, 0]) if j == 1 else (upto[0, j - 2], upto[1, j - 2])
        held.append(local[j - 1] + step_by(state, maps))
    work = out[GROUP]
    for j, item in enumerate(held):
        work[j] = item
    for ref, at in zip(out, partners()):
        ref[...] = work[at].astype(BF16)


def entering_kernel(third, near_one, second, far_one, got, other, parts, upto, local, *out):
    first_core = place() % CORES == 0
    first = near_one[...].astype(F32) + far_one[...].astype(F32)
    state = third[...].astype(F32)
    rows = state.shape[0]
    for below, (one, two) in ((second[...].astype(F32), (other, got)), (first, (got, other))):
        factor = jnp.where(first_core, one[...], two[...])
        y = dot_rows(jnp.concatenate(two_parts(state), axis=0), factor)
        state = below + (y[:rows] + y[rows:])
    sweep_plane(state, parts, upto, local, out)


def entering_from_kernel(base, parts, upto, local, *out):
    sweep_plane(base[...], parts, upto, local, out)


def entering(body, args):
    half, columns = args[0].shape
    return call(
        body,
        "entering",
        [IN_VMEM] * len(args),
        [shape(half, columns)] * GROUP,
        [pltpu.VMEM((GROUP, half, columns), F32)],
        1.4,
    )(*args)


def waves_kernel(own, far, across, near, prop, image, out, arrived, wave, sem):
    collect((own, far, across, near), arrived)
    energies, orbitals, _ = prop.shape
    split = GROUP // energies
    pieces = sem.shape[1]
    size = orbitals // pieces
    moves = []
    for e in range(energies):
        incoming = jnp.concatenate([arrived[e * split + h] for h in range(split)], axis=0)
        for c in range(pieces):
            at = slice(c * size, (c + 1) * size)
            wave[e, at, :] = (dot_rows(prop[e, at, :], incoming) + image[e, at, :]).astype(BF16)
            moves.append(pltpu.make_async_copy(wave.at[e, pl.ds(c * size, size)], out.at[e, pl.ds(c * size, size)], sem.at[e, c]))
            moves[-1].start()
    for move in moves:
        move.wait()


def final_waves(arrived, prop, image):
    half, columns = arrived[0].shape
    energies = prop.shape[0]
    return pl.pallas_call(
        waves_kernel,
        name="waves",
        in_specs=[IN_VMEM] * (GROUP + 2),
        out_shape=shape(*image.shape),
        out_specs=IN_HBM,
        scratch_shapes=[
            pltpu.VMEM((GROUP, half, columns), BF16),
            pltpu.VMEM(image.shape, BF16),
            pltpu.SemaphoreType.DMA((energies, 2)),
        ],
        compiler_params=pltpu.CompilerParams(vmem_limit_bytes=VMEM_SMALL),
        cost_estimate=pl.CostEstimate(flops=int(1.3 * PEAK), bytes_accessed=0, transcendentals=0),
    )(*arrived, prop, image)


def to_near(item, sections):
    return lax.ppermute(item, "sec", [(s, s ^ 1) for s in range(sections)])


def to_across(item, sections):
    return lax.ppermute(item, "sec", [(s, s // GROUP * GROUP + (s % GROUP + CORES) % GROUP) for s in range(sections)])


def to_far(item, sections):
    return lax.ppermute(item, "sec", [(s, s // GROUP * GROUP + (s % GROUP + CORES) % GROUP ^ 1) for s in range(sections)])


def exchange(own, far, across, near, sections):
    return [own, to_far(far, sections), to_across(across, sections), to_near(near, sections)]


def up_shift(sections, k):
    return [(s, s + GROUP * k) for s in range(sections - GROUP * k)]


def maps_up(total_map, sections):
    pairs = []
    for i in range(GROUP):
        if i % CORES == 0:
            pairs += [(GROUP + i, 2 * GROUP + i), (2 * GROUP + i, 3 * GROUP + i)]
        else:
            pairs += [(GROUP + i, 3 * GROUP + i)]
    got = lax.ppermute(total_map, "sec", pairs)
    return got, lax.ppermute(got, "sec", [(s, s ^ 1) for s in range(2 * GROUP, sections)])


def between(item, *planes):
    pairs = [(p * GROUP + i, q * GROUP + i) for p, q in planes for i in range(GROUP)]
    return lax.ppermute(item, "sec", pairs)


def scan_below(total_map, total, sections):
    shift = lax.ppermute(total.astype(F32), "sec", up_shift(sections, 1))
    joined = lax.ppermute(total_map, "sec", up_shift(sections, 1))
    stride = 1
    while stride < sections // GROUP:
        other = lax.ppermute(shift, "sec", up_shift(sections, stride))
        other_map = lax.ppermute(joined, "sec", up_shift(sections, stride))
        shift = shift + dot_wide(other, joined.T)
        joined = dot_wide(joined, other_map)
        stride *= 2
    return shift


def per_device(green, injected, coupling, pattern, owner, pair_blocks):
    sections = lax.axis_size("sec")
    green, inject = green[0], injected[0]

    coupling, tiles = coupling[0], pattern[0].T
    outgoing = outgoing_pairs(owner[:, 0], pair_blocks.T, green, inject, sections)
    received = lax.all_to_all(outgoing, "sec", split_axis=0, concat_axis=0, tiled=True)

    own_map, other_map, *face_rows = face_maps(tiles, green, coupling)
    across = to_across(other_map, sections)
    near = to_near(own_map, sections)

    source = placed_source(received, inject)
    quarters = face_quarters(source, face_rows)
    shifts = exchange(*quarters, sections)
    across = handed_on(across, quarters[0])
    far = to_near(across, sections)
    four = sections // GROUP == 4
    total_map, parts = chain([own_map, far, across, near], BF16 if four else F32)
    early = image_and_maps(green, source, parts)
    maps = maps_up(total_map, sections) if four else []
    total, local = plane_total(shifts, parts, early[0])
    if four:
        fourth = between(total, (1, 2), (2, 3))
        third = between(total, (0, 2), (1, 3))
        second = between(total, (0, 1))
        first = between(total, (0, 3))
        image, upto = image_and_maps(green, source, parts, early)
        entered = entering(entering_kernel, (first, second, third, fourth, *maps, parts, upto, local))
    else:
        base = scan_below(total_map, total, sections)
        image, upto = image_and_maps(green, source, parts, early)
        entered = entering(entering_from_kernel, (base, parts, upto, local))
    arrived = exchange(*entered, sections)
    prop = propagator(tiles, green, coupling, entered[0])
    return final_waves(arrived, prop, image)[None]


def solution(mesh):
    in_specs = (
        P("sec", "grp", None, None),
        P("sec", "grp", None, None),
        P("sec", None, None),
        P("sec", None, None),
        P("sec", None),
        P("sec", None),
    )
    out_specs = P("sec", "grp", None, None)
    return jax.shard_map(
        per_device, mesh=mesh, in_specs=in_specs, out_specs=out_specs, check_vma=False
    )
```

```python
import functools

import jax
import jax.numpy as jnp
from jax import lax
from jax.experimental import pallas as pl
from jax.experimental.pallas import tpu as pltpu
from jax.sharding import PartitionSpec as P

BLK = 32
CAP = 2
GROUP = 4
HEAD = 8
CORES = 2

HIGH = lax.Precision.HIGHEST
F32 = jnp.float32
BF16 = jnp.bfloat16
VMEM_SMALL = 16 * 1024 * 1024
VMEM_WHOLE = 63400000
PEAK = 1.15e9

IN_VMEM = pl.BlockSpec(memory_space=pltpu.VMEM)
IN_SMEM = pl.BlockSpec(memory_space=pltpu.SMEM)
IN_HBM = pl.BlockSpec(memory_space=pltpu.HBM)
IN_PLACE = pl.BlockSpec(memory_space=pl.ANY)


def shape(*dims, dtype=BF16):
    return jax.ShapeDtypeStruct(dims, dtype)


def call(body, name, ins, outs, scratch, micros, vmem=VMEM_SMALL, aliases=None):
    places = list(range(len(outs))) if isinstance(outs, list) else 0
    return pl.pallas_call(
        body,
        name=name,
        in_specs=ins,
        out_shape=outs,
        out_specs=jax.tree.map(lambda k: IN_PLACE if k in (aliases or {}).values() else IN_VMEM, places),
        input_output_aliases=aliases or {},
        scratch_shapes=scratch,
        compiler_params=pltpu.CompilerParams(vmem_limit_bytes=vmem),
        cost_estimate=pl.CostEstimate(flops=int(micros * PEAK), bytes_accessed=0, transcendentals=0),
    )


def place():
    return lax.axis_index("sec") % GROUP


def partners():
    here = place()
    across = (here + CORES) % GROUP
    return here, across ^ 1, across, here ^ 1


def dot(a, b):
    return jnp.dot(a, b, preferred_element_type=F32)


def dot_wide(a, b):
    return jnp.dot(a, b, precision=HIGH, preferred_element_type=F32)


def two_parts(x):
    high = x.astype(BF16)
    return high, (x - high.astype(F32)).astype(BF16)


def dot_rows(a, b):
    return lax.dot_general(a, b, (((1,), (1,)), ((), ())), preferred_element_type=F32)


def step_by(state, maps):
    high, low = two_parts(state)
    rows = state.shape[0]
    y = dot_rows(jnp.concatenate([high, low], axis=0), maps[0])
    return y[:rows] + (y[rows:] + dot_rows(high, maps[1]))


def mask_tiles(pattern, coupling):
    high, wide = coupling.shape[0] // pattern.shape[1], coupling.shape[1] // pattern.shape[0]
    for i in range(pattern.shape[1]):
        for j in range(pattern.shape[0]):
            at = (slice(i * high, (i + 1) * high), slice(j * wide, (j + 1) * wide))
            tile = coupling[at]
            coupling[at] = jnp.where(pattern[j, i] == 1, tile, jnp.zeros_like(tile))


def pairs_kernel(owner_in, blocks_in, green, inject_in, out, owner, blocks, inject, held, product, slot_of, counts, sem, side, done, *packets):
    energies, orbitals, _ = green.shape
    sections = out.shape[0]
    count = owner.shape[0]
    named = held.shape[1] < orbitals
    parts = sem.shape[1]
    size = held.shape[1] // parts
    small = [
        pltpu.make_async_copy(src, dst, side.at[k])
        for k, (src, dst) in enumerate(((owner_in, owner), (blocks_in, blocks), (inject_in, inject)))
    ]
    for move in small:
        move.start()

    def copy_of(e, c, q):
        first = pl.multiple_of(blocks[0, q] * BLK, BLK)
        to = pl.multiple_of(q * BLK, BLK)
        return pltpu.make_async_copy(green.at[e, pl.ds(first, BLK)], held.at[e, pl.ds(to, BLK)], sem.at[e, c])

    def part_of(e, c):
        at = pl.ds(c * size, size)
        return pltpu.make_async_copy(green.at[e, at], held.at[e, at], sem.at[e, c])

    if not named:
        for e in range(energies):
            for c in range(parts):
                part_of(e, c).start()
    for move in small[:2]:
        move.wait()
    if named:
        for e in range(energies):
            for c in range(parts):
                lax.fori_loop(
                    c * (count // parts),
                    (c + 1) * (count // parts),
                    lambda q, _, e=e, c=c: copy_of(e, c, q).start(),
                    None,
                    unroll=4,
                )
    rows = CAP * BLK
    head = packets[-1]
    columns = out.shape[2]
    lane = lax.broadcasted_iota(jnp.int32, (HEAD, columns), 1)
    none = jnp.where(lane < CAP, -1.0, 0.0).astype(BF16)

    def blank(d, _):
        counts[d] = 0
        for packet in packets:
            packet[d, :rows, :] = jnp.zeros((rows, columns), BF16)
        head[d, rows : rows + HEAD, :] = none
        return 0

    lax.fori_loop(0, sections, blank, 0)

    def rank(q, _):
        d = owner[q]
        r = counts[d]
        counts[d] = r + 1
        slot_of[q] = r
        line = head[d, rows : rows + HEAD, :].astype(F32)
        line = jnp.where(lane == r, blocks[1, q].astype(F32), line)
        head[d, rows : rows + HEAD, :] = line.astype(BF16)
        return 0

    lax.fori_loop(0, count, rank, 0)
    small[2].wait()
    moves = []
    for e, packet in enumerate(packets):
        for c in range(parts):
            part_of(e, c).wait()
            at = slice(c * size, (c + 1) * size)
            product[e, at, :] = dot(held[e, at, :], inject[e]).astype(BF16)

        def fill(q, _):
            first = pl.multiple_of((q if named else blocks[0, q]) * BLK, BLK)
            to = pl.multiple_of(slot_of[q] * BLK, BLK)
            packet[owner[q], pl.ds(to, BLK), :] = product[e, pl.ds(first, BLK), :]
            return 0

        lax.fori_loop(0, count, fill, 0, unroll=4)
        moves.append(pltpu.make_async_copy(packet, out.at[:, pl.ds(e * rows, packet.shape[1])], done.at[e]))
        moves[-1].start()
    for move in moves:
        move.wait()


def outgoing_pairs(owner, blocks, green, inject, sections):
    energies, orbitals, _ = green.shape
    columns = inject.shape[2]
    rows = min(orbitals, owner.shape[0] * BLK)
    part = CAP * BLK
    parts = 2
    return pl.pallas_call(
        pairs_kernel,
        name="pairs",
        in_specs=[IN_HBM] * 4,
        out_shape=shape(sections, part * energies + HEAD, columns),
        out_specs=IN_HBM,
        scratch_shapes=[
            pltpu.SMEM(owner.shape, jnp.int32),
            pltpu.SMEM(blocks.shape, jnp.int32),
            pltpu.VMEM(inject.shape, BF16),
            pltpu.VMEM((energies, rows, orbitals), BF16),
            pltpu.VMEM((energies, rows, columns), BF16),
            pltpu.SMEM(owner.shape, jnp.int32),
            pltpu.SMEM((sections,), jnp.int32),
            pltpu.SemaphoreType.DMA((energies, parts)),
            pltpu.SemaphoreType.DMA((3,)),
            pltpu.SemaphoreType.DMA((energies,)),
        ]
        + [pltpu.VMEM((sections, part + (HEAD if e == energies - 1 else 0), columns), BF16) for e in range(energies)],
        compiler_params=pltpu.CompilerParams(vmem_limit_bytes=VMEM_WHOLE),
        cost_estimate=pl.CostEstimate(flops=int(4.0 * PEAK), bytes_accessed=0, transcendentals=0),
    )(owner, blocks, green, inject)


def maps_kernel(pattern, green, coupling, own, other, *refs):
    face_rows, (couple, maps) = refs[:-2], refs[-2:]
    energies, orbitals, _ = green.shape
    face = coupling.shape[1]
    couple[...] = coupling[...]
    mask_tiles(pattern, couple)
    for e in range(energies):
        rows = green[e, orbitals - face :, :]
        face_rows[e][...] = rows
        maps[e] = dot(rows, couple[...])
    mine = place() // CORES
    own[...] = maps[mine]
    other[...] = maps[1 - mine]


def face_maps(pattern, green, coupling):
    orbitals, face = coupling.shape
    square = shape(face, face, dtype=F32)
    return call(
        maps_kernel,
        "face_maps",
        [IN_SMEM, IN_VMEM, IN_VMEM],
        [square, square] + [shape(face, orbitals)] * green.shape[0],
        [pltpu.VMEM(coupling.shape, BF16), pltpu.VMEM((green.shape[0], face, face), F32)],
        1.2,
    )(pattern, green, coupling)


def prop_kernel(pattern, green, coupling, _tie, out, couple):
    couple[...] = coupling[...]
    mask_tiles(pattern, couple)
    for e in range(green.shape[0]):
        out[e] = dot(green[e], couple[...]).astype(BF16)


def propagator(pattern, green, coupling, tie):
    energies, orbitals, _ = green.shape
    return call(
        prop_kernel,
        "prop",
        [IN_SMEM, IN_VMEM, IN_VMEM, IN_PLACE],
        shape(energies, orbitals, coupling.shape[1]),
        [pltpu.VMEM(coupling.shape, BF16)],
        1.5,
    )(pattern, green, coupling, tie)


def times(a, b):
    return dot(a[0], b[0]) + (dot(a[0], b[1]) + dot(a[1], b[0]))


def chain_kernel(own, far, across, near, total_out, parts, maps):
    collect((own, far, across, near), maps)
    split = [two_parts(maps[j]) for j in range(GROUP)]
    lower, upper = two_parts(times(split[1], split[0])), two_parts(times(split[3], split[2]))
    total_out[...] = times(upper, lower).astype(total_out.dtype)
    for j, (high, low) in enumerate(split):
        parts[0, j] = high
        parts[1, j] = low


def chain(maps, dtype):
    face = maps[0].shape[0]
    return call(
        chain_kernel,
        "chain_maps",
        [IN_VMEM] * GROUP,
        [shape(face, face, dtype=dtype), shape(2, GROUP, face, face)],
        [pltpu.VMEM((GROUP, face, face), F32)],
        0.9,
    )(*maps)


def source_kernel(received, inject, source, heads, targets, total, sem):
    energies, orbitals, columns = inject.shape
    sections = received.shape[0]
    rows = CAP * energies * BLK

    def read(s, _):
        block = received[s, rows : rows + HEAD, :].astype(F32)
        heads[pl.ds(s, 1), :] = block[:1].astype(jnp.int32)
        return 0

    lax.fori_loop(0, sections, read, 0, unroll=min(sections, 8))
    fetch = pltpu.make_async_copy(heads, targets, sem)
    fetch.start()
    total[...] = inject[...].astype(F32)
    fetch.wait()

    def add(s, _):
        for r in range(CAP):
            first = pl.multiple_of(jnp.maximum(targets[s, r], 0) * BLK, BLK)
            for e in range(energies):
                item = received[s, (e * CAP + r) * BLK : (e * CAP + r + 1) * BLK, :]
                total[e, pl.ds(first, BLK), :] += item.astype(F32)
        return 0

    lax.fori_loop(0, sections, add, 0, unroll=min(sections, 8))
    source[...] = total[...].astype(BF16)


def placed_source(received, inject):
    energies, orbitals, columns = inject.shape
    sections = received.shape[0]
    return call(
        source_kernel,
        "source",
        [IN_VMEM] * 2,
        shape(*inject.shape),
        [
            pltpu.VMEM((sections, columns), jnp.int32),
            pltpu.SMEM((sections, columns), jnp.int32),
            pltpu.VMEM(inject.shape, F32),
            pltpu.SemaphoreType.DMA,
        ],
        1.0,
    )(received, inject)


def quarters_kernel(source, *refs):
    energies = source.shape[0]
    face_rows = refs[:energies]
    own, far, across, near, quarters = refs[energies:]
    split = GROUP // energies
    size = quarters.shape[1]
    for e in range(energies):
        wide = dot(face_rows[e][...], source[e]).astype(BF16).T
        for h in range(split):
            quarters[e * split + h] = wide[h * size : (h + 1) * size]
    for out, at in zip((own, far, across, near), partners()):
        out[...] = quarters[at]


def face_quarters(source, face_rows):
    energies, _, columns = source.shape
    face = face_rows[0].shape[0]
    rows = columns * energies // GROUP
    return call(
        quarters_kernel,
        "face_quarters",
        [IN_VMEM] * (1 + energies),
        [shape(rows, face)] * GROUP,
        [pltpu.VMEM((GROUP, rows, face), BF16)],
        0.6,
    )(source, *face_rows)


def after_kernel(_packets, _map, _same_map):
    pass


def handed_on(item, packets):
    return call(
        after_kernel,
        "after_exchange",
        [IN_PLACE] * 2,
        [shape(*item.shape, dtype=item.dtype)],
        [],
        0.1,
        aliases={1: 0},
    )(packets, item)[0]


def collect(refs, held):
    for ref, at in zip(refs, partners()):
        held[at] = ref[...]


def total_kernel(own, far, across, near, parts, _image, out, local, shifts):
    collect((own, far, across, near), shifts)
    state = shifts[0].astype(F32)
    for j in range(1, GROUP):
        local[j - 1] = state
        state = shifts[j].astype(F32) + step_by(state, (parts[0, j], parts[1, j]))
    out[...] = state.astype(BF16)


def plane_total(shifts, parts, tie):
    rows, face = shifts[0].shape
    return call(
        total_kernel,
        "plane_total",
        [IN_VMEM] * (GROUP + 1) + [IN_PLACE],
        [shape(rows, face), shape(GROUP - 1, rows, face, dtype=F32)],
        [pltpu.VMEM((GROUP, rows, face), BF16)],
        3.0,
    )(*shifts, parts, tie)


def work_kernel(early, *refs):
    green, source, parts = refs[:3]
    held, (image, upto) = refs[3:-2], refs[-2:]
    low_plane = lax.axis_index("sec") // GROUP == 0

    @pl.when(low_plane if early else jnp.logical_not(low_plane))
    def _():
        for e in range(green.shape[0]):
            image[e] = dot(green[e], source[e])
        maps = (parts[0, 0], parts[1, 0])
        for j in range(1, GROUP - 1):
            maps = two_parts(times((parts[0, j], parts[1, j]), maps))
            upto[0, j - 1], upto[1, j - 1] = maps

    if held:

        @pl.when(low_plane)
        def _():
            image[...] = held[0][...]
            upto[...] = held[1][...]


def image_and_maps(green, source, parts, held=()):
    _, _, face, _ = parts.shape
    return call(
        functools.partial(work_kernel, not held),
        "image_and_maps",
        [IN_VMEM] * (3 + len(held)),
        [shape(*source.shape, dtype=F32), shape(2, GROUP - 2, face, face)],
        [],
        2.0,
    )(green, source, parts, *held)


def sweep_plane(state, parts, upto, local, out):
    held = [state]
    for j in range(1, GROUP):
        maps = (parts[0, 0], parts[1, 0]) if j == 1 else (upto[0, j - 2], upto[1, j - 2])
        held.append(local[j - 1] + step_by(state, maps))
    work = out[GROUP]
    for j, item in enumerate(held):
        work[j] = item.astype(BF16)
    for ref, at in zip(out, partners()):
        ref[...] = work[at]


def entering_kernel(third, near_one, second, far_one, got, other, parts, upto, local, *out):
    first_core = place() % CORES == 0
    first = near_one[...].astype(F32) + far_one[...].astype(F32)
    state = third[...].astype(F32)
    rows = state.shape[0]
    for below, (one, two) in ((second[...].astype(F32), (other, got)), (first, (got, other))):
        factor = jnp.where(first_core, one[...], two[...])
        y = dot_rows(jnp.concatenate(two_parts(state), axis=0), factor)
        state = below + (y[:rows] + y[rows:])
    sweep_plane(state, parts, upto, local, out)


def entering_from_kernel(base, parts, upto, local, *out):
    sweep_plane(base[...], parts, upto, local, out)


def entering(body, args):
    half, columns = args[0].shape
    return call(
        body,
        "entering",
        [IN_VMEM] * len(args),
        [shape(half, columns)] * GROUP,
        [pltpu.VMEM((GROUP, half, columns), BF16)],
        1.4,
    )(*args)


def waves_kernel(own, far, across, near, prop, image, out, arrived, wave, sem):
    collect((own, far, across, near), arrived)
    energies, orbitals, _ = prop.shape
    split = GROUP // energies
    pieces = sem.shape[1]
    size = orbitals // pieces
    moves = []
    for e in range(energies):
        incoming = jnp.concatenate([arrived[e * split + h] for h in range(split)], axis=0)
        for c in range(pieces):
            at = slice(c * size, (c + 1) * size)
            wave[e, at, :] = (dot_rows(prop[e, at, :], incoming) + image[e, at, :]).astype(BF16)
            moves.append(pltpu.make_async_copy(wave.at[e, pl.ds(c * size, size)], out.at[e, pl.ds(c * size, size)], sem.at[e, c]))
            moves[-1].start()
    for move in moves:
        move.wait()


def final_waves(arrived, prop, image):
    half, columns = arrived[0].shape
    energies = prop.shape[0]
    return pl.pallas_call(
        waves_kernel,
        name="waves",
        in_specs=[IN_VMEM] * (GROUP + 2),
        out_shape=shape(*image.shape),
        out_specs=IN_HBM,
        scratch_shapes=[
            pltpu.VMEM((GROUP, half, columns), BF16),
            pltpu.VMEM(image.shape, BF16),
            pltpu.SemaphoreType.DMA((energies, 2)),
        ],
        compiler_params=pltpu.CompilerParams(vmem_limit_bytes=VMEM_SMALL),
        cost_estimate=pl.CostEstimate(flops=int(1.3 * PEAK), bytes_accessed=0, transcendentals=0),
    )(*arrived, prop, image)


def to_near(item, sections):
    return lax.ppermute(item, "sec", [(s, s ^ 1) for s in range(sections)])


def to_across(item, sections):
    return lax.ppermute(item, "sec", [(s, s // GROUP * GROUP + (s % GROUP + CORES) % GROUP) for s in range(sections)])


def to_far(item, sections):
    return lax.ppermute(item, "sec", [(s, s // GROUP * GROUP + (s % GROUP + CORES) % GROUP ^ 1) for s in range(sections)])


def exchange(own, far, across, near, sections):
    return [own, to_far(far, sections), to_across(across, sections), to_near(near, sections)]


def up_shift(sections, k):
    return [(s, s + GROUP * k) for s in range(sections - GROUP * k)]


def maps_up(total_map, sections):
    pairs = []
    for i in range(GROUP):
        if i % CORES == 0:
            pairs += [(GROUP + i, 2 * GROUP + i), (2 * GROUP + i, 3 * GROUP + i)]
        else:
            pairs += [(GROUP + i, 3 * GROUP + i)]
    got = lax.ppermute(total_map, "sec", pairs)
    return got, lax.ppermute(got, "sec", [(s, s ^ 1) for s in range(2 * GROUP, sections)])


def between(item, *planes):
    pairs = [(p * GROUP + i, q * GROUP + i) for p, q in planes for i in range(GROUP)]
    return lax.ppermute(item, "sec", pairs)


def scan_below(total_map, total, sections):
    shift = lax.ppermute(total.astype(F32), "sec", up_shift(sections, 1))
    joined = lax.ppermute(total_map, "sec", up_shift(sections, 1))
    stride = 1
    while stride < sections // GROUP:
        other = lax.ppermute(shift, "sec", up_shift(sections, stride))
        other_map = lax.ppermute(joined, "sec", up_shift(sections, stride))
        shift = shift + dot_wide(other, joined.T)
        joined = dot_wide(joined, other_map)
        stride *= 2
    return shift


def per_device(green, injected, coupling, pattern, owner, pair_blocks):
    sections = lax.axis_size("sec")
    green, inject = green[0], injected[0]

    coupling, tiles = coupling[0], pattern[0].T
    outgoing = outgoing_pairs(owner[:, 0], pair_blocks.T, green, inject, sections)
    received = lax.all_to_all(outgoing, "sec", split_axis=0, concat_axis=0, tiled=True)

    own_map, other_map, *face_rows = face_maps(tiles, green, coupling)
    across = to_across(other_map, sections)
    near = to_near(own_map, sections)

    source = placed_source(received, inject)
    quarters = face_quarters(source, face_rows)
    shifts = exchange(*quarters, sections)
    across = handed_on(across, quarters[0])
    far = to_near(across, sections)
    four = sections // GROUP == 4
    total_map, parts = chain([own_map, far, across, near], BF16 if four else F32)
    early = image_and_maps(green, source, parts)
    maps = maps_up(total_map, sections) if four else []
    total, local = plane_total(shifts, parts, early[0])
    if four:
        fourth = between(total, (1, 2), (2, 3))
        third = between(total, (0, 2), (1, 3))
        second = between(total, (0, 1))
        first = between(total, (0, 3))
        image, upto = image_and_maps(green, source, parts, early)
        entered = entering(entering_kernel, (first, second, third, fourth, *maps, parts, upto, local))
    else:
        base = scan_below(total_map, total, sections)
        image, upto = image_and_maps(green, source, parts, early)
        entered = entering(entering_from_kernel, (base, parts, upto, local))
    arrived = exchange(*entered, sections)
    prop = propagator(tiles, green, coupling, entered[0])
    return final_waves(arrived, prop, image)[None]


def solution(mesh):
    in_specs = (
        P("sec", "grp", None, None),
        P("sec", "grp", None, None),
        P("sec", None, None),
        P("sec", None, None),
        P("sec", None),
        P("sec", None),
    )
    out_specs = P("sec", "grp", None, None)
    return jax.shard_map(
        per_device, mesh=mesh, in_specs=in_specs, out_specs=out_specs, check_vma=False
    )
```

```python
import functools

import jax
import jax.numpy as jnp
from jax import lax
from jax.experimental import pallas as pl
from jax.experimental.pallas import tpu as pltpu
from jax.sharding import PartitionSpec as P

BLK = 32
CAP = 2
GROUP = 4
HEAD = 8
CORES = 2

HIGH = lax.Precision.HIGHEST
F32 = jnp.float32
BF16 = jnp.bfloat16
VMEM_SMALL = 16 * 1024 * 1024
VMEM_WHOLE = 63400000
PEAK = 1.15e9

IN_VMEM = pl.BlockSpec(memory_space=pltpu.VMEM)
IN_SMEM = pl.BlockSpec(memory_space=pltpu.SMEM)
IN_HBM = pl.BlockSpec(memory_space=pltpu.HBM)
IN_PLACE = pl.BlockSpec(memory_space=pl.ANY)


def shape(*dims, dtype=BF16):
    return jax.ShapeDtypeStruct(dims, dtype)


def call(body, name, ins, outs, scratch, micros, vmem=VMEM_SMALL, aliases=None):
    places = list(range(len(outs))) if isinstance(outs, list) else 0
    return pl.pallas_call(
        body,
        name=name,
        in_specs=ins,
        out_shape=outs,
        out_specs=jax.tree.map(lambda k: IN_PLACE if k in (aliases or {}).values() else IN_VMEM, places),
        input_output_aliases=aliases or {},
        scratch_shapes=scratch,
        compiler_params=pltpu.CompilerParams(vmem_limit_bytes=vmem),
        cost_estimate=pl.CostEstimate(flops=int(micros * PEAK), bytes_accessed=0, transcendentals=0),
    )


def place():
    return lax.axis_index("sec") % GROUP


def partners():
    here = place()
    across = (here + CORES) % GROUP
    return here, across ^ 1, across, here ^ 1


def dot(a, b):
    return jnp.dot(a, b, preferred_element_type=F32)


def dot_wide(a, b):
    return jnp.dot(a, b, precision=HIGH, preferred_element_type=F32)


def two_parts(x):
    high = x.astype(BF16)
    return high, (x - high.astype(F32)).astype(BF16)


def dot_rows(a, b):
    return lax.dot_general(a, b, (((1,), (1,)), ((), ())), preferred_element_type=F32)


def step_by(state, maps):
    high, low = two_parts(state)
    rows = state.shape[0]
    y = dot_rows(jnp.concatenate([high, low], axis=0), maps[0])
    return y[:rows] + (y[rows:] + dot_rows(high, maps[1]))


def mask_tiles(pattern, coupling, couple):
    high, wide = coupling.shape[0] // pattern.shape[1], coupling.shape[1] // pattern.shape[0]
    for i in range(pattern.shape[1]):
        for j in range(pattern.shape[0]):
            at = (slice(i * high, (i + 1) * high), slice(j * wide, (j + 1) * wide))
            tile = coupling[at]
            couple[at] = jnp.where(pattern[j, i] == 1, tile, jnp.zeros_like(tile))


def pairs_kernel(owner_in, blocks_in, green, inject_in, out, owner, blocks, inject, held, product, slot_of, counts, sem, side, done, *packets):
    energies, orbitals, _ = green.shape
    sections = out.shape[0]
    count = owner.shape[0]
    named = held.shape[1] < orbitals
    parts = sem.shape[1]
    size = held.shape[1] // parts
    small = [
        pltpu.make_async_copy(src, dst, side.at[k])
        for k, (src, dst) in enumerate(((owner_in, owner), (blocks_in, blocks), (inject_in, inject)))
    ]
    for move in small:
        move.start()

    def copy_of(e, c, q):
        first = pl.multiple_of(blocks[0, q] * BLK, BLK)
        to = pl.multiple_of(q * BLK, BLK)
        return pltpu.make_async_copy(green.at[e, pl.ds(first, BLK)], held.at[e, pl.ds(to, BLK)], sem.at[e, c])

    def part_of(e, c):
        at = pl.ds(c * size, size)
        return pltpu.make_async_copy(green.at[e, at], held.at[e, at], sem.at[e, c])

    if not named:
        for e in range(energies):
            for c in range(parts):
                part_of(e, c).start()
    for move in small[:2]:
        move.wait()
    if named:
        for e in range(energies):
            for c in range(parts):
                lax.fori_loop(
                    c * (count // parts),
                    (c + 1) * (count // parts),
                    lambda q, _, e=e, c=c: copy_of(e, c, q).start(),
                    None,
                    unroll=4,
                )
    rows = CAP * BLK
    head = packets[-1]
    columns = out.shape[2]
    lane = lax.broadcasted_iota(jnp.int32, (HEAD, columns), 1)
    none = jnp.where(lane < CAP, -1.0, 0.0).astype(BF16)

    def blank(d, _):
        counts[d] = 0
        for packet in packets:
            packet[d, :rows, :] = jnp.zeros((rows, columns), BF16)
        head[d, rows : rows + HEAD, :] = none
        return 0

    lax.fori_loop(0, sections, blank, 0)

    def rank(q, _):
        d = owner[q]
        r = counts[d]
        counts[d] = r + 1
        slot_of[q] = r
        line = head[d, rows : rows + HEAD, :].astype(F32)
        line = jnp.where(lane == r, blocks[1, q].astype(F32), line)
        head[d, rows : rows + HEAD, :] = line.astype(BF16)
        return 0

    lax.fori_loop(0, count, rank, 0)
    small[2].wait()
    moves = []
    for e, packet in enumerate(packets):
        for c in range(parts):
            part_of(e, c).wait()
            at = slice(c * size, (c + 1) * size)
            product[e, at, :] = dot(held[e, at, :], inject[e]).astype(BF16)

        def fill(q, _):
            first = pl.multiple_of((q if named else blocks[0, q]) * BLK, BLK)
            to = pl.multiple_of(slot_of[q] * BLK, BLK)
            packet[owner[q], pl.ds(to, BLK), :] = product[e, pl.ds(first, BLK), :]
            return 0

        lax.fori_loop(0, count, fill, 0, unroll=4)
        moves.append(pltpu.make_async_copy(packet, out.at[:, pl.ds(e * rows, packet.shape[1])], done.at[e]))
        moves[-1].start()
    for move in moves:
        move.wait()


def outgoing_pairs(owner, blocks, green, inject, sections):
    energies, orbitals, _ = green.shape
    columns = inject.shape[2]
    rows = min(orbitals, owner.shape[0] * BLK)
    part = CAP * BLK
    parts = 2
    return pl.pallas_call(
        pairs_kernel,
        name="pairs",
        in_specs=[IN_HBM] * 4,
        out_shape=shape(sections, part * energies + HEAD, columns),
        out_specs=IN_HBM,
        scratch_shapes=[
            pltpu.SMEM(owner.shape, jnp.int32),
            pltpu.SMEM(blocks.shape, jnp.int32),
            pltpu.VMEM(inject.shape, BF16),
            pltpu.VMEM((energies, rows, orbitals), BF16),
            pltpu.VMEM((energies, rows, columns), BF16),
            pltpu.SMEM(owner.shape, jnp.int32),
            pltpu.SMEM((sections,), jnp.int32),
            pltpu.SemaphoreType.DMA((energies, parts)),
            pltpu.SemaphoreType.DMA((3,)),
            pltpu.SemaphoreType.DMA((energies,)),
        ]
        + [pltpu.VMEM((sections, part + (HEAD if e == energies - 1 else 0), columns), BF16) for e in range(energies)],
        compiler_params=pltpu.CompilerParams(vmem_limit_bytes=VMEM_WHOLE),
        cost_estimate=pl.CostEstimate(flops=int(4.0 * PEAK), bytes_accessed=0, transcendentals=0),
    )(owner, blocks, green, inject)


def maps_kernel(pattern, green, coupling, own, other, *refs):
    face_rows, (couple, maps) = refs[:-2], refs[-2:]
    energies, orbitals, _ = green.shape
    face = coupling.shape[1]
    mask_tiles(pattern, coupling, couple)
    for e in range(energies):
        rows = green[e, orbitals - face :, :]
        face_rows[e][...] = rows
        maps[e] = dot(rows, couple[...])
    mine = place() // CORES
    own[...] = maps[mine]
    other[...] = maps[1 - mine]


def face_maps(pattern, green, coupling):
    orbitals, face = coupling.shape
    square = shape(face, face, dtype=F32)
    return call(
        maps_kernel,
        "face_maps",
        [IN_SMEM, IN_VMEM, IN_VMEM],
        [square, square] + [shape(face, orbitals)] * green.shape[0],
        [pltpu.VMEM(coupling.shape, BF16), pltpu.VMEM((green.shape[0], face, face), F32)],
        1.2,
    )(pattern, green, coupling)


def prop_kernel(pattern, green, coupling, _tie, out, couple):
    mask_tiles(pattern, coupling, couple)
    for e in range(green.shape[0]):
        out[e] = dot(green[e], couple[...]).astype(BF16)


def propagator(pattern, green, coupling, tie):
    energies, orbitals, _ = green.shape
    return call(
        prop_kernel,
        "prop",
        [IN_SMEM, IN_VMEM, IN_VMEM, IN_PLACE],
        shape(energies, orbitals, coupling.shape[1]),
        [pltpu.VMEM(coupling.shape, BF16)],
        1.5,
    )(pattern, green, coupling, tie)


def times(a, b):
    return dot(a[0], b[0]) + (dot(a[0], b[1]) + dot(a[1], b[0]))


def chain_kernel(own, far, across, near, total_out, parts, maps):
    collect((own, far, across, near), maps)
    split = [two_parts(maps[j]) for j in range(GROUP)]
    lower, upper = two_parts(times(split[1], split[0])), two_parts(times(split[3], split[2]))
    total_out[...] = times(upper, lower).astype(total_out.dtype)
    for j, (high, low) in enumerate(split):
        parts[0, j] = high
        parts[1, j] = low


def chain(maps, dtype):
    face = maps[0].shape[0]
    return call(
        chain_kernel,
        "chain_maps",
        [IN_VMEM] * GROUP,
        [shape(face, face, dtype=dtype), shape(2, GROUP, face, face)],
        [pltpu.VMEM((GROUP, face, face), F32)],
        0.9,
    )(*maps)


def source_kernel(received, inject, source, heads, targets, total, sem):
    energies, orbitals, columns = inject.shape
    sections = received.shape[0]
    rows = CAP * energies * BLK

    def read(s, _):
        block = received[s, rows : rows + HEAD, :].astype(F32)
        heads[pl.ds(s, 1), :] = block[:1].astype(jnp.int32)
        return 0

    lax.fori_loop(0, sections, read, 0, unroll=min(sections, 8))
    fetch = pltpu.make_async_copy(heads, targets, sem)
    fetch.start()
    total[...] = inject[...].astype(F32)
    fetch.wait()

    def add(s, _):
        for r in range(CAP):
            first = pl.multiple_of(jnp.maximum(targets[s, r], 0) * BLK, BLK)
            for e in range(energies):
                item = received[s, (e * CAP + r) * BLK : (e * CAP + r + 1) * BLK, :]
                total[e, pl.ds(first, BLK), :] += item.astype(F32)
        return 0

    lax.fori_loop(0, sections, add, 0, unroll=min(sections, 8))
    source[...] = total[...].astype(BF16)


def placed_source(received, inject):
    energies, orbitals, columns = inject.shape
    sections = received.shape[0]
    return call(
        source_kernel,
        "source",
        [IN_VMEM] * 2,
        shape(*inject.shape),
        [
            pltpu.VMEM((sections, columns), jnp.int32),
            pltpu.SMEM((sections, columns), jnp.int32),
            pltpu.VMEM(inject.shape, F32),
            pltpu.SemaphoreType.DMA,
        ],
        1.0,
    )(received, inject)


def quarters_kernel(source, *refs):
    energies = source.shape[0]
    face_rows = refs[:energies]
    own, far, across, near, quarters = refs[energies:]
    split = GROUP // energies
    size = quarters.shape[1]
    for e in range(energies):
        wide = dot(face_rows[e][...], source[e]).T
        for h in range(split):
            quarters[e * split + h] = wide[h * size : (h + 1) * size]
    for out, at in zip((own, far, across, near), partners()):
        out[...] = quarters[at].astype(BF16)


def face_quarters(source, face_rows):
    energies, _, columns = source.shape
    face = face_rows[0].shape[0]
    rows = columns * energies // GROUP
    return call(
        quarters_kernel,
        "face_quarters",
        [IN_VMEM] * (1 + energies),
        [shape(rows, face)] * GROUP,
        [pltpu.VMEM((GROUP, rows, face), F32)],
        0.6,
    )(source, *face_rows)


def after_kernel(_packets, _map, _same_map):
    pass


def handed_on(item, packets):
    return call(
        after_kernel,
        "after_exchange",
        [IN_PLACE] * 2,
        [shape(*item.shape, dtype=item.dtype)],
        [],
        0.1,
        aliases={1: 0},
    )(packets, item)[0]


def collect(refs, held):
    for ref, at in zip(refs, partners()):
        held[at] = ref[...]


def total_kernel(own, far, across, near, parts, _image, out, local, shifts):
    collect((own, far, across, near), shifts)
    state = shifts[0].astype(F32)
    for j in range(1, GROUP):
        local[j - 1] = state
        state = shifts[j].astype(F32) + step_by(state, (parts[0, j], parts[1, j]))
    out[...] = state.astype(BF16)


def plane_total(shifts, parts, tie):
    rows, face = shifts[0].shape
    return call(
        total_kernel,
        "plane_total",
        [IN_VMEM] * (GROUP + 1) + [IN_PLACE],
        [shape(rows, face), shape(GROUP - 1, rows, face, dtype=F32)],
        [pltpu.VMEM((GROUP, rows, face), BF16)],
        3.0,
    )(*shifts, parts, tie)


def work_kernel(early, *refs):
    green, source, parts = refs[:3]
    held, (image, upto) = refs[3:-2], refs[-2:]
    low_plane = lax.axis_index("sec") // GROUP == 0

    @pl.when(low_plane if early else jnp.logical_not(low_plane))
    def _():
        for e in range(green.shape[0]):
            image[e] = dot(green[e], source[e])
        maps = (parts[0, 0], parts[1, 0])
        for j in range(1, GROUP - 1):
            maps = two_parts(times((parts[0, j], parts[1, j]), maps))
            upto[0, j - 1], upto[1, j - 1] = maps

    if held:

        @pl.when(low_plane)
        def _():
            image[...] = held[0][...]
            upto[...] = held[1][...]


def image_and_maps(green, source, parts, held=()):
    _, _, face, _ = parts.shape
    return call(
        functools.partial(work_kernel, not held),
        "image_and_maps",
        [IN_VMEM] * (3 + len(held)),
        [shape(*source.shape, dtype=F32), shape(2, GROUP - 2, face, face)],
        [],
        2.0,
    )(green, source, parts, *held)


def sweep_plane(state, parts, upto, local, out):
    held = [state]
    for j in range(1, GROUP):
        maps = (parts[0, 0], parts[1, 0]) if j == 1 else (upto[0, j - 2], upto[1, j - 2])
        held.append(local[j - 1] + step_by(state, maps))
    work = out[GROUP]
    for j, item in enumerate(held):
        work[j] = item
    for ref, at in zip(out, partners()):
        ref[...] = work[at].astype(BF16)


def entering_kernel(third, near_one, second, far_one, got, other, parts, upto, local, *out):
    first_core = place() % CORES == 0
    first = near_one[...].astype(F32) + far_one[...].astype(F32)
    state = third[...].astype(F32)
    rows = state.shape[0]
    for below, (one, two) in ((second[...].astype(F32), (other, got)), (first, (got, other))):
        factor = jnp.where(first_core, one[...], two[...])
        y = dot_rows(jnp.concatenate(two_parts(state), axis=0), factor)
        state = below + (y[:rows] + y[rows:])
    sweep_plane(state, parts, upto, local, out)


def entering_from_kernel(base, parts, upto, local, *out):
    sweep_plane(base[...], parts, upto, local, out)


def entering(body, args):
    half, columns = args[0].shape
    return call(
        body,
        "entering",
        [IN_VMEM] * len(args),
        [shape(half, columns)] * GROUP,
        [pltpu.VMEM((GROUP, half, columns), F32)],
        1.4,
    )(*args)


def waves_kernel(own, far, across, near, prop, image, out, arrived, wave, sem):
    collect((own, far, across, near), arrived)
    energies, orbitals, _ = prop.shape
    split = GROUP // energies
    pieces = sem.shape[1]
    size = orbitals // pieces
    moves = []
    for e in range(energies):
        incoming = jnp.concatenate([arrived[e * split + h] for h in range(split)], axis=0)
        for c in range(pieces):
            at = slice(c * size, (c + 1) * size)
            wave[e, at, :] = (dot_rows(prop[e, at, :], incoming) + image[e, at, :]).astype(BF16)
            moves.append(pltpu.make_async_copy(wave.at[e, pl.ds(c * size, size)], out.at[e, pl.ds(c * size, size)], sem.at[e, c]))
            moves[-1].start()
    for move in moves:
        move.wait()


def final_waves(arrived, prop, image):
    half, columns = arrived[0].shape
    energies = prop.shape[0]
    return pl.pallas_call(
        waves_kernel,
        name="waves",
        in_specs=[IN_VMEM] * (GROUP + 2),
        out_shape=shape(*image.shape),
        out_specs=IN_HBM,
        scratch_shapes=[
            pltpu.VMEM((GROUP, half, columns), BF16),
            pltpu.VMEM(image.shape, BF16),
            pltpu.SemaphoreType.DMA((energies, 2)),
        ],
        compiler_params=pltpu.CompilerParams(vmem_limit_bytes=VMEM_SMALL),
        cost_estimate=pl.CostEstimate(flops=int(1.3 * PEAK), bytes_accessed=0, transcendentals=0),
    )(*arrived, prop, image)


def to_near(item, sections):
    return lax.ppermute(item, "sec", [(s, s ^ 1) for s in range(sections)])


def to_across(item, sections):
    return lax.ppermute(item, "sec", [(s, s // GROUP * GROUP + (s % GROUP + CORES) % GROUP) for s in range(sections)])


def to_far(item, sections):
    return lax.ppermute(item, "sec", [(s, s // GROUP * GROUP + (s % GROUP + CORES) % GROUP ^ 1) for s in range(sections)])


def exchange(own, far, across, near, sections):
    return [own, to_far(far, sections), to_across(across, sections), to_near(near, sections)]


def up_shift(sections, k):
    return [(s, s + GROUP * k) for s in range(sections - GROUP * k)]


def maps_up(total_map, sections):
    pairs = []
    for i in range(GROUP):
        if i % CORES == 0:
            pairs += [(GROUP + i, 2 * GROUP + i), (2 * GROUP + i, 3 * GROUP + i)]
        else:
            pairs += [(GROUP + i, 3 * GROUP + i)]
    got = lax.ppermute(total_map, "sec", pairs)
    return got, lax.ppermute(got, "sec", [(s, s ^ 1) for s in range(2 * GROUP, sections)])


def between(item, *planes):
    pairs = [(p * GROUP + i, q * GROUP + i) for p, q in planes for i in range(GROUP)]
    return lax.ppermute(item, "sec", pairs)


def scan_below(total_map, total, sections):
    shift = lax.ppermute(total.astype(F32), "sec", up_shift(sections, 1))
    joined = lax.ppermute(total_map, "sec", up_shift(sections, 1))
    stride = 1
    while stride < sections // GROUP:
        other = lax.ppermute(shift, "sec", up_shift(sections, stride))
        other_map = lax.ppermute(joined, "sec", up_shift(sections, stride))
        shift = shift + dot_wide(other, joined.T)
        joined = dot_wide(joined, other_map)
        stride *= 2
    return shift


def per_device(green, injected, coupling, pattern, owner, pair_blocks):
    sections = lax.axis_size("sec")
    green, inject = green[0], injected[0]

    coupling, tiles = coupling[0], pattern[0].T
    outgoing = outgoing_pairs(owner[:, 0], pair_blocks.T, green, inject, sections)
    received = lax.all_to_all(outgoing, "sec", split_axis=0, concat_axis=0, tiled=True)

    own_map, other_map, *face_rows = face_maps(tiles, green, coupling)
    across = to_across(other_map, sections)
    near = to_near(own_map, sections)

    source = placed_source(received, inject)
    quarters = face_quarters(source, face_rows)
    shifts = exchange(*quarters, sections)
    across = handed_on(across, quarters[0])
    far = to_near(across, sections)
    four = sections // GROUP == 4
    total_map, parts = chain([own_map, far, across, near], BF16 if four else F32)
    early = image_and_maps(green, source, parts)
    maps = maps_up(total_map, sections) if four else []
    total, local = plane_total(shifts, parts, early[0])
    if four:
        fourth = between(total, (1, 2), (2, 3))
        third = between(total, (0, 2), (1, 3))
        second = between(total, (0, 1))
        first = between(total, (0, 3))
        image, upto = image_and_maps(green, source, parts, early)
        entered = entering(entering_kernel, (first, second, third, fourth, *maps, parts, upto, local))
    else:
        base = scan_below(total_map, total, sections)
        image, upto = image_and_maps(green, source, parts, early)
        entered = entering(entering_from_kernel, (base, parts, upto, local))
    arrived = exchange(*entered, sections)
    prop = propagator(tiles, green, coupling, entered[0])
    return final_waves(arrived, prop, image)[None]


def solution(mesh):
    in_specs = (
        P("sec", "grp", None, None),
        P("sec", "grp", None, None),
        P("sec", None, None),
        P("sec", None, None),
        P("sec", None),
        P("sec", None),
    )
    out_specs = P("sec", "grp", None, None)
    return jax.shard_map(
        per_device, mesh=mesh, in_specs=in_specs, out_specs=out_specs, check_vma=False
    )
```
